32 devices in a mesh: dp: 8 (over y, x, core), tensor: 4 (over z).
Axes of the slice: x: 2, y: 2, z: 4, core: 2. Of those that a mesh axis runs over, the one named last changes fastest.
Arguments:
- tokens: bfloat16 [16384, 1024], P(('dp', 'tensor')), may hold values from -6 to 6
- cotangent: bfloat16 [16384, 1024], P(('dp', 'tensor')), may hold values from -6 to 6
- segments: int32 [16384], P('dp'), may hold values from 0 to 18, as said below
- attn_w: float32 [4, 1024, 1024], P(None, 'dp', 'tensor')
- mlp_w: float32 [2, 1024, 4096], P(None, 'dp', 'tensor')
- vectors: float32 [12, 1024], replicated
- attn_mom: float32 [4, 1024, 1024], P(None, 'dp', 'tensor')
- mlp_mom: float32 [2, 1024, 4096], P(None, 'dp', 'tensor')
- vector_mom: float32 [12, 1024], replicated, may hold values from -768 to 768
Outputs:
- block_out: bfloat16 [16384, 1024], P(('dp', 'tensor'))
- dx: float32 [16384, 1024], P(('dp', 'tensor'))
- attn_mom_new: float32 [4, 1024, 1024], P(None, 'dp', 'tensor')
- attn_new: float32 [4, 1024, 1024], P(None, 'dp', 'tensor')
- mlp_mom_new: float32 [2, 1024, 4096], P(None, 'dp', 'tensor')
- mlp_new: float32 [2, 1024, 4096], P(None, 'dp', 'tensor')
- vector_mom_new: float32 [12, 1024], replicated
- vector_new: float32 [12, 1024], replicated
The draws below stay inside these ranges and needn't reach their ends.
Inputs may be any that keep to these rules, and one draw needn't show every extreme that they name: `segments`: within each sequence of 1024 tokens the ids above zero never fall; an id above zero is one document of 60 to 800 tokens, the last document of a sequence possibly cut shorter, and the last document of every sequence has the id 1024 // 60 + 1; zero marks padding of fewer than 60 tokens at a sequence's end.
All inputs are finite; a program needn't handle non-finite values.
Results may differ from the reference program's by a relative error of at most 0.033.
Values may be sent and summed in bfloat16 or wider, within the bound.
A program may use at most 128 MiB of HBM per device.

```python
import math
import jax
import jax.numpy as jnp
from jax import lax

D = 1024
HEADS = 16
HD = 64
FF = 4096
SEQ = 1024
DOC_MIN = 60
DOC_MAX = 800
NS_STEPS = 5
TOKENS = 16384


def draw_segments(key, part):
    key = jax.random.fold_in(key, 5)
    seq_total = TOKENS // SEQ
    most_docs = SEQ // DOC_MIN + 1
    length_key, padding_key = jax.random.split(key)
    doc_lengths = jax.random.randint(length_key, (seq_total, most_docs), DOC_MIN, DOC_MAX + 1)
    doc_ends = jnp.cumsum(doc_lengths, axis=1)
    positions = jnp.arange(SEQ)
    doc_ids = jnp.sum((positions[None, :, None] >= doc_ends[:, None, :]).astype(jnp.int32), axis=2) + 1
    pad_count = jax.random.randint(padding_key, (seq_total, 1), 0, DOC_MIN)
    is_pad = positions[None, :] >= SEQ - pad_count
    last_doc = jnp.max(jnp.where(is_pad, 0, doc_ids), axis=1, keepdims=True)
    shifted = doc_ids + (most_docs - last_doc)
    seg_ids = jnp.where(is_pad, 0, shifted)
    return seg_ids.reshape(TOKENS).astype(jnp.int32)


def draw_attn_w(key, part):
    key = jax.random.fold_in(key, 7)
    base = jax.random.truncated_normal(key, -6.0, 6.0, (4, D, D), jnp.float32)
    factors = jnp.array([1.0, 1.0, 1.0, 2.0], jnp.float32) * D ** (-0.5)
    return base * factors[:, None, None]


def draw_mlp_w(key, part):
    key = jax.random.fold_in(key, 9)
    base = jax.random.truncated_normal(key, -6.0, 6.0, (2, D, FF), jnp.float32)
    factors = jnp.array([D ** (-0.5), FF ** (-0.5)], jnp.float32)
    return base * factors[:, None, None]


def draw_vectors(key, part):
    key = jax.random.fold_in(key, 13)
    base = 0.3 * jax.random.truncated_normal(key, -6.0, 6.0, (12, D), jnp.float32)
    row_ids = jnp.arange(12)[:, None]
    gain_rows = (row_ids == 0) | (row_ids == 5)
    return jnp.where(gain_rows, 1.0 + jnp.tanh(base), base)


def draw_attn_mom(key, part):
    key = jax.random.fold_in(key, 17)
    base = jax.random.truncated_normal(key, -6.0, 6.0, (4, D, D), jnp.float32)
    factors = jnp.array([0.1, 0.1, 1.0, 0.2], jnp.float32) * TOKENS ** 0.5
    return base * factors[:, None, None]


def draw_mlp_mom(key, part):
    key = jax.random.fold_in(key, 19)
    base = jax.random.truncated_normal(key, -6.0, 6.0, (2, D, FF), jnp.float32)
    factors = jnp.array([0.3, 0.6], jnp.float32) * TOKENS ** 0.5
    return base * factors[:, None, None]


def steps_of(rng, extent, cuts, low, top_value):
    level = 1.0
    for axis_at, blocks in cuts:
        draws = jax.random.uniform(jax.random.fold_in(jax.random.fold_in(rng, 6), axis_at), (blocks,), jnp.float32, low / len(cuts), top_value / len(cuts))
        level = level * jnp.repeat(jnp.exp(draws), extent[axis_at] // blocks).reshape((-1,) + (1,) * (len(extent) - 1 - axis_at))
    return level


def noise(rng, dims, width, reach, shards=(), dtype=jnp.bfloat16):
    level = steps_of(rng, dims, shards, -0.22, 0.18) if shards else 1.0
    values = jax.random.normal(rng, dims, jnp.float32) * width * level
    return jnp.minimum(jnp.maximum(values, -reach), reach).astype(dtype)


def setup_inputs(seed: int = 0) -> dict:
    streams_of = jax.random.split(jax.random.key(seed), 10)
    return {
        "tokens": noise(streams_of[0], (TOKENS, D), 1.0, 6.0, ((0, 32),)),
        "cotangent": noise(streams_of[1], (TOKENS, D), 1.0, 6.0, ((0, 32),)),
        "segments": draw_segments(jax.random.fold_in(streams_of[9], 71), 0),
        "attn_w": draw_attn_w(jax.random.fold_in(streams_of[9], 71), 0),
        "mlp_w": draw_mlp_w(jax.random.fold_in(streams_of[9], 71), 0),
        "vectors": draw_vectors(jax.random.fold_in(streams_of[9], 71), 0),
        "attn_mom": draw_attn_mom(jax.random.fold_in(streams_of[9], 71), 0),
        "mlp_mom": draw_mlp_mom(jax.random.fold_in(streams_of[9], 71), 0),
        "vector_mom": noise(streams_of[8], (12, D), (TOKENS ** 0.5), 768.0, (), jnp.float32),
    }


@jax.custom_vjp
def low(v):
    return lax.optimization_barrier(v.astype(jnp.bfloat16)).astype(jnp.float32)

@jax.custom_vjp
def low_back(v):
    return v

def low_keep(v):
    return (low(v), None)

def low_pass(kept, grad):
    return (grad,)

def back_keep(v):
    return (v, None)

def back_low(kept, grad):
    return (low(grad),)
low.defvjp(low_keep, low_pass)
low_back.defvjp(back_keep, back_low)
highest = lax.Precision.HIGHEST
coeff_a = 3.4445
coeff_b = -4.775
coeff_c = 2.0315

def norm_rows(row_data, gain, shift):
    center = lax.optimization_barrier(jnp.mean(row_data, axis=-1, keepdims=True))
    centred = row_data - center
    spread = lax.optimization_barrier(jnp.mean(centred * centred, axis=-1, keepdims=True))
    return centred * lax.rsqrt(spread + 1e-05) * gain + shift

def all_slopes():
    head_ids = jnp.arange(HEADS).astype(jnp.float32)
    return jnp.exp2(-(8.0 / HEADS) * (head_ids + 1.0))

def attend(pieces):
    query, key_rows, value_rows, seg_ids = pieces
    scores = jnp.einsum('qhd,khd->hqk', query, key_rows, precision=highest) * (1.0 / math.sqrt(HD))
    positions = jnp.arange(SEQ)
    distance = (positions[:, None] - positions[None, :]).astype(jnp.float32)
    scores = scores - all_slopes()[:, None, None] * distance[None]
    scores = low_back(scores)
    same_doc = (seg_ids[:, None] == seg_ids[None, :]) & (seg_ids[:, None] > 0) & (positions[None, :] <= positions[:, None])
    allowed = same_doc | (positions[None, :] == positions[:, None])
    scores = jnp.where(allowed[None], scores, -1e+30)
    attn_probs = low(jax.nn.softmax(scores, axis=-1))
    return jnp.einsum('hqk,khd->qhd', attn_probs, value_rows, precision=highest)

def forward(x_rows, attn_w, mlp_w, vectors, seg_ids):
    attn_low = low(attn_w)
    mlp_low = low(mlp_w)
    normed = low(norm_rows(x_rows, vectors[0], vectors[1]))
    query = low_back(low(jnp.dot(normed, attn_low[0], precision=highest) + vectors[2]))
    key_rows = low_back(low(jnp.dot(normed, attn_low[1], precision=highest)))
    value_rows = low_back(low(jnp.dot(normed, attn_low[2], precision=highest) + vectors[3]))
    seq_count = x_rows.shape[0] // SEQ
    seq_shape = (seq_count, SEQ, HEADS, HD)
    mixed = lax.map(jax.checkpoint(attend), (query.reshape(seq_shape), key_rows.reshape(seq_shape), value_rows.reshape(seq_shape), seg_ids.reshape(seq_count, SEQ)))
    mixed = low(low_back(mixed.reshape(x_rows.shape[0], D)))
    branch = low_back(jnp.dot(mixed, attn_low[3].T, precision=highest))
    middle = x_rows + branch + vectors[4]
    hidden_in = low(norm_rows(middle, vectors[5], vectors[6]))
    hidden_bias = vectors[8:].reshape(FF)
    hidden_pre = low_back(jnp.dot(hidden_in, mlp_low[0], precision=highest) + hidden_bias)
    hidden_act = low(jax.nn.gelu(hidden_pre, approximate=True))
    out_branch = low_back(jnp.dot(hidden_act, mlp_low[1].T, precision=highest))
    return middle + out_branch + vectors[7]

def orthogonal(matrix):
    rounded = low(matrix)
    frob_norm = jnp.sqrt(jnp.sum(rounded * rounded))
    iterate = low(rounded / (frob_norm + 1e-06))
    for repeat in range(NS_STEPS):
        square = low(jnp.dot(iterate, iterate.T, precision=highest))
        poly_term = low(coeff_b * square + coeff_c * jnp.dot(square, square, precision=highest))
        iterate = low(coeff_a * iterate + jnp.dot(poly_term, iterate, precision=highest))
    return iterate

def reference(tokens, cotangent, segments, attn_w, mlp_w, vectors, attn_mom, mlp_mom, vector_mom):
    group_size = 4 * SEQ
    group_count = TOKENS // group_size
    inputs = (tokens.astype(jnp.float32).reshape(group_count, group_size, D), cotangent.astype(jnp.float32).reshape(group_count, group_size, D), segments.reshape(group_count, group_size))

    def one_group(totals, pieces):
        x_part, cot_part, seg_part = pieces

        def run_block(x_in, attn_in, mlp_in, vector_in):
            return forward(x_in, attn_in, mlp_in, vector_in, seg_part)
        output, pull_back = jax.vjp(run_block, x_part, attn_w, mlp_w, vectors)
        grad_x, grad_attn, grad_mlp, grad_vec = pull_back(cot_part)
        totals = (totals[0] + grad_attn, totals[1] + grad_mlp, totals[2] + grad_vec)
        return (totals, (output.astype(jnp.bfloat16), grad_x))
    start_totals = (jnp.zeros_like(attn_w), jnp.zeros_like(mlp_w), jnp.zeros_like(vectors))
    totals, results = lax.scan(one_group, start_totals, inputs)
    grad_attn, grad_mlp, grad_vec = totals
    output = results[0].reshape(TOKENS, D)
    grad_tokens = results[1].reshape(TOKENS, D)
    attn_mom_new = 0.5 * attn_mom + grad_attn
    mlp_mom_new = 0.5 * mlp_mom + grad_mlp
    attn_new = jnp.stack([attn_w[index] - math.sqrt(D / D) * orthogonal(attn_mom_new[index]) for index in range(4)])
    mlp_new = jnp.stack([mlp_w[index] - math.sqrt(FF / D) * orthogonal(mlp_mom_new[index]) for index in range(2)])
    vector_mom_new = 0.5 * vector_mom + grad_vec
    vector_new = vectors - 0.1 / math.sqrt(TOKENS) * vector_mom_new
    return (output, grad_tokens, attn_mom_new, attn_new, mlp_mom_new, mlp_new, vector_mom_new, vector_new)
```

```python
import functools
import math

import jax
import jax.numpy as jnp
from jax import lax
from jax.experimental import pallas as pl
from jax.experimental.pallas import tpu as pltpu
from jax.sharding import PartitionSpec as P

D = 1024
HEADS = 16
HD = 64
FF = 4096
SEQ = 1024
NS_STEPS = 5
MESH = pl.DeviceIdType.MESH


coeff_a = 3.4445
coeff_b = -4.775
coeff_c = 2.0315


def norm_rows(row_data, gain, shift):
    center = jnp.mean(row_data, axis=-1, keepdims=True)
    centred = row_data - center
    spread = jnp.mean(centred * centred, axis=-1, keepdims=True)
    return centred * lax.rsqrt(spread + 1e-05) * gain + shift


def gelu_tanh(values):
    return jax.nn.gelu(values, approximate=True)


def contract_last(left, right):
    return lax.dot_general(
        left, right, (((1,), (1,)), ((), ())), preferred_element_type=jnp.float32
    )


def contract_first(left, right):
    return lax.dot_general(
        left, right, (((0,), (0,)), ((), ())), preferred_element_type=jnp.float32
    )


def head_slopes(first_head, head_count):
    head_ids = (first_head + jnp.arange(head_count)).astype(jnp.float32)
    return jnp.exp2(-(8.0 / HEADS) * (head_ids + 1.0))


def masked_scores(row_query, key_rows, row_segs, seg_ids, row_start, slopes):
    scores = jnp.einsum("qhd,khd->hqk", row_query, key_rows, preferred_element_type=jnp.float32) * (
        1.0 / math.sqrt(HD)
    )
    query_pos = row_start + jnp.arange(row_query.shape[0])
    key_pos = jnp.arange(key_rows.shape[0])
    distance = (query_pos[:, None] - key_pos[None, :]).astype(jnp.float32)
    scores = scores - slopes[:, None, None] * distance[None]
    same_doc = (
        (row_segs[:, None] == seg_ids[None, :])
        & (row_segs[:, None] > 0)
        & (key_pos[None, :] <= query_pos[:, None])
    )
    allowed = same_doc | (key_pos[None, :] == query_pos[:, None])
    return jnp.where(allowed[None], scores, -1e30)


def attend_forward(query, key_rows, value_rows, seg_ids, slopes, row_block):
    length = key_rows.shape[0]

    def one_block(row_start):
        row_query = lax.dynamic_slice_in_dim(query, row_start, row_block, 0)
        row_segs = lax.dynamic_slice_in_dim(seg_ids, row_start, row_block, 0)
        scores = masked_scores(row_query, key_rows, row_segs, seg_ids, row_start, slopes)
        row_max = jnp.max(scores, axis=-1, keepdims=True)
        exp_scores = jnp.exp(scores - row_max)
        row_total = jnp.sum(exp_scores, axis=-1, keepdims=True)
        attn_probs = (exp_scores / row_total).astype(jnp.bfloat16)
        mixed = jnp.einsum(
            "hqk,khd->qhd", attn_probs, value_rows, preferred_element_type=jnp.float32
        )
        return (mixed.astype(jnp.bfloat16), (row_max + jnp.log(row_total))[..., 0])

    block_starts = jnp.arange(length // row_block) * row_block
    mixed, log_sums = lax.map(one_block, block_starts)
    return (mixed.reshape(length, -1), log_sums)


def attend_backward(query, key_rows, value_rows, seg_ids, log_sums, grad_mixed, slopes, row_block):
    length, head_count, head_dim = key_rows.shape
    factor = 1.0 / math.sqrt(HD)

    def one_block(carry, pieces):
        row_start, row_lse = pieces
        row_query = lax.dynamic_slice_in_dim(query, row_start, row_block, 0)
        row_grad = lax.dynamic_slice_in_dim(grad_mixed, row_start, row_block, 0)
        row_segs = lax.dynamic_slice_in_dim(seg_ids, row_start, row_block, 0)
        scores = masked_scores(row_query, key_rows, row_segs, seg_ids, row_start, slopes)
        attn_probs = jnp.exp(scores - row_lse[:, :, None])
        grad_probs = jnp.einsum(
            "qhd,khd->hqk", row_grad, value_rows, preferred_element_type=jnp.float32
        )
        inner = jnp.sum(grad_probs * attn_probs, axis=-1, keepdims=True)
        grad_scores = (attn_probs * (grad_probs - inner)).astype(jnp.bfloat16)
        grad_query = (
            jnp.einsum("hqk,khd->qhd", grad_scores, key_rows, preferred_element_type=jnp.float32)
            * factor
        )
        grad_keys = (
            carry[0]
            + jnp.einsum("hqk,qhd->khd", grad_scores, row_query, preferred_element_type=jnp.float32)
            * factor
        )
        grad_values = carry[1] + jnp.einsum(
            "hqk,qhd->khd",
            attn_probs.astype(jnp.bfloat16),
            row_grad,
            preferred_element_type=jnp.float32,
        )
        return ((grad_keys, grad_values), grad_query)

    empty = jnp.zeros((length, head_count, head_dim), jnp.float32)
    block_starts = jnp.arange(length // row_block) * row_block
    (grad_keys, grad_values), grad_query = lax.scan(
        one_block, (empty, empty), (block_starts, log_sums)
    )
    return (
        grad_query.reshape(length, -1),
        grad_keys.reshape(length, -1),
        grad_values.reshape(length, -1),
    )


def newton_rows(row_iterate):
    for repeat in range(NS_STEPS + 1):
        whole_iterate = lax.all_gather(row_iterate, "tensor", axis=0, tiled=True)
        if repeat == NS_STEPS:
            break
        square_rows = contract_last(row_iterate, whole_iterate).astype(jnp.bfloat16)
        whole_square = lax.all_gather(square_rows, "tensor", axis=0, tiled=True)
        poly_rows = (
            coeff_b * square_rows.astype(jnp.float32)
            + coeff_c * jnp.dot(square_rows, whole_square, preferred_element_type=jnp.float32)
        ).astype(jnp.bfloat16)
        row_iterate = (
            coeff_a * row_iterate.astype(jnp.float32)
            + jnp.dot(poly_rows, whole_iterate, preferred_element_type=jnp.float32)
        ).astype(jnp.bfloat16)
    return whole_iterate


def on_device(tokens, cotangent, segments, attn_w, mlp_w, vectors, attn_mom, mlp_mom, vector_mom):
    tensor_size = lax.axis_size("tensor")
    dp_size = lax.axis_size("dp")
    tensor_index = lax.axis_index("tensor")
    dp_index = lax.axis_index("dp")
    row_count = tokens.shape[0]
    model_width = tokens.shape[1]
    local_width = attn_w.shape[2]
    local_hidden = mlp_w.shape[2]
    head_count = local_width // HD
    row_block = min(512, SEQ)
    total_tokens = row_count * tensor_size * dp_size
    gathered_attn, gathered_mlp = (
        lax.all_gather(attn_w.astype(jnp.bfloat16), "dp", axis=1, tiled=True),
        lax.all_gather(mlp_w.astype(jnp.bfloat16), "dp", axis=1, tiled=True),
    )
    hidden_bias = vectors[8:].reshape(-1)
    query_bias = lax.dynamic_slice_in_dim(vectors[2], tensor_index * local_width, local_width)
    value_bias = lax.dynamic_slice_in_dim(vectors[3], tensor_index * local_width, local_width)
    x_rows = tokens.astype(jnp.float32)
    normed, pull_first = jax.vjp(norm_rows, x_rows, vectors[0], vectors[1])
    all_normed = lax.all_gather(normed.astype(jnp.bfloat16), "tensor", axis=0, tiled=True)
    seq_count = all_normed.shape[0] // SEQ
    projected = jnp.einsum(
        "td,mdc->mtc", all_normed, gathered_attn[:3], preferred_element_type=jnp.float32
    )
    query = (projected[0] + query_bias).astype(jnp.bfloat16)
    key_rows = projected[1].astype(jnp.bfloat16)
    value_rows = (projected[2] + value_bias).astype(jnp.bfloat16)
    slopes = head_slopes(tensor_index * head_count, head_count)
    seq_shape = (seq_count, SEQ, head_count, HD)
    seq_segs = segments.reshape(seq_count, SEQ)

    def forward_seq(pieces):
        return attend_forward(pieces[0], pieces[1], pieces[2], pieces[3], slopes, row_block)

    mixed, log_sums = lax.map(
        forward_seq,
        (
            query.reshape(seq_shape),
            key_rows.reshape(seq_shape),
            value_rows.reshape(seq_shape),
            seq_segs,
        ),
    )
    mixed = mixed.reshape(-1, local_width)
    w_out = gathered_attn[3]
    middle = (
        x_rows
        + lax.psum_scatter(
            contract_last(mixed, w_out).astype(jnp.bfloat16),
            "tensor",
            scatter_dimension=0,
            tiled=True,
        ).astype(jnp.float32)
        + vectors[4]
    )
    hidden_normed, pull_second = jax.vjp(norm_rows, middle, vectors[5], vectors[6])
    hidden_low = hidden_normed.astype(jnp.bfloat16)
    grad_rows = cotangent.astype(jnp.float32)
    all_hidden = lax.all_gather(hidden_low, "tensor", axis=0, tiled=True)
    w_up = gathered_mlp[0]
    w_down = gathered_mlp[1]
    bias_local = lax.dynamic_slice_in_dim(hidden_bias, tensor_index * local_hidden, local_hidden)
    hidden_pre = jnp.dot(all_hidden, w_up, preferred_element_type=jnp.float32) + bias_local
    act_float, gelu_pull = jax.vjp(gelu_tanh, hidden_pre)
    hidden_act = act_float.astype(jnp.bfloat16)
    output = (
        middle
        + lax.psum_scatter(
            contract_last(hidden_act, w_down).astype(jnp.bfloat16),
            "tensor",
            scatter_dimension=0,
            tiled=True,
        ).astype(jnp.float32)
        + vectors[7]
    )
    all_grad = lax.all_gather(grad_rows.astype(jnp.bfloat16), "tensor", axis=0, tiled=True)
    grad_down = contract_first(all_grad, hidden_act)
    grad_act = jnp.dot(all_grad, w_down, preferred_element_type=jnp.float32)
    grad_pre = gelu_pull(grad_act)[0].astype(jnp.bfloat16)
    grad_up = contract_first(all_hidden, grad_pre)
    bias_part = jnp.sum(grad_pre, axis=0, dtype=jnp.float32)
    hidden_grad = lax.dynamic_update_slice_in_dim(
        jnp.zeros(hidden_bias.shape, jnp.float32), bias_part, tensor_index * local_hidden, 0
    )
    grad_hidden_in = lax.psum_scatter(
        contract_last(grad_pre, w_up).astype(jnp.bfloat16),
        "tensor",
        scatter_dimension=0,
        tiled=True,
    ).astype(jnp.float32)
    mlp_grads = jnp.stack([grad_up, grad_down])
    second_grads = pull_second(grad_hidden_in)
    grad_middle = grad_rows + second_grads[0]
    all_grad_mid = lax.all_gather(grad_middle.astype(jnp.bfloat16), "tensor", axis=0, tiled=True)
    grad_out_w = contract_first(all_grad_mid, mixed)
    grad_mixed = jnp.dot(all_grad_mid, w_out, preferred_element_type=jnp.float32).astype(
        jnp.bfloat16
    )

    def backward_seq(pieces):
        return attend_backward(
            pieces[0], pieces[1], pieces[2], pieces[3], pieces[4], pieces[5], slopes, row_block
        )

    grad_query, grad_keys, grad_values = lax.map(
        backward_seq,
        (
            query.reshape(seq_shape),
            key_rows.reshape(seq_shape),
            value_rows.reshape(seq_shape),
            seq_segs,
            log_sums,
            grad_mixed.reshape(seq_shape),
        ),
    )
    grad_qkv = (
        jnp.stack([grad_query, grad_keys, grad_values])
        .reshape(3, -1, local_width)
        .astype(jnp.bfloat16)
    )
    grad_proj_w = jnp.einsum(
        "td,mtc->mdc", all_normed, grad_qkv, preferred_element_type=jnp.float32
    )
    bias_sums = jnp.sum(grad_qkv, axis=1, dtype=jnp.float32)
    grad_normed = lax.psum_scatter(
        jnp.einsum(
            "mtc,mdc->td", grad_qkv, gathered_attn[:3], preferred_element_type=jnp.float32
        ).astype(jnp.bfloat16),
        "tensor",
        scatter_dimension=0,
        tiled=True,
    ).astype(jnp.float32)
    first_grads = pull_first(grad_normed)
    grad_tokens = grad_middle + first_grads[0]

    def placed(piece, full_size, offset):
        return lax.dynamic_update_slice_in_dim(
            jnp.zeros((full_size,), jnp.float32), piece, offset, 0
        )

    width_offset = tensor_index * local_width
    vector_rows = jnp.stack(
        [
            first_grads[1],
            first_grads[2],
            placed(bias_sums[0], model_width, width_offset),
            placed(bias_sums[2], model_width, width_offset),
            jnp.sum(grad_middle, axis=0),
            second_grads[1],
            second_grads[2],
            jnp.sum(grad_rows, axis=0),
        ]
    )
    vector_local = jnp.concatenate([vector_rows, hidden_grad.reshape(4, model_width)], axis=0)
    attn_grads = jnp.concatenate([grad_proj_w, grad_out_w[None]], axis=0)
    attn_sum, mlp_sum = (
        lax.psum_scatter(
            attn_grads.astype(jnp.bfloat16), "dp", scatter_dimension=1, tiled=True
        ).astype(jnp.float32),
        lax.psum_scatter(
            mlp_grads.astype(jnp.bfloat16), "dp", scatter_dimension=1, tiled=True
        ).astype(jnp.float32),
    )
    attn_mom_new = 0.5 * attn_mom + attn_sum
    mlp_mom_new = 0.5 * mlp_mom + mlp_sum
    attn_round = attn_mom_new.astype(jnp.bfloat16)
    mlp_round = mlp_mom_new.astype(jnp.bfloat16)
    attn_float = attn_round.astype(jnp.float32)
    mlp_float = mlp_round.astype(jnp.float32)
    norm_parts = jnp.concatenate(
        [jnp.sum(attn_float * attn_float, axis=(1, 2)), jnp.sum(mlp_float * mlp_float, axis=(1, 2))]
    )
    vector_grads, norm_sums = lax.psum((vector_local, norm_parts), ("dp", "tensor"))
    frob_norms = jnp.sqrt(norm_sums)
    owners = [order * dp_size // 6 for order in range(6)]
    owned_norm = jnp.zeros((), jnp.float32)
    for order in range(6):
        owned_norm = owned_norm + jnp.where(dp_index == owners[order], frob_norms[order], 0.0)
    block_rows = attn_w.shape[1]
    slice_rows = model_width // tensor_size
    full_cols = local_hidden * tensor_size
    rows_attn, rows_mlp = (
        lax.all_gather(attn_round, "tensor", axis=2, tiled=True),
        lax.all_gather(mlp_round, "tensor", axis=2, tiled=True),
    )
    padded_attn = jnp.pad(rows_attn, ((0, 0), (0, 0), (0, full_cols - model_width)))
    all_rows = jnp.concatenate([padded_attn, rows_mlp], axis=0)
    outgoing = jnp.zeros((dp_size, block_rows, full_cols), jnp.bfloat16)
    for order in range(6):
        outgoing = outgoing.at[owners[order]].set(all_rows[order])
    incoming = lax.all_to_all(outgoing, "dp", split_axis=0, concat_axis=0, tiled=True)
    owned_whole = incoming.reshape(model_width, full_cols)
    mine = lax.dynamic_slice_in_dim(owned_whole, tensor_index * slice_rows, slice_rows, 0)
    attn_col = tensor_index * local_width
    row_iterate = (mine.astype(jnp.float32) / (owned_norm + 1e-06)).astype(jnp.bfloat16)
    result = newton_rows(row_iterate)
    returned = lax.all_to_all(
        result.reshape(dp_size, block_rows, full_cols),
        "dp",
        split_axis=0,
        concat_axis=0,
        tiled=True,
    )
    attn_blocks = []
    for order in range(4):
        piece = lax.dynamic_slice_in_dim(returned[owners[order]], attn_col, local_width, 1)
        attn_blocks.append(attn_w[order] - piece.astype(jnp.float32))
    mlp_blocks = []
    for order in range(2):
        piece = lax.dynamic_slice_in_dim(
            returned[owners[4 + order]], tensor_index * local_hidden, local_hidden, 1
        )
        mlp_blocks.append(mlp_w[order] - math.sqrt(FF / D) * piece.astype(jnp.float32))
    attn_new = jnp.stack(attn_blocks)
    mlp_new = jnp.stack(mlp_blocks)
    vector_mom_new = 0.5 * vector_mom + vector_grads
    vector_new = vectors - 0.1 / math.sqrt(total_tokens) * vector_mom_new
    return (
        output.astype(jnp.bfloat16),
        grad_tokens,
        attn_mom_new,
        attn_new,
        mlp_mom_new,
        mlp_new,
        vector_mom_new,
        vector_new,
    )


CORES = 2


class Place:
    def __init__(self):
        self.dp = lax.axis_index("dp")
        self.tensor = lax.axis_index("tensor")
        self.core = lax.rem(self.dp, 2)
        self.chip = self.dp // 2
        self.x = lax.rem(self.chip, 2)
        self.y = self.chip // 2
        self.twin = (self.dp + 1 - 2 * self.core, self.tensor)
        self.across_x = (self.dp + 2 - 4 * self.x, self.tensor)
        self.across_y = (self.dp + 4 - 8 * self.y, self.tensor)
        self.right = (self.dp, self.tensor + 1)
        self.left = (self.dp, self.tensor - 1)


def greet(place, line):
    barrier = pltpu.get_barrier_semaphore()

    def signal(device):
        pl.semaphore_signal(barrier, inc=1, device_id=device, device_id_type=MESH)

    signal(place.twin)
    signal(place.across_x)
    signal(place.across_y)

    for other in range(line):

        @pl.when(place.tensor != other)
        def _():
            signal((place.dp, other))

    pl.semaphore_wait(barrier, 3 + line - 1)


def columns(start, size):
    return pl.ds(pl.multiple_of(start, 128), size)


def gather_kernel(line, attn_ref, mlp_ref, qkv_ref, out_ref, up_ref, down_ref, own_sem, send_sem, recv_sem):
    place = Place()
    x, y, t = place.x, place.y, place.tensor
    narrow = attn_ref.shape[2] // 2
    wide = mlp_ref.shape[2] // 4

    def attn_source(lo, hi):
        return lambda core: attn_ref.at[lo:hi, :, columns(core * narrow, narrow)]

    def mlp_source(index, part):
        return lambda core: mlp_ref.at[index : index + 1, :, columns((2 * core + part) * wide, wide)]

    groups = [
        (qkv_ref, narrow, attn_source(0, 3)),
        (out_ref, narrow, attn_source(3, 4)),
        (up_ref.at[0:1], wide, mlp_source(0, 0)),
        (up_ref.at[1:2], wide, mlp_source(0, 1)),
        (down_ref.at[0:1], wide, mlp_source(1, 0)),
        (down_ref.at[1:2], wide, mlp_source(1, 1)),
    ]
    greet(place, line)

    def copy(group, slot, source, target, device):
        return pltpu.make_async_remote_copy(
            src_ref=source,
            dst_ref=target,
            send_sem=send_sem.at[group, slot],
            recv_sem=recv_sem.at[group, slot],
            device_id=device,
            device_id_type=MESH,
        )

    def same(group, slot, region, device):
        return copy(group, slot, region, region, device)

    def chunk(group, index):
        ref, width, _ = groups[group]
        return ref.at[:, y, x, :, :, columns(index * width, width)]

    def corner(group, ys, xs, half):
        return groups[group][0].at[:, ys, xs, half]

    def entry(group, half):
        ref, width, _ = groups[group]
        return ref.at[:, y, x, half, :, columns(t * width, width)]

    both = pl.ds(0, 2)
    steps = range(1, line)
    to_right, to_left, half_x, half_y, rest_y, rest_x = 1, line, 2 * line - 1, 2 * line, 2 * line + 1, 2 * line + 2

    def own(group):
        return pltpu.make_async_copy(
            groups[group][2](place.core), entry(group, place.core), own_sem.at[group]
        )

    def first(group):
        target = entry(group, place.core)
        return copy(group, 0, groups[group][2](1 - place.core), target, place.twin)

    def start_line(group):
        own(group).wait()
        same(group, 0, entry(group, 1 - place.core), place.twin).wait_recv()

        @pl.when(t < line - 1)
        def _():
            same(group, to_right, chunk(group, t), place.right).start()

        @pl.when(t > 0)
        def _():
            same(group, to_left, chunk(group, t), place.left).start()

    def run_line(group):
        for step in steps:

            @pl.when(t >= step)
            def _():
                same(group, to_right + step - 1, chunk(group, t - step), place.left).wait_recv()
                if step < line - 1:

                    @pl.when(t < line - 1)
                    def _():
                        same(group, to_right + step, chunk(group, t - step), place.right).start()

            @pl.when(t + step <= line - 1)
            def _():
                same(group, to_left + step - 1, chunk(group, t + step), place.right).wait_recv()
                if step < line - 1:

                    @pl.when(t > 0)
                    def _():
                        same(group, to_left + step, chunk(group, t + step), place.left).start()

    def start_plane(group):
        same(group, half_x, corner(group, y, x, 0), place.across_x).start()
        same(group, half_y, corner(group, y, x, 1), place.across_y).start()

    def run_plane(group):
        same(group, half_x, corner(group, y, 1 - x, 0), place.across_x).wait_recv()
        same(group, rest_y, corner(group, y, both, 0), place.across_y).start()
        same(group, half_y, corner(group, 1 - y, x, 1), place.across_y).wait_recv()
        same(group, rest_x, corner(group, both, x, 1), place.across_x).start()

    def end_plane(group):
        same(group, rest_y, corner(group, 1 - y, both, 0), place.across_y).wait_recv()
        same(group, rest_x, corner(group, both, 1 - x, 1), place.across_x).wait_recv()

    def wait_sends(group):
        first(group).wait_send()
        for step in steps:

            @pl.when((t - step + 1 >= 0) & (t < line - 1))
            def _():
                same(group, to_right + step - 1, chunk(group, t - step + 1), place.right).wait_send()

            @pl.when((t + step - 1 <= line - 1) & (t > 0))
            def _():
                same(group, to_left + step - 1, chunk(group, t + step - 1), place.left).wait_send()

        same(group, half_x, corner(group, y, x, 0), place.across_x).wait_send()
        same(group, half_y, corner(group, y, x, 1), place.across_y).wait_send()
        same(group, rest_y, corner(group, y, both, 0), place.across_y).wait_send()
        same(group, rest_x, corner(group, both, x, 1), place.across_x).wait_send()

    count = len(groups)
    for group in range(count):
        own(group).start()
        first(group).start()
    for group in range(count):
        start_line(group)
    for group in range(count + 1):
        if group < count:
            run_line(group)
            start_plane(group)
        if group >= 1:
            run_plane(group - 1)
    for group in range(count):
        end_plane(group)
    for group in range(count):
        wait_sends(group)


def gather_weights(attn_low, mlp_low, line):
    narrow = attn_low.shape[2] // 2 * line
    wide = mlp_low.shape[2] // 4 * line
    rows = attn_low.shape[1]
    shapes = [(3, narrow), (1, narrow), (2, wide), (2, wide)]
    slots = 2 * line + 3
    gathered = pl.pallas_call(
        functools.partial(gather_kernel, line),
        out_shape=[
            jax.ShapeDtypeStruct((count, 2, 2, 2, rows, width), jnp.bfloat16) for count, width in shapes
        ],
        in_specs=[pl.BlockSpec(memory_space=pl.ANY)] * 2,
        out_specs=[pl.BlockSpec(memory_space=pl.ANY)] * 4,
        scratch_shapes=[
            pltpu.SemaphoreType.DMA((6,)),
            pltpu.SemaphoreType.DMA((6, slots)),
            pltpu.SemaphoreType.DMA((6, slots)),
        ],
        compiler_params=pltpu.CompilerParams(collective_id=1, has_side_effects=True),
        name="gather_weights",
    )(attn_low, mlp_low)
    return [whole.reshape(whole.shape[0], 8 * rows, -1) for whole in gathered]


def add_blocks(target, sources):
    count, rows = target.shape[0], target.shape[1]
    per = rows // 32

    def body(step, carry):
        at = (step // per, pl.ds(pl.multiple_of(lax.rem(step, per) * 32, 32), 32))
        total = sources[0][at].astype(jnp.float32)
        for source in sources[1:]:
            total = total + source[at].astype(jnp.float32)
        target[at] = total.astype(target.dtype)
        return carry

    lax.fori_loop(0, count * per, body, 0)


def sum_kernel(line, down_ref, up_ref, out_ref, qkv_ref, vec_ref, attn_home, mlp_home, vec_out, *scratch):
    place = Place()
    x, y, t, core = place.x, place.y, place.tensor, place.core
    group_count = 6
    names = ("own_a", "own_b", "got_a", "got_b", "last_a", "last_b", "plane", "from_left", "from_right", "done")
    buffers = []
    for group in range(group_count):
        start = group * len(names)
        buffers.append(dict(zip(names, scratch[start : start + len(names)])))
    own_sem, send_sem, recv_sem, vec_sum, vec_got, vec_line, vec_sem = scratch[group_count * len(names) :]
    narrow = attn_home.shape[2] // 2
    wide = mlp_home.shape[2] // 4

    def attn_target(lo, hi):
        return lambda: attn_home.at[lo:hi, :, columns(core * narrow, narrow)]

    def mlp_target(index, part):
        return lambda: mlp_home.at[index : index + 1, :, columns((2 * core + part) * wide, wide)]

    groups = [
        (down_ref.at[0:1], wide, mlp_target(1, 0)),
        (down_ref.at[1:2], wide, mlp_target(1, 1)),
        (up_ref.at[0:1], wide, mlp_target(0, 0)),
        (up_ref.at[1:2], wide, mlp_target(0, 1)),
        (out_ref, narrow, attn_target(3, 4)),
        (qkv_ref, narrow, attn_target(0, 3)),
    ]
    greet(place, line)
    both = pl.ds(0, 2)
    one_a, one_b, two_a, two_b, home_slot = 0, 1, 2, 3, 4
    rightward, leftward = 5, 5 + line

    def copy(group, slot, source, target, device):
        return pltpu.make_async_remote_copy(
            src_ref=source,
            dst_ref=target,
            send_sem=send_sem.at[group, slot],
            recv_sem=recv_sem.at[group, slot],
            device_id=device,
            device_id_type=MESH,
        )

    def loads(group):
        ref, held = groups[group][0], buffers[group]
        return (
            pltpu.make_async_copy(ref.at[:, y, both, 0], held["own_a"], own_sem.at[group, 0]),
            pltpu.make_async_copy(ref.at[:, both, x, 1], held["own_b"], own_sem.at[group, 1]),
        )

    def first_copies(group):
        ref, held = groups[group][0], buffers[group]
        return (
            copy(group, one_a, ref.at[:, 1 - y, both, 0], held["got_a"], place.across_y),
            copy(group, one_b, ref.at[:, both, 1 - x, 1], held["got_b"], place.across_x),
        )

    def second_copies(group):
        held = buffers[group]
        return (
            copy(group, two_a, held["own_a"].at[:, 1 - x], held["last_a"], place.across_x),
            copy(group, two_b, held["own_b"].at[:, 1 - y], held["last_b"], place.across_y),
        )

    def start(group):
        for each in first_copies(group) + loads(group):
            each.start()

    def plane_one(group):
        held = buffers[group]
        sends = second_copies(group)
        for part, other, mine in (("a", 1 - x, x), ("b", 1 - y, y)):
            index = 0 if part == "a" else 1
            loads(group)[index].wait()
            first_copies(group)[index].wait_recv()
            own, got = held["own_" + part], held["got_" + part]
            add_blocks(own.at[:, other], (own.at[:, other], got.at[:, other]))
            sends[index].start()
            add_blocks(own.at[:, mine], (own.at[:, mine], got.at[:, mine]))

    def plane_two(group):
        held = buffers[group]
        for index, (part, mine) in enumerate((("a", x), ("b", y))):
            second_copies(group)[index].wait_recv()
            add_blocks(held["plane"].at[:, index], (held["own_" + part].at[:, mine], held["last_" + part]))

    def piece(group, name, index, half):
        width = groups[group][1]
        return buffers[group][name].at[:, half, :, index * width : (index + 1) * width]

    def hop(group, index, right):
        width = groups[group][1]
        cut = slice(index * width, (index + 1) * width)
        held = buffers[group]
        slot = (rightward if right else leftward) + index
        target = held["from_left" if right else "from_right"]
        return copy(
            group, slot, held["plane"].at[:, :, :, cut], target.at[:, :, :, cut], place.right if right else place.left
        )

    def run_line(group):
        for step in range(line - 1):
            for right in (True, False):
                index = line - 1 - step if right else step
                name = "from_left" if right else "from_right"

                @pl.when((t < index) if right else (t > index))
                def _():
                    @pl.when((t > 0) if right else (t < line - 1))
                    def _():
                        hop(group, index, right).wait_recv()
                        for half in range(2):
                            plane = piece(group, "plane", index, half)
                            add_blocks(plane, (plane, piece(group, name, index, half)))

                    hop(group, index, right).start()

    def end_line(group):
        held = buffers[group]
        for index in range(line):

            @pl.when(t == index)
            def _():
                names = ["plane"]
                if index > 0:
                    hop(group, index, True).wait_recv()
                    names.append("from_left")
                if index < line - 1:
                    hop(group, index, False).wait_recv()
                    names.append("from_right")
                for half in range(2):
                    add_blocks(held["done"].at[:, half], [piece(group, name, index, half) for name in names])

        for each in homes(group):
            each.start()

    def homes(group):
        done, target = buffers[group]["done"], groups[group][2]
        return (
            pltpu.make_async_copy(done.at[:, core], target(), own_sem.at[group, 2]),
            copy(group, home_slot, done.at[:, 1 - core], target(), place.twin),
        )

    def finish(group):
        local, remote = homes(group)
        local.wait()
        remote.wait()
        for each in first_copies(group) + second_copies(group):
            each.wait_send()
        for step in range(line - 1):
            for right in (True, False):
                index = line - 1 - step if right else step

                @pl.when((t < index) if right else (t > index))
                def _():
                    hop(group, index, right).wait_send()

    partners = (place.twin, place.across_x, place.across_y)

    def vec_copy(stage):
        return pltpu.make_async_remote_copy(
            src_ref=vec_sum.at[stage],
            dst_ref=vec_got.at[stage],
            send_sem=vec_sem.at[0, stage],
            recv_sem=vec_sem.at[1, stage],
            device_id=partners[stage],
            device_id_type=MESH,
        )

    def vec_hop(other, source):
        return pltpu.make_async_remote_copy(
            src_ref=vec_sum.at[3],
            dst_ref=vec_line.at[source],
            send_sem=vec_sem.at[2, other],
            recv_sem=vec_sem.at[3, source],
            device_id=(place.dp, other),
            device_id_type=MESH,
        )

    def vec_step(stage):
        if 0 < stage <= 3:
            vec_copy(stage - 1).wait()
            vec_sum[stage] = vec_sum[stage - 1] + vec_got[stage - 1]
        if stage < 3:
            vec_copy(stage).start()
        if stage == 3:
            vec_line[t] = vec_sum[3]
        for other in range(line):

            @pl.when(t != other)
            def _():
                if stage == 3:
                    vec_hop(other, t).start()
                if stage == 4:
                    vec_hop(other, t).wait_send()
                    vec_hop(t, other).wait_recv()

        if stage == 4:
            total = vec_line[0]
            for other in range(1, line):
                total = total + vec_line[other]
            vec_out[...] = total

    vec_sum[0] = vec_ref[...]
    for group in range(group_count):
        start(group)
    for group in range(group_count + 2):
        if group < 5:
            vec_step(group)
        if group < group_count:
            plane_one(group)
        if 1 <= group <= group_count:
            plane_two(group - 1)
            run_line(group - 1)
        if group >= 2:
            end_line(group - 2)
    for group in range(group_count):
        finish(group)


def sum_gradients(down, up, out, qkv, vec, line):
    rows = qkv.shape[1] // 8
    narrow, wide = qkv.shape[2], down.shape[2]
    counts = [(1, wide)] * 4 + [(1, narrow), (3, narrow)]
    scratch = []
    for count, width in counts:
        pair = pltpu.VMEM((count, 2, rows, width), jnp.bfloat16)
        single = pltpu.VMEM((count, rows, width), jnp.bfloat16)
        done = pltpu.VMEM((count, 2, rows, width // line), jnp.bfloat16)
        scratch += [pair] * 4 + [single] * 2 + [pair] * 3 + [done]
    slots = 5 + 2 * line
    return pl.pallas_call(
        functools.partial(sum_kernel, line),
        out_shape=[
            jax.ShapeDtypeStruct((4, rows, 2 * narrow // line), jnp.bfloat16),
            jax.ShapeDtypeStruct((2, rows, 4 * wide // line), jnp.bfloat16),
            jax.ShapeDtypeStruct(vec.shape, jnp.float32),
        ],
        in_specs=[pl.BlockSpec(memory_space=pl.ANY)] * 4 + [pl.BlockSpec(memory_space=pltpu.VMEM)],
        out_specs=[pl.BlockSpec(memory_space=pl.ANY)] * 2 + [pl.BlockSpec(memory_space=pltpu.VMEM)],
        scratch_shapes=scratch
        + [
            pltpu.SemaphoreType.DMA((6, 3)),
            pltpu.SemaphoreType.DMA((6, slots)),
            pltpu.SemaphoreType.DMA((6, slots)),
            pltpu.VMEM((4,) + vec.shape, jnp.float32),
            pltpu.VMEM((3,) + vec.shape, jnp.float32),
            pltpu.VMEM((line,) + vec.shape, jnp.float32),
            pltpu.SemaphoreType.DMA((4, max(line, 3))),
        ],
        compiler_params=pltpu.CompilerParams(
            collective_id=2, has_side_effects=True, vmem_limit_bytes=48 * 1024 * 1024
        ),
        name="sum_gradients",
    )(*(each.reshape(each.shape[0], 2, 2, 2, rows, each.shape[2]) for each in (down, up, out, qkv)), vec)


LOG2E = 1.4426950408889634
FAR = 1e32
ROW_BLOCK = 256


def fill_distance(seg_rows, seg_cols, distance):
    def body(step, carry):
        start = pl.multiple_of(step * 64, 64)
        shape = (64, distance.shape[1])
        row = lax.broadcasted_iota(jnp.int32, shape, 0) + start
        col = lax.broadcasted_iota(jnp.int32, shape, 1)
        segs = seg_rows[pl.ds(start, 64), :]
        same = (segs == seg_cols[...]) & (segs > 0) & (col <= row)
        allowed = same | (col == row)
        distance[pl.ds(start, 64), :] = jnp.where(allowed, (row - col).astype(jnp.float32), FAR)
        return carry

    lax.fori_loop(0, distance.shape[0] // 64, body, 0)


def head_lanes(dtype):
    lane = lax.broadcasted_iota(jnp.int32, (1, 2 * HD), 1)
    first = (lane < HD).astype(jnp.float32)
    return (first.astype(dtype), (1.0 - first).astype(dtype))


def attend_kernel(slopes, seg_rows, seg_cols, qkv, mixed, lse, distance):
    group = pl.program_id(0)
    length = qkv.shape[1]

    @pl.when(group == 0)
    def _():
        fill_distance(seg_rows, seg_cols, distance)

    masks = head_lanes(jnp.bfloat16)
    first = head_lanes(jnp.float32)[0] > 0.5
    factor = LOG2E / math.sqrt(HD)
    keys_t = qkv[1].T
    for start in range(0, length, ROW_BLOCK):
        stop = start + ROW_BLOCK
        rows = slice(start, stop)
        parts, sums = [], []
        for head in range(2):
            slope = slopes[2 * group + head] * LOG2E
            scores = jnp.dot(
                qkv[0, rows, :] * masks[head], keys_t[:, :stop], preferred_element_type=jnp.float32
            )
            scores = scores * factor - slope * distance[rows, :stop]
            top = jnp.max(scores, axis=1, keepdims=True)
            probs = jnp.exp2(scores - top)
            total = jnp.sum(probs, axis=1, keepdims=True)
            out = jnp.dot(probs.astype(jnp.bfloat16), qkv[2, :stop, :], preferred_element_type=jnp.float32)
            parts.append(out / total)
            sums.append(top + jnp.log2(total))
        mixed[rows, :] = jnp.where(first, parts[0], parts[1]).astype(jnp.bfloat16)
        lse[rows, :] = jnp.where(first, sums[0], sums[1])


def attend_back_kernel(slopes, seg_rows, seg_cols, qkv, grad, mixed, lse, out, distance, dk_acc, dv_acc):
    group = pl.program_id(0)
    length = qkv.shape[1]

    @pl.when(group == 0)
    def _():
        fill_distance(seg_rows, seg_cols, distance)

    masks = head_lanes(jnp.bfloat16)
    wide_masks = head_lanes(jnp.float32)
    first = wide_masks[0] > 0.5
    factor = LOG2E / math.sqrt(HD)
    shrink = 1.0 / math.sqrt(HD)
    keys_t = qkv[1].T
    values_t = qkv[2].T
    dk_acc[...] = jnp.zeros_like(dk_acc)
    dv_acc[...] = jnp.zeros_like(dv_acc)
    for start in range(0, length, ROW_BLOCK):
        stop = start + ROW_BLOCK
        rows = slice(start, stop)
        query, grads = qkv[0, rows, :], grad[rows, :]
        query_t, grads_t = query.T, grads.T
        product = grads.astype(jnp.float32) * mixed[rows, :].astype(jnp.float32)
        parts = []
        for head in range(2):
            slope = slopes[2 * group + head] * LOG2E
            lanes = slice(head * HD, (head + 1) * HD)
            scores = jnp.dot(query * masks[head], keys_t[:, :stop], preferred_element_type=jnp.float32)
            log_sum = lse[rows, head * HD : head * HD + 1]
            probs = jnp.exp2(scores * factor - slope * distance[rows, :stop] - log_sum)
            grad_probs = jnp.dot(grads * masks[head], values_t[:, :stop], preferred_element_type=jnp.float32)
            inner = jnp.sum(product * wide_masks[head], axis=1, keepdims=True)
            grad_scores = (probs * (grad_probs - inner)).astype(jnp.bfloat16)
            parts.append(jnp.dot(grad_scores, qkv[1, :stop, :], preferred_element_type=jnp.float32))
            dk_acc[lanes, :stop] += jnp.dot(query_t[lanes, :], grad_scores, preferred_element_type=jnp.float32)
            dv_acc[lanes, :stop] += jnp.dot(
                grads_t[lanes, :], probs.astype(jnp.bfloat16), preferred_element_type=jnp.float32
            )
        out[0, rows, :] = (jnp.where(first, parts[0], parts[1]) * shrink).astype(jnp.bfloat16)
    out[1] = (dk_acc[...].T * shrink).astype(jnp.bfloat16)
    out[2] = dv_acc[...].T.astype(jnp.bfloat16)


def attention_specs(length):
    return [
        pl.BlockSpec(memory_space=pltpu.SMEM),
        pl.BlockSpec((length, 1), lambda g: (0, 0)),
        pl.BlockSpec((1, length), lambda g: (0, 0)),
        pl.BlockSpec((3, length, 2 * HD), lambda g: (0, 0, g)),
    ]


def attend(slopes, seg_ids, qkv):
    _, length, width = qkv.shape
    rows = pl.BlockSpec((length, 2 * HD), lambda g: (0, g))
    return pl.pallas_call(
        attend_kernel,
        grid=(width // (2 * HD),),
        out_shape=[
            jax.ShapeDtypeStruct((length, width), jnp.bfloat16),
            jax.ShapeDtypeStruct((length, width), jnp.float32),
        ],
        in_specs=attention_specs(length),
        out_specs=[rows, rows],
        scratch_shapes=[pltpu.VMEM((length, length), jnp.float32)],
        compiler_params=pltpu.CompilerParams(vmem_limit_bytes=48 * 1024 * 1024),
        name="attend",
    )(slopes, seg_ids.reshape(-1, 1), seg_ids.reshape(1, -1), qkv)


def attend_back(slopes, seg_ids, qkv, grad, mixed, lse):
    _, length, width = qkv.shape
    rows = pl.BlockSpec((length, 2 * HD), lambda g: (0, g))
    return pl.pallas_call(
        attend_back_kernel,
        grid=(width // (2 * HD),),
        out_shape=jax.ShapeDtypeStruct(qkv.shape, jnp.bfloat16),
        in_specs=attention_specs(length) + [rows] * 3,
        out_specs=pl.BlockSpec((3, length, 2 * HD), lambda g: (0, 0, g)),
        scratch_shapes=[
            pltpu.VMEM((length, length), jnp.float32),
            pltpu.VMEM((2 * HD, length), jnp.float32),
            pltpu.VMEM((2 * HD, length), jnp.float32),
        ],
        compiler_params=pltpu.CompilerParams(vmem_limit_bytes=48 * 1024 * 1024),
        name="attend_back",
    )(slopes, seg_ids.reshape(-1, 1), seg_ids.reshape(1, -1), qkv, grad, mixed, lse)


OWNERS = ((0, 0), (3, 0), (1, 3), (2, 3), (0, 1), (3, 2))


def newton_kernel(line, attn_ref, mlp_ref, attn_home, mlp_home, thin, full, gram, sent, got, poly, norm_own, norm_got,
                  home_sem, start_sem, send_sem, back_sem, norm_sem, block_send, block_recv):
    place = Place()
    d, t, core = place.dp, place.tensor, place.core
    me = d * line + t
    devices = 8 * line
    rows = attn_ref.shape[1]
    narrow, wide = attn_ref.shape[2] // 2, mlp_ref.shape[2] // 2
    barrier = pltpu.get_barrier_semaphore()

    def place_of(index):
        return (index // line, lax.rem(index, line))

    def meet(step, carry):
        pl.semaphore_signal(
            barrier, inc=1, device_id=place_of(lax.rem(me + step, devices)), device_id_type=MESH
        )
        return carry

    lax.fori_loop(1, devices, meet, 0)
    pl.semaphore_wait(barrier, devices - 1)

    jobs = []
    for order, (chip, z) in enumerate(OWNERS):
        for half in range(2):
            jobs.append((order, half, (2 * chip + half) * line + min(z, line - 1)))

    def source(order, half):
        if order < 4:
            return attn_ref.at[order, :, half * narrow : (half + 1) * narrow]
        return mlp_ref.at[order - 4, :, half * wide : (half + 1) * wide]

    def held(order, index):
        dp, tensor = place_of(index)
        row = pl.ds(pl.multiple_of(dp * rows, rows), rows)
        if order < 4:
            return thin.at[row, columns(tensor * narrow, narrow)]
        return full.at[row, columns(tensor * wide, wide)]

    def target(order, half):
        if order < 4:
            return attn_home.at[order, :, half * narrow : (half + 1) * narrow]
        return mlp_home.at[order - 4, :, half * wide : (half + 1) * wide]

    def remote(order, half, index):
        return pltpu.make_async_remote_copy(
            src_ref=source(order, half),
            dst_ref=held(order, me),
            send_sem=home_sem.at[order, half],
            recv_sem=start_sem.at[0],
            device_id=place_of(index),
            device_id_type=MESH,
        )

    def local(order, half):
        return pltpu.make_async_copy(source(order, half), held(order, me), start_sem.at[0])

    for order, half, owner in jobs:

        @pl.when(me == owner)
        def _():
            local(order, half).start()

        @pl.when(me != owner)
        def _():
            remote(order, half, owner).start()

    def contract_rows(left, right):
        return lax.dot_general(left, right, (((1,), (1,)), ((), ())), preferred_element_type=jnp.float32)

    def orthogonalize(matrix):
        size, width = matrix.shape
        block = 256
        pltpu.make_async_copy(matrix, matrix, start_sem.at[0]).wait()

        def add_squares(step, total):
            piece = matrix[pl.ds(pl.multiple_of(step * 32, 32), 32), :].astype(jnp.float32)
            piece = piece * piece
            return total + jnp.sum(piece.reshape(4, 8, width // 128, 128), axis=(0, 2))

        squares = lax.fori_loop(0, size // 32, add_squares, jnp.zeros((8, 128), jnp.float32))
        norm_own[...] = jnp.zeros((8, 128), jnp.float32) + jnp.sum(squares)
        swap = pltpu.make_async_remote_copy(
            src_ref=norm_own,
            dst_ref=norm_got,
            send_sem=norm_sem.at[0],
            recv_sem=norm_sem.at[1],
            device_id=place.twin,
            device_id_type=MESH,
        )
        swap.start()
        swap.wait()
        scale = 1.0 / (jnp.sqrt(norm_own[...] + norm_got[...]) + 1e-06)
        scale = scale[0:1, 0:1]

        def scale_rows(step, carry):
            at = pl.ds(pl.multiple_of(step * 32, 32), 32)
            matrix[at, :] = (matrix[at, :].astype(jnp.float32) * scale).astype(jnp.bfloat16)
            return carry

        lax.fori_loop(0, size // 32, scale_rows, 0)
        blocks = size // block

        def swap_block(slot, index):
            return pltpu.make_async_remote_copy(
                src_ref=sent.at[index],
                dst_ref=got.at[slot, index],
                send_sem=block_send.at[index],
                recv_sem=block_recv.at[slot, index],
                device_id=place.twin,
                device_id_type=MESH,
            )

        for repeat in range(NS_STEPS):
            slot = repeat % 2

            def share(index, carry):
                at = pl.ds(pl.multiple_of(index * block, block), block)
                sent[index] = contract_rows(matrix[at, :], matrix[...]).astype(jnp.bfloat16)
                swap_block(slot, index).start()
                return carry

            lax.fori_loop(0, blocks, share, 0)

            def add(index, carry):
                at = pl.ds(pl.multiple_of(index * block, block), block)
                swap_block(slot, index).wait()
                total = sent[index].astype(jnp.float32) + got[slot, index].astype(jnp.float32)
                gram[at, :] = total.astype(jnp.bfloat16)
                return carry

            lax.fori_loop(0, blocks, add, 0)

            def polynomial(index, carry):
                at = pl.ds(pl.multiple_of(index * block, block), block)
                square = jnp.dot(gram[at, :], gram[...], preferred_element_type=jnp.float32)
                poly[at, :] = (coeff_b * gram[at, :].astype(jnp.float32) + coeff_c * square).astype(jnp.bfloat16)
                return carry

            lax.fori_loop(0, blocks, polynomial, 0)

            def advance(index, carry):
                at = columns(index * block, block)
                piece = matrix[:, at]
                moved = jnp.dot(poly[...], piece, preferred_element_type=jnp.float32)
                matrix[:, at] = (coeff_a * piece.astype(jnp.float32) + moved).astype(jnp.bfloat16)
                return carry

            lax.fori_loop(0, width // block, advance, 0)

    def back(order, half, index):
        return pltpu.make_async_remote_copy(
            src_ref=held(order, index),
            dst_ref=target(order, half),
            send_sem=send_sem.at[0],
            recv_sem=back_sem.at[order, half],
            device_id=place_of(index),
            device_id_type=MESH,
        )

    def keep(order, half):
        return pltpu.make_async_copy(held(order, me), target(order, half), back_sem.at[order, half])

    for kind, orders in ((thin, range(4)), (full, range(4, 6))):
        owns = functools.reduce(lambda a, b: a | b, [me == owner for order, _, owner in jobs if order in orders])

        @pl.when(owns)
        def _():
            orthogonalize(kind)

    for order, half, owner in jobs:

        @pl.when(me == owner)
        def _():
            def send(step, carry):
                back(order, half, lax.rem(me + step, devices)).start()
                return carry

            keep(order, half).start()
            lax.fori_loop(1, devices, send, 0)

    for order, half, owner in jobs:
        keep(order, half).wait()

    for order, half, owner in jobs:

        @pl.when(me == owner)
        def _():
            def sent_one(step, carry):
                back(order, half, lax.rem(me + step, devices)).wait_send()
                return carry

            lax.fori_loop(1, devices, sent_one, 0)

        @pl.when(me != owner)
        def _():
            remote(order, half, owner).wait_send()


def newton_schulz(attn_round, mlp_round, line):
    rows = attn_round.shape[1] * 8
    narrow, wide = attn_round.shape[2] // 2 * line, mlp_round.shape[2] // 2 * line
    low, dma = jnp.bfloat16, pltpu.SemaphoreType.DMA
    return pl.pallas_call(
        functools.partial(newton_kernel, line),
        out_shape=[
            jax.ShapeDtypeStruct(attn_round.shape, low),
            jax.ShapeDtypeStruct(mlp_round.shape, low),
        ],
        in_specs=[pl.BlockSpec(memory_space=pl.ANY)] * 2,
        out_specs=[pl.BlockSpec(memory_space=pl.ANY)] * 2,
        scratch_shapes=[
            pltpu.VMEM((rows, narrow), low),
            pltpu.VMEM((rows, wide), low),
            pltpu.VMEM((rows, rows), low),
            pltpu.VMEM((rows // 256, 256, rows), low),
            pltpu.VMEM((2, rows // 256, 256, rows), low),
            pltpu.VMEM((rows, rows), low),
            pltpu.VMEM((8, 128), jnp.float32),
            pltpu.VMEM((8, 128), jnp.float32),
            dma((6, 2)),
            dma((1,)),
            dma((1,)),
            dma((6, 2)),
            dma((2,)),
            dma((rows // 256,)),
            dma((2, rows // 256)),
        ],
        compiler_params=pltpu.CompilerParams(
            collective_id=3, has_side_effects=True, vmem_limit_bytes=48 * 1024 * 1024
        ),
        name="newton_schulz",
    )(attn_round, mlp_round)


def pair_swap(value):
    dp, line = lax.axis_size("dp"), lax.axis_size("tensor")
    pairs = [(i * line + k, (i ^ 1) * line + k) for i in range(dp) for k in range(line)]
    return lax.ppermute(value, ("dp", "tensor"), pairs)


def corner_swap(value, place):
    dp, line = lax.axis_size("dp"), lax.axis_size("tensor")
    pairs = []
    for i in range(1, dp, 2):
        for k in range(0, line, 2):
            pairs += [(i * line + k, (i - 1) * line + k + 1), ((i - 1) * line + k + 1, i * line + k)]
    moved = lax.ppermute(value, ("dp", "tensor"), pairs)
    return jnp.where(place.core == lax.rem(place.tensor, 2), value, moved)


def both_halves(value, place):
    other = pair_swap(value)
    first = place.core == 0
    return jnp.concatenate([jnp.where(first, value, other), jnp.where(first, other, value)], axis=0)


def my_half(whole, place):
    size = whole.shape[0] // CORES
    return lax.dynamic_slice_in_dim(whole, place.core * size, size, 0)


def sum_rows(partial, place):
    size = partial.shape[0] // CORES
    away = lax.dynamic_slice_in_dim(partial, (1 - place.core) * size, size, 0)
    return my_half(partial, place).astype(jnp.float32) + pair_swap(away).astype(jnp.float32)


def sum_whole(partial):
    return partial.astype(jnp.float32) + pair_swap(partial).astype(jnp.float32)


def norm_parts(rows):
    centred = rows - jnp.mean(rows, axis=-1, keepdims=True)
    spread = lax.rsqrt(jnp.mean(centred * centred, axis=-1, keepdims=True) + 1e-05)
    return centred * spread, spread


def norm_back(grad, gain, xhat, spread):
    scaled = grad * gain
    return spread * (
        scaled
        - jnp.mean(scaled, axis=-1, keepdims=True)
        - xhat * jnp.mean(scaled * xhat, axis=-1, keepdims=True)
    )


def on_chip_pair(tokens, cotangent, segments, attn_w, mlp_w, vectors, attn_mom, mlp_mom, vector_mom):
    line = lax.axis_size("tensor")
    place = Place()
    core, t = place.core, place.tensor
    width = tokens.shape[1]
    narrow, wide = attn_w.shape[2] // 2, mlp_w.shape[2] // 4
    total_tokens = tokens.shape[0] * line * lax.axis_size("dp")

    wqkv, wout, w_up, w_down = gather_weights(
        attn_w.astype(jnp.bfloat16), mlp_w.astype(jnp.bfloat16), line
    )
    wout = wout[0]

    def my_columns(row):
        return lax.dynamic_index_in_dim(row.reshape(line, 2, narrow), core, 1, False).reshape(-1)

    def place_columns(piece):
        spread = jnp.zeros((line, 2, narrow), jnp.float32)
        return lax.dynamic_update_slice(spread, piece.reshape(line, 1, narrow), (0, core, 0)).reshape(-1)

    hidden_bias = lax.dynamic_index_in_dim(vectors[8:].reshape(line, 2, 2, wide), core, 1, False)
    hidden_bias = hidden_bias.transpose(1, 0, 2).reshape(2, line * wide)

    x_rows = both_halves(corner_swap(tokens, place), place).astype(jnp.float32)
    grad_low = both_halves(corner_swap(cotangent, place), place)
    seg_pairs = segments.reshape(-1, SEQ)
    seg_own = lax.dynamic_index_in_dim(seg_pairs, t // 2, 0, False)
    seg_ids = jnp.where(core == lax.rem(t, 2), seg_own, pair_swap(seg_own))

    xhat_one, spread_one = norm_parts(x_rows)
    normed = (xhat_one * vectors[0] + vectors[1]).astype(jnp.bfloat16)
    projected = jnp.einsum("td,mdc->mtc", normed, wqkv, preferred_element_type=jnp.float32)
    biases = jnp.stack([my_columns(vectors[2]), jnp.zeros((narrow * line,), jnp.float32), my_columns(vectors[3])])
    qkv = (projected + biases[:, None]).astype(jnp.bfloat16)
    local_heads = qkv.shape[2] // HD
    per = narrow // HD
    local_ids = jnp.arange(local_heads)
    head_ids = (local_ids // per) * (2 * per) + core * per + local_ids % per
    slopes = jnp.exp2(-(8.0 / HEADS) * (head_ids.astype(jnp.float32) + 1.0))
    mixed, log_sums = attend(slopes, seg_ids, qkv)
    branch = sum_whole(contract_last(mixed, wout).astype(jnp.bfloat16))
    middle = x_rows + branch + vectors[4]
    xhat_two, spread_two = norm_parts(middle)
    hidden_low = (xhat_two * vectors[5] + vectors[6]).astype(jnp.bfloat16)
    hidden_pre = (
        jnp.einsum("td,sdc->stc", hidden_low, w_up, preferred_element_type=jnp.float32) + hidden_bias[:, None]
    )
    act_float, gelu_pull = jax.vjp(gelu_tanh, hidden_pre)
    hidden_act = act_float.astype(jnp.bfloat16)
    out_part = jnp.einsum("stc,sdc->td", hidden_act, w_down, preferred_element_type=jnp.float32)
    output = my_half(middle, place) + sum_rows(out_part.astype(jnp.bfloat16), place) + vectors[7]
    output = corner_swap(output.astype(jnp.bfloat16), place)

    grad_down = jnp.einsum("td,stc->sdc", grad_low, hidden_act, preferred_element_type=jnp.float32)
    grad_act = jnp.einsum("td,sdc->stc", grad_low, w_down, preferred_element_type=jnp.float32)
    grad_pre = gelu_pull(grad_act)[0].astype(jnp.bfloat16)
    grad_up = jnp.einsum("td,stc->sdc", hidden_low, grad_pre, preferred_element_type=jnp.float32)
    hidden_sums = jnp.sum(grad_pre, axis=1, dtype=jnp.float32)
    hidden_part = jnp.einsum("stc,sdc->td", grad_pre, w_up, preferred_element_type=jnp.float32)
    grad_hidden = sum_whole(hidden_part.astype(jnp.bfloat16))
    grad_middle = grad_low.astype(jnp.float32) + norm_back(grad_hidden, vectors[5], xhat_two, spread_two)
    grad_mid_low = grad_middle.astype(jnp.bfloat16)
    grad_out = contract_first(grad_mid_low, mixed)
    grad_mixed = jnp.dot(grad_mid_low, wout, preferred_element_type=jnp.float32).astype(jnp.bfloat16)
    grad_qkv = attend_back(slopes, seg_ids, qkv, grad_mixed, mixed, log_sums)
    grad_proj = jnp.einsum("td,mtc->mdc", normed, grad_qkv, preferred_element_type=jnp.float32)
    bias_sums = jnp.sum(grad_qkv, axis=1, dtype=jnp.float32)
    normed_part = jnp.einsum("mtc,mdc->td", grad_qkv, wqkv, preferred_element_type=jnp.float32)
    grad_normed = sum_rows(normed_part.astype(jnp.bfloat16), place)
    xhat_mine, spread_mine = my_half(xhat_one, place), my_half(spread_one, place)
    grad_mid_mine = my_half(grad_middle, place)
    grad_tokens = grad_mid_mine + norm_back(grad_normed, vectors[0], xhat_mine, spread_mine)
    grad_tokens = corner_swap(grad_tokens.astype(jnp.bfloat16), place).astype(jnp.float32)

    hidden_mine = my_half(grad_hidden, place)
    hidden_grad = lax.dynamic_update_slice(
        jnp.zeros((line, 2, 2, wide), jnp.float32),
        hidden_sums.reshape(2, line, wide).transpose(1, 0, 2)[:, None],
        (0, core, 0, 0),
    )
    vector_rows = jnp.stack(
        [
            jnp.sum(grad_normed * xhat_mine, axis=0),
            jnp.sum(grad_normed, axis=0),
            place_columns(bias_sums[0]),
            place_columns(bias_sums[2]),
            jnp.sum(grad_mid_mine, axis=0),
            jnp.sum(hidden_mine * my_half(xhat_two, place), axis=0),
            jnp.sum(hidden_mine, axis=0),
            jnp.sum(my_half(grad_low, place), axis=0, dtype=jnp.float32),
        ]
    )
    vector_local = jnp.concatenate([vector_rows, hidden_grad.reshape(-1, width)], axis=0)
    padding = jnp.zeros((4, width), jnp.float32)
    low = jnp.bfloat16
    attn_sum, mlp_sum, vector_sum = sum_gradients(
        grad_down.astype(low),
        grad_up.astype(low),
        grad_out.astype(low)[None],
        grad_proj.astype(low),
        jnp.concatenate([vector_local, padding], axis=0),
        line,
    )
    vector_grads = vector_sum[: vector_local.shape[0]]
    attn_mom_new = 0.5 * attn_mom + attn_sum.astype(jnp.float32)
    mlp_mom_new = 0.5 * mlp_mom + mlp_sum.astype(jnp.float32)
    attn_ortho, mlp_ortho = newton_schulz(attn_mom_new.astype(low), mlp_mom_new.astype(low), line)
    attn_new = attn_w - attn_ortho.astype(jnp.float32)
    mlp_new = mlp_w - math.sqrt(FF / D) * mlp_ortho.astype(jnp.float32)
    vector_mom_new = 0.5 * vector_mom + vector_grads
    vector_new = vectors - 0.1 / math.sqrt(total_tokens) * vector_mom_new
    return (
        output,
        grad_tokens,
        attn_mom_new,
        attn_new,
        mlp_mom_new,
        mlp_new,
        vector_mom_new,
        vector_new,
    )


def solution(mesh):
    in_specs = (
        P(("dp", "tensor"), None),
        P(("dp", "tensor"), None),
        P("dp"),
        P(None, "dp", "tensor"),
        P(None, "dp", "tensor"),
        P(),
        P(None, "dp", "tensor"),
        P(None, "dp", "tensor"),
        P(),
    )
    out_specs = (
        P(("dp", "tensor"), None),
        P(("dp", "tensor"), None),
        P(None, "dp", "tensor"),
        P(None, "dp", "tensor"),
        P(None, "dp", "tensor"),
        P(None, "dp", "tensor"),
        P(),
        P(),
    )
    chips_of_two = (mesh.shape["dp"], mesh.shape["tensor"]) == (8, 4)
    return jax.shard_map(
        on_chip_pair if chips_of_two else on_device, mesh=mesh, in_specs=in_specs, out_specs=out_specs, check_vma=False
    )
```

```python
import functools
import math

import jax
import jax.numpy as jnp
from jax import lax
from jax.experimental import pallas as pl
from jax.experimental.pallas import tpu as pltpu
from jax.sharding import PartitionSpec as P

D = 1024
HEADS = 16
HD = 64
FF = 4096
SEQ = 1024
NS_STEPS = 5
MESH = pl.DeviceIdType.MESH


coeff_a = 3.4445
coeff_b = -4.775
coeff_c = 2.0315


def norm_rows(row_data, gain, shift):
    center = jnp.mean(row_data, axis=-1, keepdims=True)
    centred = row_data - center
    spread = jnp.mean(centred * centred, axis=-1, keepdims=True)
    return centred * lax.rsqrt(spread + 1e-05) * gain + shift


def gelu_tanh(values):
    return jax.nn.gelu(values, approximate=True)


def contract_last(left, right):
    return lax.dot_general(
        left, right, (((1,), (1,)), ((), ())), preferred_element_type=jnp.float32
    )


def contract_first(left, right):
    return lax.dot_general(
        left, right, (((0,), (0,)), ((), ())), preferred_element_type=jnp.float32
    )


def head_slopes(first_head, head_count):
    head_ids = (first_head + jnp.arange(head_count)).astype(jnp.float32)
    return jnp.exp2(-(8.0 / HEADS) * (head_ids + 1.0))


def masked_scores(row_query, key_rows, row_segs, seg_ids, row_start, slopes):
    scores = jnp.einsum("qhd,khd->hqk", row_query, key_rows, preferred_element_type=jnp.float32) * (
        1.0 / math.sqrt(HD)
    )
    query_pos = row_start + jnp.arange(row_query.shape[0])
    key_pos = jnp.arange(key_rows.shape[0])
    distance = (query_pos[:, None] - key_pos[None, :]).astype(jnp.float32)
    scores = scores - slopes[:, None, None] * distance[None]
    same_doc = (
        (row_segs[:, None] == seg_ids[None, :])
        & (row_segs[:, None] > 0)
        & (key_pos[None, :] <= query_pos[:, None])
    )
    allowed = same_doc | (key_pos[None, :] == query_pos[:, None])
    return jnp.where(allowed[None], scores, -1e30)


def attend_forward(query, key_rows, value_rows, seg_ids, slopes, row_block):
    length = key_rows.shape[0]

    def one_block(row_start):
        row_query = lax.dynamic_slice_in_dim(query, row_start, row_block, 0)
        row_segs = lax.dynamic_slice_in_dim(seg_ids, row_start, row_block, 0)
        scores = masked_scores(row_query, key_rows, row_segs, seg_ids, row_start, slopes)
        row_max = jnp.max(scores, axis=-1, keepdims=True)
        exp_scores = jnp.exp(scores - row_max)
        row_total = jnp.sum(exp_scores, axis=-1, keepdims=True)
        attn_probs = (exp_scores / row_total).astype(jnp.bfloat16)
        mixed = jnp.einsum(
            "hqk,khd->qhd", attn_probs, value_rows, preferred_element_type=jnp.float32
        )
        return (mixed.astype(jnp.bfloat16), (row_max + jnp.log(row_total))[..., 0])

    block_starts = jnp.arange(length // row_block) * row_block
    mixed, log_sums = lax.map(one_block, block_starts)
    return (mixed.reshape(length, -1), log_sums)


def attend_backward(query, key_rows, value_rows, seg_ids, log_sums, grad_mixed, slopes, row_block):
    length, head_count, head_dim = key_rows.shape
    factor = 1.0 / math.sqrt(HD)

    def one_block(carry, pieces):
        row_start, row_lse = pieces
        row_query = lax.dynamic_slice_in_dim(query, row_start, row_block, 0)
        row_grad = lax.dynamic_slice_in_dim(grad_mixed, row_start, row_block, 0)
        row_segs = lax.dynamic_slice_in_dim(seg_ids, row_start, row_block, 0)
        scores = masked_scores(row_query, key_rows, row_segs, seg_ids, row_start, slopes)
        attn_probs = jnp.exp(scores - row_lse[:, :, None])
        grad_probs = jnp.einsum(
            "qhd,khd->hqk", row_grad, value_rows, preferred_element_type=jnp.float32
        )
        inner = jnp.sum(grad_probs * attn_probs, axis=-1, keepdims=True)
        grad_scores = (attn_probs * (grad_probs - inner)).astype(jnp.bfloat16)
        grad_query = (
            jnp.einsum("hqk,khd->qhd", grad_scores, key_rows, preferred_element_type=jnp.float32)
            * factor
        )
        grad_keys = (
            carry[0]
            + jnp.einsum("hqk,qhd->khd", grad_scores, row_query, preferred_element_type=jnp.float32)
            * factor
        )
        grad_values = carry[1] + jnp.einsum(
            "hqk,qhd->khd",
            attn_probs.astype(jnp.bfloat16),
            row_grad,
            preferred_element_type=jnp.float32,
        )
        return ((grad_keys, grad_values), grad_query)

    empty = jnp.zeros((length, head_count, head_dim), jnp.float32)
    block_starts = jnp.arange(length // row_block) * row_block
    (grad_keys, grad_values), grad_query = lax.scan(
        one_block, (empty, empty), (block_starts, log_sums)
    )
    return (
        grad_query.reshape(length, -1),
        grad_keys.reshape(length, -1),
        grad_values.reshape(length, -1),
    )


def newton_rows(row_iterate):
    for repeat in range(NS_STEPS + 1):
        whole_iterate = lax.all_gather(row_iterate, "tensor", axis=0, tiled=True)
        if repeat == NS_STEPS:
            break
        square_rows = contract_last(row_iterate, whole_iterate).astype(jnp.bfloat16)
        whole_square = lax.all_gather(square_rows, "tensor", axis=0, tiled=True)
        poly_rows = (
            coeff_b * square_rows.astype(jnp.float32)
            + coeff_c * jnp.dot(square_rows, whole_square, preferred_element_type=jnp.float32)
        ).astype(jnp.bfloat16)
        row_iterate = (
            coeff_a * row_iterate.astype(jnp.float32)
            + jnp.dot(poly_rows, whole_iterate, preferred_element_type=jnp.float32)
        ).astype(jnp.bfloat16)
    return whole_iterate


def on_device(tokens, cotangent, segments, attn_w, mlp_w, vectors, attn_mom, mlp_mom, vector_mom):
    tensor_size = lax.axis_size("tensor")
    dp_size = lax.axis_size("dp")
    tensor_index = lax.axis_index("tensor")
    dp_index = lax.axis_index("dp")
    row_count = tokens.shape[0]
    model_width = tokens.shape[1]
    local_width = attn_w.shape[2]
    local_hidden = mlp_w.shape[2]
    head_count = local_width // HD
    row_block = min(512, SEQ)
    total_tokens = row_count * tensor_size * dp_size
    gathered_attn, gathered_mlp = (
        lax.all_gather(attn_w.astype(jnp.bfloat16), "dp", axis=1, tiled=True),
        lax.all_gather(mlp_w.astype(jnp.bfloat16), "dp", axis=1, tiled=True),
    )
    hidden_bias = vectors[8:].reshape(-1)
    query_bias = lax.dynamic_slice_in_dim(vectors[2], tensor_index * local_width, local_width)
    value_bias = lax.dynamic_slice_in_dim(vectors[3], tensor_index * local_width, local_width)
    x_rows = tokens.astype(jnp.float32)
    normed, pull_first = jax.vjp(norm_rows, x_rows, vectors[0], vectors[1])
    all_normed = lax.all_gather(normed.astype(jnp.bfloat16), "tensor", axis=0, tiled=True)
    seq_count = all_normed.shape[0] // SEQ
    projected = jnp.einsum(
        "td,mdc->mtc", all_normed, gathered_attn[:3], preferred_element_type=jnp.float32
    )
    query = (projected[0] + query_bias).astype(jnp.bfloat16)
    key_rows = projected[1].astype(jnp.bfloat16)
    value_rows = (projected[2] + value_bias).astype(jnp.bfloat16)
    slopes = head_slopes(tensor_index * head_count, head_count)
    seq_shape = (seq_count, SEQ, head_count, HD)
    seq_segs = segments.reshape(seq_count, SEQ)

    def forward_seq(pieces):
        return attend_forward(pieces[0], pieces[1], pieces[2], pieces[3], slopes, row_block)

    mixed, log_sums = lax.map(
        forward_seq,
        (
            query.reshape(seq_shape),
            key_rows.reshape(seq_shape),
            value_rows.reshape(seq_shape),
            seq_segs,
        ),
    )
    mixed = mixed.reshape(-1, local_width)
    w_out = gathered_attn[3]
    middle = (
        x_rows
        + lax.psum_scatter(
            contract_last(mixed, w_out).astype(jnp.bfloat16),
            "tensor",
            scatter_dimension=0,
            tiled=True,
        ).astype(jnp.float32)
        + vectors[4]
    )
    hidden_normed, pull_second = jax.vjp(norm_rows, middle, vectors[5], vectors[6])
    hidden_low = hidden_normed.astype(jnp.bfloat16)
    grad_rows = cotangent.astype(jnp.float32)
    all_hidden = lax.all_gather(hidden_low, "tensor", axis=0, tiled=True)
    w_up = gathered_mlp[0]
    w_down = gathered_mlp[1]
    bias_local = lax.dynamic_slice_in_dim(hidden_bias, tensor_index * local_hidden, local_hidden)
    hidden_pre = jnp.dot(all_hidden, w_up, preferred_element_type=jnp.float32) + bias_local
    act_float, gelu_pull = jax.vjp(gelu_tanh, hidden_pre)
    hidden_act = act_float.astype(jnp.bfloat16)
    output = (
        middle
        + lax.psum_scatter(
            contract_last(hidden_act, w_down).astype(jnp.bfloat16),
            "tensor",
            scatter_dimension=0,
            tiled=True,
        ).astype(jnp.float32)
        + vectors[7]
    )
    all_grad = lax.all_gather(grad_rows.astype(jnp.bfloat16), "tensor", axis=0, tiled=True)
    grad_down = contract_first(all_grad, hidden_act)
    grad_act = jnp.dot(all_grad, w_down, preferred_element_type=jnp.float32)
    grad_pre = gelu_pull(grad_act)[0].astype(jnp.bfloat16)
    grad_up = contract_first(all_hidden, grad_pre)
    bias_part = jnp.sum(grad_pre, axis=0, dtype=jnp.float32)
    hidden_grad = lax.dynamic_update_slice_in_dim(
        jnp.zeros(hidden_bias.shape, jnp.float32), bias_part, tensor_index * local_hidden, 0
    )
    grad_hidden_in = lax.psum_scatter(
        contract_last(grad_pre, w_up).astype(jnp.bfloat16),
        "tensor",
        scatter_dimension=0,
        tiled=True,
    ).astype(jnp.float32)
    mlp_grads = jnp.stack([grad_up, grad_down])
    second_grads = pull_second(grad_hidden_in)
    grad_middle = grad_rows + second_grads[0]
    all_grad_mid = lax.all_gather(grad_middle.astype(jnp.bfloat16), "tensor", axis=0, tiled=True)
    grad_out_w = contract_first(all_grad_mid, mixed)
    grad_mixed = jnp.dot(all_grad_mid, w_out, preferred_element_type=jnp.float32).astype(
        jnp.bfloat16
    )

    def backward_seq(pieces):
        return attend_backward(
            pieces[0], pieces[1], pieces[2], pieces[3], pieces[4], pieces[5], slopes, row_block
        )

    grad_query, grad_keys, grad_values = lax.map(
        backward_seq,
        (
            query.reshape(seq_shape),
            key_rows.reshape(seq_shape),
            value_rows.reshape(seq_shape),
            seq_segs,
            log_sums,
            grad_mixed.reshape(seq_shape),
        ),
    )
    grad_qkv = (
        jnp.stack([grad_query, grad_keys, grad_values])
        .reshape(3, -1, local_width)
        .astype(jnp.bfloat16)
    )
    grad_proj_w = jnp.einsum(
        "td,mtc->mdc", all_normed, grad_qkv, preferred_element_type=jnp.float32
    )
    bias_sums = jnp.sum(grad_qkv, axis=1, dtype=jnp.float32)
    grad_normed = lax.psum_scatter(
        jnp.einsum(
            "mtc,mdc->td", grad_qkv, gathered_attn[:3], preferred_element_type=jnp.float32
        ).astype(jnp.bfloat16),
        "tensor",
        scatter_dimension=0,
        tiled=True,
    ).astype(jnp.float32)
    first_grads = pull_first(grad_normed)
    grad_tokens = grad_middle + first_grads[0]

    def placed(piece, full_size, offset):
        return lax.dynamic_update_slice_in_dim(
            jnp.zeros((full_size,), jnp.float32), piece, offset, 0
        )

    width_offset = tensor_index * local_width
    vector_rows = jnp.stack(
        [
            first_grads[1],
            first_grads[2],
            placed(bias_sums[0], model_width, width_offset),
            placed(bias_sums[2], model_width, width_offset),
            jnp.sum(grad_middle, axis=0),
            second_grads[1],
            second_grads[2],
            jnp.sum(grad_rows, axis=0),
        ]
    )
    vector_local = jnp.concatenate([vector_rows, hidden_grad.reshape(4, model_width)], axis=0)
    attn_grads = jnp.concatenate([grad_proj_w, grad_out_w[None]], axis=0)
    attn_sum, mlp_sum = (
        lax.psum_scatter(
            attn_grads.astype(jnp.bfloat16), "dp", scatter_dimension=1, tiled=True
        ).astype(jnp.float32),
        lax.psum_scatter(
            mlp_grads.astype(jnp.bfloat16), "dp", scatter_dimension=1, tiled=True
        ).astype(jnp.float32),
    )
    attn_mom_new = 0.5 * attn_mom + attn_sum
    mlp_mom_new = 0.5 * mlp_mom + mlp_sum
    attn_round = attn_mom_new.astype(jnp.bfloat16)
    mlp_round = mlp_mom_new.astype(jnp.bfloat16)
    attn_float = attn_round.astype(jnp.float32)
    mlp_float = mlp_round.astype(jnp.float32)
    norm_parts = jnp.concatenate(
        [jnp.sum(attn_float * attn_float, axis=(1, 2)), jnp.sum(mlp_float * mlp_float, axis=(1, 2))]
    )
    vector_grads, norm_sums = lax.psum((vector_local, norm_parts), ("dp", "tensor"))
    frob_norms = jnp.sqrt(norm_sums)
    owners = [order * dp_size // 6 for order in range(6)]
    owned_norm = jnp.zeros((), jnp.float32)
    for order in range(6):
        owned_norm = owned_norm + jnp.where(dp_index == owners[order], frob_norms[order], 0.0)
    block_rows = attn_w.shape[1]
    slice_rows = model_width // tensor_size
    full_cols = local_hidden * tensor_size
    rows_attn, rows_mlp = (
        lax.all_gather(attn_round, "tensor", axis=2, tiled=True),
        lax.all_gather(mlp_round, "tensor", axis=2, tiled=True),
    )
    padded_attn = jnp.pad(rows_attn, ((0, 0), (0, 0), (0, full_cols - model_width)))
    all_rows = jnp.concatenate([padded_attn, rows_mlp], axis=0)
    outgoing = jnp.zeros((dp_size, block_rows, full_cols), jnp.bfloat16)
    for order in range(6):
        outgoing = outgoing.at[owners[order]].set(all_rows[order])
    incoming = lax.all_to_all(outgoing, "dp", split_axis=0, concat_axis=0, tiled=True)
    owned_whole = incoming.reshape(model_width, full_cols)
    mine = lax.dynamic_slice_in_dim(owned_whole, tensor_index * slice_rows, slice_rows, 0)
    attn_col = tensor_index * local_width
    row_iterate = (mine.astype(jnp.float32) / (owned_norm + 1e-06)).astype(jnp.bfloat16)
    result = newton_rows(row_iterate)
    returned = lax.all_to_all(
        result.reshape(dp_size, block_rows, full_cols),
        "dp",
        split_axis=0,
        concat_axis=0,
        tiled=True,
    )
    attn_blocks = []
    for order in range(4):
        piece = lax.dynamic_slice_in_dim(returned[owners[order]], attn_col, local_width, 1)
        attn_blocks.append(attn_w[order] - piece.astype(jnp.float32))
    mlp_blocks = []
    for order in range(2):
        piece = lax.dynamic_slice_in_dim(
            returned[owners[4 + order]], tensor_index * local_hidden, local_hidden, 1
        )
        mlp_blocks.append(mlp_w[order] - math.sqrt(FF / D) * piece.astype(jnp.float32))
    attn_new = jnp.stack(attn_blocks)
    mlp_new = jnp.stack(mlp_blocks)
    vector_mom_new = 0.5 * vector_mom + vector_grads
    vector_new = vectors - 0.1 / math.sqrt(total_tokens) * vector_mom_new
    return (
        output.astype(jnp.bfloat16),
        grad_tokens,
        attn_mom_new,
        attn_new,
        mlp_mom_new,
        mlp_new,
        vector_mom_new,
        vector_new,
    )


CORES = 2


class Place:
    def __init__(self):
        self.dp = lax.axis_index("dp")
        self.tensor = lax.axis_index("tensor")
        self.core = lax.rem(self.dp, 2)
        self.chip = self.dp // 2
        self.x = lax.rem(self.chip, 2)
        self.y = self.chip // 2
        self.twin = (self.dp + 1 - 2 * self.core, self.tensor)
        self.across_x = (self.dp + 2 - 4 * self.x, self.tensor)
        self.across_y = (self.dp + 4 - 8 * self.y, self.tensor)
        self.right = (self.dp, self.tensor + 1)
        self.left = (self.dp, self.tensor - 1)


def greet(place, line):
    barrier = pltpu.get_barrier_semaphore()

    def signal(device):
        pl.semaphore_signal(barrier, inc=1, device_id=device, device_id_type=MESH)

    signal(place.twin)
    signal(place.across_x)
    signal(place.across_y)

    for other in range(line):

        @pl.when(place.tensor != other)
        def _():
            signal((place.dp, other))

    pl.semaphore_wait(barrier, 3 + line - 1)


def columns(start, size):
    return pl.ds(pl.multiple_of(start, 128), size)


def gather_kernel(line, attn_ref, mlp_ref, qkv_ref, out_ref, up_ref, down_ref, own_sem, send_sem, recv_sem):
    place = Place()
    x, y, t = place.x, place.y, place.tensor
    narrow = attn_ref.shape[2] // 2
    wide = mlp_ref.shape[2] // 4

    def attn_source(lo, hi):
        return lambda core: attn_ref.at[lo:hi, :, columns(core * narrow, narrow)]

    def mlp_source(index, part):
        return lambda core: mlp_ref.at[index : index + 1, :, columns((2 * core + part) * wide, wide)]

    groups = [
        (qkv_ref, narrow, attn_source(0, 3)),
        (out_ref, narrow, attn_source(3, 4)),
        (up_ref.at[0:1], wide, mlp_source(0, 0)),
        (up_ref.at[1:2], wide, mlp_source(0, 1)),
        (down_ref.at[0:1], wide, mlp_source(1, 0)),
        (down_ref.at[1:2], wide, mlp_source(1, 1)),
    ]
    greet(place, line)

    def copy(group, slot, source, target, device):
        return pltpu.make_async_remote_copy(
            src_ref=source,
            dst_ref=target,
            send_sem=send_sem.at[group, slot],
            recv_sem=recv_sem.at[group, slot],
            device_id=device,
            device_id_type=MESH,
        )

    def same(group, slot, region, device):
        return copy(group, slot, region, region, device)

    def chunk(group, index):
        ref, width, _ = groups[group]
        return ref.at[:, y, x, :, :, columns(index * width, width)]

    def corner(group, ys, xs, half):
        return groups[group][0].at[:, ys, xs, half]

    def entry(group, half):
        ref, width, _ = groups[group]
        return ref.at[:, y, x, half, :, columns(t * width, width)]

    both = pl.ds(0, 2)
    last = len(groups) - 1
    to_right, to_left, half_x, half_y, rest_y, rest_x = 1, line, 2 * line - 1, 2 * line, 2 * line + 1, 2 * line + 2

    def chunk(group, index):
        ref, width, _ = groups[group]
        cols = columns(index * width, width)
        if group == last:
            return ref.at[:, :, :, :, :, cols]
        return ref.at[:, y, x, :, :, cols]

    def corner(group, ys, xs, half):
        ref, width, _ = groups[group]
        if group == last:
            return ref.at[:, ys, xs, half, :, columns(t * width, width)]
        return ref.at[:, ys, xs, half]

    def entry(group, half):
        ref, width, _ = groups[group]
        return ref.at[:, y, x, half, :, columns(t * width, width)]

    def own(group):
        return pltpu.make_async_copy(
            groups[group][2](place.core), entry(group, place.core), own_sem.at[group]
        )

    def first(group):
        target = entry(group, place.core)
        return copy(group, 0, groups[group][2](1 - place.core), target, place.twin)

    def enter(group):
        own(group).wait()
        same(group, 0, entry(group, 1 - place.core), place.twin).wait_recv()

    def line_start(group):
        @pl.when(t < line - 1)
        def _():
            same(group, to_right, chunk(group, t), place.right).start()

        @pl.when(t > 0)
        def _():
            same(group, to_left, chunk(group, t), place.left).start()

    def line_step(group, step):
        @pl.when(t >= step)
        def _():
            same(group, to_right + step - 1, chunk(group, t - step), place.left).wait_recv()
            if step < line - 1:

                @pl.when(t < line - 1)
                def _():
                    same(group, to_right + step, chunk(group, t - step), place.right).start()

        @pl.when(t + step <= line - 1)
        def _():
            same(group, to_left + step - 1, chunk(group, t + step), place.right).wait_recv()
            if step < line - 1:

                @pl.when(t > 0)
                def _():
                    same(group, to_left + step, chunk(group, t + step), place.left).start()

    def plane_start(group):
        same(group, half_x, corner(group, y, x, 0), place.across_x).start()
        same(group, half_y, corner(group, y, x, 1), place.across_y).start()

    def plane_step(group):
        same(group, half_x, corner(group, y, 1 - x, 0), place.across_x).wait_recv()
        same(group, rest_y, corner(group, y, both, 0), place.across_y).start()
        same(group, half_y, corner(group, 1 - y, x, 1), place.across_y).wait_recv()
        same(group, rest_x, corner(group, both, x, 1), place.across_x).start()

    def plane_end(group):
        same(group, rest_y, corner(group, 1 - y, both, 0), place.across_y).wait_recv()
        same(group, rest_x, corner(group, both, 1 - x, 1), place.across_x).wait_recv()

    def wait_sends(group):
        first(group).wait_send()
        for step in range(1, line):

            @pl.when((t - step + 1 >= 0) & (t < line - 1))
            def _():
                same(group, to_right + step - 1, chunk(group, t - step + 1), place.right).wait_send()

            @pl.when((t + step - 1 <= line - 1) & (t > 0))
            def _():
                same(group, to_left + step - 1, chunk(group, t + step - 1), place.left).wait_send()

        same(group, half_x, corner(group, y, x, 0), place.across_x).wait_send()
        same(group, half_y, corner(group, y, x, 1), place.across_y).wait_send()
        same(group, rest_y, corner(group, y, both, 0), place.across_y).wait_send()
        same(group, rest_x, corner(group, both, x, 1), place.across_x).wait_send()

    def line_tail(group, after):
        for step in range(1, line - 1):
            line_step(group, step)
        if after is not None:
            enter(after)
            line_start(after)
        line_step(group, line - 1)

    out, qkv, up_a, up_b, down_a = 1, 0, 2, 3, 4
    for group in (out, last, qkv, up_a, up_b, down_a):
        own(group).start()
        first(group).start()
    enter(out)
    line_start(out)
    enter(last)
    plane_start(last)
    line_tail(out, qkv)
    plane_start(out)
    plane_step(last)
    plane_step(out)
    line_tail(qkv, up_a)
    plane_start(qkv)
    plane_end(last)
    line_tail(up_a, up_b)
    plane_end(out)
    plane_step(qkv)
    plane_start(up_a)
    line_tail(up_b, down_a)
    plane_end(qkv)
    line_tail(down_a, None)
    line_start(last)
    plane_step(up_a)
    plane_start(up_b)
    line_step(last, 1)
    plane_end(up_a)
    plane_step(up_b)
    plane_start(down_a)
    for step in range(2, line - 1):
        line_step(last, step)
    plane_end(up_b)
    line_step(last, line - 1)
    plane_step(down_a)
    plane_end(down_a)
    for group in range(len(groups)):
        wait_sends(group)


def gather_weights(attn_low, mlp_low, line):
    narrow = attn_low.shape[2] // 2 * line
    wide = mlp_low.shape[2] // 4 * line
    rows = attn_low.shape[1]
    shapes = [(3, narrow), (1, narrow), (2, wide), (2, wide)]
    slots = 2 * line + 3
    gathered = pl.pallas_call(
        functools.partial(gather_kernel, line),
        out_shape=[
            jax.ShapeDtypeStruct((count, 2, 2, 2, rows, width), jnp.bfloat16) for count, width in shapes
        ],
        in_specs=[pl.BlockSpec(memory_space=pl.ANY)] * 2,
        out_specs=[pl.BlockSpec(memory_space=pl.ANY)] * 4,
        scratch_shapes=[
            pltpu.SemaphoreType.DMA((6,)),
            pltpu.SemaphoreType.DMA((6, slots)),
            pltpu.SemaphoreType.DMA((6, slots)),
        ],
        compiler_params=pltpu.CompilerParams(collective_id=1, has_side_effects=True),
        name="gather_weights",
    )(attn_low, mlp_low)
    return [whole.reshape(whole.shape[0], 8 * rows, -1) for whole in gathered]


def add_blocks(target, sources):
    lead, rows = target.shape[:-2], target.shape[-2]
    per = rows // 32

    def body(step, carry):
        block, at = step // per, []
        for size in lead[::-1]:
            at.insert(0, lax.rem(block, size))
            block = block // size
        at = tuple(at) + (pl.ds(pl.multiple_of(lax.rem(step, per) * 32, 32), 32),)
        total = sources[0][at].astype(jnp.float32)
        for source in sources[1:]:
            total = total + source[at].astype(jnp.float32)
        target[at] = total.astype(target.dtype)
        return carry

    lax.fori_loop(0, math.prod(lead) * per, body, 0)


class PlaneSum:
    @staticmethod
    def scratch(count, rows, width):
        pair = pltpu.VMEM((count, 2, rows, width), jnp.bfloat16)
        single = pltpu.VMEM((count, rows, width), jnp.bfloat16)
        dma = pltpu.SemaphoreType.DMA
        return [pair] * 4 + [single] * 2 + [dma((2,)), dma((4,)), dma((4,))]

    SCRATCH = 9

    def __init__(self, place, source, result, scratch):
        self.place, self.source, self.result = place, source, result
        self.own, self.got, self.last = scratch[0:2], scratch[2:4], scratch[4:6]
        self.own_sem, self.send_sem, self.recv_sem = scratch[6:9]

    def copy(self, slot, source, target, device):
        return pltpu.make_async_remote_copy(
            src_ref=source,
            dst_ref=target,
            send_sem=self.send_sem.at[slot],
            recv_sem=self.recv_sem.at[slot],
            device_id=device,
            device_id_type=MESH,
        )

    def cut(self, index, mine):
        both, place = pl.ds(0, 2), self.place
        if index == 0:
            return self.source.at[:, place.y if mine else 1 - place.y, both, 0]
        return self.source.at[:, both, place.x if mine else 1 - place.x, 1]

    def load(self, index):
        return pltpu.make_async_copy(self.cut(index, True), self.own[index], self.own_sem.at[index])

    def first(self, index):
        device = self.place.across_x if index else self.place.across_y
        return self.copy(index, self.cut(index, False), self.got[index], device)

    def second(self, index):
        mine = self.place.y if index else self.place.x
        device = self.place.across_y if index else self.place.across_x
        return self.copy(2 + index, self.own[index].at[:, 1 - mine], self.last[index], device)

    def start(self):
        for index in range(2):
            self.first(index).start()
            self.load(index).start()

    def one(self):
        for index in range(2):
            mine = self.place.y if index else self.place.x
            self.load(index).wait()
            self.first(index).wait_recv()
            own, got = self.own[index], self.got[index]
            add_blocks(own.at[:, 1 - mine], (own.at[:, 1 - mine], got.at[:, 1 - mine]))
            self.second(index).start()
            add_blocks(own.at[:, mine], (own.at[:, mine], got.at[:, mine]))

    def two(self):
        for index in range(2):
            mine = self.place.y if index else self.place.x
            self.second(index).wait_recv()
            add_blocks(self.result.at[:, index], (self.own[index].at[:, mine], self.last[index]))

    def sent(self):
        for index in range(2):
            self.first(index).wait_send()
            self.second(index).wait_send()


class LineSum:
    @staticmethod
    def scratch(shape, line):
        dma = pltpu.SemaphoreType.DMA
        return [pltpu.VMEM(shape, jnp.bfloat16)] * 2 + [dma((2, line)), dma((2, line))]

    SCRATCH = 4

    def __init__(self, place, line, value, result, scratch):
        self.place, self.line, self.value, self.result = place, line, value, result
        self.got = scratch[0:2]
        self.send_sem, self.recv_sem = scratch[2:4]
        self.width = value.shape[-1] // line

    def part(self, ref, index):
        return ref.at[(slice(None),) * (len(ref.shape) - 1) + (slice(index * self.width, (index + 1) * self.width),)]

    def hop(self, index, left):
        return pltpu.make_async_remote_copy(
            src_ref=self.part(self.value, index),
            dst_ref=self.part(self.got[left], index),
            send_sem=self.send_sem.at[left, index],
            recv_sem=self.recv_sem.at[left, index],
            device_id=self.place.left if left else self.place.right,
            device_id_type=MESH,
        )

    def step(self, step):
        for left in range(2):
            for index in range(self.line):
                away = index if left else self.line - 1 - index
                order = step - away
                plane = self.line - 1 - order if left else order
                if order < 0 or (plane <= index if left else plane >= index):
                    continue

                @pl.when(self.place.tensor == plane)
                def _():
                    if order > 0:
                        self.hop(index, left).wait_recv()
                        value = self.part(self.value, index)
                        add_blocks(value, (value, self.part(self.got[left], index)))
                    if away > 0:
                        self.hop(index - 1 if left else index + 1, left).wait_send()
                    self.hop(index, left).start()

    def end(self):
        for index in range(self.line):

            @pl.when(self.place.tensor == index)
            def _():
                sources = [self.part(self.value, index)]
                for left in range(2):
                    if index < self.line - 1 if left else index > 0:
                        self.hop(index, left).wait_recv()
                        sources.append(self.part(self.got[left], index))
                add_blocks(self.result, sources)

    def sent(self):
        for index in range(self.line):

            @pl.when(self.place.tensor == index)
            def _():
                if index > 0:
                    self.hop(index - 1, 1).wait_send()
                if index < self.line - 1:
                    self.hop(index + 1, 0).wait_send()


class HomeCopy:
    def __init__(self, place, value, target, scratch):
        self.place, self.value, self.target = place, value, target
        self.own_sem, self.sem = scratch

    SCRATCH = 2

    @staticmethod
    def scratch():
        return [pltpu.SemaphoreType.DMA((1,)), pltpu.SemaphoreType.DMA((2,))]

    def keep(self):
        return pltpu.make_async_copy(self.value.at[:, self.place.core], self.target, self.own_sem.at[0])

    def give(self):
        return pltpu.make_async_remote_copy(
            src_ref=self.value.at[:, 1 - self.place.core],
            dst_ref=self.target,
            send_sem=self.sem.at[0],
            recv_sem=self.sem.at[1],
            device_id=self.place.twin,
            device_id_type=MESH,
        )

    def start(self):
        self.keep().start()
        self.give().start()

    def wait(self):
        self.keep().wait()
        self.give().wait()


class GroupSum:
    @staticmethod
    def scratch(count, rows, width, line, line_first=False):
        low = jnp.bfloat16
        part = width // line
        done = pltpu.VMEM((count, 2, rows, part), low)
        if line_first:
            whole = (count, 2, 2, 2, rows, width)
            held = [pltpu.VMEM(whole, low), pltpu.VMEM(whole[:-1] + (part,), low), pltpu.SemaphoreType.DMA((1,))]
            plane, along = PlaneSum.scratch(count, rows, part), LineSum.scratch(whole, line)
        else:
            middle = (count, 2, rows, width)
            held = [pltpu.VMEM(middle, low)]
            plane, along = PlaneSum.scratch(count, rows, width), LineSum.scratch(middle, line)
        return held + [done] + plane + along + HomeCopy.scratch()

    def __init__(self, place, line, source, target, scratch, line_first=False):
        scratch = list(scratch)

        def take(count):
            taken = scratch[:count]
            del scratch[:count]
            return taken

        if line_first:
            whole, middle, load_sem = take(3)
            self.load = lambda: pltpu.make_async_copy(source, whole, load_sem.at[0])
        else:
            (middle,) = take(1)
        (done,) = take(1)
        plane, along = take(PlaneSum.SCRATCH), take(LineSum.SCRATCH)
        if line_first:
            self.line = LineSum(place, line, whole, middle, along)
            self.plane = PlaneSum(place, middle, done, plane)
        else:
            self.plane = PlaneSum(place, source, middle, plane)
            self.line = LineSum(place, line, middle, done, along)
        self.home = HomeCopy(place, done, target, take(HomeCopy.SCRATCH))

    def finish(self):
        self.home.wait()
        self.plane.sent()
        self.line.sent()


class VectorSum:
    @staticmethod
    def scratch(shape, line):
        return [
            pltpu.VMEM((4,) + shape, jnp.float32),
            pltpu.VMEM((3,) + shape, jnp.float32),
            pltpu.VMEM((line,) + shape, jnp.float32),
            pltpu.SemaphoreType.DMA((4, max(line, 3))),
        ]

    def __init__(self, place, line, scratch):
        self.place, self.line = place, line
        self.sums, self.got, self.along, self.sem = scratch

    def copy(self, stage):
        place = self.place
        return pltpu.make_async_remote_copy(
            src_ref=self.sums.at[stage],
            dst_ref=self.got.at[stage],
            send_sem=self.sem.at[0, stage],
            recv_sem=self.sem.at[1, stage],
            device_id=(place.twin, place.across_x, place.across_y)[stage],
            device_id_type=MESH,
        )

    def hop(self, other, source):
        return pltpu.make_async_remote_copy(
            src_ref=self.sums.at[3],
            dst_ref=self.along.at[source],
            send_sem=self.sem.at[2, other],
            recv_sem=self.sem.at[3, source],
            device_id=(self.place.dp, other),
            device_id_type=MESH,
        )

    def start(self, value):
        self.sums[0] = value
        self.copy(0).start()

    def step(self, stage):
        self.copy(stage).wait()
        self.sums[stage + 1] = self.sums[stage] + self.got[stage]
        if stage < 2:
            self.copy(stage + 1).start()
            return
        self.along[self.place.tensor] = self.sums[3]
        for other in range(self.line):

            @pl.when(self.place.tensor != other)
            def _():
                self.hop(other, self.place.tensor).start()

    def end(self):
        t = self.place.tensor
        for other in range(self.line):

            @pl.when(t != other)
            def _():
                self.hop(other, t).wait_send()
                self.hop(t, other).wait_recv()

        total = self.along[0]
        for other in range(1, self.line):
            total = total + self.along[other]
        return total


LOG2E = 1.4426950408889634
FAR = 1e32
ROW_BLOCK = 256


def fill_distance(seg_rows, seg_cols, distance):
    def body(step, carry):
        start = pl.multiple_of(step * 64, 64)
        shape = (64, distance.shape[1])
        row = lax.broadcasted_iota(jnp.int32, shape, 0) + start
        col = lax.broadcasted_iota(jnp.int32, shape, 1)
        segs = seg_rows[pl.ds(start, 64), :]
        same = (segs == seg_cols[...]) & (segs > 0) & (col <= row)
        allowed = same | (col == row)
        distance[pl.ds(start, 64), :] = jnp.where(allowed, (row - col).astype(jnp.float32), FAR)
        return carry

    lax.fori_loop(0, distance.shape[0] // 64, body, 0)


def head_lanes(dtype):
    lane = lax.broadcasted_iota(jnp.int32, (1, 2 * HD), 1)
    first = (lane < HD).astype(jnp.float32)
    return (first.astype(dtype), (1.0 - first).astype(dtype))


def attend_kernel(slopes, seg_rows, seg_cols, qkv, mixed, lse, distance):
    group = pl.program_id(0)
    length = qkv.shape[1]

    @pl.when(group == 0)
    def _():
        fill_distance(seg_rows, seg_cols, distance)

    masks = head_lanes(jnp.bfloat16)
    first = head_lanes(jnp.float32)[0] > 0.5
    factor = LOG2E / math.sqrt(HD)
    keys_t = qkv[1].T
    for start in range(0, length, ROW_BLOCK):
        stop = start + ROW_BLOCK
        rows = slice(start, stop)
        parts, sums = [], []
        for head in range(2):
            slope = slopes[2 * group + head] * LOG2E
            scores = jnp.dot(
                qkv[0, rows, :] * masks[head], keys_t[:, :stop], preferred_element_type=jnp.float32
            )
            scores = scores * factor - slope * distance[rows, :stop]
            top = jnp.max(scores, axis=1, keepdims=True)
            probs = jnp.exp2(scores - top)
            total = jnp.sum(probs, axis=1, keepdims=True)
            out = jnp.dot(probs.astype(jnp.bfloat16), qkv[2, :stop, :], preferred_element_type=jnp.float32)
            parts.append(out / total)
            sums.append(top + jnp.log2(total))
        mixed[rows, :] = jnp.where(first, parts[0], parts[1]).astype(jnp.bfloat16)
        lse[rows, :] = jnp.where(first, sums[0], sums[1])


def attend_back_group(group, slopes, qkv, grad, mixed, lse, out, distance, dk_acc, dv_acc):
    length = qkv.shape[1]
    cols = columns(group * 2 * HD, 2 * HD)
    masks = head_lanes(jnp.bfloat16)
    wide_masks = head_lanes(jnp.float32)
    first = wide_masks[0] > 0.5
    factor = LOG2E / math.sqrt(HD)
    shrink = 1.0 / math.sqrt(HD)
    keys, values = qkv[1, :, cols], qkv[2, :, cols]
    keys_t = keys.T
    values_t = values.T
    dk_acc[...] = jnp.zeros_like(dk_acc)
    dv_acc[...] = jnp.zeros_like(dv_acc)
    for start in range(0, length, ROW_BLOCK):
        stop = start + ROW_BLOCK
        rows = slice(start, stop)
        query, grads, log_sums = qkv[0, rows, cols], grad[rows, cols], lse[rows, cols]
        query_t, grads_t = query.T, grads.T
        product = grads.astype(jnp.float32) * mixed[rows, cols].astype(jnp.float32)
        parts = []
        for head in range(2):
            slope = slopes[2 * group + head] * LOG2E
            lanes = slice(head * HD, (head + 1) * HD)
            scores = jnp.dot(query * masks[head], keys_t[:, :stop], preferred_element_type=jnp.float32)
            log_sum = log_sums[:, head * HD : head * HD + 1]
            probs = jnp.exp2(scores * factor - slope * distance[rows, :stop] - log_sum)
            grad_probs = jnp.dot(grads * masks[head], values_t[:, :stop], preferred_element_type=jnp.float32)
            inner = jnp.sum(product * wide_masks[head], axis=1, keepdims=True)
            grad_scores = (probs * (grad_probs - inner)).astype(jnp.bfloat16)
            parts.append(jnp.dot(grad_scores, keys[:stop], preferred_element_type=jnp.float32))
            dk_acc[lanes, :stop] += jnp.dot(query_t[lanes, :], grad_scores, preferred_element_type=jnp.float32)
            dv_acc[lanes, :stop] += jnp.dot(
                grads_t[lanes, :], probs.astype(jnp.bfloat16), preferred_element_type=jnp.float32
            )
        out[0, rows, cols] = (jnp.where(first, parts[0], parts[1]) * shrink).astype(jnp.bfloat16)
    out[1, :, cols] = (dk_acc[...].T * shrink).astype(jnp.bfloat16)
    out[2, :, cols] = dv_acc[...].T.astype(jnp.bfloat16)


def back_kernel(
    line, down_ref, up_ref, slopes, seg_rows, seg_cols, qkv, grad, mixed, lse, mlp_home, out, distance, dk_acc, dv_acc, *scratch
):
    place = Place()
    wide = mlp_home.shape[2] // 4
    groups = []
    for order, (ref, index, part) in enumerate(((down_ref, 1, 0), (down_ref, 1, 1), (up_ref, 0, 0), (up_ref, 0, 1))):
        target = mlp_home.at[index : index + 1, :, columns((2 * place.core + part) * wide, wide)]
        groups.append(
            GroupSum(place, line, ref.at[part : part + 1], target, scratch[order], line_first=order == 3)
        )
    one, two, three, last = groups

    def attend(group):
        attend_back_group(group, slopes, qkv, grad, mixed, lse, out, distance, dk_acc, dv_acc)

    greet(place, line)
    one.plane.start()
    last.load().start()
    last.load().wait()
    last.line.step(0)
    fill_distance(seg_rows, seg_cols, distance)
    pairs = qkv.shape[2] // (2 * HD)

    def body(group, carry):
        attend(group)
        return carry

    lax.fori_loop(0, pairs // 2, body, 0)
    one.plane.one()
    two.plane.start()
    last.line.step(1)
    lax.fori_loop(pairs // 2, pairs, body, 0)
    one.plane.two()
    one.line.step(0)
    two.plane.one()
    three.plane.start()
    for step in range(2, line - 1):
        last.line.step(step)
    for step in range(1, line - 1):
        one.line.step(step)
    two.plane.two()
    two.line.step(0)
    one.line.end()
    one.home.start()
    last.line.end()
    last.plane.start()
    three.plane.one()
    for step in range(1, line - 1):
        two.line.step(step)
    last.plane.one()
    three.plane.two()
    three.line.step(0)
    two.line.end()
    two.home.start()
    last.plane.two()
    last.home.start()
    for step in range(1, line - 1):
        three.line.step(step)
    three.line.end()
    three.home.start()
    for group in groups:
        group.finish()


def attention_specs(length):
    return [
        pl.BlockSpec(memory_space=pltpu.SMEM),
        pl.BlockSpec((length, 1), lambda g: (0, 0)),
        pl.BlockSpec((1, length), lambda g: (0, 0)),
        pl.BlockSpec((3, length, 2 * HD), lambda g: (0, 0, g)),
    ]


def attend(slopes, seg_ids, qkv):
    _, length, width = qkv.shape
    rows = pl.BlockSpec((length, 2 * HD), lambda g: (0, g))
    return pl.pallas_call(
        attend_kernel,
        grid=(width // (2 * HD),),
        out_shape=[
            jax.ShapeDtypeStruct((length, width), jnp.bfloat16),
            jax.ShapeDtypeStruct((length, width), jnp.float32),
        ],
        in_specs=attention_specs(length),
        out_specs=[rows, rows],
        scratch_shapes=[pltpu.VMEM((length, length), jnp.float32)],
        compiler_params=pltpu.CompilerParams(vmem_limit_bytes=48 * 1024 * 1024),
        name="attend",
    )(slopes, seg_ids.reshape(-1, 1), seg_ids.reshape(1, -1), qkv)


def attend_back(down, up, slopes, seg_ids, qkv, grad, mixed, lse, line):
    _, length, width = qkv.shape
    rows, wide = down.shape[1] // 8, down.shape[2]
    vmem = pl.BlockSpec(memory_space=pltpu.VMEM)
    hbm = pl.BlockSpec(memory_space=pl.ANY)
    return pl.pallas_call(
        functools.partial(back_kernel, line),
        out_shape=[
            jax.ShapeDtypeStruct((2, rows, 4 * wide // line), jnp.bfloat16),
            jax.ShapeDtypeStruct(qkv.shape, jnp.bfloat16),
        ],
        in_specs=[hbm] * 2 + [pl.BlockSpec(memory_space=pltpu.SMEM)] + [vmem] * 6,
        out_specs=[hbm, vmem],
        scratch_shapes=[
            pltpu.VMEM((length, length), jnp.float32),
            pltpu.VMEM((2 * HD, length), jnp.float32),
            pltpu.VMEM((2 * HD, length), jnp.float32),
        ]
        + [GroupSum.scratch(1, rows, wide, line, line_first=order == 3) for order in range(4)],
        compiler_params=pltpu.CompilerParams(
            collective_id=2, has_side_effects=True, vmem_limit_bytes=56 * 1024 * 1024
        ),
        name="attend_back",
    )(
        *(each.reshape(2, 2, 2, 2, rows, wide) for each in (down, up)),
        slopes,
        seg_ids.reshape(-1, 1),
        seg_ids.reshape(1, -1),
        qkv,
        grad,
        mixed,
        lse,
    )


OWNERS = ((1, 0, 0), (1, 0, 3), (0, 1, 0), (0, 1, 3), (0, 0, 1), (1, 1, 2))


def finish_kernel(line, out_ref, qkv_ref, vec_ref, mom_ref, mlp_ref, mom_out, vec_out, attn_home, mlp_home, *scratch):
    (thin, full, gram, sent, got, poly, norm_own, norm_got, attn_sum, attn_ref) = scratch[:10]
    (home_sem, start_sem, send_sem, back_sem, norm_sem, block_send, block_recv, pass_send, pass_recv) = scratch[10:19]
    place = Place()
    x, y, t, core = place.x, place.y, place.tensor, place.core
    me = place.dp * line + t
    devices = 8 * line
    rows = mlp_ref.shape[1]
    narrow, wide = attn_ref.shape[2] // 2, mlp_ref.shape[2] // 2
    barrier = pltpu.get_barrier_semaphore()

    def place_of(index):
        return (index // line, lax.rem(index, line))

    def index_of(xs, ys, cores, z):
        return ((2 * ys + xs) * 2 + cores) * line + z

    def meet(step, carry):
        pl.semaphore_signal(
            barrier, inc=1, device_id=place_of(lax.rem(me + step, devices)), device_id_type=MESH
        )
        return carry

    lax.fori_loop(1, devices, meet, 0)
    pl.semaphore_wait(barrier, devices - 1)

    part = attn_ref.shape[2] // 2

    def target_sum(lo, hi):
        return attn_sum.at[lo:hi, :, columns(core * part, part)]

    sums = (
        GroupSum(place, line, out_ref, target_sum(3, 4), scratch[23]),
        GroupSum(place, line, qkv_ref, target_sum(0, 3), scratch[24]),
    )
    vector = VectorSum(place, line, scratch[19:23])

    def source(order, half):
        if order < 4:
            return attn_ref.at[order, :, half * narrow : (half + 1) * narrow]
        return mlp_ref.at[order - 4, :, half * wide : (half + 1) * wide]

    def held(order, index):
        dp, tensor = place_of(index)
        row = pl.ds(pl.multiple_of(dp * rows, rows), rows)
        if order < 4:
            return thin.at[row, columns(tensor * narrow, narrow)]
        return full.at[row, columns(tensor * wide, wide)]

    def target(order, half):
        if order < 4:
            return attn_home.at[order, :, half * narrow : (half + 1) * narrow]
        return mlp_home.at[order - 4, :, half * wide : (half + 1) * wide]

    def remote(source_ref, target_ref, send, recv, index):
        return pltpu.make_async_remote_copy(
            src_ref=source_ref,
            dst_ref=target_ref,
            send_sem=send,
            recv_sem=recv,
            device_id=place_of(index),
            device_id_type=MESH,
        )

    def owner_of(order, half):
        ox, oy, oz = OWNERS[order]
        return index_of(ox, oy, half, oz)

    def collect(order, half):
        return remote(source(order, half), held(order, me), home_sem.at[order, half], start_sem.at[0], owner_of(order, half))

    def collect_own(order, half):
        return pltpu.make_async_copy(source(order, half), held(order, me), start_sem.at[0])

    def sides(order):
        oz = OWNERS[order][2]
        above, below = list(range(oz + 1, line)), list(range(oz))
        return (above, below) if len(above) > len(below) else (below, above)

    def is_one_of(value, options):
        found = value < 0
        for option in options:
            found = found | (value == option)
        return found

    def by_way(order):
        ox, oy, oz = OWNERS[order]
        return (y != oy) & (t != oz) & ((x != ox) | is_one_of(t, sides(order)[1]))

    def to_way(order, half):
        ox, oy, _ = OWNERS[order]
        which = jnp.where(x == ox, 1, 0)
        return remote(
            source(order, half),
            held(order, me),
            home_sem.at[order, half],
            pass_recv.at[which, core],
            index_of(ox, oy, half, t),
        )

    def pass_on(order, which, cores):
        ox, oy, oz = OWNERS[order]
        region = held(order, index_of(1 - ox if which == 0 else ox, 1 - oy, cores, t))
        return remote(
            region, region, pass_send.at[which, cores], start_sem.at[0], index_of(ox, oy, core, oz)
        )

    def pass_in(order, which, cores):
        ox, oy, _ = OWNERS[order]
        index = index_of(1 - ox if which == 0 else ox, 1 - oy, cores, t)
        region = held(order, index)
        return remote(region, region, pass_send.at[which, cores], pass_recv.at[which, cores], index)

    def when_passing(order, action):
        ox, oy, oz = OWNERS[order]
        here = (x == ox) & (y == oy)
        far, lone = sides(order)
        for which, planes in ((0, far + lone), (1, lone)):

            @pl.when(here & is_one_of(t, planes))
            def _():
                for cores in range(2):
                    action(order, which, cores)

    for order in (5, 4):
        for half in range(2):

            @pl.when(by_way(order))
            def _():
                to_way(order, half).start()

            @pl.when((me != owner_of(order, half)) & jnp.logical_not(by_way(order)))
            def _():
                collect(order, half).start()

            @pl.when(me == owner_of(order, half))
            def _():
                collect_own(order, half).start()

    vector.start(vec_ref[...])

    def forward(order, which, cores):
        pass_in(order, which, cores).wait_recv()
        pass_on(order, which, cores).start()

    for order in (5, 4):
        when_passing(order, forward)

    for order in (4, 5):
        for half in range(2):

            @pl.when(me != owner_of(order, half))
            def _():
                collect(order, half).wait_send()

    for group in sums:
        group.plane.start()
    for stage in range(3):
        vector.step(stage)

    def contract_rows(left, right):
        return lax.dot_general(left, right, (((1,), (1,)), ((), ())), preferred_element_type=jnp.float32)

    block = 256

    def swap_block(slot, index):
        return pltpu.make_async_remote_copy(
            src_ref=sent.at[index],
            dst_ref=got.at[slot, index],
            send_sem=block_send.at[index],
            recv_sem=block_recv.at[slot, index],
            device_id=place.twin,
            device_id_type=MESH,
        )

    def begin(matrix):
        size, width = matrix.shape
        pltpu.make_async_copy(matrix, matrix, start_sem.at[0]).wait()

        def add_squares(step, total):
            piece = matrix[pl.ds(pl.multiple_of(step * 32, 32), 32), :].astype(jnp.float32)
            piece = piece * piece
            return total + jnp.sum(piece.reshape(4, 8, width // 128, 128), axis=(0, 2))

        squares = lax.fori_loop(0, size // 32, add_squares, jnp.zeros((8, 128), jnp.float32))
        norm_own[...] = jnp.zeros((8, 128), jnp.float32) + jnp.sum(squares)
        swap = pltpu.make_async_remote_copy(
            src_ref=norm_own,
            dst_ref=norm_got,
            send_sem=norm_sem.at[0],
            recv_sem=norm_sem.at[1],
            device_id=place.twin,
            device_id_type=MESH,
        )
        swap.start()
        swap.wait()
        scale = 1.0 / (jnp.sqrt(norm_own[...] + norm_got[...]) + 1e-06)
        scale = scale[0:1, 0:1]

        def scale_rows(step, carry):
            at = pl.ds(pl.multiple_of(step * 32, 32), 32)
            matrix[at, :] = (matrix[at, :].astype(jnp.float32) * scale).astype(jnp.bfloat16)
            return carry

        lax.fori_loop(0, size // 32, scale_rows, 0)

    def iterate(matrix, repeat, part):
        size, width = matrix.shape
        blocks = size // block
        slot = repeat % 2
        if part == 0:
            make_gram(matrix, blocks, slot)
        else:
            make_next(matrix, blocks, width)

    def make_gram(matrix, blocks, slot):

        def share(index, carry):
            at = pl.ds(pl.multiple_of(index * block, block), block)
            sent[index] = contract_rows(matrix[at, :], matrix[...]).astype(jnp.bfloat16)
            swap_block(slot, index).start()
            return carry

        lax.fori_loop(0, blocks, share, 0)

        def add(index, carry):
            at = pl.ds(pl.multiple_of(index * block, block), block)
            swap_block(slot, index).wait()
            total = sent[index].astype(jnp.float32) + got[slot, index].astype(jnp.float32)
            gram[at, :] = total.astype(jnp.bfloat16)
            return carry

        lax.fori_loop(0, blocks, add, 0)

    def make_next(matrix, blocks, width):
        def polynomial(index, carry):
            at = pl.ds(pl.multiple_of(index * block, block), block)
            square = jnp.dot(gram[at, :], gram[...], preferred_element_type=jnp.float32)
            poly[at, :] = (coeff_b * gram[at, :].astype(jnp.float32) + coeff_c * square).astype(jnp.bfloat16)
            return carry

        lax.fori_loop(0, blocks, polynomial, 0)

        def advance(index, carry):
            at = columns(index * block, block)
            piece = matrix[:, at]
            moved = jnp.dot(poly[...], piece, preferred_element_type=jnp.float32)
            matrix[:, at] = (coeff_a * piece.astype(jnp.float32) + moved).astype(jnp.bfloat16)
            return carry

        lax.fori_loop(0, width // block, advance, 0)

    def owns(order):
        ox, oy, oz = OWNERS[order]
        return (x == ox) & (y == oy) & (t == oz)

    owns_full = owns(4) | owns(5)
    owns_thin = owns(0) | owns(1) | owns(2) | owns(3)

    def update_attn():
        for group in sums:
            group.finish()
        fresh = 0.5 * mom_ref[...] + attn_sum[...].astype(jnp.float32)
        mom_out[...] = fresh
        attn_ref[...] = fresh.astype(jnp.bfloat16)
        for order in range(4):
            for half in range(2):

                @pl.when(me == owner_of(order, half))
                def _():
                    collect_own(order, half).start()

                @pl.when(me != owner_of(order, half))
                def _():
                    collect(order, half).start()

    def between(repeat, part):
        if repeat == 0 and part == 0:
            for group in sums:
                group.plane.two()
                group.line.step(0)
        if repeat == 0 and part == 1:
            for step in range(1, line - 1):
                for group in sums:
                    group.line.step(step)
        if repeat == 1 and part == 0:
            for group in sums:
                group.line.end()
                group.home.start()
        if repeat == 1 and part == 1:
            update_attn()

    @pl.when(owns_full)
    def _():
        begin(full)

    for group in sums:
        group.plane.one()
    vec_out[...] = vector.end()
    for repeat in range(NS_STEPS):
        for part in range(2):

            @pl.when(owns_full)
            def _():
                iterate(full, repeat, part)

            between(repeat, part)

    def keep(order, half):
        return pltpu.make_async_copy(held(order, me), target(order, half), back_sem.at[order, half])

    def back(order, half, index):
        return remote(held(order, index), target(order, half), send_sem.at[0], back_sem.at[order, half], index)

    def place_in(index):
        dp, z = place_of(index)
        return lax.rem(dp // 2, 2), dp // 4, z, lax.rem(dp, 2)

    def one_aside(order, xs, ys):
        ox, oy, _ = OWNERS[order]
        return (xs != ox) != (ys != oy)

    def back_by_way(order, index):
        xs, ys, z, _ = place_in(index)
        return one_aside(order, xs, ys) & is_one_of(z, sides(order)[0])

    def to_back_way(order, half, index):
        xs, ys, z, cores = place_in(index)
        region = held(order, index)
        first = sides(order)[0][0]
        return remote(
            region, region, send_sem.at[0], pass_recv.at[z - first, cores], index_of(xs, ys, half, OWNERS[order][2])
        )

    def back_in(order, which, cores):
        index = index_of(x, y, cores, sides(order)[0][which])
        region = held(order, index)
        return remote(region, region, pass_send.at[which, cores], pass_recv.at[which, cores], index)

    def back_on(order, half, which, cores):
        index = index_of(x, y, cores, sides(order)[0][which])
        return remote(
            held(order, index), target(order, half), pass_send.at[which, cores], back_sem.at[order, half], index
        )

    def when_back_way(order, action):
        for half in range(2):

            @pl.when(one_aside(order, x, y) & (t == OWNERS[order][2]) & (core == half))
            def _():
                for which in range(len(sides(order)[0])):
                    for cores in range(2):
                        action(order, half, which, cores)

    def each_device(order, half, action, passed):
        def body(step, carry):
            index = lax.rem(me + step, devices)
            if order < 4:
                action(order, half, index)
            else:

                @pl.when(back_by_way(order, index) == passed)
                def _():
                    action(order, half, index)

            return carry

        lax.fori_loop(1, devices, body, 0)

    def give_back(orders):
        for order in orders:
            for half in range(2):

                @pl.when(me == owner_of(order, half))
                def _():
                    if order >= 4:
                        each_device(order, half, lambda *at: to_back_way(*at).start(), True)
                    each_device(order, half, lambda *at: back(*at).start(), False)
                    keep(order, half).start()

    give_back((4, 5))

    @pl.when(owns_thin)
    def _():
        begin(thin)
        for repeat in range(NS_STEPS):
            for part in range(2):
                iterate(thin, repeat, part)

    give_back(range(4))

    def return_rows(order, half, which, cores):
        back_in(order, which, cores).wait_recv()
        back_on(order, half, which, cores).start()

    for order in (4, 5):
        when_back_way(order, return_rows)

    for order in range(6):
        for half in range(2):
            keep(order, half).wait()

            @pl.when(me == owner_of(order, half))
            def _():
                if order >= 4:
                    each_device(order, half, lambda *at: to_back_way(*at).wait_send(), True)
                each_device(order, half, lambda *at: back(*at).wait_send(), False)

            if order < 4:

                @pl.when(me != owner_of(order, half))
                def _():
                    collect(order, half).wait_send()

    for order in (4, 5):
        when_passing(order, lambda *at: pass_on(*at).wait_send())
        when_back_way(order, lambda *at: back_on(*at).wait_send())


def finish(out, qkv, vec, attn_mom, mlp_round, line):
    rows = attn_mom.shape[1]
    size, part = 8 * rows, attn_mom.shape[2] // 2
    narrow, wide = part * line, mlp_round.shape[2] // 2 * line
    low, dma = jnp.bfloat16, pltpu.SemaphoreType.DMA
    hbm = pl.BlockSpec(memory_space=pl.ANY)
    vmem = pl.BlockSpec(memory_space=pltpu.VMEM)
    return pl.pallas_call(
        functools.partial(finish_kernel, line),
        out_shape=[
            jax.ShapeDtypeStruct(attn_mom.shape, jnp.float32),
            jax.ShapeDtypeStruct(vec.shape, jnp.float32),
            jax.ShapeDtypeStruct(attn_mom.shape, low),
            jax.ShapeDtypeStruct(mlp_round.shape, low),
        ],
        in_specs=[hbm, hbm, vmem, vmem, hbm],
        out_specs=[vmem, vmem, hbm, hbm],
        scratch_shapes=[
            pltpu.VMEM((size, narrow), low),
            pltpu.VMEM((size, wide), low),
            pltpu.VMEM((size, size), low),
            pltpu.VMEM((size // 256, 256, size), low),
            pltpu.VMEM((2, size // 256, 256, size), low),
            pltpu.VMEM((size, size), low),
            pltpu.VMEM((8, 128), jnp.float32),
            pltpu.VMEM((8, 128), jnp.float32),
            pltpu.VMEM(attn_mom.shape, low),
            pltpu.VMEM(attn_mom.shape, low),
            dma((6, 2)),
            dma((1,)),
            dma((1,)),
            dma((6, 2)),
            dma((2,)),
            dma((size // 256,)),
            dma((2, size // 256)),
            dma((2, 2)),
            dma((2, 2)),
        ]
        + VectorSum.scratch(vec.shape, line)
        + [GroupSum.scratch(count, rows, narrow, line) for count in (1, 3)],
        compiler_params=pltpu.CompilerParams(
            collective_id=3, has_side_effects=True, vmem_limit_bytes=54 * 1024 * 1024
        ),
        name="finish",
    )(
        *(each.reshape(each.shape[0], 2, 2, 2, rows, narrow) for each in (out, qkv)),
        vec,
        attn_mom,
        mlp_round,
    )


def pair_swap(value):
    dp, line = lax.axis_size("dp"), lax.axis_size("tensor")
    pairs = [(i * line + k, (i ^ 1) * line + k) for i in range(dp) for k in range(line)]
    return lax.ppermute(value, ("dp", "tensor"), pairs)


def corner_swap(value, place):
    dp, line = lax.axis_size("dp"), lax.axis_size("tensor")
    pairs = []
    for i in range(1, dp, 2):
        for k in range(0, line, 2):
            pairs += [(i * line + k, (i - 1) * line + k + 1), ((i - 1) * line + k + 1, i * line + k)]
    moved = lax.ppermute(value, ("dp", "tensor"), pairs)
    return jnp.where(place.core == lax.rem(place.tensor, 2), value, moved)


def both_halves(value, place):
    other = pair_swap(value)
    first = place.core == 0
    return jnp.concatenate([jnp.where(first, value, other), jnp.where(first, other, value)], axis=0)


def my_half(whole, place):
    size = whole.shape[0] // CORES
    return lax.dynamic_slice_in_dim(whole, place.core * size, size, 0)


def sum_rows(partial, place):
    size = partial.shape[0] // CORES
    away = lax.dynamic_slice_in_dim(partial, (1 - place.core) * size, size, 0)
    return my_half(partial, place).astype(jnp.float32) + pair_swap(away).astype(jnp.float32)


def sum_whole(partial):
    return partial.astype(jnp.float32) + pair_swap(partial).astype(jnp.float32)


def norm_parts(rows):
    centred = rows - jnp.mean(rows, axis=-1, keepdims=True)
    spread = lax.rsqrt(jnp.mean(centred * centred, axis=-1, keepdims=True) + 1e-05)
    return centred * spread, spread


def norm_back(grad, gain, xhat, spread):
    scaled = grad * gain
    return spread * (
        scaled
        - jnp.mean(scaled, axis=-1, keepdims=True)
        - xhat * jnp.mean(scaled * xhat, axis=-1, keepdims=True)
    )


def on_chip_pair(tokens, cotangent, segments, attn_w, mlp_w, vectors, attn_mom, mlp_mom, vector_mom):
    line = lax.axis_size("tensor")
    place = Place()
    core, t = place.core, place.tensor
    width = tokens.shape[1]
    narrow, wide = attn_w.shape[2] // 2, mlp_w.shape[2] // 4
    total_tokens = tokens.shape[0] * line * lax.axis_size("dp")

    wqkv, wout, w_up, w_down = gather_weights(
        attn_w.astype(jnp.bfloat16), mlp_w.astype(jnp.bfloat16), line
    )
    wout = wout[0]

    def my_columns(row):
        return lax.dynamic_index_in_dim(row.reshape(line, 2, narrow), core, 1, False).reshape(-1)

    def place_columns(piece):
        spread = jnp.zeros((line, 2, narrow), jnp.float32)
        return lax.dynamic_update_slice(spread, piece.reshape(line, 1, narrow), (0, core, 0)).reshape(-1)

    hidden_bias = lax.dynamic_index_in_dim(vectors[8:].reshape(line, 2, 2, wide), core, 1, False)
    hidden_bias = hidden_bias.transpose(1, 0, 2).reshape(2, line * wide)

    x_rows = both_halves(corner_swap(tokens, place), place).astype(jnp.float32)
    grad_low = both_halves(corner_swap(cotangent, place), place)
    seg_pairs = segments.reshape(-1, SEQ)
    seg_own = lax.dynamic_index_in_dim(seg_pairs, t // 2, 0, False)
    seg_ids = jnp.where(core == lax.rem(t, 2), seg_own, pair_swap(seg_own))

    xhat_one, spread_one = norm_parts(x_rows)
    normed = (xhat_one * vectors[0] + vectors[1]).astype(jnp.bfloat16)
    projected = jnp.einsum("td,mdc->mtc", normed, wqkv, preferred_element_type=jnp.float32)
    biases = jnp.stack([my_columns(vectors[2]), jnp.zeros((narrow * line,), jnp.float32), my_columns(vectors[3])])
    qkv = (projected + biases[:, None]).astype(jnp.bfloat16)
    local_heads = qkv.shape[2] // HD
    per = narrow // HD
    local_ids = jnp.arange(local_heads)
    head_ids = (local_ids // per) * (2 * per) + core * per + local_ids % per
    slopes = jnp.exp2(-(8.0 / HEADS) * (head_ids.astype(jnp.float32) + 1.0))
    mixed, log_sums = attend(slopes, seg_ids, qkv)
    branch = sum_whole(contract_last(mixed, wout).astype(jnp.bfloat16))
    middle = x_rows + branch + vectors[4]
    xhat_two, spread_two = norm_parts(middle)
    hidden_low = (xhat_two * vectors[5] + vectors[6]).astype(jnp.bfloat16)
    hidden_pre = (
        jnp.einsum("td,sdc->stc", hidden_low, w_up, preferred_element_type=jnp.float32) + hidden_bias[:, None]
    )
    act_float, gelu_pull = jax.vjp(gelu_tanh, hidden_pre)
    hidden_act = act_float.astype(jnp.bfloat16)
    out_part = jnp.einsum("stc,sdc->td", hidden_act, w_down, preferred_element_type=jnp.float32)
    output = my_half(middle, place) + sum_rows(out_part.astype(jnp.bfloat16), place) + vectors[7]
    output = corner_swap(output.astype(jnp.bfloat16), place)

    grad_down = jnp.einsum("td,stc->sdc", grad_low, hidden_act, preferred_element_type=jnp.float32)
    grad_act = jnp.einsum("td,sdc->stc", grad_low, w_down, preferred_element_type=jnp.float32)
    grad_pre = gelu_pull(grad_act)[0].astype(jnp.bfloat16)
    grad_up = jnp.einsum("td,stc->sdc", hidden_low, grad_pre, preferred_element_type=jnp.float32)
    hidden_sums = jnp.sum(grad_pre, axis=1, dtype=jnp.float32)
    hidden_part = jnp.einsum("stc,sdc->td", grad_pre, w_up, preferred_element_type=jnp.float32)
    grad_hidden = sum_whole(hidden_part.astype(jnp.bfloat16))
    grad_middle = grad_low.astype(jnp.float32) + norm_back(grad_hidden, vectors[5], xhat_two, spread_two)
    grad_mid_low = grad_middle.astype(jnp.bfloat16)
    grad_out = contract_first(grad_mid_low, mixed)
    grad_mixed = jnp.dot(grad_mid_low, wout, preferred_element_type=jnp.float32).astype(jnp.bfloat16)
    low = jnp.bfloat16
    mlp_sum, grad_qkv = attend_back(
        grad_down.astype(low), grad_up.astype(low), slopes, seg_ids, qkv, grad_mixed, mixed, log_sums, line
    )
    grad_proj = jnp.einsum("td,mtc->mdc", normed, grad_qkv, preferred_element_type=jnp.float32)
    bias_sums = jnp.sum(grad_qkv, axis=1, dtype=jnp.float32)
    normed_part = jnp.einsum("mtc,mdc->td", grad_qkv, wqkv, preferred_element_type=jnp.float32)
    grad_normed = sum_rows(normed_part.astype(jnp.bfloat16), place)
    xhat_mine, spread_mine = my_half(xhat_one, place), my_half(spread_one, place)
    grad_mid_mine = my_half(grad_middle, place)
    grad_tokens = grad_mid_mine + norm_back(grad_normed, vectors[0], xhat_mine, spread_mine)
    grad_tokens = corner_swap(grad_tokens.astype(jnp.bfloat16), place).astype(jnp.float32)

    hidden_mine = my_half(grad_hidden, place)
    hidden_grad = lax.dynamic_update_slice(
        jnp.zeros((line, 2, 2, wide), jnp.float32),
        hidden_sums.reshape(2, line, wide).transpose(1, 0, 2)[:, None],
        (0, core, 0, 0),
    )
    vector_rows = jnp.stack(
        [
            jnp.sum(grad_normed * xhat_mine, axis=0),
            jnp.sum(grad_normed, axis=0),
            place_columns(bias_sums[0]),
            place_columns(bias_sums[2]),
            jnp.sum(grad_mid_mine, axis=0),
            jnp.sum(hidden_mine * my_half(xhat_two, place), axis=0),
            jnp.sum(hidden_mine, axis=0),
            jnp.sum(my_half(grad_low, place), axis=0, dtype=jnp.float32),
        ]
    )
    vector_local = jnp.concatenate([vector_rows, hidden_grad.reshape(-1, width)], axis=0)
    padding = jnp.zeros((4, width), jnp.float32)
    mlp_mom_new = 0.5 * mlp_mom + mlp_sum.astype(jnp.float32)
    attn_mom_new, vector_sum, attn_ortho, mlp_ortho = finish(
        grad_out.astype(low)[None],
        grad_proj.astype(low),
        jnp.concatenate([vector_local, padding], axis=0),
        attn_mom,
        mlp_mom_new.astype(low),
        line,
    )
    vector_grads = vector_sum[: vector_local.shape[0]]
    attn_new = attn_w - attn_ortho.astype(jnp.float32)
    mlp_new = mlp_w - math.sqrt(FF / D) * mlp_ortho.astype(jnp.float32)
    vector_mom_new = 0.5 * vector_mom + vector_grads
    vector_new = vectors - 0.1 / math.sqrt(total_tokens) * vector_mom_new
    return (
        output,
        grad_tokens,
        attn_mom_new,
        attn_new,
        mlp_mom_new,
        mlp_new,
        vector_mom_new,
        vector_new,
    )


def solution(mesh):
    in_specs = (
        P(("dp", "tensor"), None),
        P(("dp", "tensor"), None),
        P("dp"),
        P(None, "dp", "tensor"),
        P(None, "dp", "tensor"),
        P(),
        P(None, "dp", "tensor"),
        P(None, "dp", "tensor"),
        P(),
    )
    out_specs = (
        P(("dp", "tensor"), None),
        P(("dp", "tensor"), None),
        P(None, "dp", "tensor"),
        P(None, "dp", "tensor"),
        P(None, "dp", "tensor"),
        P(None, "dp", "tensor"),
        P(),
        P(),
    )
    chips_of_two = (mesh.shape["dp"], mesh.shape["tensor"]) == (8, 4)
    return jax.shard_map(
        on_chip_pair if chips_of_two else on_device, mesh=mesh, in_specs=in_specs, out_specs=out_specs, check_vma=False
    )
```

```python
import functools
import math

import jax
import jax.numpy as jnp
from jax import lax
from jax.experimental import pallas as pl
from jax.experimental.pallas import tpu as pltpu
from jax.sharding import PartitionSpec as P

D = 1024
HEADS = 16
HD = 64
FF = 4096
SEQ = 1024
NS_STEPS = 5
MESH = pl.DeviceIdType.MESH


coeff_a = 3.4445
coeff_b = -4.775
coeff_c = 2.0315


def norm_rows(row_data, gain, shift):
    center = jnp.mean(row_data, axis=-1, keepdims=True)
    centred = row_data - center
    spread = jnp.mean(centred * centred, axis=-1, keepdims=True)
    return centred * lax.rsqrt(spread + 1e-05) * gain + shift


def gelu_tanh(values):
    return jax.nn.gelu(values, approximate=True)


def contract_last(left, right):
    return lax.dot_general(
        left, right, (((1,), (1,)), ((), ())), preferred_element_type=jnp.float32
    )


def contract_first(left, right):
    return lax.dot_general(
        left, right, (((0,), (0,)), ((), ())), preferred_element_type=jnp.float32
    )


def head_slopes(first_head, head_count):
    head_ids = (first_head + jnp.arange(head_count)).astype(jnp.float32)
    return jnp.exp2(-(8.0 / HEADS) * (head_ids + 1.0))


def masked_scores(row_query, key_rows, row_segs, seg_ids, row_start, slopes):
    scores = jnp.einsum("qhd,khd->hqk", row_query, key_rows, preferred_element_type=jnp.float32) * (
        1.0 / math.sqrt(HD)
    )
    query_pos = row_start + jnp.arange(row_query.shape[0])
    key_pos = jnp.arange(key_rows.shape[0])
    distance = (query_pos[:, None] - key_pos[None, :]).astype(jnp.float32)
    scores = scores - slopes[:, None, None] * distance[None]
    same_doc = (
        (row_segs[:, None] == seg_ids[None, :])
        & (row_segs[:, None] > 0)
        & (key_pos[None, :] <= query_pos[:, None])
    )
    allowed = same_doc | (key_pos[None, :] == query_pos[:, None])
    return jnp.where(allowed[None], scores, -1e30)


def attend_forward(query, key_rows, value_rows, seg_ids, slopes, row_block):
    length = key_rows.shape[0]

    def one_block(row_start):
        row_query = lax.dynamic_slice_in_dim(query, row_start, row_block, 0)
        row_segs = lax.dynamic_slice_in_dim(seg_ids, row_start, row_block, 0)
        scores = masked_scores(row_query, key_rows, row_segs, seg_ids, row_start, slopes)
        row_max = jnp.max(scores, axis=-1, keepdims=True)
        exp_scores = jnp.exp(scores - row_max)
        row_total = jnp.sum(exp_scores, axis=-1, keepdims=True)
        attn_probs = (exp_scores / row_total).astype(jnp.bfloat16)
        mixed = jnp.einsum(
            "hqk,khd->qhd", attn_probs, value_rows, preferred_element_type=jnp.float32
        )
        return (mixed.astype(jnp.bfloat16), (row_max + jnp.log(row_total))[..., 0])

    block_starts = jnp.arange(length // row_block) * row_block
    mixed, log_sums = lax.map(one_block, block_starts)
    return (mixed.reshape(length, -1), log_sums)


def attend_backward(query, key_rows, value_rows, seg_ids, log_sums, grad_mixed, slopes, row_block):
    length, head_count, head_dim = key_rows.shape
    factor = 1.0 / math.sqrt(HD)

    def one_block(carry, pieces):
        row_start, row_lse = pieces
        row_query = lax.dynamic_slice_in_dim(query, row_start, row_block, 0)
        row_grad = lax.dynamic_slice_in_dim(grad_mixed, row_start, row_block, 0)
        row_segs = lax.dynamic_slice_in_dim(seg_ids, row_start, row_block, 0)
        scores = masked_scores(row_query, key_rows, row_segs, seg_ids, row_start, slopes)
        attn_probs = jnp.exp(scores - row_lse[:, :, None])
        grad_probs = jnp.einsum(
            "qhd,khd->hqk", row_grad, value_rows, preferred_element_type=jnp.float32
        )
        inner = jnp.sum(grad_probs * attn_probs, axis=-1, keepdims=True)
        grad_scores = (attn_probs * (grad_probs - inner)).astype(jnp.bfloat16)
        grad_query = (
            jnp.einsum("hqk,khd->qhd", grad_scores, key_rows, preferred_element_type=jnp.float32)
            * factor
        )
        grad_keys = (
            carry[0]
            + jnp.einsum("hqk,qhd->khd", grad_scores, row_query, preferred_element_type=jnp.float32)
            * factor
        )
        grad_values = carry[1] + jnp.einsum(
            "hqk,qhd->khd",
            attn_probs.astype(jnp.bfloat16),
            row_grad,
            preferred_element_type=jnp.float32,
        )
        return ((grad_keys, grad_values), grad_query)

    empty = jnp.zeros((length, head_count, head_dim), jnp.float32)
    block_starts = jnp.arange(length // row_block) * row_block
    (grad_keys, grad_values), grad_query = lax.scan(
        one_block, (empty, empty), (block_starts, log_sums)
    )
    return (
        grad_query.reshape(length, -1),
        grad_keys.reshape(length, -1),
        grad_values.reshape(length, -1),
    )


def newton_rows(row_iterate):
    for repeat in range(NS_STEPS + 1):
        whole_iterate = lax.all_gather(row_iterate, "tensor", axis=0, tiled=True)
        if repeat == NS_STEPS:
            break
        square_rows = contract_last(row_iterate, whole_iterate).astype(jnp.bfloat16)
        whole_square = lax.all_gather(square_rows, "tensor", axis=0, tiled=True)
        poly_rows = (
            coeff_b * square_rows.astype(jnp.float32)
            + coeff_c * jnp.dot(square_rows, whole_square, preferred_element_type=jnp.float32)
        ).astype(jnp.bfloat16)
        row_iterate = (
            coeff_a * row_iterate.astype(jnp.float32)
            + jnp.dot(poly_rows, whole_iterate, preferred_element_type=jnp.float32)
        ).astype(jnp.bfloat16)
    return whole_iterate


def on_device(tokens, cotangent, segments, attn_w, mlp_w, vectors, attn_mom, mlp_mom, vector_mom):
    tensor_size = lax.axis_size("tensor")
    dp_size = lax.axis_size("dp")
    tensor_index = lax.axis_index("tensor")
    dp_index = lax.axis_index("dp")
    row_count = tokens.shape[0]
    model_width = tokens.shape[1]
    local_width = attn_w.shape[2]
    local_hidden = mlp_w.shape[2]
    head_count = local_width // HD
    row_block = min(512, SEQ)
    total_tokens = row_count * tensor_size * dp_size
    gathered_attn, gathered_mlp = (
        lax.all_gather(attn_w.astype(jnp.bfloat16), "dp", axis=1, tiled=True),
        lax.all_gather(mlp_w.astype(jnp.bfloat16), "dp", axis=1, tiled=True),
    )
    hidden_bias = vectors[8:].reshape(-1)
    query_bias = lax.dynamic_slice_in_dim(vectors[2], tensor_index * local_width, local_width)
    value_bias = lax.dynamic_slice_in_dim(vectors[3], tensor_index * local_width, local_width)
    x_rows = tokens.astype(jnp.float32)
    normed, pull_first = jax.vjp(norm_rows, x_rows, vectors[0], vectors[1])
    all_normed = lax.all_gather(normed.astype(jnp.bfloat16), "tensor", axis=0, tiled=True)
    seq_count = all_normed.shape[0] // SEQ
    projected = jnp.einsum(
        "td,mdc->mtc", all_normed, gathered_attn[:3], preferred_element_type=jnp.float32
    )
    query = (projected[0] + query_bias).astype(jnp.bfloat16)
    key_rows = projected[1].astype(jnp.bfloat16)
    value_rows = (projected[2] + value_bias).astype(jnp.bfloat16)
    slopes = head_slopes(tensor_index * head_count, head_count)
    seq_shape = (seq_count, SEQ, head_count, HD)
    seq_segs = segments.reshape(seq_count, SEQ)

    def forward_seq(pieces):
        return attend_forward(pieces[0], pieces[1], pieces[2], pieces[3], slopes, row_block)

    mixed, log_sums = lax.map(
        forward_seq,
        (
            query.reshape(seq_shape),
            key_rows.reshape(seq_shape),
            value_rows.reshape(seq_shape),
            seq_segs,
        ),
    )
    mixed = mixed.reshape(-1, local_width)
    w_out = gathered_attn[3]
    middle = (
        x_rows
        + lax.psum_scatter(
            contract_last(mixed, w_out).astype(jnp.bfloat16),
            "tensor",
            scatter_dimension=0,
            tiled=True,
        ).astype(jnp.float32)
        + vectors[4]
    )
    hidden_normed, pull_second = jax.vjp(norm_rows, middle, vectors[5], vectors[6])
    hidden_low = hidden_normed.astype(jnp.bfloat16)
    grad_rows = cotangent.astype(jnp.float32)
    all_hidden = lax.all_gather(hidden_low, "tensor", axis=0, tiled=True)
    w_up = gathered_mlp[0]
    w_down = gathered_mlp[1]
    bias_local = lax.dynamic_slice_in_dim(hidden_bias, tensor_index * local_hidden, local_hidden)
    hidden_pre = jnp.dot(all_hidden, w_up, preferred_element_type=jnp.float32) + bias_local
    act_float, gelu_pull = jax.vjp(gelu_tanh, hidden_pre)
    hidden_act = act_float.astype(jnp.bfloat16)
    output = (
        middle
        + lax.psum_scatter(
            contract_last(hidden_act, w_down).astype(jnp.bfloat16),
            "tensor",
            scatter_dimension=0,
            tiled=True,
        ).astype(jnp.float32)
        + vectors[7]
    )
    all_grad = lax.all_gather(grad_rows.astype(jnp.bfloat16), "tensor", axis=0, tiled=True)
    grad_down = contract_first(all_grad, hidden_act)
    grad_act = jnp.dot(all_grad, w_down, preferred_element_type=jnp.float32)
    grad_pre = gelu_pull(grad_act)[0].astype(jnp.bfloat16)
    grad_up = contract_first(all_hidden, grad_pre)
    bias_part = jnp.sum(grad_pre, axis=0, dtype=jnp.float32)
    hidden_grad = lax.dynamic_update_slice_in_dim(
        jnp.zeros(hidden_bias.shape, jnp.float32), bias_part, tensor_index * local_hidden, 0
    )
    grad_hidden_in = lax.psum_scatter(
        contract_last(grad_pre, w_up).astype(jnp.bfloat16),
        "tensor",
        scatter_dimension=0,
        tiled=True,
    ).astype(jnp.float32)
    mlp_grads = jnp.stack([grad_up, grad_down])
    second_grads = pull_second(grad_hidden_in)
    grad_middle = grad_rows + second_grads[0]
    all_grad_mid = lax.all_gather(grad_middle.astype(jnp.bfloat16), "tensor", axis=0, tiled=True)
    grad_out_w = contract_first(all_grad_mid, mixed)
    grad_mixed = jnp.dot(all_grad_mid, w_out, preferred_element_type=jnp.float32).astype(
        jnp.bfloat16
    )

    def backward_seq(pieces):
        return attend_backward(
            pieces[0], pieces[1], pieces[2], pieces[3], pieces[4], pieces[5], slopes, row_block
        )

    grad_query, grad_keys, grad_values = lax.map(
        backward_seq,
        (
            query.reshape(seq_shape),
            key_rows.reshape(seq_shape),
            value_rows.reshape(seq_shape),
            seq_segs,
            log_sums,
            grad_mixed.reshape(seq_shape),
        ),
    )
    grad_qkv = (
        jnp.stack([grad_query, grad_keys, grad_values])
        .reshape(3, -1, local_width)
        .astype(jnp.bfloat16)
    )
    grad_proj_w = jnp.einsum(
        "td,mtc->mdc", all_normed, grad_qkv, preferred_element_type=jnp.float32
    )
    bias_sums = jnp.sum(grad_qkv, axis=1, dtype=jnp.float32)
    grad_normed = lax.psum_scatter(
        jnp.einsum(
            "mtc,mdc->td", grad_qkv, gathered_attn[:3], preferred_element_type=jnp.float32
        ).astype(jnp.bfloat16),
        "tensor",
        scatter_dimension=0,
        tiled=True,
    ).astype(jnp.float32)
    first_grads = pull_first(grad_normed)
    grad_tokens = grad_middle + first_grads[0]

    def placed(piece, full_size, offset):
        return lax.dynamic_update_slice_in_dim(
            jnp.zeros((full_size,), jnp.float32), piece, offset, 0
        )

    width_offset = tensor_index * local_width
    vector_rows = jnp.stack(
        [
            first_grads[1],
            first_grads[2],
            placed(bias_sums[0], model_width, width_offset),
            placed(bias_sums[2], model_width, width_offset),
            jnp.sum(grad_middle, axis=0),
            second_grads[1],
            second_grads[2],
            jnp.sum(grad_rows, axis=0),
        ]
    )
    vector_local = jnp.concatenate([vector_rows, hidden_grad.reshape(4, model_width)], axis=0)
    attn_grads = jnp.concatenate([grad_proj_w, grad_out_w[None]], axis=0)
    attn_sum, mlp_sum = (
        lax.psum_scatter(
            attn_grads.astype(jnp.bfloat16), "dp", scatter_dimension=1, tiled=True
        ).astype(jnp.float32),
        lax.psum_scatter(
            mlp_grads.astype(jnp.bfloat16), "dp", scatter_dimension=1, tiled=True
        ).astype(jnp.float32),
    )
    attn_mom_new = 0.5 * attn_mom + attn_sum
    mlp_mom_new = 0.5 * mlp_mom + mlp_sum
    attn_round = attn_mom_new.astype(jnp.bfloat16)
    mlp_round = mlp_mom_new.astype(jnp.bfloat16)
    attn_float = attn_round.astype(jnp.float32)
    mlp_float = mlp_round.astype(jnp.float32)
    norm_parts = jnp.concatenate(
        [jnp.sum(attn_float * attn_float, axis=(1, 2)), jnp.sum(mlp_float * mlp_float, axis=(1, 2))]
    )
    vector_grads, norm_sums = lax.psum((vector_local, norm_parts), ("dp", "tensor"))
    frob_norms = jnp.sqrt(norm_sums)
    owners = [order * dp_size // 6 for order in range(6)]
    owned_norm = jnp.zeros((), jnp.float32)
    for order in range(6):
        owned_norm = owned_norm + jnp.where(dp_index == owners[order], frob_norms[order], 0.0)
    block_rows = attn_w.shape[1]
    slice_rows = model_width // tensor_size
    full_cols = local_hidden * tensor_size
    rows_attn, rows_mlp = (
        lax.all_gather(attn_round, "tensor", axis=2, tiled=True),
        lax.all_gather(mlp_round, "tensor", axis=2, tiled=True),
    )
    padded_attn = jnp.pad(rows_attn, ((0, 0), (0, 0), (0, full_cols - model_width)))
    all_rows = jnp.concatenate([padded_attn, rows_mlp], axis=0)
    outgoing = jnp.zeros((dp_size, block_rows, full_cols), jnp.bfloat16)
    for order in range(6):
        outgoing = outgoing.at[owners[order]].set(all_rows[order])
    incoming = lax.all_to_all(outgoing, "dp", split_axis=0, concat_axis=0, tiled=True)
    owned_whole = incoming.reshape(model_width, full_cols)
    mine = lax.dynamic_slice_in_dim(owned_whole, tensor_index * slice_rows, slice_rows, 0)
    attn_col = tensor_index * local_width
    row_iterate = (mine.astype(jnp.float32) / (owned_norm + 1e-06)).astype(jnp.bfloat16)
    result = newton_rows(row_iterate)
    returned = lax.all_to_all(
        result.reshape(dp_size, block_rows, full_cols),
        "dp",
        split_axis=0,
        concat_axis=0,
        tiled=True,
    )
    attn_blocks = []
    for order in range(4):
        piece = lax.dynamic_slice_in_dim(returned[owners[order]], attn_col, local_width, 1)
        attn_blocks.append(attn_w[order] - piece.astype(jnp.float32))
    mlp_blocks = []
    for order in range(2):
        piece = lax.dynamic_slice_in_dim(
            returned[owners[4 + order]], tensor_index * local_hidden, local_hidden, 1
        )
        mlp_blocks.append(mlp_w[order] - math.sqrt(FF / D) * piece.astype(jnp.float32))
    attn_new = jnp.stack(attn_blocks)
    mlp_new = jnp.stack(mlp_blocks)
    vector_mom_new = 0.5 * vector_mom + vector_grads
    vector_new = vectors - 0.1 / math.sqrt(total_tokens) * vector_mom_new
    return (
        output.astype(jnp.bfloat16),
        grad_tokens,
        attn_mom_new,
        attn_new,
        mlp_mom_new,
        mlp_new,
        vector_mom_new,
        vector_new,
    )


CORES = 2


class Place:
    def __init__(self):
        self.dp = lax.axis_index("dp")
        self.tensor = lax.axis_index("tensor")
        self.core = lax.rem(self.dp, 2)
        self.chip = self.dp // 2
        self.x = lax.rem(self.chip, 2)
        self.y = self.chip // 2
        self.twin = (self.dp + 1 - 2 * self.core, self.tensor)
        self.across_x = (self.dp + 2 - 4 * self.x, self.tensor)
        self.across_y = (self.dp + 4 - 8 * self.y, self.tensor)
        self.right = (self.dp, self.tensor + 1)
        self.left = (self.dp, self.tensor - 1)
        self.stays = self.core == lax.rem(self.tensor, 2)
        self.corner = (self.dp + 1 - 2 * self.core, self.tensor - 1 + 2 * self.core)


def greet(place, line):
    barrier = pltpu.get_barrier_semaphore()

    def signal(device):
        pl.semaphore_signal(barrier, inc=1, device_id=device, device_id_type=MESH)

    signal(place.twin)
    signal(place.across_x)
    signal(place.across_y)

    for other in range(line):

        @pl.when(place.tensor != other)
        def _():
            signal((place.dp, other))

    @pl.when(jnp.logical_not(place.stays))
    def _():
        signal(place.corner)

    pl.semaphore_wait(barrier, jnp.where(place.stays, 3 + line - 1, 3 + line))


def columns(start, size):
    return pl.ds(pl.multiple_of(start, 128), size)


class RowSwap:
    SCRATCH = 2

    @staticmethod
    def scratch():
        return [pltpu.SemaphoreType.DMA((1,)), pltpu.SemaphoreType.DMA((4,))]

    def __init__(self, place, rows_ref, whole_ref, scratch):
        self.place, self.rows_ref, self.whole_ref = place, rows_ref, whole_ref
        self.own_sem, self.sem = scratch
        self.size = rows_ref.shape[0]

    def at(self, core):
        return self.whole_ref.at[pl.ds(pl.multiple_of(core * self.size, self.size), self.size), :]

    def copy(self, slot, source, target, device):
        return pltpu.make_async_remote_copy(
            src_ref=source,
            dst_ref=target,
            send_sem=self.sem.at[slot],
            recv_sem=self.sem.at[slot + 1],
            device_id=device,
            device_id_type=MESH,
        )

    def own(self):
        return pltpu.make_async_copy(self.rows_ref, self.at(self.place.core), self.own_sem.at[0])

    def away(self):
        return self.copy(0, self.rows_ref, self.at(1 - self.place.core), self.place.corner)

    def hand_own(self):
        return self.copy(2, self.rows_ref, self.at(self.place.core), self.place.twin)

    def hand_got(self):
        return self.copy(2, self.at(self.place.core), self.at(self.place.core), self.place.twin)

    def start(self):
        @pl.when(self.place.stays)
        def _():
            self.own().start()
            self.hand_own().start()

        @pl.when(jnp.logical_not(self.place.stays))
        def _():
            self.away().start()

    def step(self):
        @pl.when(jnp.logical_not(self.place.stays))
        def _():
            self.away().wait()
            self.hand_got().start()

    def end(self):
        @pl.when(self.place.stays)
        def _():
            self.own().wait()

        self.hand_got().wait()


class WeightGather:
    def __init__(self, place, line, groups, scratch):
        self.place, self.line, self.groups = place, line, groups
        self.own_sem, self.send_sem, self.recv_sem = scratch
        self.last = len(groups) - 1
        self.to_right, self.to_left = 1, line
        self.half_x, self.half_y, self.rest_y, self.rest_x = (2 * line - 1 + k for k in range(4))

    @staticmethod
    def scratch(count, line):
        dma = pltpu.SemaphoreType.DMA
        return [dma((count,)), dma((count, 2 * line + 3)), dma((count, 2 * line + 3))]

    def copy(self, group, slot, source, target, device):
        return pltpu.make_async_remote_copy(
            src_ref=source,
            dst_ref=target,
            send_sem=self.send_sem.at[group, slot],
            recv_sem=self.recv_sem.at[group, slot],
            device_id=device,
            device_id_type=MESH,
        )

    def same(self, group, slot, region, device):
        return self.copy(group, slot, region, region, device)

    def chunk(self, group, index):
        ref, width, _ = self.groups[group]
        cols = columns(index * width, width)
        if group == self.last:
            return ref.at[:, :, :, :, :, cols]
        return ref.at[:, self.place.y, self.place.x, :, :, cols]

    def corner(self, group, ys, xs, half):
        ref, width, _ = self.groups[group]
        if group == self.last:
            return ref.at[:, ys, xs, half, :, columns(self.place.tensor * width, width)]
        return ref.at[:, ys, xs, half]

    def entry(self, group, half):
        ref, width, _ = self.groups[group]
        return ref.at[:, self.place.y, self.place.x, half, :, columns(self.place.tensor * width, width)]

    def own(self, group):
        core = self.place.core
        return pltpu.make_async_copy(self.groups[group][2](core), self.entry(group, core), self.own_sem.at[group])

    def first(self, group):
        core = self.place.core
        return self.copy(group, 0, self.groups[group][2](1 - core), self.entry(group, core), self.place.twin)

    def begin(self, group):
        self.own(group).start()
        self.first(group).start()

    def enter(self, group):
        self.own(group).wait()
        self.same(group, 0, self.entry(group, 1 - self.place.core), self.place.twin).wait_recv()

    def hop(self, group, step, left):
        t = self.place.tensor
        index = t + step - 1 if left else t - step + 1
        slot = (self.to_left if left else self.to_right) + step - 1
        return self.same(group, slot, self.chunk(group, index), self.place.left if left else self.place.right)

    def arrival(self, group, step, left):
        t = self.place.tensor
        index = t + step if left else t - step
        slot = (self.to_left if left else self.to_right) + step - 1
        return self.same(group, slot, self.chunk(group, index), self.place.right if left else self.place.left)

    def sends(self, step, left):
        t, line = self.place.tensor, self.line
        return (t > 0) & (t + step <= line) if left else (t < line - 1) & (t >= step - 1)

    def line_start(self, group):
        for left in (False, True):

            @pl.when(self.sends(1, left))
            def _():
                self.hop(group, 1, left).start()

    def line_step(self, group, step):
        t, line = self.place.tensor, self.line
        for left in (False, True):

            @pl.when(t + step <= line - 1 if left else t >= step)
            def _():
                self.arrival(group, step, left).wait_recv()

            if step < line - 1:

                @pl.when(self.sends(step + 1, left))
                def _():
                    self.hop(group, step + 1, left).start()

    def line_most(self, group):
        for step in range(1, self.line - 1):
            self.line_step(group, step)

    def line_end(self, group):
        self.line_step(group, self.line - 1)

    def plane_start(self, group):
        place = self.place
        self.same(group, self.half_x, self.corner(group, place.y, place.x, 0), place.across_x).start()
        self.same(group, self.half_y, self.corner(group, place.y, place.x, 1), place.across_y).start()

    def plane_step(self, group):
        place, both = self.place, pl.ds(0, 2)
        self.same(group, self.half_x, self.corner(group, place.y, 1 - place.x, 0), place.across_x).wait_recv()
        self.same(group, self.rest_y, self.corner(group, place.y, both, 0), place.across_y).start()
        self.same(group, self.half_y, self.corner(group, 1 - place.y, place.x, 1), place.across_y).wait_recv()
        self.same(group, self.rest_x, self.corner(group, both, place.x, 1), place.across_x).start()

    def plane_end(self, group):
        place, both = self.place, pl.ds(0, 2)
        self.same(group, self.rest_y, self.corner(group, 1 - place.y, both, 0), place.across_y).wait_recv()
        self.same(group, self.rest_x, self.corner(group, both, 1 - place.x, 1), place.across_x).wait_recv()

    def wait_sends(self, group):
        place, both = self.place, pl.ds(0, 2)
        self.first(group).wait_send()
        for step in range(1, self.line):
            for left in (False, True):

                @pl.when(self.sends(step, left))
                def _():
                    self.hop(group, step, left).wait_send()

        self.same(group, self.half_x, self.corner(group, place.y, place.x, 0), place.across_x).wait_send()
        self.same(group, self.half_y, self.corner(group, place.y, place.x, 1), place.across_y).wait_send()
        self.same(group, self.rest_y, self.corner(group, place.y, both, 0), place.across_y).wait_send()
        self.same(group, self.rest_x, self.corner(group, both, place.x, 1), place.across_x).wait_send()


def add_blocks(target, sources):
    lead, rows = target.shape[:-2], target.shape[-2]
    per = rows // 32

    def body(step, carry):
        block, at = step // per, []
        for size in lead[::-1]:
            at.insert(0, lax.rem(block, size))
            block = block // size
        at = tuple(at) + (pl.ds(pl.multiple_of(lax.rem(step, per) * 32, 32), 32),)
        total = sources[0][at].astype(jnp.float32)
        for source in sources[1:]:
            total = total + source[at].astype(jnp.float32)
        target[at] = total.astype(target.dtype)
        return carry

    lax.fori_loop(0, math.prod(lead) * per, body, 0)


class PlaneSum:
    @staticmethod
    def scratch(count, rows, width):
        pair = pltpu.VMEM((count, 2, rows, width), jnp.bfloat16)
        single = pltpu.VMEM((count, rows, width), jnp.bfloat16)
        dma = pltpu.SemaphoreType.DMA
        return [pair] * 4 + [single] * 2 + [dma((2,)), dma((4,)), dma((4,))]

    SCRATCH = 9

    def __init__(self, place, source, result, scratch):
        self.place, self.source, self.result = place, source, result
        self.own, self.got, self.last = scratch[0:2], scratch[2:4], scratch[4:6]
        self.own_sem, self.send_sem, self.recv_sem = scratch[6:9]

    def copy(self, slot, source, target, device):
        return pltpu.make_async_remote_copy(
            src_ref=source,
            dst_ref=target,
            send_sem=self.send_sem.at[slot],
            recv_sem=self.recv_sem.at[slot],
            device_id=device,
            device_id_type=MESH,
        )

    def cut(self, index, mine):
        both, place = pl.ds(0, 2), self.place
        if index == 0:
            return self.source.at[:, place.y if mine else 1 - place.y, both, 0]
        return self.source.at[:, both, place.x if mine else 1 - place.x, 1]

    def load(self, index):
        return pltpu.make_async_copy(self.cut(index, True), self.own[index], self.own_sem.at[index])

    def first(self, index):
        device = self.place.across_x if index else self.place.across_y
        return self.copy(index, self.cut(index, False), self.got[index], device)

    def second(self, index):
        mine = self.place.y if index else self.place.x
        device = self.place.across_y if index else self.place.across_x
        return self.copy(2 + index, self.own[index].at[:, 1 - mine], self.last[index], device)

    def start(self):
        for index in range(2):
            self.first(index).start()
            self.load(index).start()

    def one(self):
        for index in range(2):
            mine = self.place.y if index else self.place.x
            self.load(index).wait()
            self.first(index).wait_recv()
            own, got = self.own[index], self.got[index]
            add_blocks(own.at[:, 1 - mine], (own.at[:, 1 - mine], got.at[:, 1 - mine]))
            self.second(index).start()
            add_blocks(own.at[:, mine], (own.at[:, mine], got.at[:, mine]))

    def two(self):
        for index in range(2):
            mine = self.place.y if index else self.place.x
            self.second(index).wait_recv()
            add_blocks(self.result.at[:, index], (self.own[index].at[:, mine], self.last[index]))

    def sent(self):
        for index in range(2):
            self.first(index).wait_send()
            self.second(index).wait_send()


class LineSum:
    @staticmethod
    def scratch(shape, line):
        dma = pltpu.SemaphoreType.DMA
        return [pltpu.VMEM(shape, jnp.bfloat16)] * 2 + [dma((2, line)), dma((2, line))]

    SCRATCH = 4

    def __init__(self, place, line, value, result, scratch):
        self.place, self.line, self.value, self.result = place, line, value, result
        self.got = scratch[0:2]
        self.send_sem, self.recv_sem = scratch[2:4]
        self.width = value.shape[-1] // line

    def part(self, ref, index):
        return ref.at[(slice(None),) * (len(ref.shape) - 1) + (slice(index * self.width, (index + 1) * self.width),)]

    def hop(self, index, left):
        return pltpu.make_async_remote_copy(
            src_ref=self.part(self.value, index),
            dst_ref=self.part(self.got[left], index),
            send_sem=self.send_sem.at[left, index],
            recv_sem=self.recv_sem.at[left, index],
            device_id=self.place.left if left else self.place.right,
            device_id_type=MESH,
        )

    def step(self, step):
        for left in range(2):
            for index in range(self.line):
                away = index if left else self.line - 1 - index
                order = step - away
                plane = self.line - 1 - order if left else order
                if order < 0 or (plane <= index if left else plane >= index):
                    continue

                @pl.when(self.place.tensor == plane)
                def _():
                    if order > 0:
                        self.hop(index, left).wait_recv()
                        value = self.part(self.value, index)
                        add_blocks(value, (value, self.part(self.got[left], index)))
                    if away > 0:
                        self.hop(index - 1 if left else index + 1, left).wait_send()
                    self.hop(index, left).start()

    def end(self):
        for index in range(self.line):

            @pl.when(self.place.tensor == index)
            def _():
                sources = [self.part(self.value, index)]
                for left in range(2):
                    if index < self.line - 1 if left else index > 0:
                        self.hop(index, left).wait_recv()
                        sources.append(self.part(self.got[left], index))
                add_blocks(self.result, sources)

    def sent(self):
        for index in range(self.line):

            @pl.when(self.place.tensor == index)
            def _():
                if index > 0:
                    self.hop(index - 1, 1).wait_send()
                if index < self.line - 1:
                    self.hop(index + 1, 0).wait_send()


class HomeCopy:
    def __init__(self, place, value, target, scratch):
        self.place, self.value, self.target = place, value, target
        self.own_sem, self.sem = scratch

    SCRATCH = 2

    @staticmethod
    def scratch():
        return [pltpu.SemaphoreType.DMA((1,)), pltpu.SemaphoreType.DMA((2,))]

    def keep(self):
        return pltpu.make_async_copy(self.value.at[:, self.place.core], self.target, self.own_sem.at[0])

    def give(self):
        return pltpu.make_async_remote_copy(
            src_ref=self.value.at[:, 1 - self.place.core],
            dst_ref=self.target,
            send_sem=self.sem.at[0],
            recv_sem=self.sem.at[1],
            device_id=self.place.twin,
            device_id_type=MESH,
        )

    def start(self):
        self.keep().start()
        self.give().start()

    def wait(self):
        self.keep().wait()
        self.give().wait()


class GroupSum:
    @staticmethod
    def scratch(count, rows, width, line, line_first=False):
        low = jnp.bfloat16
        part = width // line
        done = pltpu.VMEM((count, 2, rows, part), low)
        if line_first:
            whole = (count, 2, 2, 2, rows, width)
            held = [pltpu.VMEM(whole, low), pltpu.VMEM(whole[:-1] + (part,), low), pltpu.SemaphoreType.DMA((1,))]
            plane, along = PlaneSum.scratch(count, rows, part), LineSum.scratch(whole, line)
        else:
            middle = (count, 2, rows, width)
            held = [pltpu.VMEM(middle, low)]
            plane, along = PlaneSum.scratch(count, rows, width), LineSum.scratch(middle, line)
        return held + [done] + plane + along + HomeCopy.scratch()

    def __init__(self, place, line, source, target, scratch, line_first=False):
        scratch = list(scratch)

        def take(count):
            taken = scratch[:count]
            del scratch[:count]
            return taken

        if line_first:
            whole, middle, load_sem = take(3)
            self.load = lambda: pltpu.make_async_copy(source, whole, load_sem.at[0])
        else:
            (middle,) = take(1)
        (done,) = take(1)
        plane, along = take(PlaneSum.SCRATCH), take(LineSum.SCRATCH)
        if line_first:
            self.line = LineSum(place, line, whole, middle, along)
            self.plane = PlaneSum(place, middle, done, plane)
        else:
            self.plane = PlaneSum(place, source, middle, plane)
            self.line = LineSum(place, line, middle, done, along)
        self.home = HomeCopy(place, done, target, take(HomeCopy.SCRATCH))

    def finish(self):
        self.home.wait()
        self.plane.sent()
        self.line.sent()


class VectorSum:
    @staticmethod
    def scratch(shape, line):
        return [
            pltpu.VMEM((4,) + shape, jnp.float32),
            pltpu.VMEM((3,) + shape, jnp.float32),
            pltpu.VMEM((line,) + shape, jnp.float32),
            pltpu.SemaphoreType.DMA((4, max(line, 3))),
        ]

    def __init__(self, place, line, scratch):
        self.place, self.line = place, line
        self.sums, self.got, self.along, self.sem = scratch

    def copy(self, stage):
        place = self.place
        return pltpu.make_async_remote_copy(
            src_ref=self.sums.at[stage],
            dst_ref=self.got.at[stage],
            send_sem=self.sem.at[0, stage],
            recv_sem=self.sem.at[1, stage],
            device_id=(place.twin, place.across_x, place.across_y)[stage],
            device_id_type=MESH,
        )

    def hop(self, other, source):
        return pltpu.make_async_remote_copy(
            src_ref=self.sums.at[3],
            dst_ref=self.along.at[source],
            send_sem=self.sem.at[2, other],
            recv_sem=self.sem.at[3, source],
            device_id=(self.place.dp, other),
            device_id_type=MESH,
        )

    def start(self, value, first_rows):
        self.sums[0] = value
        for index, row in enumerate(first_rows):
            self.sums[0, index : index + 1, :] = row
        self.copy(0).start()

    def step(self, stage):
        self.copy(stage).wait()
        self.sums[stage + 1] = self.sums[stage] + self.got[stage]
        if stage < 2:
            self.copy(stage + 1).start()
            return
        self.along[self.place.tensor] = self.sums[3]
        for other in range(self.line):

            @pl.when(self.place.tensor != other)
            def _():
                self.hop(other, self.place.tensor).start()

    def end(self):
        t = self.place.tensor
        for other in range(self.line):

            @pl.when(t != other)
            def _():
                self.hop(other, t).wait_send()
                self.hop(t, other).wait_recv()

        total = self.along[0]
        for other in range(1, self.line):
            total = total + self.along[other]
        return total


LOG2E = 1.4426950408889634
FAR = 1e32
ROW_BLOCK = 256


def fill_distance(seg_rows, seg_cols, distance):
    def body(step, carry):
        start = pl.multiple_of(step * 64, 64)
        shape = (64, distance.shape[1])
        row = lax.broadcasted_iota(jnp.int32, shape, 0) + start
        col = lax.broadcasted_iota(jnp.int32, shape, 1)
        segs = seg_rows[pl.ds(start, 64), :]
        same = (segs == seg_cols[...]) & (segs > 0) & (col <= row)
        allowed = same | (col == row)
        distance[pl.ds(start, 64), :] = jnp.where(allowed, (row - col).astype(jnp.float32), FAR)
        return carry

    lax.fori_loop(0, distance.shape[0] // 64, body, 0)


def head_lanes(dtype):
    lane = lax.broadcasted_iota(jnp.int32, (1, 2 * HD), 1)
    first = (lane < HD).astype(jnp.float32)
    return (first.astype(dtype), (1.0 - first).astype(dtype))


def attend_group(group, slopes, qkv, mixed, lse, distance):
    length = qkv.shape[1]
    cols = columns(group * 2 * HD, 2 * HD)
    masks = head_lanes(jnp.bfloat16)
    first = head_lanes(jnp.float32)[0] > 0.5
    factor = LOG2E / math.sqrt(HD)
    keys_t = qkv[1, :, cols].T
    values = qkv[2, :, cols]
    for start in range(0, length, ROW_BLOCK):
        stop = start + ROW_BLOCK
        rows = slice(start, stop)
        query = qkv[0, rows, cols]
        parts, sums = [], []
        for head in range(2):
            slope = slopes[2 * group + head] * LOG2E
            scores = jnp.dot(query * masks[head], keys_t[:, :stop], preferred_element_type=jnp.float32)
            scores = scores * factor - slope * distance[rows, :stop]
            top = jnp.max(scores, axis=1, keepdims=True)
            probs = jnp.exp2(scores - top)
            total = jnp.sum(probs, axis=1, keepdims=True)
            out = jnp.dot(probs.astype(jnp.bfloat16), values[:stop], preferred_element_type=jnp.float32)
            parts.append(out / total)
            sums.append(top + jnp.log2(total))
        mixed[rows, cols] = jnp.where(first, parts[0], parts[1]).astype(jnp.bfloat16)
        lse[rows, cols] = jnp.where(first, sums[0], sums[1])


def normalize(rows):
    centred = rows - jnp.mean(rows, axis=1, keepdims=True)
    return centred * lax.rsqrt(jnp.mean(centred * centred, axis=1, keepdims=True) + 1e-05)


def forward_kernel(
    line, attn_ref, mlp_ref, tokens_ref, slopes, seg_rows, seg_cols, qkv_bias, hidden_bias, vectors,
    qkv_w, out_w, up_w, down_w, tokens_out, qkv_out, mixed_out, lse_out, normed_out, middle_out,
    hidden_out, act_out, bend_out, *scratch
):
    (x_v, normed, qkv_wv, out_wv, up_wv, qkv, mixed, lse, distance, part, got, middle, hidden, act, bend) = scratch[:15]
    load_sem, store_sem, swap_send, swap_recv = scratch[15:19]
    place = Place()
    narrow, wide = attn_ref.shape[2] // 2, mlp_ref.shape[2] // 4
    size = normed.shape[0]

    def attn_source(index):
        return lambda core: attn_ref.at[index : index + 1, :, columns(core * narrow, narrow)]

    def mlp_source(index, half):
        return lambda core: mlp_ref.at[index : index + 1, :, columns((2 * core + half) * wide, wide)]

    groups = [(qkv_w.at[index : index + 1], narrow, attn_source(index)) for index in range(3)]
    groups.append((out_w, narrow, attn_source(3)))
    groups += [(up_w.at[half : half + 1], wide, mlp_source(0, half)) for half in range(2)]
    groups += [(down_w.at[half : half + 1], wide, mlp_source(1, half)) for half in range(2)]
    query, key, value, outer, up_a, up_b, down_a, down_b = range(8)
    gather = WeightGather(place, line, groups, scratch[19:22])
    tokens = RowSwap(place, tokens_ref, tokens_out, scratch[22:24])

    def load(group):
        if group < 3:
            source, target = qkv_w.at[group], qkv_wv.at[group]
        elif group == outer:
            source, target = out_w, out_wv
        else:
            source, target = up_w.at[group - up_a], up_wv.at[group - up_a]
        return pltpu.make_async_copy(source, target, load_sem.at[group])

    x_load = pltpu.make_async_copy(tokens_out, x_v, load_sem.at[7])
    pairs = (
        (qkv, qkv_out),
        (mixed, mixed_out),
        (lse, lse_out),
        (normed, normed_out),
        (middle, middle_out),
        (hidden, hidden_out),
        (act.at[0], act_out.at[0]),
        (act.at[1], act_out.at[1]),
        (bend.at[0], bend_out.at[0]),
        (bend.at[1], bend_out.at[1]),
    )

    def store(index):
        return pltpu.make_async_copy(*pairs[index], store_sem.at[index])

    def normalize_tokens():
        def body(step, carry):
            at = pl.ds(pl.multiple_of(step * 32, 32), 32)
            normal = normalize(x_v[at, :].astype(jnp.float32))
            normed[at, :] = (normal * vectors[0:1, :] + vectors[1:2, :]).astype(jnp.bfloat16)
            return carry

        lax.fori_loop(0, size // 32, body, 0, unroll=4)

    def project(group):
        load(group).wait()
        weight = qkv_wv[group].reshape(size, qkv.shape[2])

        def body(step, carry):
            at = pl.ds(pl.multiple_of(step * 512, 512), 512)
            out = jnp.dot(normed[at, :], weight, preferred_element_type=jnp.float32)
            qkv[group, at, :] = (out + qkv_bias[group : group + 1, :]).astype(jnp.bfloat16)
            return carry

        lax.fori_loop(0, size // 512, body, 0)

    def swap(index):
        at = pl.ds(pl.multiple_of(index * 256, 256), 256)
        return pltpu.make_async_remote_copy(
            src_ref=part.at[at, :],
            dst_ref=got.at[at, :],
            send_sem=swap_send.at[index],
            recv_sem=swap_recv.at[index],
            device_id=place.twin,
            device_id_type=MESH,
        )

    def project_out(index, carry):
        at = pl.ds(pl.multiple_of(index * 256, 256), 256)
        weight = out_wv[0].reshape(size, mixed.shape[1])
        part[at, :] = contract_last(mixed[at, :], weight).astype(jnp.bfloat16)
        swap(index).start()
        return carry

    def add_branch(index, carry):
        swap(index).wait()

        def body(step, carry):
            at = pl.ds(pl.multiple_of(index * 256 + step * 32, 32), 32)
            branch = part[at, :].astype(jnp.float32) + got[at, :].astype(jnp.float32)
            total = x_v[at, :].astype(jnp.float32) + branch + vectors[4:5, :]
            middle[at, :] = total
            hidden[at, :] = (normalize(total) * vectors[5:6, :] + vectors[6:7, :]).astype(jnp.bfloat16)
            return carry

        return lax.fori_loop(0, 8, body, carry, unroll=4)

    def feed(half):
        load(up_a + half).wait()

        def body(step, carry):
            at = pl.ds(pl.multiple_of(step * 256, 256), 256)
            weight = up_wv[half].reshape(size, act.shape[2])
            pre = jnp.dot(hidden[at, :], weight, preferred_element_type=jnp.float32)
            pre = pre + hidden_bias[half : half + 1, :]
            square = pre * pre
            bent = jnp.tanh(0.7978845608 * pre * (1.0 + 0.044715 * square))
            inner = 0.7978845608 * (1.0 + 3.0 * 0.044715 * square)
            act[half, at, :] = (0.5 * pre * (1.0 + bent)).astype(jnp.bfloat16)
            bend[half, at, :] = (0.5 * (1.0 + bent) + 0.5 * pre * (1.0 - bent * bent) * inner).astype(jnp.bfloat16)
            return carry

        lax.fori_loop(0, size // 256, body, 0)
        store(6 + half).start()
        store(8 + half).start()

    greet(place, line)
    for group in (query, down_b, key, value, outer, up_a, up_b, down_a):
        gather.begin(group)
    gather.enter(query)
    gather.line_start(query)
    gather.enter(down_b)
    gather.plane_start(down_b)
    gather.enter(key)
    gather.line_most(query)
    gather.line_start(key)
    tokens.start()
    gather.line_end(query)
    gather.plane_start(query)
    gather.plane_step(down_b)
    gather.enter(value)
    gather.line_most(key)
    gather.line_start(value)
    gather.line_end(key)
    gather.plane_step(query)
    gather.plane_start(key)
    gather.plane_end(down_b)
    gather.line_most(value)
    gather.line_end(value)
    gather.enter(outer)
    gather.line_start(outer)
    gather.plane_end(query)
    load(query).start()
    gather.plane_step(key)
    gather.plane_start(value)
    tokens.step()
    fill_distance(seg_rows, seg_cols, distance)
    gather.enter(up_a)
    gather.line_most(outer)
    gather.line_start(up_a)
    gather.plane_end(key)
    load(key).start()
    gather.line_end(outer)
    gather.plane_step(value)
    gather.plane_start(outer)
    tokens.end()
    x_load.start()
    x_load.wait()
    normalize_tokens()
    store(3).start()
    gather.enter(up_b)
    gather.line_most(up_a)
    gather.line_start(up_b)
    project(query)
    gather.line_end(up_a)
    gather.line_start(down_b)
    gather.plane_end(value)
    load(value).start()
    gather.plane_step(outer)
    gather.plane_start(up_a)
    project(key)
    project(value)
    store(0).start()

    def beside(index):
        if index == 0:
            gather.enter(down_a)
            gather.line_most(up_b)
            gather.line_start(down_a)
            gather.plane_end(outer)
            load(outer).start()
        if index == 1:
            gather.line_end(up_b)
            gather.plane_step(up_a)
            gather.plane_start(up_b)
        if index == 2:
            gather.line_step(down_b, 1)
        if index == 3:
            gather.line_most(down_a)

    def attend(index, carry):
        attend_group(index, slopes, qkv, mixed, lse, distance)
        for order in range(4):

            @pl.when(index == order)
            def _():
                beside(order)

        return carry

    lax.fori_loop(0, qkv.shape[2] // (2 * HD), attend, 0)
    store(1).start()
    store(2).start()
    load(outer).wait()
    lax.fori_loop(0, size // 256, project_out, 0)
    gather.plane_step(up_b)
    gather.line_end(down_a)
    gather.plane_start(down_a)
    lax.fori_loop(0, size // 256, add_branch, 0)
    store(4).start()
    store(5).start()
    gather.plane_end(up_a)
    load(up_a).start()
    feed(0)
    for step in range(2, line - 1):
        gather.line_step(down_b, step)
    gather.plane_step(down_a)
    gather.plane_end(up_b)
    load(up_b).start()
    feed(1)
    gather.line_end(down_b)
    gather.plane_end(down_a)
    for index in range(len(pairs)):
        store(index).wait()
    for group in range(len(groups)):
        gather.wait_sends(group)


def forward(attn_low, mlp_low, tokens, slopes, seg_ids, qkv_bias, hidden_bias, vectors, line):
    rows = attn_low.shape[1]
    narrow, wide = attn_low.shape[2] // 2 * line, mlp_low.shape[2] // 4 * line
    length, width = 2 * tokens.shape[0], tokens.shape[1]
    low, dma = jnp.bfloat16, pltpu.SemaphoreType.DMA
    vmem = pl.BlockSpec(memory_space=pltpu.VMEM)
    hbm = pl.BlockSpec(memory_space=pl.ANY)

    def whole(count, columns_held):
        return (count, 2, 2, 2, rows, columns_held)

    kept = [
        ((3, length, narrow), low),
        ((length, narrow), low),
        ((length, narrow), jnp.float32),
        ((length, width), low),
        ((length, width), jnp.float32),
        ((length, width), low),
        ((2, length, wide), low),
        ((2, length, wide), low),
    ]
    outs = [(whole(3, narrow), low), (whole(1, narrow), low), (whole(2, wide), low), (whole(2, wide), low)]
    outs += [((length, width), low)] + kept
    held = [(length, width)] * 2 + [whole(3, narrow), whole(1, narrow), whole(2, wide)]
    results = pl.pallas_call(
        functools.partial(forward_kernel, line),
        out_shape=[jax.ShapeDtypeStruct(*each) for each in outs],
        in_specs=[hbm] * 3 + [pl.BlockSpec(memory_space=pltpu.SMEM)] + [vmem] * 5,
        out_specs=[hbm] * len(outs),
        scratch_shapes=[pltpu.VMEM(each, low) for each in held]
        + [pltpu.VMEM(*each) for each in kept[:3]]
        + [pltpu.VMEM((length, length), jnp.float32)]
        + [pltpu.VMEM((length, width), low)] * 2
        + [pltpu.VMEM(*each) for each in kept[4:]]
        + [dma((8,)), dma((10,)), dma((length // 256,)), dma((length // 256,))]
        + WeightGather.scratch(8, line)
        + RowSwap.scratch(),
        compiler_params=pltpu.CompilerParams(
            collective_id=1, has_side_effects=True, vmem_limit_bytes=62 * 1024 * 1024
        ),
        name="forward",
    )(
        attn_low,
        mlp_low,
        tokens,
        slopes,
        seg_ids.reshape(-1, 1),
        seg_ids.reshape(1, -1),
        qkv_bias,
        hidden_bias,
        vectors,
    )
    return [each.reshape(each.shape[0], length, -1) for each in results[:4]] + list(results[4:])


def attend_back_group(group, slopes, qkv, grad, mixed, lse, out, distance, dk_acc, dv_acc):
    length = qkv.shape[1]
    cols = columns(group * 2 * HD, 2 * HD)
    masks = head_lanes(jnp.bfloat16)
    wide_masks = head_lanes(jnp.float32)
    first = wide_masks[0] > 0.5
    factor = LOG2E / math.sqrt(HD)
    shrink = 1.0 / math.sqrt(HD)
    keys, values = qkv[1, :, cols], qkv[2, :, cols]
    keys_t = keys.T
    values_t = values.T
    dk_acc[...] = jnp.zeros_like(dk_acc)
    dv_acc[...] = jnp.zeros_like(dv_acc)
    for start in range(0, length, ROW_BLOCK):
        stop = start + ROW_BLOCK
        rows = slice(start, stop)
        query, grads, log_sums = qkv[0, rows, cols], grad[rows, cols], lse[rows, cols]
        query_t, grads_t = query.T, grads.T
        product = grads.astype(jnp.float32) * mixed[rows, cols].astype(jnp.float32)
        parts = []
        for head in range(2):
            slope = slopes[2 * group + head] * LOG2E
            lanes = slice(head * HD, (head + 1) * HD)
            scores = jnp.dot(query * masks[head], keys_t[:, :stop], preferred_element_type=jnp.float32)
            log_sum = log_sums[:, head * HD : head * HD + 1]
            probs = jnp.exp2(scores * factor - slope * distance[rows, :stop] - log_sum)
            grad_probs = jnp.dot(grads * masks[head], values_t[:, :stop], preferred_element_type=jnp.float32)
            inner = jnp.sum(product * wide_masks[head], axis=1, keepdims=True)
            grad_scores = (probs * (grad_probs - inner)).astype(jnp.bfloat16)
            parts.append(jnp.dot(grad_scores, keys[:stop], preferred_element_type=jnp.float32))
            dk_acc[lanes, :stop] += jnp.dot(query_t[lanes, :], grad_scores, preferred_element_type=jnp.float32)
            dv_acc[lanes, :stop] += jnp.dot(
                grads_t[lanes, :], probs.astype(jnp.bfloat16), preferred_element_type=jnp.float32
            )
        out[0, rows, cols] = (jnp.where(first, parts[0], parts[1]) * shrink).astype(jnp.bfloat16)
    out[1, :, cols] = (dk_acc[...].T * shrink).astype(jnp.bfloat16)
    out[2, :, cols] = dv_acc[...].T.astype(jnp.bfloat16)


def back_kernel(
    line, down_ref, up_ref, out_ref, slopes, seg_rows, seg_cols, qkv, grad, mixed, lse, weights, normed,
    mlp_home, attn_home, normed_part, bias_sums, grads, projected, distance, dk_acc, dv_acc, *scratch
):
    place = Place()
    wide, narrow = mlp_home.shape[2] // 4, attn_home.shape[2] // 2

    def mlp_target(index, part):
        return mlp_home.at[index : index + 1, :, columns((2 * place.core + part) * wide, wide)]

    def attn_target(lo, hi):
        return attn_home.at[lo:hi, :, columns(place.core * narrow, narrow)]

    groups = [
        GroupSum(place, line, down_ref.at[0:1], mlp_target(1, 0), scratch[0]),
        GroupSum(place, line, down_ref.at[1:2], mlp_target(1, 1), scratch[1]),
        GroupSum(place, line, up_ref.at[0:1], mlp_target(0, 0), scratch[2]),
        GroupSum(place, line, out_ref, attn_target(3, 4), scratch[3]),
        GroupSum(place, line, projected, attn_target(0, 3), scratch[4]),
        GroupSum(place, line, up_ref.at[1:2], mlp_target(0, 1), scratch[5], line_first=True),
    ]
    one, two, three, outer, inner, last = groups

    def attend(group, carry):
        attend_back_group(group, slopes, qkv, grad, mixed, lse, grads, distance, dk_acc, dv_acc)
        return carry

    def project(index, carry):
        left = normed[:, columns(index * 256, 256)].T
        for order in range(3):
            piece = jnp.dot(left, grads[order], preferred_element_type=jnp.float32).astype(jnp.bfloat16)
            projected[order, index // 2, lax.rem(index, 2)] = piece.reshape(2, 128, piece.shape[1])
        return carry

    def unproject(index, carry):
        at = pl.ds(pl.multiple_of(index * 256, 256), 256)
        total = contract_last(grads[0, at, :], weights[0])
        for order in range(1, 3):
            total = total + contract_last(grads[order, at, :], weights[order])
        normed_part[at, :] = total.astype(jnp.bfloat16)
        return carry

    greet(place, line)
    one.plane.start()
    last.load().start()
    last.load().wait()
    last.line.step(0)
    fill_distance(seg_rows, seg_cols, distance)
    pairs = qkv.shape[2] // (2 * HD)
    lax.fori_loop(0, pairs // 2, attend, 0)
    one.plane.one()
    two.plane.start()
    last.line.step(1)
    lax.fori_loop(pairs // 2, pairs, attend, 0)
    one.plane.two()
    one.line.step(0)
    two.plane.one()
    lax.fori_loop(0, normed.shape[1] // 256, project, 0)
    inner.plane.start()
    for step in range(2, line - 1):
        last.line.step(step)
    for step in range(1, line - 1):
        one.line.step(step)
    two.plane.two()
    two.line.step(0)
    lax.fori_loop(0, normed.shape[0] // 256, unproject, 0)
    for order in range(3):
        bias_sums[order : order + 1, :] = jnp.sum(grads[order].astype(jnp.float32), axis=0, keepdims=True)
    one.line.end()
    one.home.start()
    last.line.end()
    last.plane.start()
    inner.plane.one()
    three.plane.start()
    for step in range(1, line - 1):
        two.line.step(step)
    last.plane.one()
    two.line.end()
    two.home.start()
    inner.plane.two()
    inner.line.step(0)
    last.plane.two()
    last.home.start()
    three.plane.one()
    outer.plane.start()
    for step in range(1, line - 1):
        inner.line.step(step)
    three.plane.two()
    three.line.step(0)
    inner.line.end()
    inner.home.start()
    outer.plane.one()
    three.line.step(1)
    outer.plane.two()
    outer.line.step(0)
    for step in range(2, line - 1):
        three.line.step(step)
    for step in range(1, line - 1):
        outer.line.step(step)
    three.line.end()
    three.home.start()
    outer.line.end()
    outer.home.start()
    for group in groups:
        group.finish()


def attend_back(down, up, out, slopes, seg_ids, qkv, grad, mixed, lse, weights, normed, line):
    _, length, width = qkv.shape
    rows, wide = down.shape[1] // 8, down.shape[2]
    size = normed.shape[1]
    vmem = pl.BlockSpec(memory_space=pltpu.VMEM)
    hbm = pl.BlockSpec(memory_space=pl.ANY)
    low = jnp.bfloat16
    return pl.pallas_call(
        functools.partial(back_kernel, line),
        out_shape=[
            jax.ShapeDtypeStruct((2, rows, 4 * wide // line), low),
            jax.ShapeDtypeStruct((4, rows, 2 * width // line), low),
            jax.ShapeDtypeStruct((length, size), low),
            jax.ShapeDtypeStruct((3, width), jnp.float32),
        ],
        in_specs=[hbm] * 3 + [pl.BlockSpec(memory_space=pltpu.SMEM)] + [vmem] * 8,
        out_specs=[hbm, hbm, vmem, vmem],
        scratch_shapes=[
            pltpu.VMEM(qkv.shape, low),
            pltpu.VMEM((3, 2, 2, 2, rows, width), low),
            pltpu.VMEM((length, length), jnp.float32),
            pltpu.VMEM((2 * HD, length), jnp.float32),
            pltpu.VMEM((2 * HD, length), jnp.float32),
        ]
        + [GroupSum.scratch(1, rows, wide, line)] * 3
        + [GroupSum.scratch(1, rows, width, line), GroupSum.scratch(3, rows, width, line)]
        + [GroupSum.scratch(1, rows, wide, line, line_first=True)],
        compiler_params=pltpu.CompilerParams(
            collective_id=2, has_side_effects=True, vmem_limit_bytes=62 * 1024 * 1024
        ),
        name="attend_back",
    )(
        *(each.reshape(-1, 2, 2, 2, rows, each.shape[2]) for each in (down, up, out)),
        slopes,
        seg_ids.reshape(-1, 1),
        seg_ids.reshape(1, -1),
        qkv,
        grad,
        mixed,
        lse,
        weights,
        normed,
    )


OWNERS = ((1, 0, 0), (1, 0, 3), (0, 1, 0), (0, 1, 3), (0, 0, 1), (1, 1, 2))


def finish_kernel(
    line, attn_ref, mlp_ref, vec_ref, gain, part_ref, xhat, spread, grad_mid, attn_home, mlp_home, vec_out, dx_out, *scratch
):
    (thin, full, gram, sent, got, poly, norm_own, norm_got, dx, away, mine) = scratch[:11]
    (home_sem, start_sem, send_sem, back_sem, norm_sem, block_send, block_recv, pass_send, pass_recv, dx_sem) = scratch[11:21]
    place = Place()
    x, y, t, core = place.x, place.y, place.tensor, place.core
    me = place.dp * line + t
    devices = 8 * line
    rows = mlp_ref.shape[1]
    narrow, wide = attn_ref.shape[2] // 2, mlp_ref.shape[2] // 2
    barrier = pltpu.get_barrier_semaphore()

    def place_of(index):
        return (index // line, lax.rem(index, line))

    def index_of(xs, ys, cores, z):
        return ((2 * ys + xs) * 2 + cores) * line + z

    def meet(step, carry):
        pl.semaphore_signal(
            barrier, inc=1, device_id=place_of(lax.rem(me + step, devices)), device_id_type=MESH
        )
        return carry

    lax.fori_loop(1, devices, meet, 0)
    pl.semaphore_wait(barrier, devices - 1)

    vector = VectorSum(place, line, scratch[21:25])

    def source(order, half):
        if order < 4:
            return attn_ref.at[order, :, half * narrow : (half + 1) * narrow]
        return mlp_ref.at[order - 4, :, half * wide : (half + 1) * wide]

    def held(order, index):
        dp, tensor = place_of(index)
        row = pl.ds(pl.multiple_of(dp * rows, rows), rows)
        if order < 4:
            return thin.at[row, columns(tensor * narrow, narrow)]
        return full.at[row, columns(tensor * wide, wide)]

    def target(order, half):
        if order < 4:
            return attn_home.at[order, :, half * narrow : (half + 1) * narrow]
        return mlp_home.at[order - 4, :, half * wide : (half + 1) * wide]

    def remote(source_ref, target_ref, send, recv, index):
        return pltpu.make_async_remote_copy(
            src_ref=source_ref,
            dst_ref=target_ref,
            send_sem=send,
            recv_sem=recv,
            device_id=place_of(index),
            device_id_type=MESH,
        )

    def owner_of(order, half):
        ox, oy, oz = OWNERS[order]
        return index_of(ox, oy, half, oz)

    def collect(order, half):
        return remote(source(order, half), held(order, me), home_sem.at[order, half], start_sem.at[0], owner_of(order, half))

    def collect_own(order, half):
        return pltpu.make_async_copy(source(order, half), held(order, me), start_sem.at[0])

    def sides(order):
        oz = OWNERS[order][2]
        above, below = list(range(oz + 1, line)), list(range(oz))
        return (above, below) if len(above) > len(below) else (below, above)

    def is_one_of(value, options):
        found = value < 0
        for option in options:
            found = found | (value == option)
        return found

    def by_way(order):
        ox, oy, oz = OWNERS[order]
        return (y != oy) & (t != oz) & ((x != ox) | is_one_of(t, sides(order)[1]))

    def to_way(order, half):
        ox, oy, _ = OWNERS[order]
        which = jnp.where(x == ox, 1, 0)
        return remote(
            source(order, half),
            held(order, me),
            home_sem.at[order, half],
            pass_recv.at[which, core],
            index_of(ox, oy, half, t),
        )

    def pass_on(order, which, cores):
        ox, oy, oz = OWNERS[order]
        region = held(order, index_of(1 - ox if which == 0 else ox, 1 - oy, cores, t))
        return remote(
            region, region, pass_send.at[which, cores], start_sem.at[0], index_of(ox, oy, core, oz)
        )

    def pass_in(order, which, cores):
        ox, oy, _ = OWNERS[order]
        index = index_of(1 - ox if which == 0 else ox, 1 - oy, cores, t)
        region = held(order, index)
        return remote(region, region, pass_send.at[which, cores], pass_recv.at[which, cores], index)

    def when_passing(order, action):
        ox, oy, oz = OWNERS[order]
        here = (x == ox) & (y == oy)
        far, lone = sides(order)
        for which, planes in ((0, far + lone), (1, lone)):

            @pl.when(here & is_one_of(t, planes))
            def _():
                for cores in range(2):
                    action(order, which, cores)

    half_rows = dx.shape[0]

    def rows_of(cores):
        return part_ref.at[pl.ds(pl.multiple_of(cores * half_rows, half_rows), half_rows), :]

    part_swap = pltpu.make_async_remote_copy(
        src_ref=rows_of(1 - core),
        dst_ref=away,
        send_sem=dx_sem.at[0],
        recv_sem=dx_sem.at[1],
        device_id=place.twin,
        device_id_type=MESH,
    )
    part_load = pltpu.make_async_copy(rows_of(core), mine, dx_sem.at[2])
    part_swap.start()
    part_load.start()

    for order in (5, 4, 0, 1, 2, 3):
        for half in range(2):
            direct = me != owner_of(order, half)
            if order >= 4:

                @pl.when(by_way(order))
                def _():
                    to_way(order, half).start()

                direct = direct & jnp.logical_not(by_way(order))

            @pl.when(direct)
            def _():
                collect(order, half).start()

            @pl.when(me == owner_of(order, half))
            def _():
                collect_own(order, half).start()

    def forward(order, which, cores):
        pass_in(order, which, cores).wait_recv()
        pass_on(order, which, cores).start()

    for order in (5, 4):
        when_passing(order, forward)

    part_swap.wait()
    part_load.wait()
    step_rows = 16

    def dx_rows(step, sums):
        at = pl.ds(pl.multiple_of(step * step_rows, step_rows), step_rows)
        grad = mine[at, :].astype(jnp.float32) + away[at, :].astype(jnp.float32)
        hat = xhat[at, :]
        product = grad * hat
        scaled = grad * gain[...]
        inner = jnp.mean(scaled * hat, axis=1, keepdims=True)
        back_grad = spread[at, :] * (scaled - jnp.mean(scaled, axis=1, keepdims=True) - hat * inner)
        dx[at, :] = (grad_mid[at, :] + back_grad).astype(jnp.bfloat16)
        fold = (step_rows // 8, 8, grad.shape[1])
        return (
            sums[0] + jnp.sum(product.reshape(fold), axis=0),
            sums[1] + jnp.sum(grad.reshape(fold), axis=0),
        )

    empty = jnp.zeros((8, gain.shape[1]), jnp.float32)
    gain_sum, shift_sum = lax.fori_loop(0, half_rows // step_rows, dx_rows, (empty, empty))
    dx_keep = pltpu.make_async_copy(dx, dx_out, dx_sem.at[2])
    dx_away = pltpu.make_async_remote_copy(
        src_ref=dx,
        dst_ref=dx_out,
        send_sem=dx_sem.at[3],
        recv_sem=dx_sem.at[4],
        device_id=place.corner,
        device_id_type=MESH,
    )

    @pl.when(place.stays)
    def _():
        dx_keep.start()

    @pl.when(jnp.logical_not(place.stays))
    def _():
        dx_away.start()

    vector.start(
        vec_ref[...],
        (jnp.sum(gain_sum, axis=0, keepdims=True), jnp.sum(shift_sum, axis=0, keepdims=True)),
    )

    def contract_rows(left, right):
        return lax.dot_general(left, right, (((1,), (1,)), ((), ())), preferred_element_type=jnp.float32)

    block = 256

    def swap_block(slot, index):
        return pltpu.make_async_remote_copy(
            src_ref=sent.at[index],
            dst_ref=got.at[slot, index],
            send_sem=block_send.at[index],
            recv_sem=block_recv.at[slot, index],
            device_id=place.twin,
            device_id_type=MESH,
        )

    def begin(matrix):
        size, width = matrix.shape
        pltpu.make_async_copy(matrix, matrix, start_sem.at[0]).wait()

        def add_squares(step, total):
            piece = matrix[pl.ds(pl.multiple_of(step * 32, 32), 32), :].astype(jnp.float32)
            piece = piece * piece
            return total + jnp.sum(piece.reshape(4, 8, width // 128, 128), axis=(0, 2))

        squares = lax.fori_loop(0, size // 32, add_squares, jnp.zeros((8, 128), jnp.float32))
        norm_own[...] = jnp.zeros((8, 128), jnp.float32) + jnp.sum(squares)
        swap = pltpu.make_async_remote_copy(
            src_ref=norm_own,
            dst_ref=norm_got,
            send_sem=norm_sem.at[0],
            recv_sem=norm_sem.at[1],
            device_id=place.twin,
            device_id_type=MESH,
        )
        swap.start()
        swap.wait()
        scale = 1.0 / (jnp.sqrt(norm_own[...] + norm_got[...]) + 1e-06)
        scale = scale[0:1, 0:1]

        def scale_rows(step, carry):
            at = pl.ds(pl.multiple_of(step * 32, 32), 32)
            matrix[at, :] = (matrix[at, :].astype(jnp.float32) * scale).astype(jnp.bfloat16)
            return carry

        lax.fori_loop(0, size // 32, scale_rows, 0)

    def iterate(matrix, repeat):
        size, width = matrix.shape
        blocks = size // block
        slot = repeat % 2

        def share(index, carry):
            at = pl.ds(pl.multiple_of(index * block, block), block)
            sent[index] = contract_rows(matrix[at, :], matrix[...]).astype(jnp.bfloat16)
            swap_block(slot, index).start()
            return carry

        lax.fori_loop(0, blocks, share, 0)

        def add(index, carry):
            at = pl.ds(pl.multiple_of(index * block, block), block)
            swap_block(slot, index).wait()
            total = sent[index].astype(jnp.float32) + got[slot, index].astype(jnp.float32)
            gram[at, :] = total.astype(jnp.bfloat16)
            return carry

        lax.fori_loop(0, blocks, add, 0)
        square = jnp.dot(gram[...], gram[...], preferred_element_type=jnp.float32)
        poly[...] = (coeff_b * gram[...].astype(jnp.float32) + coeff_c * square).astype(jnp.bfloat16)
        step_width = min(width, 1024)

        def advance(index, carry):
            at = columns(index * step_width, step_width)
            moved = jnp.dot(poly[...], matrix[:, at], preferred_element_type=jnp.float32)
            matrix[:, at] = (coeff_a * matrix[:, at].astype(jnp.float32) + moved).astype(jnp.bfloat16)
            return carry

        lax.fori_loop(0, width // step_width, advance, 0)

    def owns(order):
        ox, oy, oz = OWNERS[order]
        return (x == ox) & (y == oy) & (t == oz)

    owns_full = owns(4) | owns(5)
    owns_thin = owns(0) | owns(1) | owns(2) | owns(3)

    @pl.when(owns_thin)
    def _():
        begin(thin)

    @pl.when(owns_full)
    def _():
        begin(full)

    for repeat in range(NS_STEPS):

        @pl.when(owns_thin)
        def _():
            iterate(thin, repeat)

        @pl.when(owns_full)
        def _():
            iterate(full, repeat)

        if repeat < 3:
            vector.step(repeat)
        if repeat == 3:
            vec_out[...] = vector.end()

    def keep(order, half):
        return pltpu.make_async_copy(held(order, me), target(order, half), back_sem.at[order, half])

    def back(order, half, index):
        return remote(held(order, index), target(order, half), send_sem.at[0], back_sem.at[order, half], index)

    def place_in(index):
        dp, z = place_of(index)
        return lax.rem(dp // 2, 2), dp // 4, z, lax.rem(dp, 2)

    def one_aside(order, xs, ys):
        ox, oy, _ = OWNERS[order]
        return (xs != ox) != (ys != oy)

    def back_by_way(order, index):
        xs, ys, z, _ = place_in(index)
        return one_aside(order, xs, ys) & is_one_of(z, sides(order)[0])

    def to_back_way(order, half, index):
        xs, ys, z, cores = place_in(index)
        region = held(order, index)
        first = sides(order)[0][0]
        return remote(
            region, region, send_sem.at[0], pass_recv.at[z - first, cores], index_of(xs, ys, half, OWNERS[order][2])
        )

    def back_in(order, which, cores):
        index = index_of(x, y, cores, sides(order)[0][which])
        region = held(order, index)
        return remote(region, region, pass_send.at[which, cores], pass_recv.at[which, cores], index)

    def back_on(order, half, which, cores):
        index = index_of(x, y, cores, sides(order)[0][which])
        return remote(
            held(order, index), target(order, half), pass_send.at[which, cores], back_sem.at[order, half], index
        )

    def when_back_way(order, action):
        for half in range(2):

            @pl.when(one_aside(order, x, y) & (t == OWNERS[order][2]) & (core == half))
            def _():
                for which in range(len(sides(order)[0])):
                    for cores in range(2):
                        action(order, half, which, cores)

    def each_device(order, half, action, passed):
        def body(step, carry):
            index = lax.rem(me + step, devices)
            if order < 4:
                action(order, half, index)
            else:

                @pl.when(back_by_way(order, index) == passed)
                def _():
                    action(order, half, index)

            return carry

        lax.fori_loop(1, devices, body, 0)

    def give_back(orders):
        for order in orders:
            for half in range(2):

                @pl.when(me == owner_of(order, half))
                def _():
                    if order >= 4:
                        each_device(order, half, lambda *at: to_back_way(*at).start(), True)
                    each_device(order, half, lambda *at: back(*at).start(), False)
                    keep(order, half).start()

    give_back((4, 5, 0, 1, 2, 3))

    def return_rows(order, half, which, cores):
        back_in(order, which, cores).wait_recv()
        back_on(order, half, which, cores).start()

    for order in (4, 5):
        when_back_way(order, return_rows)

    for order in range(6):
        for half in range(2):
            keep(order, half).wait()

            @pl.when(me == owner_of(order, half))
            def _():
                if order >= 4:
                    each_device(order, half, lambda *at: to_back_way(*at).wait_send(), True)
                each_device(order, half, lambda *at: back(*at).wait_send(), False)

            @pl.when(me != owner_of(order, half))
            def _():
                collect(order, half).wait_send()

    for order in (4, 5):
        when_passing(order, lambda *at: pass_on(*at).wait_send())
        when_back_way(order, lambda *at: back_on(*at).wait_send())

    @pl.when(place.stays)
    def _():
        dx_keep.wait()

    @pl.when(jnp.logical_not(place.stays))
    def _():
        dx_away.wait()


def finish(attn_round, mlp_round, vec, gain, normed_part, xhat, spread, grad_mid, line):
    rows = attn_round.shape[1]
    size = 8 * rows
    narrow, wide = attn_round.shape[2] // 2 * line, mlp_round.shape[2] // 2 * line
    low, dma = jnp.bfloat16, pltpu.SemaphoreType.DMA
    hbm = pl.BlockSpec(memory_space=pl.ANY)
    vmem = pl.BlockSpec(memory_space=pltpu.VMEM)
    half = xhat.shape
    return pl.pallas_call(
        functools.partial(finish_kernel, line),
        out_shape=[
            jax.ShapeDtypeStruct(attn_round.shape, low),
            jax.ShapeDtypeStruct(mlp_round.shape, low),
            jax.ShapeDtypeStruct(vec.shape, jnp.float32),
            jax.ShapeDtypeStruct(half, low),
        ],
        in_specs=[hbm, hbm, vmem, vmem, hbm, vmem, vmem, vmem],
        out_specs=[hbm, hbm, vmem, hbm],
        scratch_shapes=[
            pltpu.VMEM((size, narrow), low),
            pltpu.VMEM((size, wide), low),
            pltpu.VMEM((size, size), low),
            pltpu.VMEM((size // 256, 256, size), low),
            pltpu.VMEM((2, size // 256, 256, size), low),
            pltpu.VMEM((size, size), low),
            pltpu.VMEM((8, 128), jnp.float32),
            pltpu.VMEM((8, 128), jnp.float32),
            pltpu.VMEM(half, low),
            pltpu.VMEM(half, low),
            pltpu.VMEM(half, low),
            dma((6, 2)),
            dma((1,)),
            dma((1,)),
            dma((6, 2)),
            dma((2,)),
            dma((size // 256,)),
            dma((2, size // 256)),
            dma((2, 2)),
            dma((2, 2)),
            dma((5,)),
        ]
        + VectorSum.scratch(vec.shape, line),
        compiler_params=pltpu.CompilerParams(
            collective_id=3, has_side_effects=True, vmem_limit_bytes=56 * 1024 * 1024
        ),
        name="finish",
    )(attn_round, mlp_round, vec, gain.reshape(1, -1), normed_part, xhat, spread, grad_mid)


def pair_swap(value):
    dp, line = lax.axis_size("dp"), lax.axis_size("tensor")
    pairs = [(i * line + k, (i ^ 1) * line + k) for i in range(dp) for k in range(line)]
    return lax.ppermute(value, ("dp", "tensor"), pairs)


def corner_swap(value, place):
    dp, line = lax.axis_size("dp"), lax.axis_size("tensor")
    pairs = []
    for i in range(1, dp, 2):
        for k in range(0, line, 2):
            pairs += [(i * line + k, (i - 1) * line + k + 1), ((i - 1) * line + k + 1, i * line + k)]
    moved = lax.ppermute(value, ("dp", "tensor"), pairs)
    return jnp.where(place.core == lax.rem(place.tensor, 2), value, moved)


def both_halves(value, place):
    other = pair_swap(value)
    first = place.core == 0
    return jnp.concatenate([jnp.where(first, value, other), jnp.where(first, other, value)], axis=0)


def my_half(whole, place):
    size = whole.shape[0] // CORES
    return lax.dynamic_slice_in_dim(whole, place.core * size, size, 0)


def sum_rows(partial, place):
    size = partial.shape[0] // CORES
    away = lax.dynamic_slice_in_dim(partial, (1 - place.core) * size, size, 0)
    return my_half(partial, place).astype(jnp.float32) + pair_swap(away).astype(jnp.float32)


def sum_whole(partial):
    return partial.astype(jnp.float32) + pair_swap(partial).astype(jnp.float32)


def norm_parts(rows):
    centred = rows - jnp.mean(rows, axis=-1, keepdims=True)
    spread = lax.rsqrt(jnp.mean(centred * centred, axis=-1, keepdims=True) + 1e-05)
    return centred * spread, spread


def norm_back(grad, gain, xhat, spread):
    scaled = grad * gain
    return spread * (
        scaled
        - jnp.mean(scaled, axis=-1, keepdims=True)
        - xhat * jnp.mean(scaled * xhat, axis=-1, keepdims=True)
    )


def on_chip_pair(tokens, cotangent, segments, attn_w, mlp_w, vectors, attn_mom, mlp_mom, vector_mom):
    line = lax.axis_size("tensor")
    place = Place()
    core, t = place.core, place.tensor
    width = tokens.shape[1]
    narrow, wide = attn_w.shape[2] // 2, mlp_w.shape[2] // 4
    total_tokens = tokens.shape[0] * line * lax.axis_size("dp")

    def my_columns(row):
        return lax.dynamic_index_in_dim(row.reshape(line, 2, narrow), core, 1, False).reshape(-1)

    def place_columns(piece):
        spread = jnp.zeros((line, 2, narrow), jnp.float32)
        return lax.dynamic_update_slice(spread, piece.reshape(line, 1, narrow), (0, core, 0)).reshape(-1)

    hidden_bias = lax.dynamic_index_in_dim(vectors[8:].reshape(line, 2, 2, wide), core, 1, False)
    hidden_bias = hidden_bias.transpose(1, 0, 2).reshape(2, line * wide)

    seg_pairs = segments.reshape(-1, SEQ)
    seg_own = lax.dynamic_index_in_dim(seg_pairs, t // 2, 0, False)
    seg_ids = jnp.where(core == lax.rem(t, 2), seg_own, pair_swap(seg_own))

    biases = jnp.stack([my_columns(vectors[2]), jnp.zeros((narrow * line,), jnp.float32), my_columns(vectors[3])])
    per = narrow // HD
    local_ids = jnp.arange(per * line)
    head_ids = (local_ids // per) * (2 * per) + core * per + local_ids % per
    slopes = jnp.exp2(-(8.0 / HEADS) * (head_ids.astype(jnp.float32) + 1.0))
    low = jnp.bfloat16
    (
        wqkv, wout, w_up, w_down, x_low, qkv, mixed, log_sums, normed, middle, hidden_low, hidden_act, bend
    ) = forward(
        attn_w.astype(low),
        mlp_w.astype(low),
        tokens,
        slopes,
        seg_ids,
        biases,
        hidden_bias,
        vectors,
        line,
    )
    wout = wout[0]
    cotangent, middle = lax.optimization_barrier((cotangent, middle))
    grad_low = both_halves(corner_swap(cotangent, place), place)
    xhat_one, spread_one = norm_parts(x_low.astype(jnp.float32))
    xhat_two, spread_two = norm_parts(middle)
    out_part = jnp.einsum("stc,sdc->td", hidden_act, w_down, preferred_element_type=jnp.float32)
    output = my_half(middle, place) + sum_rows(out_part.astype(jnp.bfloat16), place) + vectors[7]
    output = corner_swap(output.astype(jnp.bfloat16), place)

    grad_down = jnp.einsum("td,stc->sdc", grad_low, hidden_act, preferred_element_type=jnp.float32)
    grad_act = jnp.einsum("td,sdc->stc", grad_low, w_down, preferred_element_type=jnp.float32)
    grad_pre = (grad_act * bend.astype(jnp.float32)).astype(jnp.bfloat16)
    grad_up = jnp.einsum("td,stc->sdc", hidden_low, grad_pre, preferred_element_type=jnp.float32)
    hidden_sums = jnp.sum(grad_pre, axis=1, dtype=jnp.float32)
    hidden_part = jnp.einsum("stc,sdc->td", grad_pre, w_up, preferred_element_type=jnp.float32)
    grad_hidden = sum_whole(hidden_part.astype(jnp.bfloat16))
    grad_middle = grad_low.astype(jnp.float32) + norm_back(grad_hidden, vectors[5], xhat_two, spread_two)
    grad_mid_low = grad_middle.astype(jnp.bfloat16)
    grad_out = contract_first(grad_mid_low, mixed)
    grad_mixed = jnp.dot(grad_mid_low, wout, preferred_element_type=jnp.float32).astype(jnp.bfloat16)
    mlp_sum, attn_sum, normed_part, bias_sums = attend_back(
        grad_down.astype(low),
        grad_up.astype(low),
        grad_out.astype(low)[None],
        slopes,
        seg_ids,
        qkv,
        grad_mixed,
        mixed,
        log_sums,
        wqkv,
        normed,
        line,
    )
    grad_mid_mine = my_half(grad_middle, place)
    hidden_mine = my_half(grad_hidden, place)
    hidden_grad = lax.dynamic_update_slice(
        jnp.zeros((line, 2, 2, wide), jnp.float32),
        hidden_sums.reshape(2, line, wide).transpose(1, 0, 2)[:, None],
        (0, core, 0, 0),
    )
    vector_rows = jnp.stack(
        [
            jnp.zeros((width,), jnp.float32),
            jnp.zeros((width,), jnp.float32),
            place_columns(bias_sums[0]),
            place_columns(bias_sums[2]),
            jnp.sum(grad_mid_mine, axis=0),
            jnp.sum(hidden_mine * my_half(xhat_two, place), axis=0),
            jnp.sum(hidden_mine, axis=0),
            jnp.sum(my_half(grad_low, place), axis=0, dtype=jnp.float32),
        ]
    )
    vector_local = jnp.concatenate([vector_rows, hidden_grad.reshape(-1, width)], axis=0)
    padding = jnp.zeros((4, width), jnp.float32)
    attn_mom_new = 0.5 * attn_mom + attn_sum.astype(jnp.float32)
    mlp_mom_new = 0.5 * mlp_mom + mlp_sum.astype(jnp.float32)
    attn_ortho, mlp_ortho, vector_sum, grad_tokens = finish(
        attn_mom_new.astype(low),
        mlp_mom_new.astype(low),
        jnp.concatenate([vector_local, padding], axis=0),
        vectors[0],
        normed_part,
        my_half(xhat_one, place),
        my_half(spread_one, place),
        grad_mid_mine,
        line,
    )
    vector_grads = vector_sum[: vector_local.shape[0]]
    attn_new = attn_w - attn_ortho.astype(jnp.float32)
    mlp_new = mlp_w - math.sqrt(FF / D) * mlp_ortho.astype(jnp.float32)
    vector_mom_new = 0.5 * vector_mom + vector_grads
    vector_new = vectors - 0.1 / math.sqrt(total_tokens) * vector_mom_new
    return (
        output,
        grad_tokens.astype(jnp.float32),
        attn_mom_new,
        attn_new,
        mlp_mom_new,
        mlp_new,
        vector_mom_new,
        vector_new,
    )


def solution(mesh):
    in_specs = (
        P(("dp", "tensor"), None),
        P(("dp", "tensor"), None),
        P("dp"),
        P(None, "dp", "tensor"),
        P(None, "dp", "tensor"),
        P(),
        P(None, "dp", "tensor"),
        P(None, "dp", "tensor"),
        P(),
    )
    out_specs = (
        P(("dp", "tensor"), None),
        P(("dp", "tensor"), None),
        P(None, "dp", "tensor"),
        P(None, "dp", "tensor"),
        P(None, "dp", "tensor"),
        P(None, "dp", "tensor"),
        P(),
        P(),
    )
    chips_of_two = (mesh.shape["dp"], mesh.shape["tensor"]) == (8, 4)
    return jax.shard_map(
        on_chip_pair if chips_of_two else on_device, mesh=mesh, in_specs=in_specs, out_specs=out_specs, check_vma=False
    )
```

```python
import functools
import math

import jax
import jax.numpy as jnp
from jax import lax
from jax.experimental import pallas as pl
from jax.experimental.pallas import tpu as pltpu
from jax.sharding import PartitionSpec as P

D = 1024
HEADS = 16
HD = 64
FF = 4096
SEQ = 1024
NS_STEPS = 5
MESH = pl.DeviceIdType.MESH


coeff_a = 3.4445
coeff_b = -4.775
coeff_c = 2.0315


def norm_rows(row_data, gain, shift):
    center = jnp.mean(row_data, axis=-1, keepdims=True)
    centred = row_data - center
    spread = jnp.mean(centred * centred, axis=-1, keepdims=True)
    return centred * lax.rsqrt(spread + 1e-05) * gain + shift


def gelu_tanh(values):
    return jax.nn.gelu(values, approximate=True)


def contract_last(left, right):
    return lax.dot_general(
        left, right, (((1,), (1,)), ((), ())), preferred_element_type=jnp.float32
    )


def contract_first(left, right):
    return lax.dot_general(
        left, right, (((0,), (0,)), ((), ())), preferred_element_type=jnp.float32
    )


def head_slopes(first_head, head_count):
    head_ids = (first_head + jnp.arange(head_count)).astype(jnp.float32)
    return jnp.exp2(-(8.0 / HEADS) * (head_ids + 1.0))


def masked_scores(row_query, key_rows, row_segs, seg_ids, row_start, slopes):
    scores = jnp.einsum("qhd,khd->hqk", row_query, key_rows, preferred_element_type=jnp.float32) * (
        1.0 / math.sqrt(HD)
    )
    query_pos = row_start + jnp.arange(row_query.shape[0])
    key_pos = jnp.arange(key_rows.shape[0])
    distance = (query_pos[:, None] - key_pos[None, :]).astype(jnp.float32)
    scores = scores - slopes[:, None, None] * distance[None]
    same_doc = (
        (row_segs[:, None] == seg_ids[None, :])
        & (row_segs[:, None] > 0)
        & (key_pos[None, :] <= query_pos[:, None])
    )
    allowed = same_doc | (key_pos[None, :] == query_pos[:, None])
    return jnp.where(allowed[None], scores, -1e30)


def attend_forward(query, key_rows, value_rows, seg_ids, slopes, row_block):
    length = key_rows.shape[0]

    def one_block(row_start):
        row_query = lax.dynamic_slice_in_dim(query, row_start, row_block, 0)
        row_segs = lax.dynamic_slice_in_dim(seg_ids, row_start, row_block, 0)
        scores = masked_scores(row_query, key_rows, row_segs, seg_ids, row_start, slopes)
        row_max = jnp.max(scores, axis=-1, keepdims=True)
        exp_scores = jnp.exp(scores - row_max)
        row_total = jnp.sum(exp_scores, axis=-1, keepdims=True)
        attn_probs = (exp_scores / row_total).astype(jnp.bfloat16)
        mixed = jnp.einsum(
            "hqk,khd->qhd", attn_probs, value_rows, preferred_element_type=jnp.float32
        )
        return (mixed.astype(jnp.bfloat16), (row_max + jnp.log(row_total))[..., 0])

    block_starts = jnp.arange(length // row_block) * row_block
    mixed, log_sums = lax.map(one_block, block_starts)
    return (mixed.reshape(length, -1), log_sums)


def attend_backward(query, key_rows, value_rows, seg_ids, log_sums, grad_mixed, slopes, row_block):
    length, head_count, head_dim = key_rows.shape
    factor = 1.0 / math.sqrt(HD)

    def one_block(carry, pieces):
        row_start, row_lse = pieces
        row_query = lax.dynamic_slice_in_dim(query, row_start, row_block, 0)
        row_grad = lax.dynamic_slice_in_dim(grad_mixed, row_start, row_block, 0)
        row_segs = lax.dynamic_slice_in_dim(seg_ids, row_start, row_block, 0)
        scores = masked_scores(row_query, key_rows, row_segs, seg_ids, row_start, slopes)
        attn_probs = jnp.exp(scores - row_lse[:, :, None])
        grad_probs = jnp.einsum(
            "qhd,khd->hqk", row_grad, value_rows, preferred_element_type=jnp.float32
        )
        inner = jnp.sum(grad_probs * attn_probs, axis=-1, keepdims=True)
        grad_scores = (attn_probs * (grad_probs - inner)).astype(jnp.bfloat16)
        grad_query = (
            jnp.einsum("hqk,khd->qhd", grad_scores, key_rows, preferred_element_type=jnp.float32)
            * factor
        )
        grad_keys = (
            carry[0]
            + jnp.einsum("hqk,qhd->khd", grad_scores, row_query, preferred_element_type=jnp.float32)
            * factor
        )
        grad_values = carry[1] + jnp.einsum(
            "hqk,qhd->khd",
            attn_probs.astype(jnp.bfloat16),
            row_grad,
            preferred_element_type=jnp.float32,
        )
        return ((grad_keys, grad_values), grad_query)

    empty = jnp.zeros((length, head_count, head_dim), jnp.float32)
    block_starts = jnp.arange(length // row_block) * row_block
    (grad_keys, grad_values), grad_query = lax.scan(
        one_block, (empty, empty), (block_starts, log_sums)
    )
    return (
        grad_query.reshape(length, -1),
        grad_keys.reshape(length, -1),
        grad_values.reshape(length, -1),
    )


def newton_rows(row_iterate):
    for repeat in range(NS_STEPS + 1):
        whole_iterate = lax.all_gather(row_iterate, "tensor", axis=0, tiled=True)
        if repeat == NS_STEPS:
            break
        square_rows = contract_last(row_iterate, whole_iterate).astype(jnp.bfloat16)
        whole_square = lax.all_gather(square_rows, "tensor", axis=0, tiled=True)
        poly_rows = (
            coeff_b * square_rows.astype(jnp.float32)
            + coeff_c * jnp.dot(square_rows, whole_square, preferred_element_type=jnp.float32)
        ).astype(jnp.bfloat16)
        row_iterate = (
            coeff_a * row_iterate.astype(jnp.float32)
            + jnp.dot(poly_rows, whole_iterate, preferred_element_type=jnp.float32)
        ).astype(jnp.bfloat16)
    return whole_iterate


def on_device(tokens, cotangent, segments, attn_w, mlp_w, vectors, attn_mom, mlp_mom, vector_mom):
    tensor_size = lax.axis_size("tensor")
    dp_size = lax.axis_size("dp")
    tensor_index = lax.axis_index("tensor")
    dp_index = lax.axis_index("dp")
    row_count = tokens.shape[0]
    model_width = tokens.shape[1]
    local_width = attn_w.shape[2]
    local_hidden = mlp_w.shape[2]
    head_count = local_width // HD
    row_block = min(512, SEQ)
    total_tokens = row_count * tensor_size * dp_size
    gathered_attn, gathered_mlp = (
        lax.all_gather(attn_w.astype(jnp.bfloat16), "dp", axis=1, tiled=True),
        lax.all_gather(mlp_w.astype(jnp.bfloat16), "dp", axis=1, tiled=True),
    )
    hidden_bias = vectors[8:].reshape(-1)
    query_bias = lax.dynamic_slice_in_dim(vectors[2], tensor_index * local_width, local_width)
    value_bias = lax.dynamic_slice_in_dim(vectors[3], tensor_index * local_width, local_width)
    x_rows = tokens.astype(jnp.float32)
    normed, pull_first = jax.vjp(norm_rows, x_rows, vectors[0], vectors[1])
    all_normed = lax.all_gather(normed.astype(jnp.bfloat16), "tensor", axis=0, tiled=True)
    seq_count = all_normed.shape[0] // SEQ
    projected = jnp.einsum(
        "td,mdc->mtc", all_normed, gathered_attn[:3], preferred_element_type=jnp.float32
    )
    query = (projected[0] + query_bias).astype(jnp.bfloat16)
    key_rows = projected[1].astype(jnp.bfloat16)
    value_rows = (projected[2] + value_bias).astype(jnp.bfloat16)
    slopes = head_slopes(tensor_index * head_count, head_count)
    seq_shape = (seq_count, SEQ, head_count, HD)
    seq_segs = segments.reshape(seq_count, SEQ)

    def forward_seq(pieces):
        return attend_forward(pieces[0], pieces[1], pieces[2], pieces[3], slopes, row_block)

    mixed, log_sums = lax.map(
        forward_seq,
        (
            query.reshape(seq_shape),
            key_rows.reshape(seq_shape),
            value_rows.reshape(seq_shape),
            seq_segs,
        ),
    )
    mixed = mixed.reshape(-1, local_width)
    w_out = gathered_attn[3]
    middle = (
        x_rows
        + lax.psum_scatter(
            contract_last(mixed, w_out).astype(jnp.bfloat16),
            "tensor",
            scatter_dimension=0,
            tiled=True,
        ).astype(jnp.float32)
        + vectors[4]
    )
    hidden_normed, pull_second = jax.vjp(norm_rows, middle, vectors[5], vectors[6])
    hidden_low = hidden_normed.astype(jnp.bfloat16)
    grad_rows = cotangent.astype(jnp.float32)
    all_hidden = lax.all_gather(hidden_low, "tensor", axis=0, tiled=True)
    w_up = gathered_mlp[0]
    w_down = gathered_mlp[1]
    bias_local = lax.dynamic_slice_in_dim(hidden_bias, tensor_index * local_hidden, local_hidden)
    hidden_pre = jnp.dot(all_hidden, w_up, preferred_element_type=jnp.float32) + bias_local
    act_float, gelu_pull = jax.vjp(gelu_tanh, hidden_pre)
    hidden_act = act_float.astype(jnp.bfloat16)
    output = (
        middle
        + lax.psum_scatter(
            contract_last(hidden_act, w_down).astype(jnp.bfloat16),
            "tensor",
            scatter_dimension=0,
            tiled=True,
        ).astype(jnp.float32)
        + vectors[7]
    )
    all_grad = lax.all_gather(grad_rows.astype(jnp.bfloat16), "tensor", axis=0, tiled=True)
    grad_down = contract_first(all_grad, hidden_act)
    grad_act = jnp.dot(all_grad, w_down, preferred_element_type=jnp.float32)
    grad_pre = gelu_pull(grad_act)[0].astype(jnp.bfloat16)
    grad_up = contract_first(all_hidden, grad_pre)
    bias_part = jnp.sum(grad_pre, axis=0, dtype=jnp.float32)
    hidden_grad = lax.dynamic_update_slice_in_dim(
        jnp.zeros(hidden_bias.shape, jnp.float32), bias_part, tensor_index * local_hidden, 0
    )
    grad_hidden_in = lax.psum_scatter(
        contract_last(grad_pre, w_up).astype(jnp.bfloat16),
        "tensor",
        scatter_dimension=0,
        tiled=True,
    ).astype(jnp.float32)
    mlp_grads = jnp.stack([grad_up, grad_down])
    second_grads = pull_second(grad_hidden_in)
    grad_middle = grad_rows + second_grads[0]
    all_grad_mid = lax.all_gather(grad_middle.astype(jnp.bfloat16), "tensor", axis=0, tiled=True)
    grad_out_w = contract_first(all_grad_mid, mixed)
    grad_mixed = jnp.dot(all_grad_mid, w_out, preferred_element_type=jnp.float32).astype(
        jnp.bfloat16
    )

    def backward_seq(pieces):
        return attend_backward(
            pieces[0], pieces[1], pieces[2], pieces[3], pieces[4], pieces[5], slopes, row_block
        )

    grad_query, grad_keys, grad_values = lax.map(
        backward_seq,
        (
            query.reshape(seq_shape),
            key_rows.reshape(seq_shape),
            value_rows.reshape(seq_shape),
            seq_segs,
            log_sums,
            grad_mixed.reshape(seq_shape),
        ),
    )
    grad_qkv = (
        jnp.stack([grad_query, grad_keys, grad_values])
        .reshape(3, -1, local_width)
        .astype(jnp.bfloat16)
    )
    grad_proj_w = jnp.einsum(
        "td,mtc->mdc", all_normed, grad_qkv, preferred_element_type=jnp.float32
    )
    bias_sums = jnp.sum(grad_qkv, axis=1, dtype=jnp.float32)
    grad_normed = lax.psum_scatter(
        jnp.einsum(
            "mtc,mdc->td", grad_qkv, gathered_attn[:3], preferred_element_type=jnp.float32
        ).astype(jnp.bfloat16),
        "tensor",
        scatter_dimension=0,
        tiled=True,
    ).astype(jnp.float32)
    first_grads = pull_first(grad_normed)
    grad_tokens = grad_middle + first_grads[0]

    def placed(piece, full_size, offset):
        return lax.dynamic_update_slice_in_dim(
            jnp.zeros((full_size,), jnp.float32), piece, offset, 0
        )

    width_offset = tensor_index * local_width
    vector_rows = jnp.stack(
        [
            first_grads[1],
            first_grads[2],
            placed(bias_sums[0], model_width, width_offset),
            placed(bias_sums[2], model_width, width_offset),
            jnp.sum(grad_middle, axis=0),
            second_grads[1],
            second_grads[2],
            jnp.sum(grad_rows, axis=0),
        ]
    )
    vector_local = jnp.concatenate([vector_rows, hidden_grad.reshape(4, model_width)], axis=0)
    attn_grads = jnp.concatenate([grad_proj_w, grad_out_w[None]], axis=0)
    attn_sum, mlp_sum = (
        lax.psum_scatter(
            attn_grads.astype(jnp.bfloat16), "dp", scatter_dimension=1, tiled=True
        ).astype(jnp.float32),
        lax.psum_scatter(
            mlp_grads.astype(jnp.bfloat16), "dp", scatter_dimension=1, tiled=True
        ).astype(jnp.float32),
    )
    attn_mom_new = 0.5 * attn_mom + attn_sum
    mlp_mom_new = 0.5 * mlp_mom + mlp_sum
    attn_round = attn_mom_new.astype(jnp.bfloat16)
    mlp_round = mlp_mom_new.astype(jnp.bfloat16)
    attn_float = attn_round.astype(jnp.float32)
    mlp_float = mlp_round.astype(jnp.float32)
    norm_parts = jnp.concatenate(
        [jnp.sum(attn_float * attn_float, axis=(1, 2)), jnp.sum(mlp_float * mlp_float, axis=(1, 2))]
    )
    vector_grads, norm_sums = lax.psum((vector_local, norm_parts), ("dp", "tensor"))
    frob_norms = jnp.sqrt(norm_sums)
    owners = [order * dp_size // 6 for order in range(6)]
    owned_norm = jnp.zeros((), jnp.float32)
    for order in range(6):
        owned_norm = owned_norm + jnp.where(dp_index == owners[order], frob_norms[order], 0.0)
    block_rows = attn_w.shape[1]
    slice_rows = model_width // tensor_size
    full_cols = local_hidden * tensor_size
    rows_attn, rows_mlp = (
        lax.all_gather(attn_round, "tensor", axis=2, tiled=True),
        lax.all_gather(mlp_round, "tensor", axis=2, tiled=True),
    )
    padded_attn = jnp.pad(rows_attn, ((0, 0), (0, 0), (0, full_cols - model_width)))
    all_rows = jnp.concatenate([padded_attn, rows_mlp], axis=0)
    outgoing = jnp.zeros((dp_size, block_rows, full_cols), jnp.bfloat16)
    for order in range(6):
        outgoing = outgoing.at[owners[order]].set(all_rows[order])
    incoming = lax.all_to_all(outgoing, "dp", split_axis=0, concat_axis=0, tiled=True)
    owned_whole = incoming.reshape(model_width, full_cols)
    mine = lax.dynamic_slice_in_dim(owned_whole, tensor_index * slice_rows, slice_rows, 0)
    attn_col = tensor_index * local_width
    row_iterate = (mine.astype(jnp.float32) / (owned_norm + 1e-06)).astype(jnp.bfloat16)
    result = newton_rows(row_iterate)
    returned = lax.all_to_all(
        result.reshape(dp_size, block_rows, full_cols),
        "dp",
        split_axis=0,
        concat_axis=0,
        tiled=True,
    )
    attn_blocks = []
    for order in range(4):
        piece = lax.dynamic_slice_in_dim(returned[owners[order]], attn_col, local_width, 1)
        attn_blocks.append(attn_w[order] - piece.astype(jnp.float32))
    mlp_blocks = []
    for order in range(2):
        piece = lax.dynamic_slice_in_dim(
            returned[owners[4 + order]], tensor_index * local_hidden, local_hidden, 1
        )
        mlp_blocks.append(mlp_w[order] - math.sqrt(FF / D) * piece.astype(jnp.float32))
    attn_new = jnp.stack(attn_blocks)
    mlp_new = jnp.stack(mlp_blocks)
    vector_mom_new = 0.5 * vector_mom + vector_grads
    vector_new = vectors - 0.1 / math.sqrt(total_tokens) * vector_mom_new
    return (
        output.astype(jnp.bfloat16),
        grad_tokens,
        attn_mom_new,
        attn_new,
        mlp_mom_new,
        mlp_new,
        vector_mom_new,
        vector_new,
    )


CORES = 2


class Place:
    def __init__(self):
        self.dp = lax.axis_index("dp")
        self.tensor = lax.axis_index("tensor")
        self.line = lax.axis_size("tensor")
        self.devices = lax.axis_size("dp") * self.line
        self.me = self.dp * self.line + self.tensor
        self.core = lax.rem(self.dp, 2)
        self.chip = self.dp // 2
        self.x = lax.rem(self.chip, 2)
        self.y = self.chip // 2
        self.twin = (self.dp + 1 - 2 * self.core, self.tensor)
        self.across_x = (self.dp + 2 - 4 * self.x, self.tensor)
        self.across_y = (self.dp + 4 - 8 * self.y, self.tensor)
        self.right = (self.dp, self.tensor + 1)
        self.left = (self.dp, self.tensor - 1)
        self.stays = self.core == lax.rem(self.tensor, 2)
        self.corner = (self.dp + 1 - 2 * self.core, self.tensor - 1 + 2 * self.core)


    def of(self, index):
        return (index // self.line, lax.rem(index, self.line))

    def index(self, x, y, core, z):
        return ((2 * y + x) * 2 + core) * self.line + z


def greet(place, line):
    barrier = pltpu.get_barrier_semaphore()

    def signal(device):
        pl.semaphore_signal(barrier, inc=1, device_id=device, device_id_type=MESH)

    signal(place.twin)
    signal(place.across_x)
    signal(place.across_y)

    for other in range(line):

        @pl.when(place.tensor != other)
        def _():
            signal((place.dp, other))

    @pl.when(jnp.logical_not(place.stays))
    def _():
        signal(place.corner)

    pl.semaphore_wait(barrier, jnp.where(place.stays, 3 + line - 1, 3 + line))


OWNERS = ((1, 0, 0), (1, 0, 3), (0, 1, 0), (0, 1, 3), (0, 0, 1), (1, 1, 2))


def greet_all(place):
    barrier = pltpu.get_barrier_semaphore()

    def meet(step, carry):
        pl.semaphore_signal(
            barrier, inc=1, device_id=place.of(lax.rem(place.me + step, place.devices)), device_id_type=MESH
        )
        return carry

    lax.fori_loop(1, place.devices, meet, 0)
    pl.semaphore_wait(barrier, place.devices - 1)


def is_one_of(value, options):
    found = value < 0
    for option in options:
        found = found | (value == option)
    return found


def sides(order, line):
    oz = OWNERS[order][2]
    above, below = list(range(oz + 1, line)), list(range(oz))
    return (above, below) if len(above) > len(below) else (below, above)


def rows_held(place, whole, index, rows, width):
    dp, tensor = place.of(index)
    return whole.at[pl.ds(pl.multiple_of(dp * rows, rows), rows), columns(tensor * width, width)]


def remote(place, source, target, send, recv, index):
    return pltpu.make_async_remote_copy(
        src_ref=source,
        dst_ref=target,
        send_sem=send,
        recv_sem=recv,
        device_id=place.of(index),
        device_id_type=MESH,
    )


class Collect:
    @staticmethod
    def scratch():
        dma = pltpu.SemaphoreType.DMA
        return [dma((2, 2)), dma((1,)), dma((2, 2)), dma((2, 2))]

    SCRATCH = 4

    def __init__(self, place, source, whole, scratch):
        self.place, self.source, self.whole = place, source, whole
        self.send_sem, self.sem, self.pass_send, self.pass_recv = scratch
        self.rows, self.width = source.shape[1], source.shape[2] // 2

    def owner(self, order, half):
        ox, oy, oz = OWNERS[order]
        return self.place.index(ox, oy, half, oz)

    def piece(self, order, half):
        return self.source.at[order - 4, :, half * self.width : (half + 1) * self.width]

    def held(self, index):
        return rows_held(self.place, self.whole, index, self.rows, self.width)

    def direct(self, order, half):
        send = self.send_sem.at[order - 4, half]
        return remote(
            self.place, self.piece(order, half), self.held(self.place.me), send, self.sem.at[0], self.owner(order, half)
        )

    def own(self, order, half):
        return pltpu.make_async_copy(self.piece(order, half), self.held(self.place.me), self.sem.at[0])

    def by_way(self, order):
        place = self.place
        ox, oy, oz = OWNERS[order]
        lone = is_one_of(place.tensor, sides(order, place.line)[1])
        return (place.y != oy) & (place.tensor != oz) & ((place.x != ox) | lone)

    def to_way(self, order, half):
        place = self.place
        ox, oy, _ = OWNERS[order]
        which = jnp.where(place.x == ox, 1, 0)
        return remote(
            place,
            self.piece(order, half),
            self.held(place.me),
            self.send_sem.at[order - 4, half],
            self.pass_recv.at[which, place.core],
            place.index(ox, oy, half, place.tensor),
        )

    def passed(self, order, which, cores):
        ox, oy, _ = OWNERS[order]
        return self.place.index(1 - ox if which == 0 else ox, 1 - oy, cores, self.place.tensor)

    def pass_in(self, order, which, cores):
        index = self.passed(order, which, cores)
        region = self.held(index)
        sems = self.pass_send.at[which, cores], self.pass_recv.at[which, cores]
        return remote(self.place, region, region, *sems, index)

    def pass_on(self, order, which, cores):
        ox, oy, oz = OWNERS[order]
        region = self.held(self.passed(order, which, cores))
        owner = self.place.index(ox, oy, self.place.core, oz)
        return remote(self.place, region, region, self.pass_send.at[which, cores], self.sem.at[0], owner)

    def when_passing(self, action):
        place = self.place
        for order in (5, 4):
            ox, oy, _ = OWNERS[order]
            far, lone = sides(order, place.line)
            for which, planes in ((0, far + lone), (1, lone)):

                @pl.when((place.x == ox) & (place.y == oy) & is_one_of(place.tensor, planes))
                def _():
                    for cores in range(2):
                        action(order, which, cores)

    def each(self, action_way, action_direct, action_own):
        for order in (5, 4):
            for half in range(2):
                mine = self.place.me == self.owner(order, half)

                @pl.when(self.by_way(order))
                def _():
                    action_way(order, half)

                @pl.when(jnp.logical_not(mine) & jnp.logical_not(self.by_way(order)))
                def _():
                    action_direct(order, half)

                @pl.when(mine)
                def _():
                    action_own(order, half)

    def start(self):
        self.each(
            lambda *at: self.to_way(*at).start(), lambda *at: self.direct(*at).start(), lambda *at: self.own(*at).start()
        )

    def forward(self):
        def action(*at):
            self.pass_in(*at).wait_recv()
            self.pass_on(*at).start()

        self.when_passing(action)

    def finish(self):
        self.each(
            lambda *at: self.to_way(*at).wait_send(),
            lambda *at: self.direct(*at).wait_send(),
            lambda *at: None,
        )
        self.when_passing(lambda *at: self.pass_on(*at).wait_send())
        for order in (5, 4):
            for half in range(2):

                @pl.when(self.place.me == self.owner(order, half))
                def _():
                    pltpu.make_async_copy(self.whole, self.whole, self.sem.at[0]).wait()


def columns(start, size):
    return pl.ds(pl.multiple_of(start, 128), size)


class RowSwap:
    SCRATCH = 2

    @staticmethod
    def scratch():
        return [pltpu.SemaphoreType.DMA((1,)), pltpu.SemaphoreType.DMA((4,))]

    def __init__(self, place, rows_ref, whole_ref, scratch):
        self.place, self.rows_ref, self.whole_ref = place, rows_ref, whole_ref
        self.own_sem, self.sem = scratch
        self.size = rows_ref.shape[0]

    def at(self, core):
        return self.whole_ref.at[pl.ds(pl.multiple_of(core * self.size, self.size), self.size), :]

    def copy(self, slot, source, target, device):
        return pltpu.make_async_remote_copy(
            src_ref=source,
            dst_ref=target,
            send_sem=self.sem.at[slot],
            recv_sem=self.sem.at[slot + 1],
            device_id=device,
            device_id_type=MESH,
        )

    def own(self):
        return pltpu.make_async_copy(self.rows_ref, self.at(self.place.core), self.own_sem.at[0])

    def away(self):
        return self.copy(0, self.rows_ref, self.at(1 - self.place.core), self.place.corner)

    def hand_own(self):
        return self.copy(2, self.rows_ref, self.at(self.place.core), self.place.twin)

    def hand_got(self):
        return self.copy(2, self.at(self.place.core), self.at(self.place.core), self.place.twin)

    def start(self):
        @pl.when(self.place.stays)
        def _():
            self.own().start()
            self.hand_own().start()

        @pl.when(jnp.logical_not(self.place.stays))
        def _():
            self.away().start()

    def step(self):
        @pl.when(jnp.logical_not(self.place.stays))
        def _():
            self.away().wait()
            self.hand_got().start()

    def end(self):
        @pl.when(self.place.stays)
        def _():
            self.own().wait()

        self.hand_got().wait()


class WeightGather:
    def __init__(self, place, line, groups, scratch):
        self.place, self.line, self.groups = place, line, groups
        self.own_sem, self.send_sem, self.recv_sem = scratch
        self.last = len(groups) - 1
        self.to_right, self.to_left = 1, line
        self.half_x, self.half_y, self.rest_y, self.rest_x = (2 * line - 1 + k for k in range(4))

    @staticmethod
    def scratch(count, line):
        dma = pltpu.SemaphoreType.DMA
        return [dma((count,)), dma((count, 2 * line + 3)), dma((count, 2 * line + 3))]

    def copy(self, group, slot, source, target, device):
        return pltpu.make_async_remote_copy(
            src_ref=source,
            dst_ref=target,
            send_sem=self.send_sem.at[group, slot],
            recv_sem=self.recv_sem.at[group, slot],
            device_id=device,
            device_id_type=MESH,
        )

    def same(self, group, slot, region, device):
        return self.copy(group, slot, region, region, device)

    def chunk(self, group, index):
        ref, width, _ = self.groups[group]
        cols = columns(index * width, width)
        if group == self.last:
            return ref.at[:, :, :, :, :, cols]
        return ref.at[:, self.place.y, self.place.x, :, :, cols]

    def corner(self, group, ys, xs, half):
        ref, width, _ = self.groups[group]
        if group == self.last:
            return ref.at[:, ys, xs, half, :, columns(self.place.tensor * width, width)]
        return ref.at[:, ys, xs, half]

    def entry(self, group, half):
        ref, width, _ = self.groups[group]
        return ref.at[:, self.place.y, self.place.x, half, :, columns(self.place.tensor * width, width)]

    def own(self, group):
        core = self.place.core
        return pltpu.make_async_copy(self.groups[group][2](core), self.entry(group, core), self.own_sem.at[group])

    def first(self, group):
        core = self.place.core
        return self.copy(group, 0, self.groups[group][2](1 - core), self.entry(group, core), self.place.twin)

    def begin(self, group):
        self.own(group).start()
        self.first(group).start()

    def enter(self, group):
        self.own(group).wait()
        self.same(group, 0, self.entry(group, 1 - self.place.core), self.place.twin).wait_recv()

    def hop(self, group, step, left):
        t = self.place.tensor
        index = t + step - 1 if left else t - step + 1
        slot = (self.to_left if left else self.to_right) + step - 1
        return self.same(group, slot, self.chunk(group, index), self.place.left if left else self.place.right)

    def arrival(self, group, step, left):
        t = self.place.tensor
        index = t + step if left else t - step
        slot = (self.to_left if left else self.to_right) + step - 1
        return self.same(group, slot, self.chunk(group, index), self.place.right if left else self.place.left)

    def sends(self, step, left):
        t, line = self.place.tensor, self.line
        return (t > 0) & (t + step <= line) if left else (t < line - 1) & (t >= step - 1)

    def line_start(self, group):
        for left in (False, True):

            @pl.when(self.sends(1, left))
            def _():
                self.hop(group, 1, left).start()

    def line_step(self, group, step):
        t, line = self.place.tensor, self.line
        for left in (False, True):

            @pl.when(t + step <= line - 1 if left else t >= step)
            def _():
                self.arrival(group, step, left).wait_recv()

            if step < line - 1:

                @pl.when(self.sends(step + 1, left))
                def _():
                    self.hop(group, step + 1, left).start()

    def line_most(self, group):
        for step in range(1, self.line - 1):
            self.line_step(group, step)

    def line_end(self, group):
        self.line_step(group, self.line - 1)

    def plane_start(self, group):
        place = self.place
        self.same(group, self.half_x, self.corner(group, place.y, place.x, 0), place.across_x).start()
        self.same(group, self.half_y, self.corner(group, place.y, place.x, 1), place.across_y).start()

    def plane_step(self, group):
        place, both = self.place, pl.ds(0, 2)
        self.same(group, self.half_x, self.corner(group, place.y, 1 - place.x, 0), place.across_x).wait_recv()
        self.same(group, self.rest_y, self.corner(group, place.y, both, 0), place.across_y).start()
        self.same(group, self.half_y, self.corner(group, 1 - place.y, place.x, 1), place.across_y).wait_recv()
        self.same(group, self.rest_x, self.corner(group, both, place.x, 1), place.across_x).start()

    def plane_end(self, group):
        place, both = self.place, pl.ds(0, 2)
        self.same(group, self.rest_y, self.corner(group, 1 - place.y, both, 0), place.across_y).wait_recv()
        self.same(group, self.rest_x, self.corner(group, both, 1 - place.x, 1), place.across_x).wait_recv()

    def wait_sends(self, group):
        place, both = self.place, pl.ds(0, 2)
        self.first(group).wait_send()
        for step in range(1, self.line):
            for left in (False, True):

                @pl.when(self.sends(step, left))
                def _():
                    self.hop(group, step, left).wait_send()

        self.same(group, self.half_x, self.corner(group, place.y, place.x, 0), place.across_x).wait_send()
        self.same(group, self.half_y, self.corner(group, place.y, place.x, 1), place.across_y).wait_send()
        self.same(group, self.rest_y, self.corner(group, place.y, both, 0), place.across_y).wait_send()
        self.same(group, self.rest_x, self.corner(group, both, place.x, 1), place.across_x).wait_send()


def add_blocks(target, sources):
    lead, rows = target.shape[:-2], target.shape[-2]
    per = rows // 32

    def body(step, carry):
        block, at = step // per, []
        for size in lead[::-1]:
            at.insert(0, lax.rem(block, size))
            block = block // size
        at = tuple(at) + (pl.ds(pl.multiple_of(lax.rem(step, per) * 32, 32), 32),)
        total = sources[0][at].astype(jnp.float32)
        for source in sources[1:]:
            total = total + source[at].astype(jnp.float32)
        target[at] = total.astype(target.dtype)
        return carry

    lax.fori_loop(0, math.prod(lead) * per, body, 0)


class PlaneSum:
    @staticmethod
    def scratch(count, rows, width):
        pair = pltpu.VMEM((count, 2, rows, width), jnp.bfloat16)
        single = pltpu.VMEM((count, rows, width), jnp.bfloat16)
        dma = pltpu.SemaphoreType.DMA
        return [pair] * 4 + [single] * 2 + [dma((2,)), dma((4,)), dma((4,))]

    SCRATCH = 9

    def __init__(self, place, source, result, scratch):
        self.place, self.source, self.result = place, source, result
        self.own, self.got, self.last = scratch[0:2], scratch[2:4], scratch[4:6]
        self.own_sem, self.send_sem, self.recv_sem = scratch[6:9]

    def copy(self, slot, source, target, device):
        return pltpu.make_async_remote_copy(
            src_ref=source,
            dst_ref=target,
            send_sem=self.send_sem.at[slot],
            recv_sem=self.recv_sem.at[slot],
            device_id=device,
            device_id_type=MESH,
        )

    def cut(self, index, mine):
        both, place = pl.ds(0, 2), self.place
        if index == 0:
            return self.source.at[:, place.y if mine else 1 - place.y, both, 0]
        return self.source.at[:, both, place.x if mine else 1 - place.x, 1]

    def load(self, index):
        return pltpu.make_async_copy(self.cut(index, True), self.own[index], self.own_sem.at[index])

    def first(self, index):
        device = self.place.across_x if index else self.place.across_y
        return self.copy(index, self.cut(index, False), self.got[index], device)

    def second(self, index):
        mine = self.place.y if index else self.place.x
        device = self.place.across_y if index else self.place.across_x
        return self.copy(2 + index, self.own[index].at[:, 1 - mine], self.last[index], device)

    def start(self):
        for index in range(2):
            self.first(index).start()
            self.load(index).start()

    def one(self):
        for index in range(2):
            mine = self.place.y if index else self.place.x
            self.load(index).wait()
            self.first(index).wait_recv()
            own, got = self.own[index], self.got[index]
            add_blocks(own.at[:, 1 - mine], (own.at[:, 1 - mine], got.at[:, 1 - mine]))
            self.second(index).start()
            add_blocks(own.at[:, mine], (own.at[:, mine], got.at[:, mine]))

    def two(self):
        for index in range(2):
            mine = self.place.y if index else self.place.x
            self.second(index).wait_recv()
            add_blocks(self.result.at[:, index], (self.own[index].at[:, mine], self.last[index]))

    def sent(self):
        for index in range(2):
            self.first(index).wait_send()
            self.second(index).wait_send()


class LineSum:
    @staticmethod
    def scratch(shape, line):
        dma = pltpu.SemaphoreType.DMA
        return [pltpu.VMEM(shape, jnp.bfloat16)] * 2 + [dma((2, line)), dma((2, line))]

    SCRATCH = 4

    def __init__(self, place, line, value, result, scratch):
        self.place, self.line, self.value, self.result = place, line, value, result
        self.got = scratch[0:2]
        self.send_sem, self.recv_sem = scratch[2:4]
        self.width = value.shape[-1] // line

    def part(self, ref, index):
        return ref.at[(slice(None),) * (len(ref.shape) - 1) + (slice(index * self.width, (index + 1) * self.width),)]

    def hop(self, index, left):
        return pltpu.make_async_remote_copy(
            src_ref=self.part(self.value, index),
            dst_ref=self.part(self.got[left], index),
            send_sem=self.send_sem.at[left, index],
            recv_sem=self.recv_sem.at[left, index],
            device_id=self.place.left if left else self.place.right,
            device_id_type=MESH,
        )

    def step(self, step):
        for left in range(2):
            for index in range(self.line):
                away = index if left else self.line - 1 - index
                order = step - away
                plane = self.line - 1 - order if left else order
                if order < 0 or (plane <= index if left else plane >= index):
                    continue

                @pl.when(self.place.tensor == plane)
                def _():
                    if order > 0:
                        self.hop(index, left).wait_recv()
                        value = self.part(self.value, index)
                        add_blocks(value, (value, self.part(self.got[left], index)))
                    if away > 0:
                        self.hop(index - 1 if left else index + 1, left).wait_send()
                    self.hop(index, left).start()

    def end(self):
        for index in range(self.line):

            @pl.when(self.place.tensor == index)
            def _():
                sources = [self.part(self.value, index)]
                for left in range(2):
                    if index < self.line - 1 if left else index > 0:
                        self.hop(index, left).wait_recv()
                        sources.append(self.part(self.got[left], index))
                add_blocks(self.result, sources)

    def sent(self):
        for index in range(self.line):

            @pl.when(self.place.tensor == index)
            def _():
                if index > 0:
                    self.hop(index - 1, 1).wait_send()
                if index < self.line - 1:
                    self.hop(index + 1, 0).wait_send()


class HomeCopy:
    def __init__(self, place, value, target, scratch):
        self.place, self.value, self.target = place, value, target
        self.own_sem, self.sem = scratch

    SCRATCH = 2

    @staticmethod
    def scratch():
        return [pltpu.SemaphoreType.DMA((1,)), pltpu.SemaphoreType.DMA((2,))]

    def keep(self):
        return pltpu.make_async_copy(self.value.at[:, self.place.core], self.target, self.own_sem.at[0])

    def give(self):
        return pltpu.make_async_remote_copy(
            src_ref=self.value.at[:, 1 - self.place.core],
            dst_ref=self.target,
            send_sem=self.sem.at[0],
            recv_sem=self.sem.at[1],
            device_id=self.place.twin,
            device_id_type=MESH,
        )

    def start(self):
        self.keep().start()
        self.give().start()

    def wait(self):
        self.keep().wait()
        self.give().wait()


class GroupSum:
    @staticmethod
    def scratch(count, rows, width, line, line_first=False):
        low = jnp.bfloat16
        part = width // line
        done = pltpu.VMEM((count, 2, rows, part), low)
        if line_first:
            whole = (count, 2, 2, 2, rows, width)
            held = [pltpu.VMEM(whole, low), pltpu.VMEM(whole[:-1] + (part,), low), pltpu.SemaphoreType.DMA((1,))]
            plane, along = PlaneSum.scratch(count, rows, part), LineSum.scratch(whole, line)
        else:
            middle = (count, 2, rows, width)
            held = [pltpu.VMEM(middle, low)]
            plane, along = PlaneSum.scratch(count, rows, width), LineSum.scratch(middle, line)
        return held + [done] + plane + along + HomeCopy.scratch()

    def __init__(self, place, line, source, target, scratch, line_first=False):
        scratch = list(scratch)

        def take(count):
            taken = scratch[:count]
            del scratch[:count]
            return taken

        if line_first:
            whole, middle, load_sem = take(3)
            self.load = lambda: pltpu.make_async_copy(source, whole, load_sem.at[0])
        else:
            (middle,) = take(1)
        (done,) = take(1)
        plane, along = take(PlaneSum.SCRATCH), take(LineSum.SCRATCH)
        if line_first:
            self.line = LineSum(place, line, whole, middle, along)
            self.plane = PlaneSum(place, middle, done, plane)
        else:
            self.plane = PlaneSum(place, source, middle, plane)
            self.line = LineSum(place, line, middle, done, along)
        self.home = HomeCopy(place, done, target, take(HomeCopy.SCRATCH))

    def sent(self):
        self.plane.sent()
        self.line.sent()


class VectorSum:
    @staticmethod
    def scratch(shape, line):
        return [
            pltpu.VMEM((4,) + shape, jnp.float32),
            pltpu.VMEM((3,) + shape, jnp.float32),
            pltpu.VMEM((line,) + shape, jnp.float32),
            pltpu.SemaphoreType.DMA((4, max(line, 3))),
        ]

    def __init__(self, place, line, scratch):
        self.place, self.line = place, line
        self.sums, self.got, self.along, self.sem = scratch

    def copy(self, stage):
        place = self.place
        return pltpu.make_async_remote_copy(
            src_ref=self.sums.at[stage],
            dst_ref=self.got.at[stage],
            send_sem=self.sem.at[0, stage],
            recv_sem=self.sem.at[1, stage],
            device_id=(place.twin, place.across_x, place.across_y)[stage],
            device_id_type=MESH,
        )

    def hop(self, other, source):
        return pltpu.make_async_remote_copy(
            src_ref=self.sums.at[3],
            dst_ref=self.along.at[source],
            send_sem=self.sem.at[2, other],
            recv_sem=self.sem.at[3, source],
            device_id=(self.place.dp, other),
            device_id_type=MESH,
        )

    def start(self, value, first_rows):
        self.sums[0] = value
        for index, row in enumerate(first_rows):
            self.sums[0, index : index + 1, :] = row
        self.copy(0).start()

    def step(self, stage):
        self.copy(stage).wait()
        self.sums[stage + 1] = self.sums[stage] + self.got[stage]
        if stage < 2:
            self.copy(stage + 1).start()
            return
        self.along[self.place.tensor] = self.sums[3]
        for other in range(self.line):

            @pl.when(self.place.tensor != other)
            def _():
                self.hop(other, self.place.tensor).start()

    def end(self):
        t = self.place.tensor
        for other in range(self.line):

            @pl.when(t != other)
            def _():
                self.hop(other, t).wait_send()
                self.hop(t, other).wait_recv()

        total = self.along[0]
        for other in range(1, self.line):
            total = total + self.along[other]
        return total


LOG2E = 1.4426950408889634
FAR = 1e32
ROW_BLOCK = 256


def fill_distance(seg_rows, seg_cols, distance):
    def body(step, carry):
        start = pl.multiple_of(step * 64, 64)
        shape = (64, distance.shape[1])
        row = lax.broadcasted_iota(jnp.int32, shape, 0) + start
        col = lax.broadcasted_iota(jnp.int32, shape, 1)
        segs = seg_rows[pl.ds(start, 64), :]
        same = (segs == seg_cols[...]) & (segs > 0) & (col <= row)
        allowed = same | (col == row)
        distance[pl.ds(start, 64), :] = jnp.where(allowed, (row - col).astype(jnp.float32), FAR)
        return carry

    lax.fori_loop(0, distance.shape[0] // 64, body, 0)


def head_lanes(dtype):
    lane = lax.broadcasted_iota(jnp.int32, (1, 2 * HD), 1)
    first = (lane < HD).astype(jnp.float32)
    return (first.astype(dtype), (1.0 - first).astype(dtype))


def attend_group(group, slopes, qkv, mixed, lse, distance):
    length = qkv.shape[1]
    cols = columns(group * 2 * HD, 2 * HD)
    masks = head_lanes(jnp.bfloat16)
    first = head_lanes(jnp.float32)[0] > 0.5
    factor = LOG2E / math.sqrt(HD)
    keys_t = qkv[1, :, cols].T
    values = qkv[2, :, cols]
    for start in range(0, length, ROW_BLOCK):
        stop = start + ROW_BLOCK
        rows = slice(start, stop)
        query = qkv[0, rows, cols]
        parts, sums = [], []
        for head in range(2):
            slope = slopes[2 * group + head] * LOG2E
            scores = jnp.dot(query * masks[head], keys_t[:, :stop], preferred_element_type=jnp.float32)
            scores = scores * factor - slope * distance[rows, :stop]
            top = jnp.max(scores, axis=1, keepdims=True)
            probs = jnp.exp2(scores - top)
            total = jnp.sum(probs, axis=1, keepdims=True)
            out = jnp.dot(probs.astype(jnp.bfloat16), values[:stop], preferred_element_type=jnp.float32)
            parts.append(out / total)
            sums.append(top + jnp.log2(total))
        mixed[rows, cols] = jnp.where(first, parts[0], parts[1]).astype(jnp.bfloat16)
        lse[rows, cols] = jnp.where(first, sums[0], sums[1])


def normalize(rows):
    centred = rows - jnp.mean(rows, axis=1, keepdims=True)
    return centred * lax.rsqrt(jnp.mean(centred * centred, axis=1, keepdims=True) + 1e-05)


def forward_kernel(
    line, attn_ref, mlp_ref, tokens_ref, grads_ref, slopes, seg_rows, seg_cols, qkv_bias, hidden_bias, vectors,
    qkv_w, out_w, up_w, down_w, tokens_out, grads_out, qkv_out, mixed_out, lse_out, normed_out, middle_out,
    hidden_out, act_out, bend_out, *scratch
):
    (x_v, normed, qkv_wv, out_wv, up_wv, qkv, mixed, lse, distance, part, got, middle, hidden, act, bend) = scratch[:15]
    load_sem, store_sem, swap_send, swap_recv = scratch[15:19]
    place = Place()
    narrow, wide = attn_ref.shape[2] // 2, mlp_ref.shape[2] // 4
    size = normed.shape[0]

    def attn_source(index):
        return lambda core: attn_ref.at[index : index + 1, :, columns(core * narrow, narrow)]

    def mlp_source(index, half):
        return lambda core: mlp_ref.at[index : index + 1, :, columns((2 * core + half) * wide, wide)]

    groups = [(qkv_w.at[index : index + 1], narrow, attn_source(index)) for index in range(3)]
    groups.append((out_w, narrow, attn_source(3)))
    groups += [(up_w.at[half : half + 1], wide, mlp_source(0, half)) for half in range(2)]
    groups += [(down_w.at[half : half + 1], wide, mlp_source(1, half)) for half in range(2)]
    query, key, value, outer, up_a, up_b, down_a, down_b = range(8)
    gather = WeightGather(place, line, groups, scratch[19:22])
    tokens = RowSwap(place, tokens_ref, tokens_out, scratch[22:24])
    grads = RowSwap(place, grads_ref, grads_out, scratch[24:26])

    def load(group):
        if group < 3:
            source, target = qkv_w.at[group], qkv_wv.at[group]
        elif group == outer:
            source, target = out_w, out_wv
        else:
            source, target = up_w.at[group - up_a], up_wv.at[group - up_a]
        return pltpu.make_async_copy(source, target, load_sem.at[group])

    x_load = pltpu.make_async_copy(tokens_out, x_v, load_sem.at[7])
    pairs = (
        (qkv, qkv_out),
        (mixed, mixed_out),
        (lse, lse_out),
        (normed, normed_out),
        (middle, middle_out),
        (hidden, hidden_out),
        (act.at[0], act_out.at[0]),
        (act.at[1], act_out.at[1]),
        (bend.at[0], bend_out.at[0]),
        (bend.at[1], bend_out.at[1]),
    )

    def store(index):
        return pltpu.make_async_copy(*pairs[index], store_sem.at[index])

    def normalize_tokens():
        def body(step, carry):
            at = pl.ds(pl.multiple_of(step * 32, 32), 32)
            normal = normalize(x_v[at, :].astype(jnp.float32))
            normed[at, :] = (normal * vectors[0:1, :] + vectors[1:2, :]).astype(jnp.bfloat16)
            return carry

        lax.fori_loop(0, size // 32, body, 0, unroll=4)

    def project(group):
        load(group).wait()
        weight = qkv_wv[group].reshape(size, qkv.shape[2])

        def body(step, carry):
            at = pl.ds(pl.multiple_of(step * 512, 512), 512)
            out = jnp.dot(normed[at, :], weight, preferred_element_type=jnp.float32)
            qkv[group, at, :] = (out + qkv_bias[group : group + 1, :]).astype(jnp.bfloat16)
            return carry

        lax.fori_loop(0, size // 512, body, 0)

    def swap(index):
        at = pl.ds(pl.multiple_of(index * 256, 256), 256)
        return pltpu.make_async_remote_copy(
            src_ref=part.at[at, :],
            dst_ref=got.at[at, :],
            send_sem=swap_send.at[index],
            recv_sem=swap_recv.at[index],
            device_id=place.twin,
            device_id_type=MESH,
        )

    def project_out(index, carry):
        at = pl.ds(pl.multiple_of(index * 256, 256), 256)
        weight = out_wv[0].reshape(size, mixed.shape[1])
        part[at, :] = contract_last(mixed[at, :], weight).astype(jnp.bfloat16)
        swap(index).start()
        return carry

    def add_branch(index, carry):
        swap(index).wait()

        def body(step, carry):
            at = pl.ds(pl.multiple_of(index * 256 + step * 32, 32), 32)
            branch = part[at, :].astype(jnp.float32) + got[at, :].astype(jnp.float32)
            total = x_v[at, :].astype(jnp.float32) + branch + vectors[4:5, :]
            middle[at, :] = total
            hidden[at, :] = (normalize(total) * vectors[5:6, :] + vectors[6:7, :]).astype(jnp.bfloat16)
            return carry

        return lax.fori_loop(0, 8, body, carry, unroll=4)

    def feed(half):
        load(up_a + half).wait()

        def body(step, carry):
            at = pl.ds(pl.multiple_of(step * 256, 256), 256)
            weight = up_wv[half].reshape(size, act.shape[2])
            pre = jnp.dot(hidden[at, :], weight, preferred_element_type=jnp.float32)
            pre = pre + hidden_bias[half : half + 1, :]
            square = pre * pre
            bent = jnp.tanh(0.7978845608 * pre * (1.0 + 0.044715 * square))
            inner = 0.7978845608 * (1.0 + 3.0 * 0.044715 * square)
            act[half, at, :] = (0.5 * pre * (1.0 + bent)).astype(jnp.bfloat16)
            bend[half, at, :] = (0.5 * (1.0 + bent) + 0.5 * pre * (1.0 - bent * bent) * inner).astype(jnp.bfloat16)
            return carry

        lax.fori_loop(0, size // 256, body, 0)
        store(6 + half).start()
        store(8 + half).start()

    greet(place, line)
    for group in (query, down_b, key, value, outer, up_a, up_b, down_a):
        gather.begin(group)
    gather.enter(query)
    gather.line_start(query)
    gather.enter(down_b)
    gather.plane_start(down_b)
    gather.enter(key)
    gather.line_most(query)
    gather.line_start(key)
    tokens.start()
    gather.line_end(query)
    gather.plane_start(query)
    gather.plane_step(down_b)
    gather.enter(value)
    gather.line_most(key)
    gather.line_start(value)
    gather.line_end(key)
    gather.plane_step(query)
    gather.plane_start(key)
    gather.plane_end(down_b)
    gather.line_most(value)
    gather.line_end(value)
    gather.enter(outer)
    gather.line_start(outer)
    gather.plane_end(query)
    load(query).start()
    gather.plane_step(key)
    gather.plane_start(value)
    tokens.step()
    fill_distance(seg_rows, seg_cols, distance)
    gather.enter(up_a)
    gather.line_most(outer)
    gather.line_start(up_a)
    gather.plane_end(key)
    load(key).start()
    gather.line_end(outer)
    gather.plane_step(value)
    gather.plane_start(outer)
    tokens.end()
    x_load.start()
    x_load.wait()
    normalize_tokens()
    store(3).start()
    gather.enter(up_b)
    gather.line_most(up_a)
    gather.line_start(up_b)
    project(query)
    gather.line_end(up_a)
    gather.line_start(down_b)
    gather.plane_end(value)
    load(value).start()
    gather.plane_step(outer)
    gather.plane_start(up_a)
    project(key)
    project(value)
    store(0).start()

    def beside(index):
        if index == 0:
            gather.enter(down_a)
            gather.line_most(up_b)
            gather.line_start(down_a)
            gather.plane_end(outer)
            load(outer).start()
        if index == 1:
            gather.line_end(up_b)
            gather.plane_step(up_a)
            gather.plane_start(up_b)
        if index == 2:
            gather.line_step(down_b, 1)
        if index == 3:
            gather.line_most(down_a)

    def attend(index, carry):
        attend_group(index, slopes, qkv, mixed, lse, distance)
        for order in range(4):

            @pl.when(index == order)
            def _():
                beside(order)

        return carry

    lax.fori_loop(0, qkv.shape[2] // (2 * HD), attend, 0)
    store(1).start()
    store(2).start()
    load(outer).wait()
    lax.fori_loop(0, size // 256, project_out, 0)
    gather.plane_step(up_b)
    gather.line_end(down_a)
    gather.plane_start(down_a)
    lax.fori_loop(0, size // 256, add_branch, 0)
    store(4).start()
    store(5).start()
    for step in range(2, line - 1):
        gather.line_step(down_b, step)
    grads.start()
    gather.plane_end(up_a)
    load(up_a).start()
    feed(0)
    gather.plane_step(down_a)
    gather.plane_end(up_b)
    load(up_b).start()
    feed(1)
    gather.line_end(down_b)
    grads.step()
    gather.plane_end(down_a)
    grads.end()
    for index in range(len(pairs)):
        store(index).wait()
    for group in range(len(groups)):
        gather.wait_sends(group)


def forward(attn_low, mlp_low, tokens, grads, slopes, seg_ids, qkv_bias, hidden_bias, vectors, line):
    rows = attn_low.shape[1]
    narrow, wide = attn_low.shape[2] // 2 * line, mlp_low.shape[2] // 4 * line
    length, width = 2 * tokens.shape[0], tokens.shape[1]
    low, dma = jnp.bfloat16, pltpu.SemaphoreType.DMA
    vmem = pl.BlockSpec(memory_space=pltpu.VMEM)
    hbm = pl.BlockSpec(memory_space=pl.ANY)

    def whole(count, columns_held):
        return (count, 2, 2, 2, rows, columns_held)

    kept = [
        ((3, length, narrow), low),
        ((length, narrow), low),
        ((length, narrow), jnp.float32),
        ((length, width), low),
        ((length, width), jnp.float32),
        ((length, width), low),
        ((2, length, wide), low),
        ((2, length, wide), low),
    ]
    outs = [(whole(3, narrow), low), (whole(1, narrow), low), (whole(2, wide), low), (whole(2, wide), low)]
    outs += [((length, width), low)] * 2 + kept
    held = [(length, width)] * 2 + [whole(3, narrow), whole(1, narrow), whole(2, wide)]
    results = pl.pallas_call(
        functools.partial(forward_kernel, line),
        out_shape=[jax.ShapeDtypeStruct(*each) for each in outs],
        in_specs=[hbm] * 4 + [pl.BlockSpec(memory_space=pltpu.SMEM)] + [vmem] * 5,
        out_specs=[hbm] * len(outs),
        scratch_shapes=[pltpu.VMEM(each, low) for each in held]
        + [pltpu.VMEM(*each) for each in kept[:3]]
        + [pltpu.VMEM((length, length), jnp.float32)]
        + [pltpu.VMEM((length, width), low)] * 2
        + [pltpu.VMEM(*each) for each in kept[4:]]
        + [dma((8,)), dma((10,)), dma((length // 256,)), dma((length // 256,))]
        + WeightGather.scratch(8, line)
        + RowSwap.scratch() * 2,
        compiler_params=pltpu.CompilerParams(
            collective_id=1, has_side_effects=True, vmem_limit_bytes=62 * 1024 * 1024
        ),
        name="forward",
    )(
        attn_low,
        mlp_low,
        tokens,
        grads,
        slopes,
        seg_ids.reshape(-1, 1),
        seg_ids.reshape(1, -1),
        qkv_bias,
        hidden_bias,
        vectors,
    )
    return [each.reshape(each.shape[0], length, -1) for each in results[:4]] + list(results[4:])


def middle_kernel(
    grads_ref, act_ref, bend_ref, down_ref, up_ref, hidden_ref, middle_ref, mixed_ref, out_ref, gain,
    down_out, up_out, out_out, mixed_out, mid_out, sums_out, hidden_sums,
    grads, act, bend, down, up, hidden, middle, mixed, weight, pre, part, got, low, mid, down_v, up_v, out_v, mixed_v,
    load_sem, store_sem, send_sem, recv_sem,
):
    place = Place()
    size = grads.shape[0]
    half = size // 2
    blocks = size // 256
    sources = (
        (grads_ref, grads), (down_ref, down), (bend_ref, bend), (up_ref, up), (act_ref, act),
        (middle_ref, middle), (out_ref, weight), (hidden_ref, hidden), (mixed_ref, mixed),
    )
    load_g, load_down, load_bend, load_up, load_act, load_middle, load_out, load_hidden, load_mixed = (
        pltpu.make_async_copy(*each, load_sem.at[index]) for index, each in enumerate(sources)
    )
    for each in (load_g, load_down, load_bend, load_up, load_act, load_middle, load_out, load_hidden, load_mixed):
        each.start()
    barrier = pltpu.get_barrier_semaphore()
    pl.semaphore_signal(barrier, inc=1, device_id=place.twin, device_id_type=MESH)
    pl.semaphore_wait(barrier, 1)

    def rows(index, count=256):
        return pl.ds(pl.multiple_of(index * count, count), count)

    def swap(index):
        return pltpu.make_async_remote_copy(
            src_ref=part.at[rows(index), :],
            dst_ref=got.at[rows(index), :],
            send_sem=send_sem.at[index],
            recv_sem=recv_sem.at[index],
            device_id=place.twin,
            device_id_type=MESH,
        )

    def store(slot, index, source, target):
        return pltpu.make_async_copy(source.at[rows(index), :], target.at[rows(index), :], store_sem.at[slot, index])

    def back_hidden(index, carry):
        total = None
        for order in range(2):
            back = jnp.dot(grads[rows(index), :], down[order], preferred_element_type=jnp.float32)
            piece = (back * bend[order, rows(index), :].astype(jnp.float32)).astype(jnp.bfloat16)
            pre[order, rows(index), :] = piece
            column = jnp.sum(piece.astype(jnp.float32), axis=0, keepdims=True)
            hidden_sums[order : order + 1, :] = hidden_sums[order : order + 1, :] + column
            term = contract_last(piece, up[order])
            total = term if total is None else total + term
        part[rows(index), :] = total.astype(jnp.bfloat16)
        swap(index).start()
        return carry

    def outer_product(slot, left, rights, targets, outs):
        def body(index, carry):
            turned = left[:, columns(index * 256, 256)].T
            for order, (right, target, out) in enumerate(zip(rights, targets, outs)):
                target[rows(index), :] = jnp.dot(turned, right[...], preferred_element_type=jnp.float32).astype(jnp.bfloat16)
                store(slot + order, index, target, out).start()
            return carry

        lax.fori_loop(0, blocks, body, 0)

    def norm_rows_back(step, sums, owned):
        core = place.core if owned else 1 - place.core
        at = pl.ds(pl.multiple_of(core * half + step * 32, 32), 32)
        grad = part[at, :].astype(jnp.float32) + got[at, :].astype(jnp.float32)
        value = middle[at, :]
        centred = value - jnp.mean(value, axis=1, keepdims=True)
        spread = lax.rsqrt(jnp.mean(centred * centred, axis=1, keepdims=True) + 1e-05)
        hat = centred * spread
        scaled = grad * gain[...]
        inner = jnp.mean(scaled * hat, axis=1, keepdims=True)
        above = grads[at, :].astype(jnp.float32)
        total = above + spread * (scaled - jnp.mean(scaled, axis=1, keepdims=True) - hat * inner)
        low[at, :] = total.astype(jnp.bfloat16)
        if not owned:
            return sums
        mid[pl.ds(pl.multiple_of(step * 32, 32), 32), :] = total
        fold = (4, 8, size)
        terms = (grad * hat, grad, total, above)
        return tuple(one + jnp.sum(term.reshape(fold), axis=0) for one, term in zip(sums, terms))

    def back_mixed(index, carry):
        mixed_v[rows(index), :] = jnp.dot(low[rows(index), :], weight[0], preferred_element_type=jnp.float32).astype(
            jnp.bfloat16
        )
        store(5, index, mixed_v, mixed_out).start()
        return carry

    hidden_sums[...] = jnp.zeros_like(hidden_sums)
    load_g.wait()
    load_down.wait()
    load_bend.wait()
    load_up.wait()
    lax.fori_loop(0, blocks, back_hidden, 0)
    load_act.wait()
    outer_product(0, grads, (act.at[0], act.at[1]), (down_v.at[0], down_v.at[1]), (down_out.at[0], down_out.at[1]))
    load_middle.wait()
    for index in range(blocks):
        swap(index).wait()
    empty = tuple(jnp.zeros((8, size), jnp.float32) for _ in range(4))
    lax.fori_loop(0, half // 32, lambda step, sums: norm_rows_back(step, sums, False), (), unroll=2)
    sums = lax.fori_loop(0, half // 32, lambda step, sums: norm_rows_back(step, sums, True), empty)
    for index, each in enumerate(sums):
        sums_out[index : index + 1, :] = jnp.sum(each, axis=0, keepdims=True)
    mid_store = pltpu.make_async_copy(mid, mid_out, load_sem.at[9])
    mid_store.start()
    load_out.wait()
    lax.fori_loop(0, blocks, back_mixed, 0)
    load_hidden.wait()
    outer_product(2, hidden, (pre.at[0], pre.at[1]), (up_v.at[0], up_v.at[1]), (up_out.at[0], up_out.at[1]))
    load_mixed.wait()
    outer_product(4, low, (mixed,), (out_v.at[0],), (out_out.at[0],))
    for index in range(blocks):
        for order in range(2):
            store(order, index, down_v.at[order], down_out.at[order]).wait()
            store(2 + order, index, up_v.at[order], up_out.at[order]).wait()
        store(4, index, out_v.at[0], out_out.at[0]).wait()
        store(5, index, mixed_v, mixed_out).wait()
    mid_store.wait()


def middle_back(grads, act, bend, down, up, hidden, middle, mixed, out, gain):
    size, narrow = mixed.shape
    low, dma = jnp.bfloat16, pltpu.SemaphoreType.DMA
    hbm, vmem = pl.BlockSpec(memory_space=pl.ANY), pl.BlockSpec(memory_space=pltpu.VMEM)

    def held(each):
        return pltpu.VMEM(each.shape, each.dtype)

    square = pltpu.VMEM((size, size), low)
    pair = pltpu.VMEM(act.shape, low)
    return pl.pallas_call(
        middle_kernel,
        out_shape=[
            jax.ShapeDtypeStruct(act.shape, low),
            jax.ShapeDtypeStruct(act.shape, low),
            jax.ShapeDtypeStruct((1, size, narrow), low),
            jax.ShapeDtypeStruct((size, narrow), low),
            jax.ShapeDtypeStruct((size // 2, size), jnp.float32),
            jax.ShapeDtypeStruct((4, size), jnp.float32),
            jax.ShapeDtypeStruct((2, size), jnp.float32),
        ],
        in_specs=[hbm] * 9 + [vmem],
        out_specs=[hbm] * 5 + [vmem] * 2,
        scratch_shapes=[held(each) for each in (grads, act, bend, down, up, hidden, middle, mixed, out)]
        + [pair, square, square, square, pltpu.VMEM((size // 2, size), jnp.float32), pair, pair]
        + [pltpu.VMEM((1, size, narrow), low), pltpu.VMEM((size, narrow), low)]
        + [dma((10,)), dma((6, size // 256)), dma((size // 256,)), dma((size // 256,))],
        compiler_params=pltpu.CompilerParams(
            collective_id=4, has_side_effects=True, vmem_limit_bytes=62 * 1024 * 1024
        ),
        name="middle_back",
    )(grads, act, bend, down, up, hidden, middle, mixed, out, gain.reshape(1, -1))


def attend_back_group(group, slopes, qkv, grad, mixed, lse, out, distance, dk_acc, dv_acc):
    length = qkv.shape[1]
    cols = columns(group * 2 * HD, 2 * HD)
    masks = head_lanes(jnp.bfloat16)
    wide_masks = head_lanes(jnp.float32)
    first = wide_masks[0] > 0.5
    factor = LOG2E / math.sqrt(HD)
    shrink = 1.0 / math.sqrt(HD)
    keys, values = qkv[1, :, cols], qkv[2, :, cols]
    keys_t = keys.T
    values_t = values.T
    dk_acc[...] = jnp.zeros_like(dk_acc)
    dv_acc[...] = jnp.zeros_like(dv_acc)
    for start in range(0, length, ROW_BLOCK):
        stop = start + ROW_BLOCK
        rows = slice(start, stop)
        query, grads, log_sums = qkv[0, rows, cols], grad[rows, cols], lse[rows, cols]
        query_t, grads_t = query.T, grads.T
        product = grads.astype(jnp.float32) * mixed[rows, cols].astype(jnp.float32)
        parts = []
        for head in range(2):
            slope = slopes[2 * group + head] * LOG2E
            lanes = slice(head * HD, (head + 1) * HD)
            scores = jnp.dot(query * masks[head], keys_t[:, :stop], preferred_element_type=jnp.float32)
            log_sum = log_sums[:, head * HD : head * HD + 1]
            probs = jnp.exp2(scores * factor - slope * distance[rows, :stop] - log_sum)
            grad_probs = jnp.dot(grads * masks[head], values_t[:, :stop], preferred_element_type=jnp.float32)
            inner = jnp.sum(product * wide_masks[head], axis=1, keepdims=True)
            grad_scores = (probs * (grad_probs - inner)).astype(jnp.bfloat16)
            parts.append(jnp.dot(grad_scores, keys[:stop], preferred_element_type=jnp.float32))
            dk_acc[lanes, :stop] += jnp.dot(query_t[lanes, :], grad_scores, preferred_element_type=jnp.float32)
            dv_acc[lanes, :stop] += jnp.dot(
                grads_t[lanes, :], probs.astype(jnp.bfloat16), preferred_element_type=jnp.float32
            )
        out[0, rows, cols] = (jnp.where(first, parts[0], parts[1]) * shrink).astype(jnp.bfloat16)
    out[1, :, cols] = (dk_acc[...].T * shrink).astype(jnp.bfloat16)
    out[2, :, cols] = dv_acc[...].T.astype(jnp.bfloat16)


def back_kernel(
    line, down_ref, up_ref, out_ref, slopes, seg_rows, seg_cols, qkv, grad, mixed, lse, mlp_mom, weight_ref, normed_ref,
    act_ref, down_w, attn_home, normed_part, bias_sums, mom_out, whole, out_part,
    held, held_sem, grads, projected, distance, dk_acc, dv_acc, mlp_sum, mlp_round, *scratch
):
    place = Place()
    narrow_cols = held.shape[2]
    wide, narrow = mlp_mom.shape[2] // 4, attn_home.shape[2] // 2

    def mlp_target(index, part):
        return mlp_sum.at[index : index + 1, :, columns((2 * place.core + part) * wide, wide)]

    def attn_target(lo, hi):
        return attn_home.at[lo:hi, :, columns(place.core * narrow, narrow)]

    groups = [
        GroupSum(place, line, down_ref.at[0:1], mlp_target(1, 0), scratch[0]),
        GroupSum(place, line, down_ref.at[1:2], mlp_target(1, 1), scratch[1]),
        GroupSum(place, line, up_ref.at[0:1], mlp_target(0, 0), scratch[2]),
        GroupSum(place, line, out_ref, attn_target(3, 4), scratch[3]),
        GroupSum(place, line, projected, attn_target(0, 3), scratch[4]),
        GroupSum(place, line, up_ref.at[1:2], mlp_target(0, 1), scratch[5], line_first=True),
    ]
    one, two, three, outer, inner, last = groups
    collect = Collect(place, mlp_round, whole, scratch[6])

    def attend(group, carry):
        attend_back_group(group, slopes, qkv, grad, mixed, lse, grads, distance, dk_acc, dv_acc)
        return carry

    def halves(ref):
        return [ref.at[:, half * narrow_cols : (half + 1) * narrow_cols] for half in range(2)]

    first_loads = [pltpu.make_async_copy(weight_ref.at[order], held.at[order], held_sem.at[order]) for order in range(3)]
    for half, source in enumerate(halves(normed_ref)):
        first_loads.append(pltpu.make_async_copy(source, held.at[3 + half], held_sem.at[3 + half]))
    quarters = [source for part in range(2) for source in halves(down_w.at[part])]
    late_loads = [pltpu.make_async_copy(quarters[index], held.at[index], held_sem.at[index]) for index in range(4)]

    def act_load(block, index):
        source = act_ref.at[
            index // 2, pl.ds(pl.multiple_of(block * 256, 256), 256), (index % 2) * narrow_cols : (index % 2 + 1) * narrow_cols
        ]
        return pltpu.make_async_copy(source, held.at[4, index * 256 : (index + 1) * 256], held_sem.at[5 + index])

    def project(index, carry):
        left = held[3 + index // 2, :, columns(lax.rem(index, 2) * 256, 256)].T
        for order in range(3):
            piece = jnp.dot(left, grads[order], preferred_element_type=jnp.float32).astype(jnp.bfloat16)
            projected[order, index // 2, lax.rem(index, 2)] = piece.reshape(2, 128, piece.shape[1])
        return carry

    def unproject(index, carry):
        at = pl.ds(pl.multiple_of(index * 256, 256), 256)
        total = contract_last(grads[0, at, :], held[0])
        for order in range(1, 3):
            total = total + contract_last(grads[order, at, :], held[order])
        normed_part[at, :] = total.astype(jnp.bfloat16)
        return carry

    def feed_out(block, carry):
        for index in range(4):
            act_load(block, index).start()
        for index in range(4):
            act_load(block, index).wait()
        total = contract_last(held[4, 0:256], held[0])
        for index in range(1, 4):
            total = total + contract_last(held[4, index * 256 : (index + 1) * 256], held[index])
        at = pl.ds(pl.multiple_of(block * 256, 256), 256)
        for half in range(2):
            grads[half, at, :] = total[:, half * narrow_cols : (half + 1) * narrow_cols].astype(jnp.bfloat16)
        return carry

    def out_store(half):
        return pltpu.make_async_copy(grads.at[half], halves(out_part)[half], held_sem.at[half])

    def update(index, carry):
        at = (index // 4, pl.ds(pl.multiple_of(lax.rem(index, 4) * 32, 32), 32))
        fresh = 0.5 * mlp_mom[at] + mlp_sum[at].astype(jnp.float32)
        mom_out[at] = fresh
        mlp_round[at] = fresh.astype(jnp.bfloat16)
        return carry

    greet_all(place)
    one.plane.start()
    last.load().start()
    for each in first_loads:
        each.start()
    last.load().wait()
    last.line.step(0)
    outer.plane.start()
    fill_distance(seg_rows, seg_cols, distance)
    pairs = qkv.shape[2] // (2 * HD)
    lax.fori_loop(0, pairs // 2, attend, 0)
    one.plane.one()
    two.plane.start()
    last.line.step(1)
    lax.fori_loop(pairs // 2, pairs, attend, 0)
    one.plane.two()
    one.line.step(0)
    for each in first_loads:
        each.wait()
    lax.fori_loop(0, 4, project, 0)
    outer.plane.one()
    for step in range(2, line - 1):
        last.line.step(step)
    lax.fori_loop(0, 4, unproject, 0)
    for each in late_loads:
        each.start()
    for order in range(3):
        bias_sums[order : order + 1, :] = jnp.sum(grads[order].astype(jnp.float32), axis=0, keepdims=True)
    two.plane.one()
    three.plane.start()
    outer.plane.two()
    outer.line.step(0)
    two.plane.two()
    two.line.step(0)
    last.line.end()
    last.plane.start()
    three.plane.one()
    one.line.step(1)
    for each in late_loads:
        each.wait()
    last.plane.one()
    three.plane.two()
    inner.plane.start()
    three.line.step(0)
    lax.fori_loop(0, 2, feed_out, 0)
    for step in range(2, line - 1):
        one.line.step(step)
    last.plane.two()
    last.home.start()
    two.line.step(1)
    lax.fori_loop(2, 3, feed_out, 0)
    one.line.end()
    one.home.start()
    three.line.step(1)
    outer.line.step(1)
    lax.fori_loop(3, 4, feed_out, 0)
    for half in range(2):
        out_store(half).start()
    for group in (two, three, outer):
        for step in range(2, line - 1):
            group.line.step(step)
    two.line.end()
    two.home.start()
    three.line.end()
    three.home.start()
    for group in (one, two, last, three):
        group.home.wait()
    lax.fori_loop(0, 8, update, 0)
    inner.plane.one()
    collect.start()
    outer.line.end()
    outer.home.start()
    collect.forward()
    inner.plane.two()
    for step in range(line - 1):
        inner.line.step(step)
    inner.line.end()
    inner.home.start()
    inner.home.wait()
    outer.home.wait()
    for half in range(2):
        out_store(half).wait()
    for group in groups:
        group.sent()
    collect.finish()


def attend_back(
    down, up, out, slopes, seg_ids, qkv, grad, mixed, lse, mlp_mom, weights, normed, act, down_w, line
):
    _, length, width = qkv.shape
    rows, wide = down.shape[1] // 8, down.shape[2]
    size = normed.shape[1]
    vmem = pl.BlockSpec(memory_space=pltpu.VMEM)
    hbm = pl.BlockSpec(memory_space=pl.ANY)
    low = jnp.bfloat16
    return pl.pallas_call(
        functools.partial(back_kernel, line),
        out_shape=[
            jax.ShapeDtypeStruct((4, rows, 2 * width // line), low),
            jax.ShapeDtypeStruct((length, size), low),
            jax.ShapeDtypeStruct((3, width), jnp.float32),
            jax.ShapeDtypeStruct(mlp_mom.shape, jnp.float32),
            jax.ShapeDtypeStruct((size, 2 * wide), low),
            jax.ShapeDtypeStruct((length, size), low),
        ],
        in_specs=[hbm] * 3 + [pl.BlockSpec(memory_space=pltpu.SMEM)] + [vmem] * 7 + [hbm] * 4,
        out_specs=[hbm, vmem, vmem, vmem, hbm, hbm],
        scratch_shapes=[
            pltpu.VMEM((5, size, width), low),
            pltpu.SemaphoreType.DMA((9,)),
            pltpu.VMEM(qkv.shape, low),
            pltpu.VMEM((3, 2, 2, 2, rows, width), low),
            pltpu.VMEM((length, length), jnp.float32),
            pltpu.VMEM((2 * HD, length), jnp.float32),
            pltpu.VMEM((2 * HD, length), jnp.float32),
            pltpu.VMEM(mlp_mom.shape, low),
            pltpu.VMEM(mlp_mom.shape, low),
        ]
        + [GroupSum.scratch(1, rows, wide, line)] * 3
        + [GroupSum.scratch(1, rows, width, line), GroupSum.scratch(3, rows, width, line)]
        + [GroupSum.scratch(1, rows, wide, line, line_first=True), Collect.scratch()],
        compiler_params=pltpu.CompilerParams(
            collective_id=2, has_side_effects=True, vmem_limit_bytes=62 * 1024 * 1024
        ),
        name="attend_back",
    )(
        *(each.reshape(-1, 2, 2, 2, rows, each.shape[2]) for each in (down, up, out)),
        slopes,
        seg_ids.reshape(-1, 1),
        seg_ids.reshape(1, -1),
        qkv,
        grad,
        mixed,
        lse,
        mlp_mom,
        weights,
        normed,
        act,
        down_w,
    )


def finish_kernel(
    line, attn_ref, whole_ref, vec_ref, gain, part_ref, xhat, spread, grad_mid, out_ref, middle, bias,
    attn_home, mlp_home, vec_out, dx_out, block_out, *scratch
):
    (thin, full, gram, sent, got, poly, norm_own, norm_got, dx, away, mine) = scratch[:11]
    (home_sem, start_sem, send_sem, back_sem, norm_sem, block_send, block_recv, pass_send, pass_recv, dx_sem) = scratch[11:21]
    vector = VectorSum(Place(), line, scratch[21:25])
    out_mine, out_away, out_sem = scratch[25:28]
    place = Place()
    x, y, t, core = place.x, place.y, place.tensor, place.core
    me, devices = place.me, place.devices
    rows = attn_ref.shape[1]
    narrow, wide = attn_ref.shape[2] // 2, mlp_home.shape[2] // 2
    greet_all(place)

    def held(order, index):
        return rows_held(place, thin if order < 4 else full, index, rows, narrow if order < 4 else wide)

    def source(order, half):
        return attn_ref.at[order, :, half * narrow : (half + 1) * narrow]

    def target(order, half):
        if order < 4:
            return attn_home.at[order, :, half * narrow : (half + 1) * narrow]
        return mlp_home.at[order - 4, :, half * wide : (half + 1) * wide]

    def owner_of(order, half):
        ox, oy, oz = OWNERS[order]
        return place.index(ox, oy, half, oz)

    def owns(order):
        ox, oy, oz = OWNERS[order]
        return (x == ox) & (y == oy) & (t == oz)

    owns_full = owns(4) | owns(5)
    owns_thin = owns(0) | owns(1) | owns(2) | owns(3)

    def collect(order, half):
        return remote(
            place, source(order, half), held(order, me), home_sem.at[order, half], start_sem.at[0], owner_of(order, half)
        )

    def collect_own(order, half):
        return pltpu.make_async_copy(source(order, half), held(order, me), start_sem.at[0])

    @pl.when(owns_full)
    def _():
        pltpu.make_async_copy(whole_ref, full, start_sem.at[0]).start()

    for order in range(4):
        for half in range(2):

            @pl.when(me == owner_of(order, half))
            def _():
                collect_own(order, half).start()

            @pl.when(me != owner_of(order, half))
            def _():
                collect(order, half).start()

    half_rows = dx.shape[0]

    def rows_of(ref, cores):
        return ref.at[pl.ds(pl.multiple_of(cores * half_rows, half_rows), half_rows), :]

    part_swap = pltpu.make_async_remote_copy(
        src_ref=rows_of(part_ref, 1 - core),
        dst_ref=away,
        send_sem=dx_sem.at[0],
        recv_sem=dx_sem.at[1],
        device_id=place.twin,
        device_id_type=MESH,
    )
    part_load = pltpu.make_async_copy(rows_of(part_ref, core), mine, dx_sem.at[2])
    part_swap.start()
    part_load.start()
    out_load = pltpu.make_async_copy(rows_of(out_ref, core), out_mine, out_sem.at[0])
    out_swap = pltpu.make_async_remote_copy(
        src_ref=rows_of(out_ref, 1 - core),
        dst_ref=out_away,
        send_sem=out_sem.at[3],
        recv_sem=out_sem.at[4],
        device_id=place.twin,
        device_id_type=MESH,
    )
    out_load.start()
    out_swap.start()

    def out_rows(step, carry):
        at = pl.ds(pl.multiple_of(step * 32, 32), 32)
        total = out_mine[at, :].astype(jnp.float32) + out_away[at, :].astype(jnp.float32)
        out_mine[at, :] = (middle[at, :] + total + bias[...]).astype(jnp.bfloat16)
        return carry

    def go_home(slot, source_ref, target_ref, sem):
        keep_rows = pltpu.make_async_copy(source_ref, target_ref, sem.at[slot])
        move_rows = pltpu.make_async_remote_copy(
            src_ref=source_ref,
            dst_ref=target_ref,
            send_sem=sem.at[slot + 1],
            recv_sem=sem.at[slot + 2],
            device_id=place.corner,
            device_id_type=MESH,
        )
        return keep_rows, move_rows

    dx_moves = go_home(2, dx, dx_out, dx_sem)
    out_moves = go_home(5, out_mine, block_out, out_sem)

    def when_moving(moves, action):
        for moving in (False, True):

            @pl.when(place.stays != moving)
            def _():
                action(moves[moving])

    step_rows = 32

    def dx_rows(step, sums):
        at = pl.ds(pl.multiple_of(step * step_rows, step_rows), step_rows)
        grad = mine[at, :].astype(jnp.float32) + away[at, :].astype(jnp.float32)
        hat = xhat[at, :]
        product = grad * hat
        scaled = grad * gain[...]
        inner = jnp.mean(scaled * hat, axis=1, keepdims=True)
        back_grad = spread[at, :] * (scaled - jnp.mean(scaled, axis=1, keepdims=True) - hat * inner)
        dx[at, :] = (grad_mid[at, :] + back_grad).astype(jnp.bfloat16)
        fold = (step_rows // 8, 8, grad.shape[1])
        return (
            sums[0] + jnp.sum(product.reshape(fold), axis=0),
            sums[1] + jnp.sum(grad.reshape(fold), axis=0),
        )

    part_swap.wait()
    part_load.wait()
    empty = jnp.zeros((8, gain.shape[1]), jnp.float32)
    token_sums = lax.fori_loop(0, half_rows // step_rows, dx_rows, (empty, empty), unroll=2)
    when_moving(dx_moves, lambda move: move.start())
    vector.start(vec_ref[...], [jnp.sum(each, axis=0, keepdims=True) for each in token_sums])
    out_load.wait()
    out_swap.wait()
    lax.fori_loop(0, half_rows // 32, out_rows, 0, unroll=2)
    when_moving(out_moves, lambda move: move.start())

    def contract_rows(left, right):
        return lax.dot_general(left, right, (((1,), (1,)), ((), ())), preferred_element_type=jnp.float32)

    block = 256

    def swap_block(slot, index):
        return pltpu.make_async_remote_copy(
            src_ref=sent.at[index],
            dst_ref=got.at[slot, index],
            send_sem=block_send.at[index],
            recv_sem=block_recv.at[slot, index],
            device_id=place.twin,
            device_id_type=MESH,
        )

    def begin(matrix):
        size, width = matrix.shape
        pltpu.make_async_copy(matrix, matrix, start_sem.at[0]).wait()

        def add_squares(step, total):
            piece = matrix[pl.ds(pl.multiple_of(step * 32, 32), 32), :].astype(jnp.float32)
            piece = piece * piece
            return total + jnp.sum(piece.reshape(4, 8, width // 128, 128), axis=(0, 2))

        squares = lax.fori_loop(0, size // 32, add_squares, jnp.zeros((8, 128), jnp.float32))
        norm_own[...] = jnp.zeros((8, 128), jnp.float32) + jnp.sum(squares)
        swap = pltpu.make_async_remote_copy(
            src_ref=norm_own,
            dst_ref=norm_got,
            send_sem=norm_sem.at[0],
            recv_sem=norm_sem.at[1],
            device_id=place.twin,
            device_id_type=MESH,
        )
        swap.start()
        swap.wait()
        scale = 1.0 / (jnp.sqrt(norm_own[...] + norm_got[...]) + 1e-06)
        scale = scale[0:1, 0:1]

        def scale_rows(step, carry):
            at = pl.ds(pl.multiple_of(step * 32, 32), 32)
            matrix[at, :] = (matrix[at, :].astype(jnp.float32) * scale).astype(jnp.bfloat16)
            return carry

        lax.fori_loop(0, size // 32, scale_rows, 0)

    def iterate(matrix, repeat):
        size, width = matrix.shape
        blocks = size // block
        slot = repeat % 2

        def share(index, carry):
            at = pl.ds(pl.multiple_of(index * block, block), block)
            sent[index] = contract_rows(matrix[at, :], matrix[...]).astype(jnp.bfloat16)
            swap_block(slot, index).start()
            return carry

        lax.fori_loop(0, blocks, share, 0)

        def add(index, carry):
            at = pl.ds(pl.multiple_of(index * block, block), block)
            swap_block(slot, index).wait()
            total = sent[index].astype(jnp.float32) + got[slot, index].astype(jnp.float32)
            gram[at, :] = total.astype(jnp.bfloat16)
            return carry

        lax.fori_loop(0, blocks, add, 0)
        square = jnp.dot(gram[...], gram[...], preferred_element_type=jnp.float32)
        poly[...] = (coeff_b * gram[...].astype(jnp.float32) + coeff_c * square).astype(jnp.bfloat16)
        step_width = min(width, 1024)

        def advance(index, carry):
            at = columns(index * step_width, step_width)
            moved = jnp.dot(poly[...], matrix[:, at], preferred_element_type=jnp.float32)
            matrix[:, at] = (coeff_a * matrix[:, at].astype(jnp.float32) + moved).astype(jnp.bfloat16)
            return carry

        lax.fori_loop(0, width // step_width, advance, 0)

    @pl.when(owns_thin)
    def _():
        begin(thin)

    @pl.when(owns_full)
    def _():
        begin(full)

    for repeat in range(NS_STEPS):

        @pl.when(owns_thin)
        def _():
            iterate(thin, repeat)

        @pl.when(owns_full)
        def _():
            iterate(full, repeat)

        if repeat < 3:
            vector.step(repeat)
        if repeat == 3:
            vec_out[...] = vector.end()

    def keep(order, half):
        return pltpu.make_async_copy(held(order, me), target(order, half), back_sem.at[order, half])

    def back(order, half, index):
        return remote(place, held(order, index), target(order, half), send_sem.at[0], back_sem.at[order, half], index)

    def place_in(index):
        dp, z = place.of(index)
        return lax.rem(dp // 2, 2), dp // 4, z, lax.rem(dp, 2)

    def one_aside(order, xs, ys):
        ox, oy, _ = OWNERS[order]
        return (xs != ox) != (ys != oy)

    def back_by_way(order, index):
        xs, ys, z, _ = place_in(index)
        return one_aside(order, xs, ys) & is_one_of(z, sides(order, line)[0])

    def to_back_way(order, half, index):
        xs, ys, z, cores = place_in(index)
        region = held(order, index)
        first = sides(order, line)[0][0]
        return remote(
            place, region, region, send_sem.at[0], pass_recv.at[z - first, cores], place.index(xs, ys, half, OWNERS[order][2])
        )

    def back_in(order, which, cores):
        index = place.index(x, y, cores, sides(order, line)[0][which])
        region = held(order, index)
        return remote(place, region, region, pass_send.at[which, cores], pass_recv.at[which, cores], index)

    def back_on(order, half, which, cores):
        index = place.index(x, y, cores, sides(order, line)[0][which])
        return remote(
            place, held(order, index), target(order, half), pass_send.at[which, cores], back_sem.at[order, half], index
        )

    def when_back_way(order, action):
        for half in range(2):

            @pl.when(one_aside(order, x, y) & (t == OWNERS[order][2]) & (core == half))
            def _():
                for which in range(len(sides(order, line)[0])):
                    for cores in range(2):
                        action(order, half, which, cores)

    def each_device(order, half, action, passed):
        def body(step, carry):
            index = lax.rem(me + step, devices)
            if order < 4:
                action(order, half, index)
            else:

                @pl.when(back_by_way(order, index) == passed)
                def _():
                    action(order, half, index)

            return carry

        lax.fori_loop(1, devices, body, 0)

    def give_back(orders):
        for order in orders:
            for half in range(2):

                @pl.when(me == owner_of(order, half))
                def _():
                    if order >= 4:
                        each_device(order, half, lambda *at: to_back_way(*at).start(), True)
                    each_device(order, half, lambda *at: back(*at).start(), False)
                    keep(order, half).start()

    give_back((4, 5, 0, 1, 2, 3))

    def return_rows(order, half, which, cores):
        back_in(order, which, cores).wait_recv()
        back_on(order, half, which, cores).start()

    for order in (4, 5):
        when_back_way(order, return_rows)

    for order in range(6):
        for half in range(2):
            keep(order, half).wait()

            @pl.when(me == owner_of(order, half))
            def _():
                if order >= 4:
                    each_device(order, half, lambda *at: to_back_way(*at).wait_send(), True)
                each_device(order, half, lambda *at: back(*at).wait_send(), False)

            if order < 4:

                @pl.when(me != owner_of(order, half))
                def _():
                    collect(order, half).wait_send()

    for order in (4, 5):
        when_back_way(order, lambda *at: back_on(*at).wait_send())

    when_moving(dx_moves, lambda move: move.wait())
    when_moving(out_moves, lambda move: move.wait())


def finish(
    attn_round, mlp_whole, mlp_shape, vec, gain, normed_part, xhat, spread, grad_mid, out_part, middle, bias, line
):
    rows = attn_round.shape[1]
    size = 8 * rows
    narrow, wide = attn_round.shape[2] // 2 * line, mlp_shape[2] // 2 * line
    low, dma = jnp.bfloat16, pltpu.SemaphoreType.DMA
    hbm = pl.BlockSpec(memory_space=pl.ANY)
    vmem = pl.BlockSpec(memory_space=pltpu.VMEM)
    half = xhat.shape
    return pl.pallas_call(
        functools.partial(finish_kernel, line),
        out_shape=[
            jax.ShapeDtypeStruct(attn_round.shape, low),
            jax.ShapeDtypeStruct(mlp_shape, low),
            jax.ShapeDtypeStruct(vec.shape, jnp.float32),
            jax.ShapeDtypeStruct(half, low),
            jax.ShapeDtypeStruct(half, low),
        ],
        in_specs=[hbm, hbm, vmem, vmem, hbm, vmem, vmem, vmem, hbm, vmem, vmem],
        out_specs=[hbm, hbm, vmem, hbm, hbm],
        scratch_shapes=[
            pltpu.VMEM((size, narrow), low),
            pltpu.VMEM((size, wide), low),
            pltpu.VMEM((size, size), low),
            pltpu.VMEM((size // 256, 256, size), low),
            pltpu.VMEM((2, size // 256, 256, size), low),
            pltpu.VMEM((size, size), low),
            pltpu.VMEM((8, 128), jnp.float32),
            pltpu.VMEM((8, 128), jnp.float32),
            pltpu.VMEM(half, low),
            pltpu.VMEM(half, low),
            pltpu.VMEM(half, low),
            dma((6, 2)),
            dma((1,)),
            dma((1,)),
            dma((6, 2)),
            dma((2,)),
            dma((size // 256,)),
            dma((2, size // 256)),
            dma((2, 2)),
            dma((2, 2)),
            dma((5,)),
        ]
        + VectorSum.scratch(vec.shape, line)
        + [
            pltpu.VMEM(half, low),
            pltpu.VMEM(half, low),
            dma((8,)),
        ],
        compiler_params=pltpu.CompilerParams(
            collective_id=3, has_side_effects=True, vmem_limit_bytes=60 * 1024 * 1024
        ),
        name="finish",
    )(
        attn_round,
        mlp_whole,
        vec,
        gain.reshape(1, -1),
        normed_part,
        xhat,
        spread,
        grad_mid,
        out_part,
        middle,
        bias.reshape(1, -1),
    )


def pair_swap(value):
    dp, line = lax.axis_size("dp"), lax.axis_size("tensor")
    pairs = [(i * line + k, (i ^ 1) * line + k) for i in range(dp) for k in range(line)]
    return lax.ppermute(value, ("dp", "tensor"), pairs)


def corner_swap(value, place):
    dp, line = lax.axis_size("dp"), lax.axis_size("tensor")
    pairs = []
    for i in range(1, dp, 2):
        for k in range(0, line, 2):
            pairs += [(i * line + k, (i - 1) * line + k + 1), ((i - 1) * line + k + 1, i * line + k)]
    moved = lax.ppermute(value, ("dp", "tensor"), pairs)
    return jnp.where(place.core == lax.rem(place.tensor, 2), value, moved)


def both_halves(value, place):
    other = pair_swap(value)
    first = place.core == 0
    return jnp.concatenate([jnp.where(first, value, other), jnp.where(first, other, value)], axis=0)


def my_half(whole, place):
    size = whole.shape[0] // CORES
    return lax.dynamic_slice_in_dim(whole, place.core * size, size, 0)


def sum_rows(partial, place):
    size = partial.shape[0] // CORES
    away = lax.dynamic_slice_in_dim(partial, (1 - place.core) * size, size, 0)
    return my_half(partial, place).astype(jnp.float32) + pair_swap(away).astype(jnp.float32)


def sum_whole(partial):
    return partial.astype(jnp.float32) + pair_swap(partial).astype(jnp.float32)


def norm_parts(rows):
    centred = rows - jnp.mean(rows, axis=-1, keepdims=True)
    spread = lax.rsqrt(jnp.mean(centred * centred, axis=-1, keepdims=True) + 1e-05)
    return centred * spread, spread


def norm_back(grad, gain, xhat, spread):
    scaled = grad * gain
    return spread * (
        scaled
        - jnp.mean(scaled, axis=-1, keepdims=True)
        - xhat * jnp.mean(scaled * xhat, axis=-1, keepdims=True)
    )


def on_chip_pair(tokens, cotangent, segments, attn_w, mlp_w, vectors, attn_mom, mlp_mom, vector_mom):
    line = lax.axis_size("tensor")
    place = Place()
    core, t = place.core, place.tensor
    width = tokens.shape[1]
    narrow, wide = attn_w.shape[2] // 2, mlp_w.shape[2] // 4
    total_tokens = tokens.shape[0] * line * lax.axis_size("dp")

    def my_columns(row):
        return lax.dynamic_index_in_dim(row.reshape(line, 2, narrow), core, 1, False).reshape(-1)

    def place_columns(piece):
        spread = jnp.zeros((line, 2, narrow), jnp.float32)
        return lax.dynamic_update_slice(spread, piece.reshape(line, 1, narrow), (0, core, 0)).reshape(-1)

    hidden_bias = lax.dynamic_index_in_dim(vectors[8:].reshape(line, 2, 2, wide), core, 1, False)
    hidden_bias = hidden_bias.transpose(1, 0, 2).reshape(2, line * wide)

    seg_pairs = segments.reshape(-1, SEQ)
    seg_own = lax.dynamic_index_in_dim(seg_pairs, t // 2, 0, False)
    seg_ids = jnp.where(core == lax.rem(t, 2), seg_own, pair_swap(seg_own))

    biases = jnp.stack([my_columns(vectors[2]), jnp.zeros((narrow * line,), jnp.float32), my_columns(vectors[3])])
    per = narrow // HD
    local_ids = jnp.arange(per * line)
    head_ids = (local_ids // per) * (2 * per) + core * per + local_ids % per
    slopes = jnp.exp2(-(8.0 / HEADS) * (head_ids.astype(jnp.float32) + 1.0))
    low = jnp.bfloat16
    (
        wqkv, wout, w_up, w_down, x_low, grad_low, qkv, mixed, log_sums, normed, middle, hidden_low, hidden_act, bend
    ) = forward(
        attn_w.astype(low),
        mlp_w.astype(low),
        tokens,
        cotangent,
        slopes,
        seg_ids,
        biases,
        hidden_bias,
        vectors,
        line,
    )
    grad_down, grad_up, grad_out, grad_mixed, grad_mid_mine, middle_sums, hidden_sums = middle_back(
        grad_low, hidden_act, bend, w_down, w_up, hidden_low, middle, mixed, wout, vectors[5]
    )
    xhat_one, spread_one = norm_parts(my_half(x_low, place).astype(jnp.float32))
    attn_sum, normed_part, bias_sums, mlp_mom_new, mlp_whole, out_part = attend_back(
        grad_down,
        grad_up,
        grad_out,
        slopes,
        seg_ids,
        qkv,
        grad_mixed,
        mixed,
        log_sums,
        mlp_mom,
        wqkv,
        normed,
        hidden_act,
        w_down,
        line,
    )
    hidden_grad = lax.dynamic_update_slice(
        jnp.zeros((line, 2, 2, wide), jnp.float32),
        hidden_sums.reshape(2, line, wide).transpose(1, 0, 2)[:, None],
        (0, core, 0, 0),
    )
    vector_rows = jnp.stack(
        [
            jnp.zeros((width,), jnp.float32),
            jnp.zeros((width,), jnp.float32),
            place_columns(bias_sums[0]),
            place_columns(bias_sums[2]),
            middle_sums[2],
            middle_sums[0],
            middle_sums[1],
            middle_sums[3],
        ]
    )
    vector_local = jnp.concatenate([vector_rows, hidden_grad.reshape(-1, width)], axis=0)
    padding = jnp.zeros((4, width), jnp.float32)
    attn_mom_new = 0.5 * attn_mom + attn_sum.astype(jnp.float32)
    attn_ortho, mlp_ortho, vector_sum, grad_tokens, output = finish(
        attn_mom_new.astype(low),
        mlp_whole,
        mlp_mom.shape,
        jnp.concatenate([vector_local, padding], axis=0),
        vectors[0],
        normed_part,
        xhat_one,
        spread_one,
        grad_mid_mine,
        out_part,
        my_half(middle, place),
        vectors[7],
        line,
    )
    vector_grads = vector_sum[: vector_local.shape[0]]
    attn_new = attn_w - attn_ortho.astype(jnp.float32)
    mlp_new = mlp_w - math.sqrt(FF / D) * mlp_ortho.astype(jnp.float32)
    vector_mom_new = 0.5 * vector_mom + vector_grads
    vector_new = vectors - 0.1 / math.sqrt(total_tokens) * vector_mom_new
    return (
        output,
        grad_tokens.astype(jnp.float32),
        attn_mom_new,
        attn_new,
        mlp_mom_new,
        mlp_new,
        vector_mom_new,
        vector_new,
    )


def solution(mesh):
    in_specs = (
        P(("dp", "tensor"), None),
        P(("dp", "tensor"), None),
        P("dp"),
        P(None, "dp", "tensor"),
        P(None, "dp", "tensor"),
        P(),
        P(None, "dp", "tensor"),
        P(None, "dp", "tensor"),
        P(),
    )
    out_specs = (
        P(("dp", "tensor"), None),
        P(("dp", "tensor"), None),
        P(None, "dp", "tensor"),
        P(None, "dp", "tensor"),
        P(None, "dp", "tensor"),
        P(None, "dp", "tensor"),
        P(),
        P(),
    )
    chips_of_two = (mesh.shape["dp"], mesh.shape["tensor"]) == (8, 4)
    return jax.shard_map(
        on_chip_pair if chips_of_two else on_device, mesh=mesh, in_specs=in_specs, out_specs=out_specs, check_vma=False
    )
```

```python
import functools
import math

import jax
import jax.numpy as jnp
from jax import lax
from jax.experimental import pallas as pl
from jax.experimental.pallas import tpu as pltpu
from jax.sharding import PartitionSpec as P

D = 1024
HEADS = 16
HD = 64
FF = 4096
SEQ = 1024
NS_STEPS = 5
MESH = pl.DeviceIdType.MESH


coeff_a = 3.4445
coeff_b = -4.775
coeff_c = 2.0315


def norm_rows(row_data, gain, shift):
    center = jnp.mean(row_data, axis=-1, keepdims=True)
    centred = row_data - center
    spread = jnp.mean(centred * centred, axis=-1, keepdims=True)
    return centred * lax.rsqrt(spread + 1e-05) * gain + shift


def gelu_tanh(values):
    return jax.nn.gelu(values, approximate=True)


def contract_last(left, right):
    return lax.dot_general(
        left, right, (((1,), (1,)), ((), ())), preferred_element_type=jnp.float32
    )


def contract_first(left, right):
    return lax.dot_general(
        left, right, (((0,), (0,)), ((), ())), preferred_element_type=jnp.float32
    )


def head_slopes(first_head, head_count):
    head_ids = (first_head + jnp.arange(head_count)).astype(jnp.float32)
    return jnp.exp2(-(8.0 / HEADS) * (head_ids + 1.0))


def masked_scores(row_query, key_rows, row_segs, seg_ids, row_start, slopes):
    scores = jnp.einsum("qhd,khd->hqk", row_query, key_rows, preferred_element_type=jnp.float32) * (
        1.0 / math.sqrt(HD)
    )
    query_pos = row_start + jnp.arange(row_query.shape[0])
    key_pos = jnp.arange(key_rows.shape[0])
    distance = (query_pos[:, None] - key_pos[None, :]).astype(jnp.float32)
    scores = scores - slopes[:, None, None] * distance[None]
    same_doc = (
        (row_segs[:, None] == seg_ids[None, :])
        & (row_segs[:, None] > 0)
        & (key_pos[None, :] <= query_pos[:, None])
    )
    allowed = same_doc | (key_pos[None, :] == query_pos[:, None])
    return jnp.where(allowed[None], scores, -1e30)


def attend_forward(query, key_rows, value_rows, seg_ids, slopes, row_block):
    length = key_rows.shape[0]

    def one_block(row_start):
        row_query = lax.dynamic_slice_in_dim(query, row_start, row_block, 0)
        row_segs = lax.dynamic_slice_in_dim(seg_ids, row_start, row_block, 0)
        scores = masked_scores(row_query, key_rows, row_segs, seg_ids, row_start, slopes)
        row_max = jnp.max(scores, axis=-1, keepdims=True)
        exp_scores = jnp.exp(scores - row_max)
        row_total = jnp.sum(exp_scores, axis=-1, keepdims=True)
        attn_probs = (exp_scores / row_total).astype(jnp.bfloat16)
        mixed = jnp.einsum(
            "hqk,khd->qhd", attn_probs, value_rows, preferred_element_type=jnp.float32
        )
        return (mixed.astype(jnp.bfloat16), (row_max + jnp.log(row_total))[..., 0])

    block_starts = jnp.arange(length // row_block) * row_block
    mixed, log_sums = lax.map(one_block, block_starts)
    return (mixed.reshape(length, -1), log_sums)


def attend_backward(query, key_rows, value_rows, seg_ids, log_sums, grad_mixed, slopes, row_block):
    length, head_count, head_dim = key_rows.shape
    factor = 1.0 / math.sqrt(HD)

    def one_block(carry, pieces):
        row_start, row_lse = pieces
        row_query = lax.dynamic_slice_in_dim(query, row_start, row_block, 0)
        row_grad = lax.dynamic_slice_in_dim(grad_mixed, row_start, row_block, 0)
        row_segs = lax.dynamic_slice_in_dim(seg_ids, row_start, row_block, 0)
        scores = masked_scores(row_query, key_rows, row_segs, seg_ids, row_start, slopes)
        attn_probs = jnp.exp(scores - row_lse[:, :, None])
        grad_probs = jnp.einsum(
            "qhd,khd->hqk", row_grad, value_rows, preferred_element_type=jnp.float32
        )
        inner = jnp.sum(grad_probs * attn_probs, axis=-1, keepdims=True)
        grad_scores = (attn_probs * (grad_probs - inner)).astype(jnp.bfloat16)
        grad_query = (
            jnp.einsum("hqk,khd->qhd", grad_scores, key_rows, preferred_element_type=jnp.float32)
            * factor
        )
        grad_keys = (
            carry[0]
            + jnp.einsum("hqk,qhd->khd", grad_scores, row_query, preferred_element_type=jnp.float32)
            * factor
        )
        grad_values = carry[1] + jnp.einsum(
            "hqk,qhd->khd",
            attn_probs.astype(jnp.bfloat16),
            row_grad,
            preferred_element_type=jnp.float32,
        )
        return ((grad_keys, grad_values), grad_query)

    empty = jnp.zeros((length, head_count, head_dim), jnp.float32)
    block_starts = jnp.arange(length // row_block) * row_block
    (grad_keys, grad_values), grad_query = lax.scan(
        one_block, (empty, empty), (block_starts, log_sums)
    )
    return (
        grad_query.reshape(length, -1),
        grad_keys.reshape(length, -1),
        grad_values.reshape(length, -1),
    )


def newton_rows(row_iterate):
    for repeat in range(NS_STEPS + 1):
        whole_iterate = lax.all_gather(row_iterate, "tensor", axis=0, tiled=True)
        if repeat == NS_STEPS:
            break
        square_rows = contract_last(row_iterate, whole_iterate).astype(jnp.bfloat16)
        whole_square = lax.all_gather(square_rows, "tensor", axis=0, tiled=True)
        poly_rows = (
            coeff_b * square_rows.astype(jnp.float32)
            + coeff_c * jnp.dot(square_rows, whole_square, preferred_element_type=jnp.float32)
        ).astype(jnp.bfloat16)
        row_iterate = (
            coeff_a * row_iterate.astype(jnp.float32)
            + jnp.dot(poly_rows, whole_iterate, preferred_element_type=jnp.float32)
        ).astype(jnp.bfloat16)
    return whole_iterate


def on_device(tokens, cotangent, segments, attn_w, mlp_w, vectors, attn_mom, mlp_mom, vector_mom):
    tensor_size = lax.axis_size("tensor")
    dp_size = lax.axis_size("dp")
    tensor_index = lax.axis_index("tensor")
    dp_index = lax.axis_index("dp")
    row_count = tokens.shape[0]
    model_width = tokens.shape[1]
    local_width = attn_w.shape[2]
    local_hidden = mlp_w.shape[2]
    head_count = local_width // HD
    row_block = min(512, SEQ)
    total_tokens = row_count * tensor_size * dp_size
    gathered_attn, gathered_mlp = (
        lax.all_gather(attn_w.astype(jnp.bfloat16), "dp", axis=1, tiled=True),
        lax.all_gather(mlp_w.astype(jnp.bfloat16), "dp", axis=1, tiled=True),
    )
    hidden_bias = vectors[8:].reshape(-1)
    query_bias = lax.dynamic_slice_in_dim(vectors[2], tensor_index * local_width, local_width)
    value_bias = lax.dynamic_slice_in_dim(vectors[3], tensor_index * local_width, local_width)
    x_rows = tokens.astype(jnp.float32)
    normed, pull_first = jax.vjp(norm_rows, x_rows, vectors[0], vectors[1])
    all_normed = lax.all_gather(normed.astype(jnp.bfloat16), "tensor", axis=0, tiled=True)
    seq_count = all_normed.shape[0] // SEQ
    projected = jnp.einsum(
        "td,mdc->mtc", all_normed, gathered_attn[:3], preferred_element_type=jnp.float32
    )
    query = (projected[0] + query_bias).astype(jnp.bfloat16)
    key_rows = projected[1].astype(jnp.bfloat16)
    value_rows = (projected[2] + value_bias).astype(jnp.bfloat16)
    slopes = head_slopes(tensor_index * head_count, head_count)
    seq_shape = (seq_count, SEQ, head_count, HD)
    seq_segs = segments.reshape(seq_count, SEQ)

    def forward_seq(pieces):
        return attend_forward(pieces[0], pieces[1], pieces[2], pieces[3], slopes, row_block)

    mixed, log_sums = lax.map(
        forward_seq,
        (
            query.reshape(seq_shape),
            key_rows.reshape(seq_shape),
            value_rows.reshape(seq_shape),
            seq_segs,
        ),
    )
    mixed = mixed.reshape(-1, local_width)
    w_out = gathered_attn[3]
    middle = (
        x_rows
        + lax.psum_scatter(
            contract_last(mixed, w_out).astype(jnp.bfloat16),
            "tensor",
            scatter_dimension=0,
            tiled=True,
        ).astype(jnp.float32)
        + vectors[4]
    )
    hidden_normed, pull_second = jax.vjp(norm_rows, middle, vectors[5], vectors[6])
    hidden_low = hidden_normed.astype(jnp.bfloat16)
    grad_rows = cotangent.astype(jnp.float32)
    all_hidden = lax.all_gather(hidden_low, "tensor", axis=0, tiled=True)
    w_up = gathered_mlp[0]
    w_down = gathered_mlp[1]
    bias_local = lax.dynamic_slice_in_dim(hidden_bias, tensor_index * local_hidden, local_hidden)
    hidden_pre = jnp.dot(all_hidden, w_up, preferred_element_type=jnp.float32) + bias_local
    act_float, gelu_pull = jax.vjp(gelu_tanh, hidden_pre)
    hidden_act = act_float.astype(jnp.bfloat16)
    output = (
        middle
        + lax.psum_scatter(
            contract_last(hidden_act, w_down).astype(jnp.bfloat16),
            "tensor",
            scatter_dimension=0,
            tiled=True,
        ).astype(jnp.float32)
        + vectors[7]
    )
    all_grad = lax.all_gather(grad_rows.astype(jnp.bfloat16), "tensor", axis=0, tiled=True)
    grad_down = contract_first(all_grad, hidden_act)
    grad_act = jnp.dot(all_grad, w_down, preferred_element_type=jnp.float32)
    grad_pre = gelu_pull(grad_act)[0].astype(jnp.bfloat16)
    grad_up = contract_first(all_hidden, grad_pre)
    bias_part = jnp.sum(grad_pre, axis=0, dtype=jnp.float32)
    hidden_grad = lax.dynamic_update_slice_in_dim(
        jnp.zeros(hidden_bias.shape, jnp.float32), bias_part, tensor_index * local_hidden, 0
    )
    grad_hidden_in = lax.psum_scatter(
        contract_last(grad_pre, w_up).astype(jnp.bfloat16),
        "tensor",
        scatter_dimension=0,
        tiled=True,
    ).astype(jnp.float32)
    mlp_grads = jnp.stack([grad_up, grad_down])
    second_grads = pull_second(grad_hidden_in)
    grad_middle = grad_rows + second_grads[0]
    all_grad_mid = lax.all_gather(grad_middle.astype(jnp.bfloat16), "tensor", axis=0, tiled=True)
    grad_out_w = contract_first(all_grad_mid, mixed)
    grad_mixed = jnp.dot(all_grad_mid, w_out, preferred_element_type=jnp.float32).astype(
        jnp.bfloat16
    )

    def backward_seq(pieces):
        return attend_backward(
            pieces[0], pieces[1], pieces[2], pieces[3], pieces[4], pieces[5], slopes, row_block
        )

    grad_query, grad_keys, grad_values = lax.map(
        backward_seq,
        (
            query.reshape(seq_shape),
            key_rows.reshape(seq_shape),
            value_rows.reshape(seq_shape),
            seq_segs,
            log_sums,
            grad_mixed.reshape(seq_shape),
        ),
    )
    grad_qkv = (
        jnp.stack([grad_query, grad_keys, grad_values])
        .reshape(3, -1, local_width)
        .astype(jnp.bfloat16)
    )
    grad_proj_w = jnp.einsum(
        "td,mtc->mdc", all_normed, grad_qkv, preferred_element_type=jnp.float32
    )
    bias_sums = jnp.sum(grad_qkv, axis=1, dtype=jnp.float32)
    grad_normed = lax.psum_scatter(
        jnp.einsum(
            "mtc,mdc->td", grad_qkv, gathered_attn[:3], preferred_element_type=jnp.float32
        ).astype(jnp.bfloat16),
        "tensor",
        scatter_dimension=0,
        tiled=True,
    ).astype(jnp.float32)
    first_grads = pull_first(grad_normed)
    grad_tokens = grad_middle + first_grads[0]

    def placed(piece, full_size, offset):
        return lax.dynamic_update_slice_in_dim(
            jnp.zeros((full_size,), jnp.float32), piece, offset, 0
        )

    width_offset = tensor_index * local_width
    vector_rows = jnp.stack(
        [
            first_grads[1],
            first_grads[2],
            placed(bias_sums[0], model_width, width_offset),
            placed(bias_sums[2], model_width, width_offset),
            jnp.sum(grad_middle, axis=0),
            second_grads[1],
            second_grads[2],
            jnp.sum(grad_rows, axis=0),
        ]
    )
    vector_local = jnp.concatenate([vector_rows, hidden_grad.reshape(4, model_width)], axis=0)
    attn_grads = jnp.concatenate([grad_proj_w, grad_out_w[None]], axis=0)
    attn_sum, mlp_sum = (
        lax.psum_scatter(
            attn_grads.astype(jnp.bfloat16), "dp", scatter_dimension=1, tiled=True
        ).astype(jnp.float32),
        lax.psum_scatter(
            mlp_grads.astype(jnp.bfloat16), "dp", scatter_dimension=1, tiled=True
        ).astype(jnp.float32),
    )
    attn_mom_new = 0.5 * attn_mom + attn_sum
    mlp_mom_new = 0.5 * mlp_mom + mlp_sum
    attn_round = attn_mom_new.astype(jnp.bfloat16)
    mlp_round = mlp_mom_new.astype(jnp.bfloat16)
    attn_float = attn_round.astype(jnp.float32)
    mlp_float = mlp_round.astype(jnp.float32)
    norm_parts = jnp.concatenate(
        [jnp.sum(attn_float * attn_float, axis=(1, 2)), jnp.sum(mlp_float * mlp_float, axis=(1, 2))]
    )
    vector_grads, norm_sums = lax.psum((vector_local, norm_parts), ("dp", "tensor"))
    frob_norms = jnp.sqrt(norm_sums)
    owners = [order * dp_size // 6 for order in range(6)]
    owned_norm = jnp.zeros((), jnp.float32)
    for order in range(6):
        owned_norm = owned_norm + jnp.where(dp_index == owners[order], frob_norms[order], 0.0)
    block_rows = attn_w.shape[1]
    slice_rows = model_width // tensor_size
    full_cols = local_hidden * tensor_size
    rows_attn, rows_mlp = (
        lax.all_gather(attn_round, "tensor", axis=2, tiled=True),
        lax.all_gather(mlp_round, "tensor", axis=2, tiled=True),
    )
    padded_attn = jnp.pad(rows_attn, ((0, 0), (0, 0), (0, full_cols - model_width)))
    all_rows = jnp.concatenate([padded_attn, rows_mlp], axis=0)
    outgoing = jnp.zeros((dp_size, block_rows, full_cols), jnp.bfloat16)
    for order in range(6):
        outgoing = outgoing.at[owners[order]].set(all_rows[order])
    incoming = lax.all_to_all(outgoing, "dp", split_axis=0, concat_axis=0, tiled=True)
    owned_whole = incoming.reshape(model_width, full_cols)
    mine = lax.dynamic_slice_in_dim(owned_whole, tensor_index * slice_rows, slice_rows, 0)
    attn_col = tensor_index * local_width
    row_iterate = (mine.astype(jnp.float32) / (owned_norm + 1e-06)).astype(jnp.bfloat16)
    result = newton_rows(row_iterate)
    returned = lax.all_to_all(
        result.reshape(dp_size, block_rows, full_cols),
        "dp",
        split_axis=0,
        concat_axis=0,
        tiled=True,
    )
    attn_blocks = []
    for order in range(4):
        piece = lax.dynamic_slice_in_dim(returned[owners[order]], attn_col, local_width, 1)
        attn_blocks.append(attn_w[order] - piece.astype(jnp.float32))
    mlp_blocks = []
    for order in range(2):
        piece = lax.dynamic_slice_in_dim(
            returned[owners[4 + order]], tensor_index * local_hidden, local_hidden, 1
        )
        mlp_blocks.append(mlp_w[order] - math.sqrt(FF / D) * piece.astype(jnp.float32))
    attn_new = jnp.stack(attn_blocks)
    mlp_new = jnp.stack(mlp_blocks)
    vector_mom_new = 0.5 * vector_mom + vector_grads
    vector_new = vectors - 0.1 / math.sqrt(total_tokens) * vector_mom_new
    return (
        output.astype(jnp.bfloat16),
        grad_tokens,
        attn_mom_new,
        attn_new,
        mlp_mom_new,
        mlp_new,
        vector_mom_new,
        vector_new,
    )


CORES = 2


class Place:
    def __init__(self):
        self.dp = lax.axis_index("dp")
        self.tensor = lax.axis_index("tensor")
        self.line = lax.axis_size("tensor")
        self.devices = lax.axis_size("dp") * self.line
        self.me = self.dp * self.line + self.tensor
        self.core = lax.rem(self.dp, 2)
        self.chip = self.dp // 2
        self.x = lax.rem(self.chip, 2)
        self.y = self.chip // 2
        self.twin = (self.dp + 1 - 2 * self.core, self.tensor)
        self.across_x = (self.dp + 2 - 4 * self.x, self.tensor)
        self.across_y = (self.dp + 4 - 8 * self.y, self.tensor)
        self.right = (self.dp, self.tensor + 1)
        self.left = (self.dp, self.tensor - 1)
        self.stays = self.core == lax.rem(self.tensor, 2)
        self.corner = (self.dp + 1 - 2 * self.core, self.tensor - 1 + 2 * self.core)


    def of(self, index):
        return (index // self.line, lax.rem(index, self.line))

    def index(self, x, y, core, z):
        return ((2 * y + x) * 2 + core) * self.line + z


def greet(place, line):
    barrier = pltpu.get_barrier_semaphore()

    def signal(device):
        pl.semaphore_signal(barrier, inc=1, device_id=device, device_id_type=MESH)

    signal(place.twin)
    signal(place.across_x)
    signal(place.across_y)

    for other in range(line):

        @pl.when(place.tensor != other)
        def _():
            signal((place.dp, other))

    @pl.when(jnp.logical_not(place.stays))
    def _():
        signal(place.corner)

    pl.semaphore_wait(barrier, jnp.where(place.stays, 3 + line - 1, 3 + line))


OWNERS = ((1, 0, 0), (1, 0, 3), (0, 1, 0), (0, 1, 3), (0, 0, 1), (1, 1, 2))


def greet_all(place):
    barrier = pltpu.get_barrier_semaphore()

    def meet(step, carry):
        pl.semaphore_signal(
            barrier, inc=1, device_id=place.of(lax.rem(place.me + step, place.devices)), device_id_type=MESH
        )
        return carry

    lax.fori_loop(1, place.devices, meet, 0)
    pl.semaphore_wait(barrier, place.devices - 1)


def is_one_of(value, options):
    found = value < 0
    for option in options:
        found = found | (value == option)
    return found


def sides(order, line):
    oz = OWNERS[order][2]
    above, below = list(range(oz + 1, line)), list(range(oz))
    return (above, below) if len(above) > len(below) else (below, above)


def rows_held(place, whole, index, rows, width):
    dp, tensor = place.of(index)
    return whole.at[pl.ds(pl.multiple_of(dp * rows, rows), rows), columns(tensor * width, width)]


def remote(place, source, target, send, recv, index):
    return pltpu.make_async_remote_copy(
        src_ref=source,
        dst_ref=target,
        send_sem=send,
        recv_sem=recv,
        device_id=place.of(index),
        device_id_type=MESH,
    )


class Collect:
    @staticmethod
    def scratch():
        dma = pltpu.SemaphoreType.DMA
        return [dma((2, 2)), dma((1,)), dma((2, 2)), dma((2, 2))]

    SCRATCH = 4

    def __init__(self, place, source, whole, scratch):
        self.place, self.source, self.whole = place, source, whole
        self.send_sem, self.sem, self.pass_send, self.pass_recv = scratch
        self.rows, self.width = source.shape[1], source.shape[2] // 2

    def owner(self, order, half):
        ox, oy, oz = OWNERS[order]
        return self.place.index(ox, oy, half, oz)

    def piece(self, order, half):
        return self.source.at[order - 4, :, half * self.width : (half + 1) * self.width]

    def held(self, index):
        return rows_held(self.place, self.whole, index, self.rows, self.width)

    def direct(self, order, half):
        send = self.send_sem.at[order - 4, half]
        return remote(
            self.place, self.piece(order, half), self.held(self.place.me), send, self.sem.at[0], self.owner(order, half)
        )

    def own(self, order, half):
        return pltpu.make_async_copy(self.piece(order, half), self.held(self.place.me), self.sem.at[0])

    def by_way(self, order):
        place = self.place
        ox, oy, oz = OWNERS[order]
        lone = is_one_of(place.tensor, sides(order, place.line)[1])
        return (place.y != oy) & (place.tensor != oz) & ((place.x != ox) | lone)

    def to_way(self, order, half):
        place = self.place
        ox, oy, _ = OWNERS[order]
        which = jnp.where(place.x == ox, 1, 0)
        return remote(
            place,
            self.piece(order, half),
            self.held(place.me),
            self.send_sem.at[order - 4, half],
            self.pass_recv.at[which, place.core],
            place.index(ox, oy, half, place.tensor),
        )

    def passed(self, order, which, cores):
        ox, oy, _ = OWNERS[order]
        return self.place.index(1 - ox if which == 0 else ox, 1 - oy, cores, self.place.tensor)

    def pass_in(self, order, which, cores):
        index = self.passed(order, which, cores)
        region = self.held(index)
        sems = self.pass_send.at[which, cores], self.pass_recv.at[which, cores]
        return remote(self.place, region, region, *sems, index)

    def pass_on(self, order, which, cores):
        ox, oy, oz = OWNERS[order]
        region = self.held(self.passed(order, which, cores))
        owner = self.place.index(ox, oy, self.place.core, oz)
        return remote(self.place, region, region, self.pass_send.at[which, cores], self.sem.at[0], owner)

    def when_passing(self, action):
        place = self.place
        for order in (5, 4):
            ox, oy, _ = OWNERS[order]
            far, lone = sides(order, place.line)
            for which, planes in ((0, far + lone), (1, lone)):

                @pl.when((place.x == ox) & (place.y == oy) & is_one_of(place.tensor, planes))
                def _():
                    for cores in range(2):
                        action(order, which, cores)

    def each(self, action_way, action_direct, action_own):
        for order in (5, 4):
            for half in range(2):
                mine = self.place.me == self.owner(order, half)

                @pl.when(self.by_way(order))
                def _():
                    action_way(order, half)

                @pl.when(jnp.logical_not(mine) & jnp.logical_not(self.by_way(order)))
                def _():
                    action_direct(order, half)

                @pl.when(mine)
                def _():
                    action_own(order, half)

    def start(self):
        self.each(
            lambda *at: self.to_way(*at).start(), lambda *at: self.direct(*at).start(), lambda *at: self.own(*at).start()
        )

    def forward(self):
        def action(*at):
            self.pass_in(*at).wait_recv()
            self.pass_on(*at).start()

        self.when_passing(action)

    def finish(self):
        self.each(
            lambda *at: self.to_way(*at).wait_send(),
            lambda *at: self.direct(*at).wait_send(),
            lambda *at: None,
        )
        self.when_passing(lambda *at: self.pass_on(*at).wait_send())
        for order in (5, 4):
            for half in range(2):

                @pl.when(self.place.me == self.owner(order, half))
                def _():
                    pltpu.make_async_copy(self.whole, self.whole, self.sem.at[0]).wait()


def columns(start, size):
    return pl.ds(pl.multiple_of(start, 128), size)


class RowSwap:
    SCRATCH = 2

    @staticmethod
    def scratch():
        return [pltpu.SemaphoreType.DMA((1,)), pltpu.SemaphoreType.DMA((4,))]

    def __init__(self, place, rows_ref, whole_ref, scratch):
        self.place, self.rows_ref, self.whole_ref = place, rows_ref, whole_ref
        self.own_sem, self.sem = scratch
        self.size = rows_ref.shape[0]

    def at(self, core):
        return self.whole_ref.at[pl.ds(pl.multiple_of(core * self.size, self.size), self.size), :]

    def copy(self, slot, source, target, device):
        return pltpu.make_async_remote_copy(
            src_ref=source,
            dst_ref=target,
            send_sem=self.sem.at[slot],
            recv_sem=self.sem.at[slot + 1],
            device_id=device,
            device_id_type=MESH,
        )

    def own(self):
        return pltpu.make_async_copy(self.rows_ref, self.at(self.place.core), self.own_sem.at[0])

    def away(self):
        return self.copy(0, self.rows_ref, self.at(1 - self.place.core), self.place.corner)

    def hand_own(self):
        return self.copy(2, self.rows_ref, self.at(self.place.core), self.place.twin)

    def hand_got(self):
        return self.copy(2, self.at(self.place.core), self.at(self.place.core), self.place.twin)

    def start(self):
        @pl.when(self.place.stays)
        def _():
            self.own().start()
            self.hand_own().start()

        @pl.when(jnp.logical_not(self.place.stays))
        def _():
            self.away().start()

    def step(self):
        @pl.when(jnp.logical_not(self.place.stays))
        def _():
            self.away().wait()
            self.hand_got().start()

    def end(self):
        @pl.when(self.place.stays)
        def _():
            self.own().wait()

        self.hand_got().wait()


class WeightGather:
    def __init__(self, place, line, groups, scratch):
        self.place, self.line, self.groups = place, line, groups
        self.own_sem, self.send_sem, self.recv_sem = scratch
        self.last = len(groups) - 1
        self.to_right, self.to_left = 1, line
        self.half_x, self.half_y, self.rest_y, self.rest_x = (2 * line - 1 + k for k in range(4))

    @staticmethod
    def scratch(count, line):
        dma = pltpu.SemaphoreType.DMA
        return [dma((count,)), dma((count, 2 * line + 3)), dma((count, 2 * line + 3))]

    def copy(self, group, slot, source, target, device):
        return pltpu.make_async_remote_copy(
            src_ref=source,
            dst_ref=target,
            send_sem=self.send_sem.at[group, slot],
            recv_sem=self.recv_sem.at[group, slot],
            device_id=device,
            device_id_type=MESH,
        )

    def same(self, group, slot, region, device):
        return self.copy(group, slot, region, region, device)

    def chunk(self, group, index):
        ref, width, _ = self.groups[group]
        cols = columns(index * width, width)
        if group == self.last:
            return ref.at[:, :, :, :, :, cols]
        return ref.at[:, self.place.y, self.place.x, :, :, cols]

    def corner(self, group, ys, xs, half):
        ref, width, _ = self.groups[group]
        if group == self.last:
            return ref.at[:, ys, xs, half, :, columns(self.place.tensor * width, width)]
        return ref.at[:, ys, xs, half]

    def entry(self, group, half):
        ref, width, _ = self.groups[group]
        return ref.at[:, self.place.y, self.place.x, half, :, columns(self.place.tensor * width, width)]

    def own(self, group):
        core = self.place.core
        return pltpu.make_async_copy(self.groups[group][2](core), self.entry(group, core), self.own_sem.at[group])

    def first(self, group):
        core = self.place.core
        return self.copy(group, 0, self.groups[group][2](1 - core), self.entry(group, core), self.place.twin)

    def begin(self, group):
        self.own(group).start()
        self.first(group).start()

    def enter(self, group):
        self.own(group).wait()
        self.same(group, 0, self.entry(group, 1 - self.place.core), self.place.twin).wait_recv()

    def hop(self, group, step, left):
        t = self.place.tensor
        index = t + step - 1 if left else t - step + 1
        slot = (self.to_left if left else self.to_right) + step - 1
        return self.same(group, slot, self.chunk(group, index), self.place.left if left else self.place.right)

    def arrival(self, group, step, left):
        t = self.place.tensor
        index = t + step if left else t - step
        slot = (self.to_left if left else self.to_right) + step - 1
        return self.same(group, slot, self.chunk(group, index), self.place.right if left else self.place.left)

    def sends(self, step, left):
        t, line = self.place.tensor, self.line
        return (t > 0) & (t + step <= line) if left else (t < line - 1) & (t >= step - 1)

    def line_start(self, group):
        for left in (False, True):

            @pl.when(self.sends(1, left))
            def _():
                self.hop(group, 1, left).start()

    def line_step(self, group, step):
        t, line = self.place.tensor, self.line
        for left in (False, True):

            @pl.when(t + step <= line - 1 if left else t >= step)
            def _():
                self.arrival(group, step, left).wait_recv()

            if step < line - 1:

                @pl.when(self.sends(step + 1, left))
                def _():
                    self.hop(group, step + 1, left).start()

    def line_most(self, group):
        for step in range(1, self.line - 1):
            self.line_step(group, step)

    def line_end(self, group):
        self.line_step(group, self.line - 1)

    def plane_start(self, group):
        place = self.place
        self.same(group, self.half_x, self.corner(group, place.y, place.x, 0), place.across_x).start()
        self.same(group, self.half_y, self.corner(group, place.y, place.x, 1), place.across_y).start()

    def plane_step(self, group):
        place, both = self.place, pl.ds(0, 2)
        self.same(group, self.half_x, self.corner(group, place.y, 1 - place.x, 0), place.across_x).wait_recv()
        self.same(group, self.rest_y, self.corner(group, place.y, both, 0), place.across_y).start()
        self.same(group, self.half_y, self.corner(group, 1 - place.y, place.x, 1), place.across_y).wait_recv()
        self.same(group, self.rest_x, self.corner(group, both, place.x, 1), place.across_x).start()

    def plane_end(self, group):
        place, both = self.place, pl.ds(0, 2)
        self.same(group, self.rest_y, self.corner(group, 1 - place.y, both, 0), place.across_y).wait_recv()
        self.same(group, self.rest_x, self.corner(group, both, 1 - place.x, 1), place.across_x).wait_recv()

    def wait_sends(self, group):
        place, both = self.place, pl.ds(0, 2)
        self.first(group).wait_send()
        for step in range(1, self.line):
            for left in (False, True):

                @pl.when(self.sends(step, left))
                def _():
                    self.hop(group, step, left).wait_send()

        self.same(group, self.half_x, self.corner(group, place.y, place.x, 0), place.across_x).wait_send()
        self.same(group, self.half_y, self.corner(group, place.y, place.x, 1), place.across_y).wait_send()
        self.same(group, self.rest_y, self.corner(group, place.y, both, 0), place.across_y).wait_send()
        self.same(group, self.rest_x, self.corner(group, both, place.x, 1), place.across_x).wait_send()


def add_blocks(target, sources):
    lead, rows = target.shape[:-2], target.shape[-2]
    per = rows // 32

    def body(step, carry):
        block, at = step // per, []
        for size in lead[::-1]:
            at.insert(0, lax.rem(block, size))
            block = block // size
        at = tuple(at) + (pl.ds(pl.multiple_of(lax.rem(step, per) * 32, 32), 32),)
        total = sources[0][at].astype(jnp.float32)
        for source in sources[1:]:
            total = total + source[at].astype(jnp.float32)
        target[at] = total.astype(target.dtype)
        return carry

    lax.fori_loop(0, math.prod(lead) * per, body, 0)


class PlaneSum:
    @staticmethod
    def scratch(count, rows, width):
        pair = pltpu.VMEM((count, 2, rows, width), jnp.bfloat16)
        single = pltpu.VMEM((count, rows, width), jnp.bfloat16)
        dma = pltpu.SemaphoreType.DMA
        return [pair] * 4 + [single] * 2 + [dma((2,)), dma((4,)), dma((4,))]

    SCRATCH = 9

    def __init__(self, place, source, result, scratch):
        self.place, self.source, self.result = place, source, result
        self.own, self.got, self.last = scratch[0:2], scratch[2:4], scratch[4:6]
        self.own_sem, self.send_sem, self.recv_sem = scratch[6:9]

    def copy(self, slot, source, target, device):
        return pltpu.make_async_remote_copy(
            src_ref=source,
            dst_ref=target,
            send_sem=self.send_sem.at[slot],
            recv_sem=self.recv_sem.at[slot],
            device_id=device,
            device_id_type=MESH,
        )

    def cut(self, index, mine):
        both, place = pl.ds(0, 2), self.place
        if index == 0:
            return self.source.at[:, place.y if mine else 1 - place.y, both, 0]
        return self.source.at[:, both, place.x if mine else 1 - place.x, 1]

    def load(self, index):
        return pltpu.make_async_copy(self.cut(index, True), self.own[index], self.own_sem.at[index])

    def first(self, index):
        device = self.place.across_x if index else self.place.across_y
        return self.copy(index, self.cut(index, False), self.got[index], device)

    def second(self, index):
        mine = self.place.y if index else self.place.x
        device = self.place.across_y if index else self.place.across_x
        return self.copy(2 + index, self.own[index].at[:, 1 - mine], self.last[index], device)

    def start(self):
        for index in range(2):
            self.first(index).start()
            self.load(index).start()

    def one(self):
        for index in range(2):
            mine = self.place.y if index else self.place.x
            self.load(index).wait()
            self.first(index).wait_recv()
            own, got = self.own[index], self.got[index]
            add_blocks(own.at[:, 1 - mine], (own.at[:, 1 - mine], got.at[:, 1 - mine]))
            self.second(index).start()
            add_blocks(own.at[:, mine], (own.at[:, mine], got.at[:, mine]))

    def two(self):
        for index in range(2):
            mine = self.place.y if index else self.place.x
            self.second(index).wait_recv()
            add_blocks(self.result.at[:, index], (self.own[index].at[:, mine], self.last[index]))

    def sent(self):
        for index in range(2):
            self.first(index).wait_send()
            self.second(index).wait_send()


class LineSum:
    @staticmethod
    def scratch(shape, line):
        dma = pltpu.SemaphoreType.DMA
        return [pltpu.VMEM(shape, jnp.bfloat16)] * 2 + [dma((2, line)), dma((2, line))]

    SCRATCH = 4

    def __init__(self, place, line, value, result, scratch):
        self.place, self.line, self.value, self.result = place, line, value, result
        self.got = scratch[0:2]
        self.send_sem, self.recv_sem = scratch[2:4]
        self.width = value.shape[-1] // line

    def part(self, ref, index):
        return ref.at[(slice(None),) * (len(ref.shape) - 1) + (slice(index * self.width, (index + 1) * self.width),)]

    def hop(self, index, left):
        return pltpu.make_async_remote_copy(
            src_ref=self.part(self.value, index),
            dst_ref=self.part(self.got[left], index),
            send_sem=self.send_sem.at[left, index],
            recv_sem=self.recv_sem.at[left, index],
            device_id=self.place.left if left else self.place.right,
            device_id_type=MESH,
        )

    def step(self, step):
        for left in range(2):
            for index in range(self.line):
                away = index if left else self.line - 1 - index
                order = step - away
                plane = self.line - 1 - order if left else order
                if order < 0 or (plane <= index if left else plane >= index):
                    continue

                @pl.when(self.place.tensor == plane)
                def _():
                    if order > 0:
                        self.hop(index, left).wait_recv()
                        value = self.part(self.value, index)
                        add_blocks(value, (value, self.part(self.got[left], index)))
                    if away > 0:
                        self.hop(index - 1 if left else index + 1, left).wait_send()
                    self.hop(index, left).start()

    def end(self):
        for index in range(self.line):

            @pl.when(self.place.tensor == index)
            def _():
                sources = [self.part(self.value, index)]
                for left in range(2):
                    if index < self.line - 1 if left else index > 0:
                        self.hop(index, left).wait_recv()
                        sources.append(self.part(self.got[left], index))
                add_blocks(self.result, sources)

    def sent(self):
        for index in range(self.line):

            @pl.when(self.place.tensor == index)
            def _():
                if index > 0:
                    self.hop(index - 1, 1).wait_send()
                if index < self.line - 1:
                    self.hop(index + 1, 0).wait_send()


class HomeCopy:
    def __init__(self, place, value, target, scratch):
        self.place, self.value, self.target = place, value, target
        self.own_sem, self.sem = scratch

    SCRATCH = 2

    @staticmethod
    def scratch():
        return [pltpu.SemaphoreType.DMA((1,)), pltpu.SemaphoreType.DMA((2,))]

    def keep(self):
        return pltpu.make_async_copy(self.value.at[:, self.place.core], self.target, self.own_sem.at[0])

    def give(self):
        return pltpu.make_async_remote_copy(
            src_ref=self.value.at[:, 1 - self.place.core],
            dst_ref=self.target,
            send_sem=self.sem.at[0],
            recv_sem=self.sem.at[1],
            device_id=self.place.twin,
            device_id_type=MESH,
        )

    def start(self):
        self.keep().start()
        self.give().start()

    def wait(self):
        self.keep().wait()
        self.give().wait()


class GroupSum:
    @staticmethod
    def scratch(count, rows, width, line, line_first=False):
        low = jnp.bfloat16
        part = width // line
        done = pltpu.VMEM((count, 2, rows, part), low)
        if line_first:
            whole = (count, 2, 2, 2, rows, width)
            held = [pltpu.VMEM(whole, low), pltpu.VMEM(whole[:-1] + (part,), low), pltpu.SemaphoreType.DMA((1,))]
            plane, along = PlaneSum.scratch(count, rows, part), LineSum.scratch(whole, line)
        else:
            middle = (count, 2, rows, width)
            held = [pltpu.VMEM(middle, low)]
            plane, along = PlaneSum.scratch(count, rows, width), LineSum.scratch(middle, line)
        return held + [done] + plane + along + HomeCopy.scratch()

    def __init__(self, place, line, source, target, scratch, line_first=False):
        scratch = list(scratch)

        def take(count):
            taken = scratch[:count]
            del scratch[:count]
            return taken

        if line_first:
            whole, middle, load_sem = take(3)
            self.load = lambda: pltpu.make_async_copy(source, whole, load_sem.at[0])
        else:
            (middle,) = take(1)
        (done,) = take(1)
        plane, along = take(PlaneSum.SCRATCH), take(LineSum.SCRATCH)
        if line_first:
            self.line = LineSum(place, line, whole, middle, along)
            self.plane = PlaneSum(place, middle, done, plane)
        else:
            self.plane = PlaneSum(place, source, middle, plane)
            self.line = LineSum(place, line, middle, done, along)
        self.home = HomeCopy(place, done, target, take(HomeCopy.SCRATCH))

    def sent(self):
        self.plane.sent()
        self.line.sent()


class VectorSum:
    @staticmethod
    def scratch(shape, line):
        return [
            pltpu.VMEM((4,) + shape, jnp.float32),
            pltpu.VMEM((3,) + shape, jnp.float32),
            pltpu.VMEM((line,) + shape, jnp.float32),
            pltpu.SemaphoreType.DMA((4, max(line, 3))),
        ]

    def __init__(self, place, line, scratch):
        self.place, self.line = place, line
        self.sums, self.got, self.along, self.sem = scratch

    def copy(self, stage):
        place = self.place
        return pltpu.make_async_remote_copy(
            src_ref=self.sums.at[stage],
            dst_ref=self.got.at[stage],
            send_sem=self.sem.at[0, stage],
            recv_sem=self.sem.at[1, stage],
            device_id=(place.twin, place.across_x, place.across_y)[stage],
            device_id_type=MESH,
        )

    def hop(self, other, source):
        return pltpu.make_async_remote_copy(
            src_ref=self.sums.at[3],
            dst_ref=self.along.at[source],
            send_sem=self.sem.at[2, other],
            recv_sem=self.sem.at[3, source],
            device_id=(self.place.dp, other),
            device_id_type=MESH,
        )

    def start(self, value, first_rows):
        self.sums[0] = value
        for index, row in enumerate(first_rows):
            self.sums[0, index : index + 1, :] = row
        self.copy(0).start()

    def step(self, stage):
        self.copy(stage).wait()
        self.sums[stage + 1] = self.sums[stage] + self.got[stage]
        if stage < 2:
            self.copy(stage + 1).start()
            return
        self.along[self.place.tensor] = self.sums[3]
        for other in range(self.line):

            @pl.when(self.place.tensor != other)
            def _():
                self.hop(other, self.place.tensor).start()

    def end(self):
        t = self.place.tensor
        for other in range(self.line):

            @pl.when(t != other)
            def _():
                self.hop(other, t).wait_send()
                self.hop(t, other).wait_recv()

        total = self.along[0]
        for other in range(1, self.line):
            total = total + self.along[other]
        return total


LOG2E = 1.4426950408889634
FAR = 1e32
ROW_BLOCK = 256


def fill_distance(seg_rows, seg_cols, distance):
    def body(step, carry):
        start = pl.multiple_of(step * 64, 64)
        shape = (64, distance.shape[1])
        row = lax.broadcasted_iota(jnp.int32, shape, 0) + start
        col = lax.broadcasted_iota(jnp.int32, shape, 1)
        segs = seg_rows[pl.ds(start, 64), :]
        same = (segs == seg_cols[...]) & (segs > 0) & (col <= row)
        allowed = same | (col == row)
        distance[pl.ds(start, 64), :] = jnp.where(allowed, (row - col).astype(jnp.float32), FAR)
        return carry

    lax.fori_loop(0, distance.shape[0] // 64, body, 0)


def head_lanes(dtype):
    lane = lax.broadcasted_iota(jnp.int32, (1, 2 * HD), 1)
    first = (lane < HD).astype(jnp.float32)
    return (first.astype(dtype), (1.0 - first).astype(dtype))


def attend_group(group, slopes, qkv, mixed, lse, distance):
    length = qkv.shape[1]
    cols = columns(group * 2 * HD, 2 * HD)
    masks = head_lanes(jnp.bfloat16)
    first = head_lanes(jnp.float32)[0] > 0.5
    factor = LOG2E / math.sqrt(HD)
    keys_t = qkv[1, :, cols].T
    values = qkv[2, :, cols]
    for start in range(0, length, ROW_BLOCK):
        stop = start + ROW_BLOCK
        rows = slice(start, stop)
        query = qkv[0, rows, cols]
        parts, sums = [], []
        for head in range(2):
            slope = slopes[2 * group + head] * LOG2E
            scores = jnp.dot(query * masks[head], keys_t[:, :stop], preferred_element_type=jnp.float32)
            scores = scores * factor - slope * distance[rows, :stop]
            top = jnp.max(scores, axis=1, keepdims=True)
            probs = jnp.exp2(scores - top)
            total = jnp.sum(probs, axis=1, keepdims=True)
            out = jnp.dot(probs.astype(jnp.bfloat16), values[:stop], preferred_element_type=jnp.float32)
            parts.append(out / total)
            sums.append(top + jnp.log2(total))
        mixed[rows, cols] = jnp.where(first, parts[0], parts[1]).astype(jnp.bfloat16)
        lse[rows, cols] = jnp.where(first, sums[0], sums[1])


def normalize(rows):
    centred = rows - jnp.mean(rows, axis=1, keepdims=True)
    return centred * lax.rsqrt(jnp.mean(centred * centred, axis=1, keepdims=True) + 1e-05)


def forward_kernel(
    line, attn_ref, mlp_ref, tokens_ref, grads_ref, slopes, seg_rows, seg_cols, qkv_bias, hidden_bias, vectors,
    qkv_w, out_w, up_w, down_w, tokens_out, grads_out, qkv_out, mixed_out, lse_out, normed_out, middle_out,
    hidden_out, act_out, bend_out, *scratch
):
    (x_v, normed, qkv_wv, out_wv, up_wv, qkv, mixed, lse, distance, part, got, middle, hidden, act, bend) = scratch[:15]
    load_sem, store_sem, swap_send, swap_recv = scratch[15:19]
    place = Place()
    narrow, wide = attn_ref.shape[2] // 2, mlp_ref.shape[2] // 4
    size = normed.shape[0]

    def attn_source(index):
        return lambda core: attn_ref.at[index : index + 1, :, columns(core * narrow, narrow)]

    def mlp_source(index, half):
        return lambda core: mlp_ref.at[index : index + 1, :, columns((2 * core + half) * wide, wide)]

    groups = [(qkv_w.at[index : index + 1], narrow, attn_source(index)) for index in range(3)]
    groups.append((out_w, narrow, attn_source(3)))
    groups += [(up_w.at[half : half + 1], wide, mlp_source(0, half)) for half in range(2)]
    groups += [(down_w.at[half : half + 1], wide, mlp_source(1, half)) for half in range(2)]
    query, key, value, outer, up_a, up_b, down_a, down_b = range(8)
    gather = WeightGather(place, line, groups, scratch[19:22])
    tokens = RowSwap(place, tokens_ref, tokens_out, scratch[22:24])
    grads = RowSwap(place, grads_ref, grads_out, scratch[24:26])

    def load(group):
        if group < 3:
            source, target = qkv_w.at[group], qkv_wv.at[group]
        elif group == outer:
            source, target = out_w, out_wv
        else:
            source, target = up_w.at[group - up_a], up_wv.at[group - up_a]
        return pltpu.make_async_copy(source, target, load_sem.at[group])

    x_load = pltpu.make_async_copy(tokens_out, x_v, load_sem.at[7])
    pairs = (
        (qkv, qkv_out),
        (mixed, mixed_out),
        (lse, lse_out),
        (normed, normed_out),
        (middle, middle_out),
        (hidden, hidden_out),
        (act.at[0], act_out.at[0]),
        (act.at[1], act_out.at[1]),
        (bend.at[0], bend_out.at[0]),
        (bend.at[1], bend_out.at[1]),
    )

    def store(index):
        return pltpu.make_async_copy(*pairs[index], store_sem.at[index])

    def normalize_tokens():
        def body(step, carry):
            at = pl.ds(pl.multiple_of(step * 32, 32), 32)
            normal = normalize(x_v[at, :].astype(jnp.float32))
            normed[at, :] = (normal * vectors[0:1, :] + vectors[1:2, :]).astype(jnp.bfloat16)
            return carry

        lax.fori_loop(0, size // 32, body, 0, unroll=4)

    def project(group):
        load(group).wait()
        weight = qkv_wv[group].reshape(size, qkv.shape[2])

        def body(step, carry):
            at = pl.ds(pl.multiple_of(step * 512, 512), 512)
            out = jnp.dot(normed[at, :], weight, preferred_element_type=jnp.float32)
            qkv[group, at, :] = (out + qkv_bias[group : group + 1, :]).astype(jnp.bfloat16)
            return carry

        lax.fori_loop(0, size // 512, body, 0)

    def swap(index):
        at = pl.ds(pl.multiple_of(index * 256, 256), 256)
        return pltpu.make_async_remote_copy(
            src_ref=part.at[at, :],
            dst_ref=got.at[at, :],
            send_sem=swap_send.at[index],
            recv_sem=swap_recv.at[index],
            device_id=place.twin,
            device_id_type=MESH,
        )

    def project_out(index, carry):
        at = pl.ds(pl.multiple_of(index * 256, 256), 256)
        weight = out_wv[0].reshape(size, mixed.shape[1])
        part[at, :] = contract_last(mixed[at, :], weight).astype(jnp.bfloat16)
        swap(index).start()
        return carry

    def add_branch(index, carry):
        swap(index).wait()

        def body(step, carry):
            at = pl.ds(pl.multiple_of(index * 256 + step * 32, 32), 32)
            branch = part[at, :].astype(jnp.float32) + got[at, :].astype(jnp.float32)
            total = x_v[at, :].astype(jnp.float32) + branch + vectors[4:5, :]
            middle[at, :] = total
            hidden[at, :] = (normalize(total) * vectors[5:6, :] + vectors[6:7, :]).astype(jnp.bfloat16)
            return carry

        return lax.fori_loop(0, 8, body, carry, unroll=4)

    def feed(half):
        load(up_a + half).wait()

        def body(step, carry):
            at = pl.ds(pl.multiple_of(step * 256, 256), 256)
            weight = up_wv[half].reshape(size, act.shape[2])
            pre = jnp.dot(hidden[at, :], weight, preferred_element_type=jnp.float32)
            pre = pre + hidden_bias[half : half + 1, :]
            square = pre * pre
            bent = jnp.tanh(0.7978845608 * pre * (1.0 + 0.044715 * square))
            inner = 0.7978845608 * (1.0 + 3.0 * 0.044715 * square)
            act[half, at, :] = (0.5 * pre * (1.0 + bent)).astype(jnp.bfloat16)
            bend[half, at, :] = (0.5 * (1.0 + bent) + 0.5 * pre * (1.0 - bent * bent) * inner).astype(jnp.bfloat16)
            return carry

        lax.fori_loop(0, size // 256, body, 0)
        store(6 + half).start()
        store(8 + half).start()

    greet(place, line)
    for group in (query, down_b, key, value, outer, up_a, up_b, down_a):
        gather.begin(group)
    gather.enter(query)
    gather.line_start(query)
    gather.enter(down_b)
    gather.plane_start(down_b)
    gather.enter(key)
    gather.line_most(query)
    gather.line_start(key)
    tokens.start()
    gather.line_end(query)
    gather.plane_start(query)
    gather.plane_step(down_b)
    gather.enter(value)
    gather.line_most(key)
    gather.line_start(value)
    gather.line_end(key)
    gather.plane_step(query)
    gather.plane_start(key)
    gather.plane_end(down_b)
    gather.line_most(value)
    gather.line_end(value)
    gather.enter(outer)
    gather.line_start(outer)
    gather.plane_end(query)
    load(query).start()
    gather.plane_step(key)
    gather.plane_start(value)
    tokens.step()
    fill_distance(seg_rows, seg_cols, distance)
    gather.enter(up_a)
    gather.line_most(outer)
    gather.line_start(up_a)
    gather.plane_end(key)
    load(key).start()
    gather.line_end(outer)
    gather.plane_step(value)
    gather.plane_start(outer)
    tokens.end()
    x_load.start()
    x_load.wait()
    normalize_tokens()
    store(3).start()
    gather.enter(up_b)
    gather.line_most(up_a)
    gather.line_start(up_b)
    project(query)
    gather.line_end(up_a)
    gather.line_start(down_b)
    gather.plane_end(value)
    load(value).start()
    gather.plane_step(outer)
    gather.plane_start(up_a)
    project(key)
    project(value)
    store(0).start()

    def beside(index):
        if index == 0:
            gather.enter(down_a)
            gather.line_most(up_b)
            gather.line_start(down_a)
            gather.plane_end(outer)
            load(outer).start()
        if index == 1:
            gather.line_end(up_b)
            gather.plane_step(up_a)
            gather.plane_start(up_b)
        if index == 2:
            gather.line_step(down_b, 1)
        if index == 3:
            gather.line_most(down_a)

    def attend(index, carry):
        attend_group(index, slopes, qkv, mixed, lse, distance)
        for order in range(4):

            @pl.when(index == order)
            def _():
                beside(order)

        return carry

    lax.fori_loop(0, qkv.shape[2] // (2 * HD), attend, 0)
    store(1).start()
    store(2).start()
    load(outer).wait()
    lax.fori_loop(0, size // 256, project_out, 0)
    gather.plane_step(up_b)
    gather.line_end(down_a)
    gather.plane_start(down_a)
    lax.fori_loop(0, size // 256, add_branch, 0)
    store(4).start()
    store(5).start()
    for step in range(2, line - 1):
        gather.line_step(down_b, step)
    grads.start()
    gather.plane_end(up_a)
    load(up_a).start()
    feed(0)
    gather.plane_step(down_a)
    gather.plane_end(up_b)
    load(up_b).start()
    feed(1)
    gather.line_end(down_b)
    grads.step()
    gather.plane_end(down_a)
    grads.end()
    for index in range(len(pairs)):
        store(index).wait()
    for group in range(len(groups)):
        gather.wait_sends(group)


def forward(attn_low, mlp_low, tokens, grads, slopes, seg_ids, qkv_bias, hidden_bias, vectors, line):
    rows = attn_low.shape[1]
    narrow, wide = attn_low.shape[2] // 2 * line, mlp_low.shape[2] // 4 * line
    length, width = 2 * tokens.shape[0], tokens.shape[1]
    low, dma = jnp.bfloat16, pltpu.SemaphoreType.DMA
    vmem = pl.BlockSpec(memory_space=pltpu.VMEM)
    hbm = pl.BlockSpec(memory_space=pl.ANY)

    def whole(count, columns_held):
        return (count, 2, 2, 2, rows, columns_held)

    kept = [
        ((3, length, narrow), low),
        ((length, narrow), low),
        ((length, narrow), jnp.float32),
        ((length, width), low),
        ((length, width), jnp.float32),
        ((length, width), low),
        ((2, length, wide), low),
        ((2, length, wide), low),
    ]
    outs = [(whole(3, narrow), low), (whole(1, narrow), low), (whole(2, wide), low), (whole(2, wide), low)]
    outs += [((length, width), low)] * 2 + kept
    held = [(length, width)] * 2 + [whole(3, narrow), whole(1, narrow), whole(2, wide)]
    results = pl.pallas_call(
        functools.partial(forward_kernel, line),
        out_shape=[jax.ShapeDtypeStruct(*each) for each in outs],
        in_specs=[hbm] * 4 + [pl.BlockSpec(memory_space=pltpu.SMEM)] + [vmem] * 5,
        out_specs=[hbm] * len(outs),
        scratch_shapes=[pltpu.VMEM(each, low) for each in held]
        + [pltpu.VMEM(*each) for each in kept[:3]]
        + [pltpu.VMEM((length, length), jnp.float32)]
        + [pltpu.VMEM((length, width), low)] * 2
        + [pltpu.VMEM(*each) for each in kept[4:]]
        + [dma((8,)), dma((10,)), dma((length // 256,)), dma((length // 256,))]
        + WeightGather.scratch(8, line)
        + RowSwap.scratch() * 2,
        compiler_params=pltpu.CompilerParams(
            collective_id=1, has_side_effects=True, vmem_limit_bytes=62 * 1024 * 1024
        ),
        name="forward",
    )(
        attn_low,
        mlp_low,
        tokens,
        grads,
        slopes,
        seg_ids.reshape(-1, 1),
        seg_ids.reshape(1, -1),
        qkv_bias,
        hidden_bias,
        vectors,
    )
    return [each.reshape(each.shape[0], length, -1) for each in results[:4]] + list(results[4:])


def middle_kernel(
    line, grads_ref, act_ref, bend_ref, down_ref, up_ref, hidden_ref, middle_ref, mixed_ref, out_ref, gain,
    down_home, up_out, out_out, mixed_out, mid_out, sums_out, hidden_sums,
    grads, act, pre, down, up, hidden, middle, mixed, weight, part, got, low, mid, down_v, out_v, mixed_v,
    load_sem, store_sem, send_sem, recv_sem, *scratch
):
    place = Place()
    bend, up_v = pre, down
    wide = down_home.shape[2] // 4
    one, two = (
        GroupSum(
            place,
            line,
            down_v.at[half : half + 1],
            down_home.at[:, :, columns((2 * place.core + half) * wide, wide)],
            scratch[half],
        )
        for half in range(2)
    )
    size = grads.shape[0]
    half = size // 2
    blocks = size // 256
    sources = (
        (grads_ref, grads), (down_ref, down), (bend_ref, bend), (up_ref, up), (act_ref.at[0], act.at[0]),
        (middle_ref, middle), (out_ref, weight), (hidden_ref, hidden), (mixed_ref, mixed),
    )
    load_g, load_down, load_bend, load_up, load_act, load_middle, load_out, load_hidden, load_mixed = (
        pltpu.make_async_copy(*each, load_sem.at[index]) for index, each in enumerate(sources)
    )
    load_more = pltpu.make_async_copy(act_ref.at[1], act.at[1], load_sem.at[10])
    for each in (load_g, load_act, load_down, load_bend, load_up, load_more, load_middle, load_out, load_hidden, load_mixed):
        each.start()
    greet(place, line)

    def rows(index, count=256):
        return pl.ds(pl.multiple_of(index * count, count), count)

    def swap(index):
        return pltpu.make_async_remote_copy(
            src_ref=part.at[rows(index), :],
            dst_ref=got.at[rows(index), :],
            send_sem=send_sem.at[index],
            recv_sem=recv_sem.at[index],
            device_id=place.twin,
            device_id_type=MESH,
        )

    def store(slot, index, source, target):
        return pltpu.make_async_copy(source.at[rows(index), :], target.at[rows(index), :], store_sem.at[slot, index])

    def back_hidden(index, carry):
        total = None
        for order in range(2):
            back = jnp.dot(grads[rows(index), :], down[order], preferred_element_type=jnp.float32)
            piece = (back * bend[order, rows(index), :].astype(jnp.float32)).astype(jnp.bfloat16)
            pre[order, rows(index), :] = piece
            column = jnp.sum(piece.astype(jnp.float32), axis=0, keepdims=True)
            hidden_sums[order : order + 1, :] = hidden_sums[order : order + 1, :] + column
            term = contract_last(piece, up[order])
            total = term if total is None else total + term
        part[rows(index), :] = total.astype(jnp.bfloat16)
        swap(index).start()
        return carry

    def down_gradient(order):
        def body(index, carry):
            turned = grads[:, columns(index * 256, 256)].T
            piece = jnp.dot(turned, act[order], preferred_element_type=jnp.float32).astype(jnp.bfloat16)
            down_v[order, index // 2, lax.rem(index, 2)] = piece.reshape(2, 128, piece.shape[1])
            return carry

        lax.fori_loop(0, blocks, body, 0)

    def outer_product(slot, left, rights, targets, outs):
        def body(index, carry):
            turned = left[:, columns(index * 256, 256)].T
            for order, (right, target, out) in enumerate(zip(rights, targets, outs)):
                target[rows(index), :] = jnp.dot(turned, right[...], preferred_element_type=jnp.float32).astype(jnp.bfloat16)
                store(slot + order, index, target, out).start()
            return carry

        lax.fori_loop(0, blocks, body, 0)

    def norm_rows_back(step, sums, owned):
        core = place.core if owned else 1 - place.core
        at = pl.ds(pl.multiple_of(core * half + step * 32, 32), 32)
        grad = part[at, :].astype(jnp.float32) + got[at, :].astype(jnp.float32)
        value = middle[at, :]
        centred = value - jnp.mean(value, axis=1, keepdims=True)
        spread = lax.rsqrt(jnp.mean(centred * centred, axis=1, keepdims=True) + 1e-05)
        hat = centred * spread
        scaled = grad * gain[...]
        inner = jnp.mean(scaled * hat, axis=1, keepdims=True)
        above = grads[at, :].astype(jnp.float32)
        total = above + spread * (scaled - jnp.mean(scaled, axis=1, keepdims=True) - hat * inner)
        low[at, :] = total.astype(jnp.bfloat16)
        if not owned:
            return sums
        mid[pl.ds(pl.multiple_of(step * 32, 32), 32), :] = total
        fold = (4, 8, size)
        terms = (grad * hat, grad, total, above)
        return tuple(one + jnp.sum(term.reshape(fold), axis=0) for one, term in zip(sums, terms))

    def back_mixed(index, carry):
        mixed_v[rows(index), :] = jnp.dot(low[rows(index), :], weight[0], preferred_element_type=jnp.float32).astype(
            jnp.bfloat16
        )
        store(5, index, mixed_v, mixed_out).start()
        return carry

    hidden_sums[...] = jnp.zeros_like(hidden_sums)
    load_g.wait()
    load_act.wait()
    down_gradient(0)
    one.plane.start()
    load_more.wait()
    down_gradient(1)
    two.plane.start()
    load_down.wait()
    load_bend.wait()
    load_up.wait()
    lax.fori_loop(0, blocks // 2, back_hidden, 0)
    one.plane.one()
    lax.fori_loop(blocks // 2, blocks, back_hidden, 0)
    load_middle.wait()
    for index in range(blocks):
        swap(index).wait()
    empty = tuple(jnp.zeros((8, size), jnp.float32) for _ in range(4))
    lax.fori_loop(0, half // 32, lambda step, sums: norm_rows_back(step, sums, False), (), unroll=4)
    two.plane.one()
    one.plane.two()
    one.line.step(0)
    sums = lax.fori_loop(0, half // 32, lambda step, sums: norm_rows_back(step, sums, True), empty, unroll=4)
    for index, each in enumerate(sums):
        sums_out[index : index + 1, :] = jnp.sum(each, axis=0, keepdims=True)
    mid_store = pltpu.make_async_copy(mid, mid_out, load_sem.at[9])
    mid_store.start()
    one.line.step(1)
    load_out.wait()
    lax.fori_loop(0, blocks, back_mixed, 0)
    two.plane.two()
    two.line.step(0)
    load_mixed.wait()
    outer_product(4, low, (mixed,), (out_v.at[0],), (out_out.at[0],))
    for step in range(2, line - 1):
        one.line.step(step)
    two.line.step(1)
    load_hidden.wait()
    outer_product(2, hidden, (pre.at[0], pre.at[1]), (up_v.at[0], up_v.at[1]), (up_out.at[0], up_out.at[1]))
    one.line.end()
    one.home.start()
    for step in range(2, line - 1):
        two.line.step(step)
    two.line.end()
    two.home.start()
    for index in range(blocks):
        for order in range(2):
            store(2 + order, index, up_v.at[order], up_out.at[order]).wait()
        store(4, index, out_v.at[0], out_out.at[0]).wait()
        store(5, index, mixed_v, mixed_out).wait()
    mid_store.wait()
    for group in (one, two):
        group.home.wait()
        group.sent()


def middle_back(grads, act, bend, down, up, hidden, middle, mixed, out, gain, line):
    size, narrow = mixed.shape
    rows = size // 8
    low, dma = jnp.bfloat16, pltpu.SemaphoreType.DMA
    hbm, vmem = pl.BlockSpec(memory_space=pl.ANY), pl.BlockSpec(memory_space=pltpu.VMEM)

    def held(each):
        return pltpu.VMEM(each.shape, each.dtype)

    square = pltpu.VMEM((size, size), low)
    return pl.pallas_call(
        functools.partial(middle_kernel, line),
        out_shape=[
            jax.ShapeDtypeStruct((1, rows, 4 * size // line), low),
            jax.ShapeDtypeStruct(act.shape, low),
            jax.ShapeDtypeStruct((1, size, narrow), low),
            jax.ShapeDtypeStruct((size, narrow), low),
            jax.ShapeDtypeStruct((size // 2, size), jnp.float32),
            jax.ShapeDtypeStruct((4, size), jnp.float32),
            jax.ShapeDtypeStruct((2, size), jnp.float32),
        ],
        in_specs=[hbm] * 9 + [vmem],
        out_specs=[hbm] * 5 + [vmem] * 2,
        scratch_shapes=[held(each) for each in (grads, act, bend, down, up, hidden, middle, mixed, out)]
        + [square, square, square, pltpu.VMEM((size // 2, size), jnp.float32)]
        + [pltpu.VMEM((2, 2, 2, 2, rows, act.shape[2]), low)]
        + [pltpu.VMEM((1, size, narrow), low), pltpu.VMEM((size, narrow), low)]
        + [dma((11,)), dma((6, size // 256)), dma((size // 256,)), dma((size // 256,))]
        + [GroupSum.scratch(1, rows, act.shape[2], line)] * 2,
        compiler_params=pltpu.CompilerParams(
            collective_id=4, has_side_effects=True, vmem_limit_bytes=62 * 1024 * 1024
        ),
        name="middle_back",
    )(grads, act, bend, down, up, hidden, middle, mixed, out, gain.reshape(1, -1))


def attend_back_group(group, slopes, qkv, grad, mixed, lse, out, distance, dk_acc, dv_acc):
    length = qkv.shape[1]
    cols = columns(group * 2 * HD, 2 * HD)
    masks = head_lanes(jnp.bfloat16)
    wide_masks = head_lanes(jnp.float32)
    first = wide_masks[0] > 0.5
    factor = LOG2E / math.sqrt(HD)
    shrink = 1.0 / math.sqrt(HD)
    keys, values = qkv[1, :, cols], qkv[2, :, cols]
    keys_t = keys.T
    values_t = values.T
    dk_acc[...] = jnp.zeros_like(dk_acc)
    dv_acc[...] = jnp.zeros_like(dv_acc)
    for start in range(0, length, ROW_BLOCK):
        stop = start + ROW_BLOCK
        rows = slice(start, stop)
        query, grads, log_sums = qkv[0, rows, cols], grad[rows, cols], lse[rows, cols]
        query_t, grads_t = query.T, grads.T
        product = grads.astype(jnp.float32) * mixed[rows, cols].astype(jnp.float32)
        parts = []
        for head in range(2):
            slope = slopes[2 * group + head] * LOG2E
            lanes = slice(head * HD, (head + 1) * HD)
            scores = jnp.dot(query * masks[head], keys_t[:, :stop], preferred_element_type=jnp.float32)
            log_sum = log_sums[:, head * HD : head * HD + 1]
            probs = jnp.exp2(scores * factor - slope * distance[rows, :stop] - log_sum)
            grad_probs = jnp.dot(grads * masks[head], values_t[:, :stop], preferred_element_type=jnp.float32)
            inner = jnp.sum(product * wide_masks[head], axis=1, keepdims=True)
            grad_scores = (probs * (grad_probs - inner)).astype(jnp.bfloat16)
            parts.append(jnp.dot(grad_scores, keys[:stop], preferred_element_type=jnp.float32))
            dk_acc[lanes, :stop] += jnp.dot(query_t[lanes, :], grad_scores, preferred_element_type=jnp.float32)
            dv_acc[lanes, :stop] += jnp.dot(
                grads_t[lanes, :], probs.astype(jnp.bfloat16), preferred_element_type=jnp.float32
            )
        out[0, rows, cols] = (jnp.where(first, parts[0], parts[1]) * shrink).astype(jnp.bfloat16)
    out[1, :, cols] = (dk_acc[...].T * shrink).astype(jnp.bfloat16)
    out[2, :, cols] = dv_acc[...].T.astype(jnp.bfloat16)


def back_kernel(
    line, up_ref, out_ref, slopes, seg_rows, seg_cols, qkv, grad, mixed, lse, mlp_mom, down_sum, weight_ref, normed_ref,
    act_ref, down_w, attn_home, normed_part, bias_sums, mom_out, whole, out_part,
    held, held_sem, grads, projected, distance, dk_acc, dv_acc, up_sum, mlp_round, *scratch
):
    place = Place()
    narrow_cols = held.shape[2]
    wide, narrow = mlp_mom.shape[2] // 4, attn_home.shape[2] // 2

    def up_target(part):
        return up_sum.at[:, :, columns((2 * place.core + part) * wide, wide)]

    def attn_target(lo, hi):
        return attn_home.at[lo:hi, :, columns(place.core * narrow, narrow)]

    groups = [
        GroupSum(place, line, up_ref.at[0:1], up_target(0), scratch[0]),
        GroupSum(place, line, out_ref, attn_target(3, 4), scratch[1]),
        GroupSum(place, line, projected, attn_target(0, 3), scratch[2]),
        GroupSum(place, line, up_ref.at[1:2], up_target(1), scratch[3], line_first=True),
    ]
    three, outer, inner, last = groups
    collect = Collect(place, mlp_round, whole, scratch[4])

    def attend(group, carry):
        attend_back_group(group, slopes, qkv, grad, mixed, lse, grads, distance, dk_acc, dv_acc)
        return carry

    def halves(ref):
        return [ref.at[:, half * narrow_cols : (half + 1) * narrow_cols] for half in range(2)]

    first_loads = [pltpu.make_async_copy(weight_ref.at[order], held.at[order], held_sem.at[order]) for order in range(3)]
    for half, source in enumerate(halves(normed_ref)):
        first_loads.append(pltpu.make_async_copy(source, held.at[3 + half], held_sem.at[3 + half]))
    quarters = [source for part in range(2) for source in halves(down_w.at[part])]
    late_loads = [pltpu.make_async_copy(quarters[index], held.at[index], held_sem.at[index]) for index in range(4)]

    def act_load(block, index):
        source = act_ref.at[
            index // 2, pl.ds(pl.multiple_of(block * 256, 256), 256), (index % 2) * narrow_cols : (index % 2 + 1) * narrow_cols
        ]
        return pltpu.make_async_copy(source, held.at[4, index * 256 : (index + 1) * 256], held_sem.at[5 + index])

    def project(index, carry):
        left = held[3 + index // 2, :, columns(lax.rem(index, 2) * 256, 256)].T
        for order in range(3):
            piece = jnp.dot(left, grads[order], preferred_element_type=jnp.float32).astype(jnp.bfloat16)
            projected[order, index // 2, lax.rem(index, 2)] = piece.reshape(2, 128, piece.shape[1])
        return carry

    def unproject(index, carry):
        at = pl.ds(pl.multiple_of(index * 256, 256), 256)
        total = contract_last(grads[0, at, :], held[0])
        for order in range(1, 3):
            total = total + contract_last(grads[order, at, :], held[order])
        normed_part[at, :] = total.astype(jnp.bfloat16)
        return carry

    def feed_out(block, carry):
        for index in range(4):
            act_load(block, index).start()
        for index in range(4):
            act_load(block, index).wait()
        total = contract_last(held[4, 0:256], held[0])
        for index in range(1, 4):
            total = total + contract_last(held[4, index * 256 : (index + 1) * 256], held[index])
        at = pl.ds(pl.multiple_of(block * 256, 256), 256)
        for half in range(2):
            grads[half, at, :] = total[:, half * narrow_cols : (half + 1) * narrow_cols].astype(jnp.bfloat16)
        return carry

    def out_store(half):
        return pltpu.make_async_copy(grads.at[half], halves(out_part)[half], held_sem.at[half])

    def update(index, carry):
        at = pl.ds(pl.multiple_of(index * 32, 32), 32)
        for order, gradient in enumerate((up_sum, down_sum)):
            fresh = 0.5 * mlp_mom[order, at, :] + gradient[0, at, :].astype(jnp.float32)
            mom_out[order, at, :] = fresh
            mlp_round[order, at, :] = fresh.astype(jnp.bfloat16)
        return carry

    greet_all(place)
    three.plane.start()
    last.load().start()
    for each in first_loads:
        each.start()
    last.load().wait()
    last.line.step(0)
    outer.plane.start()
    fill_distance(seg_rows, seg_cols, distance)
    pairs = qkv.shape[2] // (2 * HD)
    lax.fori_loop(0, pairs // 2, attend, 0)
    three.plane.one()
    last.line.step(1)
    lax.fori_loop(pairs // 2, pairs, attend, 0)
    three.plane.two()
    three.line.step(0)
    outer.plane.one()
    for each in first_loads:
        each.wait()
    lax.fori_loop(0, 4, project, 0)
    for step in range(2, line - 1):
        last.line.step(step)
    inner.plane.start()
    three.line.step(1)
    outer.plane.two()
    outer.line.step(0)
    lax.fori_loop(0, 4, unproject, 0)
    for each in late_loads:
        each.start()
    for order in range(3):
        bias_sums[order : order + 1, :] = jnp.sum(grads[order].astype(jnp.float32), axis=0, keepdims=True)
    for step in range(2, line - 1):
        three.line.step(step)
    last.line.end()
    last.plane.start()
    three.line.end()
    three.home.start()
    last.plane.one()
    inner.plane.one()
    outer.line.step(1)
    last.plane.two()
    last.home.start()
    for step in range(2, line - 1):
        outer.line.step(step)
    for group in (three, last):
        group.home.wait()
    lax.fori_loop(0, mlp_mom.shape[1] // 32, update, 0)
    collect.start()
    collect.forward()
    outer.line.end()
    outer.home.start()
    inner.plane.two()
    inner.line.step(0)
    for each in late_loads:
        each.wait()
    lax.fori_loop(0, 2, feed_out, 0)
    inner.line.step(1)
    lax.fori_loop(2, 4, feed_out, 0)
    for half in range(2):
        out_store(half).start()
    for step in range(2, line - 1):
        inner.line.step(step)
    inner.line.end()
    inner.home.start()
    inner.home.wait()
    outer.home.wait()
    for half in range(2):
        out_store(half).wait()
    for group in groups:
        group.sent()
    collect.finish()


def attend_back(
    up, out, slopes, seg_ids, qkv, grad, mixed, lse, mlp_mom, down_sum, weights, normed, act, down_w, line
):
    _, length, width = qkv.shape
    rows, wide = up.shape[1] // 8, up.shape[2]
    size = normed.shape[1]
    vmem = pl.BlockSpec(memory_space=pltpu.VMEM)
    hbm = pl.BlockSpec(memory_space=pl.ANY)
    low = jnp.bfloat16
    return pl.pallas_call(
        functools.partial(back_kernel, line),
        out_shape=[
            jax.ShapeDtypeStruct((4, rows, 2 * width // line), low),
            jax.ShapeDtypeStruct((length, size), low),
            jax.ShapeDtypeStruct((3, width), jnp.float32),
            jax.ShapeDtypeStruct(mlp_mom.shape, jnp.float32),
            jax.ShapeDtypeStruct((size, 2 * wide), low),
            jax.ShapeDtypeStruct((length, size), low),
        ],
        in_specs=[hbm] * 2 + [pl.BlockSpec(memory_space=pltpu.SMEM)] + [vmem] * 8 + [hbm] * 4,
        out_specs=[hbm, vmem, vmem, vmem, hbm, hbm],
        scratch_shapes=[
            pltpu.VMEM((5, size, width), low),
            pltpu.SemaphoreType.DMA((9,)),
            pltpu.VMEM(qkv.shape, low),
            pltpu.VMEM((3, 2, 2, 2, rows, width), low),
            pltpu.VMEM((length, length), jnp.float32),
            pltpu.VMEM((2 * HD, length), jnp.float32),
            pltpu.VMEM((2 * HD, length), jnp.float32),
            pltpu.VMEM(down_sum.shape, low),
            pltpu.VMEM(mlp_mom.shape, low),
        ]
        + [GroupSum.scratch(1, rows, wide, line)]
        + [GroupSum.scratch(1, rows, width, line), GroupSum.scratch(3, rows, width, line)]
        + [GroupSum.scratch(1, rows, wide, line, line_first=True), Collect.scratch()],
        compiler_params=pltpu.CompilerParams(
            collective_id=2, has_side_effects=True, vmem_limit_bytes=62 * 1024 * 1024
        ),
        name="attend_back",
    )(
        *(each.reshape(-1, 2, 2, 2, rows, each.shape[2]) for each in (up, out)),
        slopes,
        seg_ids.reshape(-1, 1),
        seg_ids.reshape(1, -1),
        qkv,
        grad,
        mixed,
        lse,
        mlp_mom,
        down_sum,
        weights,
        normed,
        act,
        down_w,
    )


def finish_kernel(
    line, attn_ref, whole_ref, vec_ref, gain, part_ref, x_ref, grad_mid, out_ref, middle_ref, bias, attn_w, mlp_w,
    attn_new, mlp_new, vec_out, dx_new, block_out, *scratch
):
    (thin, full, gram, sent, got, poly, norm_own, norm_got, dx, away, mine) = scratch[:11]
    (home_sem, start_sem, send_sem, back_sem, norm_sem, block_send, block_recv, pass_send, pass_recv, dx_sem) = scratch[11:21]
    vector = VectorSum(Place(), line, scratch[21:25])
    out_mine, out_away, out_sem, middle, tokens, dx_out, attn_home, mlp_home = scratch[25:33]
    place = Place()
    x, y, t, core = place.x, place.y, place.tensor, place.core
    me, devices = place.me, place.devices
    rows = attn_ref.shape[1]
    narrow, wide = attn_ref.shape[2] // 2, mlp_home.shape[2] // 2
    greet_all(place)

    def held(order, index):
        return rows_held(place, thin if order < 4 else full, index, rows, narrow if order < 4 else wide)

    def source(order, half):
        return attn_ref.at[order, :, half * narrow : (half + 1) * narrow]

    def target(order, half):
        if order < 4:
            return attn_home.at[order, :, half * narrow : (half + 1) * narrow]
        return mlp_home.at[order - 4, :, half * wide : (half + 1) * wide]

    def owner_of(order, half):
        ox, oy, oz = OWNERS[order]
        return place.index(ox, oy, half, oz)

    def owns(order):
        ox, oy, oz = OWNERS[order]
        return (x == ox) & (y == oy) & (t == oz)

    owns_full = owns(4) | owns(5)
    owns_thin = owns(0) | owns(1) | owns(2) | owns(3)

    def collect(order, half):
        return remote(
            place, source(order, half), held(order, me), home_sem.at[order, half], start_sem.at[0], owner_of(order, half)
        )

    def collect_own(order, half):
        return pltpu.make_async_copy(source(order, half), held(order, me), start_sem.at[0])

    @pl.when(owns_full)
    def _():
        pltpu.make_async_copy(whole_ref, full, start_sem.at[0]).start()

    for order in range(4):
        for half in range(2):

            @pl.when(me == owner_of(order, half))
            def _():
                collect_own(order, half).start()

            @pl.when(me != owner_of(order, half))
            def _():
                collect(order, half).start()

    half_rows = dx.shape[0]

    def rows_of(ref, cores):
        return ref.at[pl.ds(pl.multiple_of(cores * half_rows, half_rows), half_rows), :]

    part_swap = pltpu.make_async_remote_copy(
        src_ref=rows_of(part_ref, 1 - core),
        dst_ref=away,
        send_sem=dx_sem.at[0],
        recv_sem=dx_sem.at[1],
        device_id=place.twin,
        device_id_type=MESH,
    )
    part_load = pltpu.make_async_copy(rows_of(part_ref, core), mine, dx_sem.at[2])
    part_swap.start()
    part_load.start()
    out_load = pltpu.make_async_copy(rows_of(out_ref, core), out_mine, out_sem.at[0])
    out_swap = pltpu.make_async_remote_copy(
        src_ref=rows_of(out_ref, 1 - core),
        dst_ref=out_away,
        send_sem=out_sem.at[3],
        recv_sem=out_sem.at[4],
        device_id=place.twin,
        device_id_type=MESH,
    )
    middle_load = pltpu.make_async_copy(rows_of(middle_ref, core), middle, out_sem.at[1])
    tokens_load = pltpu.make_async_copy(rows_of(x_ref, core), tokens, out_sem.at[2])
    for each in (tokens_load, out_load, out_swap, middle_load):
        each.start()

    def out_rows(step, carry):
        at = pl.ds(pl.multiple_of(step * 32, 32), 32)
        total = out_mine[at, :].astype(jnp.float32) + out_away[at, :].astype(jnp.float32)
        out_mine[at, :] = (middle[at, :] + total + bias[...]).astype(jnp.bfloat16)
        return carry

    def go_home(slot, source_ref, target_ref, sem):
        keep_rows = pltpu.make_async_copy(source_ref, target_ref, sem.at[slot])
        move_rows = pltpu.make_async_remote_copy(
            src_ref=source_ref,
            dst_ref=target_ref,
            send_sem=sem.at[slot + 1],
            recv_sem=sem.at[slot + 2],
            device_id=place.corner,
            device_id_type=MESH,
        )
        return keep_rows, move_rows

    dx_moves = go_home(2, dx, dx_out, dx_sem)
    out_moves = go_home(5, out_mine, block_out, out_sem)

    def when_moving(moves, action):
        for moving in (False, True):

            @pl.when(place.stays != moving)
            def _():
                action(moves[moving])

    step_rows = 32

    def dx_rows(step, sums):
        at = pl.ds(pl.multiple_of(step * step_rows, step_rows), step_rows)
        grad = mine[at, :].astype(jnp.float32) + away[at, :].astype(jnp.float32)
        value = tokens[at, :].astype(jnp.float32)
        centred = value - jnp.mean(value, axis=1, keepdims=True)
        spread = lax.rsqrt(jnp.mean(centred * centred, axis=1, keepdims=True) + 1e-05)
        hat = centred * spread
        product = grad * hat
        scaled = grad * gain[...]
        inner = jnp.mean(scaled * hat, axis=1, keepdims=True)
        back_grad = spread * (scaled - jnp.mean(scaled, axis=1, keepdims=True) - hat * inner)
        dx[at, :] = (grad_mid[at, :] + back_grad).astype(jnp.bfloat16)
        fold = (step_rows // 8, 8, grad.shape[1])
        return (
            sums[0] + jnp.sum(product.reshape(fold), axis=0),
            sums[1] + jnp.sum(grad.reshape(fold), axis=0),
        )

    part_swap.wait()
    part_load.wait()
    tokens_load.wait()
    empty = jnp.zeros((8, gain.shape[1]), jnp.float32)
    token_sums = lax.fori_loop(0, half_rows // step_rows, dx_rows, (empty, empty), unroll=2)
    when_moving(dx_moves, lambda move: move.start())
    vector.start(vec_ref[...], [jnp.sum(each, axis=0, keepdims=True) for each in token_sums])
    out_load.wait()
    out_swap.wait()
    middle_load.wait()
    lax.fori_loop(0, half_rows // 32, out_rows, 0, unroll=2)
    when_moving(out_moves, lambda move: move.start())

    def contract_rows(left, right):
        return lax.dot_general(left, right, (((1,), (1,)), ((), ())), preferred_element_type=jnp.float32)

    block = 256

    def swap_block(slot, index):
        return pltpu.make_async_remote_copy(
            src_ref=sent.at[index],
            dst_ref=got.at[slot, index],
            send_sem=block_send.at[index],
            recv_sem=block_recv.at[slot, index],
            device_id=place.twin,
            device_id_type=MESH,
        )

    def begin(matrix):
        size, width = matrix.shape
        pltpu.make_async_copy(matrix, matrix, start_sem.at[0]).wait()

        def add_squares(step, total):
            piece = matrix[pl.ds(pl.multiple_of(step * 32, 32), 32), :].astype(jnp.float32)
            piece = piece * piece
            return total + jnp.sum(piece.reshape(4, 8, width // 128, 128), axis=(0, 2))

        squares = lax.fori_loop(0, size // 32, add_squares, jnp.zeros((8, 128), jnp.float32))
        norm_own[...] = jnp.zeros((8, 128), jnp.float32) + jnp.sum(squares)
        swap = pltpu.make_async_remote_copy(
            src_ref=norm_own,
            dst_ref=norm_got,
            send_sem=norm_sem.at[0],
            recv_sem=norm_sem.at[1],
            device_id=place.twin,
            device_id_type=MESH,
        )
        swap.start()
        swap.wait()
        scale = 1.0 / (jnp.sqrt(norm_own[...] + norm_got[...]) + 1e-06)
        scale = scale[0:1, 0:1]

        def scale_rows(step, carry):
            at = pl.ds(pl.multiple_of(step * 32, 32), 32)
            matrix[at, :] = (matrix[at, :].astype(jnp.float32) * scale).astype(jnp.bfloat16)
            return carry

        lax.fori_loop(0, size // 32, scale_rows, 0)

    def iterate(matrix, repeat):
        size, width = matrix.shape
        blocks = size // block
        slot = repeat % 2

        def share(index, carry):
            at = pl.ds(pl.multiple_of(index * block, block), block)
            sent[index] = contract_rows(matrix[at, :], matrix[...]).astype(jnp.bfloat16)
            swap_block(slot, index).start()
            return carry

        lax.fori_loop(0, blocks, share, 0)

        def add(index, carry):
            at = pl.ds(pl.multiple_of(index * block, block), block)
            swap_block(slot, index).wait()
            total = sent[index].astype(jnp.float32) + got[slot, index].astype(jnp.float32)
            gram[at, :] = total.astype(jnp.bfloat16)
            return carry

        lax.fori_loop(0, blocks, add, 0)
        square = jnp.dot(gram[...], gram[...], preferred_element_type=jnp.float32)
        poly[...] = (coeff_b * gram[...].astype(jnp.float32) + coeff_c * square).astype(jnp.bfloat16)
        step_width = min(width, 1024)

        def advance(index, carry):
            at = columns(index * step_width, step_width)
            moved = jnp.dot(poly[...], matrix[:, at], preferred_element_type=jnp.float32)
            matrix[:, at] = (coeff_a * matrix[:, at].astype(jnp.float32) + moved).astype(jnp.bfloat16)
            return carry

        lax.fori_loop(0, width // step_width, advance, 0)

    @pl.when(owns_thin)
    def _():
        begin(thin)

    @pl.when(owns_full)
    def _():
        begin(full)

    for repeat in range(NS_STEPS):

        @pl.when(owns_thin)
        def _():
            iterate(thin, repeat)

        @pl.when(owns_full)
        def _():
            iterate(full, repeat)

        if repeat < 3:
            vector.step(repeat)
        if repeat == 3:
            vec_out[...] = vector.end()

    def keep(order, half):
        return pltpu.make_async_copy(held(order, me), target(order, half), back_sem.at[order, half])

    def back(order, half, index):
        return remote(place, held(order, index), target(order, half), send_sem.at[0], back_sem.at[order, half], index)

    def place_in(index):
        dp, z = place.of(index)
        return lax.rem(dp // 2, 2), dp // 4, z, lax.rem(dp, 2)

    def one_aside(order, xs, ys):
        ox, oy, _ = OWNERS[order]
        return (xs != ox) != (ys != oy)

    def back_by_way(order, index):
        xs, ys, z, _ = place_in(index)
        return one_aside(order, xs, ys) & is_one_of(z, sides(order, line)[0])

    def to_back_way(order, half, index):
        xs, ys, z, cores = place_in(index)
        region = held(order, index)
        first = sides(order, line)[0][0]
        return remote(
            place, region, region, send_sem.at[0], pass_recv.at[z - first, cores], place.index(xs, ys, half, OWNERS[order][2])
        )

    def back_in(order, which, cores):
        index = place.index(x, y, cores, sides(order, line)[0][which])
        region = held(order, index)
        return remote(place, region, region, pass_send.at[which, cores], pass_recv.at[which, cores], index)

    def back_on(order, half, which, cores):
        index = place.index(x, y, cores, sides(order, line)[0][which])
        return remote(
            place, held(order, index), target(order, half), pass_send.at[which, cores], back_sem.at[order, half], index
        )

    def when_back_way(order, action):
        for half in range(2):

            @pl.when(one_aside(order, x, y) & (t == OWNERS[order][2]) & (core == half))
            def _():
                for which in range(len(sides(order, line)[0])):
                    for cores in range(2):
                        action(order, half, which, cores)

    def each_device(order, half, action, passed):
        def body(step, carry):
            index = lax.rem(me + step, devices)
            if order < 4:
                action(order, half, index)
            else:

                @pl.when(back_by_way(order, index) == passed)
                def _():
                    action(order, half, index)

            return carry

        lax.fori_loop(1, devices, body, 0)

    def give_back(orders):
        for order in orders:
            for half in range(2):

                @pl.when(me == owner_of(order, half))
                def _():
                    if order >= 4:
                        each_device(order, half, lambda *at: to_back_way(*at).start(), True)
                    each_device(order, half, lambda *at: back(*at).start(), False)
                    keep(order, half).start()

    give_back((4, 5, 0, 1, 2, 3))

    def return_rows(order, half, which, cores):
        back_in(order, which, cores).wait_recv()
        back_on(order, half, which, cores).start()

    for order in (4, 5):
        when_back_way(order, return_rows)

    for order in range(6):
        for half in range(2):
            keep(order, half).wait()

            @pl.when(me == owner_of(order, half))
            def _():
                if order >= 4:
                    each_device(order, half, lambda *at: to_back_way(*at).wait_send(), True)
                each_device(order, half, lambda *at: back(*at).wait_send(), False)

            if order < 4:

                @pl.when(me != owner_of(order, half))
                def _():
                    collect(order, half).wait_send()

    for order in (4, 5):
        when_back_way(order, lambda *at: back_on(*at).wait_send())

    when_moving(dx_moves, lambda move: move.wait())

    def widen(step, carry):
        at = pl.ds(pl.multiple_of(step * 32, 32), 32)
        dx_new[at, :] = dx_out[at, :].astype(jnp.float32)
        return carry

    lax.fori_loop(0, half_rows // 32, widen, 0)

    def renew(step, carry):
        at = pl.ds(pl.multiple_of(step * 32, 32), 32)
        for order in range(4):
            attn_new[order, at, :] = attn_w[order, at, :] - attn_home[order, at, :].astype(jnp.float32)
        for order in range(2):
            change = math.sqrt(FF / D) * mlp_home[order, at, :].astype(jnp.float32)
            mlp_new[order, at, :] = mlp_w[order, at, :] - change
        return carry

    lax.fori_loop(0, rows // 32, renew, 0)
    when_moving(out_moves, lambda move: move.wait())


def finish(attn_round, mlp_whole, vec, gain, normed_part, tokens, grad_mid, out_part, middle, bias, attn_w, mlp_w, line):
    rows = attn_w.shape[1]
    size = 8 * rows
    narrow, wide = attn_w.shape[2] // 2 * line, mlp_w.shape[2] // 2 * line
    low, dma = jnp.bfloat16, pltpu.SemaphoreType.DMA
    hbm = pl.BlockSpec(memory_space=pl.ANY)
    vmem = pl.BlockSpec(memory_space=pltpu.VMEM)
    half = grad_mid.shape
    return pl.pallas_call(
        functools.partial(finish_kernel, line),
        out_shape=[
            jax.ShapeDtypeStruct(attn_w.shape, jnp.float32),
            jax.ShapeDtypeStruct(mlp_w.shape, jnp.float32),
            jax.ShapeDtypeStruct(vec.shape, jnp.float32),
            jax.ShapeDtypeStruct(half, jnp.float32),
            jax.ShapeDtypeStruct(half, low),
        ],
        in_specs=[hbm, hbm, vmem, vmem, hbm, hbm, vmem, hbm, hbm, vmem, vmem, vmem],
        out_specs=[vmem, vmem, vmem, vmem, hbm],
        scratch_shapes=[
            pltpu.VMEM((size, narrow), low),
            pltpu.VMEM((size, wide), low),
            pltpu.VMEM((size, size), low),
            pltpu.VMEM((size // 256, 256, size), low),
            pltpu.VMEM((2, size // 256, 256, size), low),
            pltpu.VMEM((size, size), low),
            pltpu.VMEM((8, 128), jnp.float32),
            pltpu.VMEM((8, 128), jnp.float32),
            pltpu.VMEM(half, low),
            pltpu.VMEM(half, low),
            pltpu.VMEM(half, low),
            dma((6, 2)),
            dma((1,)),
            dma((1,)),
            dma((6, 2)),
            dma((2,)),
            dma((size // 256,)),
            dma((2, size // 256)),
            dma((2, 2)),
            dma((2, 2)),
            dma((5,)),
        ]
        + VectorSum.scratch(vec.shape, line)
        + [
            pltpu.VMEM(half, low),
            pltpu.VMEM(half, low),
            dma((8,)),
            pltpu.VMEM(half, jnp.float32),
            pltpu.VMEM(half, low),
            pltpu.VMEM(half, low),
            pltpu.VMEM(attn_w.shape, low),
            pltpu.VMEM(mlp_w.shape, low),
        ],
        compiler_params=pltpu.CompilerParams(
            collective_id=3, has_side_effects=True, vmem_limit_bytes=60 * 1024 * 1024
        ),
        name="finish",
    )(
        attn_round,
        mlp_whole,
        vec,
        gain.reshape(1, -1),
        normed_part,
        tokens,
        grad_mid,
        out_part,
        middle,
        bias.reshape(1, -1),
        attn_w,
        mlp_w,
    )


def pair_swap(value):
    dp, line = lax.axis_size("dp"), lax.axis_size("tensor")
    pairs = [(i * line + k, (i ^ 1) * line + k) for i in range(dp) for k in range(line)]
    return lax.ppermute(value, ("dp", "tensor"), pairs)


def on_chip_pair(tokens, cotangent, segments, attn_w, mlp_w, vectors, attn_mom, mlp_mom, vector_mom):
    line = lax.axis_size("tensor")
    place = Place()
    core, t = place.core, place.tensor
    width = tokens.shape[1]
    narrow, wide = attn_w.shape[2] // 2, mlp_w.shape[2] // 4
    total_tokens = tokens.shape[0] * line * lax.axis_size("dp")

    def my_columns(row):
        return lax.dynamic_index_in_dim(row.reshape(line, 2, narrow), core, 1, False).reshape(-1)

    def place_columns(piece):
        spread = jnp.zeros((line, 2, narrow), jnp.float32)
        return lax.dynamic_update_slice(spread, piece.reshape(line, 1, narrow), (0, core, 0)).reshape(-1)

    hidden_bias = lax.dynamic_index_in_dim(vectors[8:].reshape(line, 2, 2, wide), core, 1, False)
    hidden_bias = hidden_bias.transpose(1, 0, 2).reshape(2, line * wide)

    seg_pairs = segments.reshape(-1, SEQ)
    seg_own = lax.dynamic_index_in_dim(seg_pairs, t // 2, 0, False)
    seg_ids = jnp.where(core == lax.rem(t, 2), seg_own, pair_swap(seg_own))

    biases = jnp.stack([my_columns(vectors[2]), jnp.zeros((narrow * line,), jnp.float32), my_columns(vectors[3])])
    per = narrow // HD
    local_ids = jnp.arange(per * line)
    head_ids = (local_ids // per) * (2 * per) + core * per + local_ids % per
    slopes = jnp.exp2(-(8.0 / HEADS) * (head_ids.astype(jnp.float32) + 1.0))
    low = jnp.bfloat16
    (
        wqkv, wout, w_up, w_down, x_low, grad_low, qkv, mixed, log_sums, normed, middle, hidden_low, hidden_act, bend
    ) = forward(
        attn_w.astype(low),
        mlp_w.astype(low),
        tokens,
        cotangent,
        slopes,
        seg_ids,
        biases,
        hidden_bias,
        vectors,
        line,
    )
    down_sum, grad_up, grad_out, grad_mixed, grad_mid_mine, middle_sums, hidden_sums = middle_back(
        grad_low, hidden_act, bend, w_down, w_up, hidden_low, middle, mixed, wout, vectors[5], line
    )
    attn_sum, normed_part, bias_sums, mlp_mom_new, mlp_whole, out_part = attend_back(
        grad_up,
        grad_out,
        slopes,
        seg_ids,
        qkv,
        grad_mixed,
        mixed,
        log_sums,
        mlp_mom,
        down_sum,
        wqkv,
        normed,
        hidden_act,
        w_down,
        line,
    )
    hidden_grad = lax.dynamic_update_slice(
        jnp.zeros((line, 2, 2, wide), jnp.float32),
        hidden_sums.reshape(2, line, wide).transpose(1, 0, 2)[:, None],
        (0, core, 0, 0),
    )
    vector_rows = jnp.stack(
        [
            jnp.zeros((width,), jnp.float32),
            jnp.zeros((width,), jnp.float32),
            place_columns(bias_sums[0]),
            place_columns(bias_sums[2]),
            middle_sums[2],
            middle_sums[0],
            middle_sums[1],
            middle_sums[3],
        ]
    )
    vector_local = jnp.concatenate([vector_rows, hidden_grad.reshape(-1, width)], axis=0)
    padding = jnp.zeros((4, width), jnp.float32)
    attn_mom_new = 0.5 * attn_mom + attn_sum.astype(jnp.float32)
    attn_new, mlp_new, vector_sum, grad_tokens, output = finish(
        attn_mom_new.astype(low),
        mlp_whole,
        jnp.concatenate([vector_local, padding], axis=0),
        vectors[0],
        normed_part,
        x_low,
        grad_mid_mine,
        out_part,
        middle,
        vectors[7],
        attn_w,
        mlp_w,
        line,
    )
    vector_grads = vector_sum[: vector_local.shape[0]]
    vector_mom_new = 0.5 * vector_mom + vector_grads
    vector_new = vectors - 0.1 / math.sqrt(total_tokens) * vector_mom_new
    return (
        output,
        grad_tokens,
        attn_mom_new,
        attn_new,
        mlp_mom_new,
        mlp_new,
        vector_mom_new,
        vector_new,
    )


def solution(mesh):
    in_specs = (
        P(("dp", "tensor"), None),
        P(("dp", "tensor"), None),
        P("dp"),
        P(None, "dp", "tensor"),
        P(None, "dp", "tensor"),
        P(),
        P(None, "dp", "tensor"),
        P(None, "dp", "tensor"),
        P(),
    )
    out_specs = (
        P(("dp", "tensor"), None),
        P(("dp", "tensor"), None),
        P(None, "dp", "tensor"),
        P(None, "dp", "tensor"),
        P(None, "dp", "tensor"),
        P(None, "dp", "tensor"),
        P(),
        P(),
    )
    chips_of_two = (mesh.shape["dp"], mesh.shape["tensor"]) == (8, 4)
    return jax.shard_map(
        on_chip_pair if chips_of_two else on_device, mesh=mesh, in_specs=in_specs, out_specs=out_specs, check_vma=False
    )
```

```python
import functools
import math

import jax
import jax.numpy as jnp
from jax import lax
from jax.experimental import pallas as pl
from jax.experimental.pallas import tpu as pltpu
from jax.sharding import PartitionSpec as P

D = 1024
HEADS = 16
HD = 64
FF = 4096
SEQ = 1024
NS_STEPS = 5
MESH = pl.DeviceIdType.MESH


coeff_a = 3.4445
coeff_b = -4.775
coeff_c = 2.0315


def norm_rows(row_data, gain, shift):
    center = jnp.mean(row_data, axis=-1, keepdims=True)
    centred = row_data - center
    spread = jnp.mean(centred * centred, axis=-1, keepdims=True)
    return centred * lax.rsqrt(spread + 1e-05) * gain + shift


def gelu_tanh(values):
    return jax.nn.gelu(values, approximate=True)


def contract_last(left, right):
    return lax.dot_general(
        left, right, (((1,), (1,)), ((), ())), preferred_element_type=jnp.float32
    )


def contract_first(left, right):
    return lax.dot_general(
        left, right, (((0,), (0,)), ((), ())), preferred_element_type=jnp.float32
    )


def head_slopes(first_head, head_count):
    head_ids = (first_head + jnp.arange(head_count)).astype(jnp.float32)
    return jnp.exp2(-(8.0 / HEADS) * (head_ids + 1.0))


def masked_scores(row_query, key_rows, row_segs, seg_ids, row_start, slopes):
    scores = jnp.einsum("qhd,khd->hqk", row_query, key_rows, preferred_element_type=jnp.float32) * (
        1.0 / math.sqrt(HD)
    )
    query_pos = row_start + jnp.arange(row_query.shape[0])
    key_pos = jnp.arange(key_rows.shape[0])
    distance = (query_pos[:, None] - key_pos[None, :]).astype(jnp.float32)
    scores = scores - slopes[:, None, None] * distance[None]
    same_doc = (
        (row_segs[:, None] == seg_ids[None, :])
        & (row_segs[:, None] > 0)
        & (key_pos[None, :] <= query_pos[:, None])
    )
    allowed = same_doc | (key_pos[None, :] == query_pos[:, None])
    return jnp.where(allowed[None], scores, -1e30)


def attend_forward(query, key_rows, value_rows, seg_ids, slopes, row_block):
    length = key_rows.shape[0]

    def one_block(row_start):
        row_query = lax.dynamic_slice_in_dim(query, row_start, row_block, 0)
        row_segs = lax.dynamic_slice_in_dim(seg_ids, row_start, row_block, 0)
        scores = masked_scores(row_query, key_rows, row_segs, seg_ids, row_start, slopes)
        row_max = jnp.max(scores, axis=-1, keepdims=True)
        exp_scores = jnp.exp(scores - row_max)
        row_total = jnp.sum(exp_scores, axis=-1, keepdims=True)
        attn_probs = (exp_scores / row_total).astype(jnp.bfloat16)
        mixed = jnp.einsum(
            "hqk,khd->qhd", attn_probs, value_rows, preferred_element_type=jnp.float32
        )
        return (mixed.astype(jnp.bfloat16), (row_max + jnp.log(row_total))[..., 0])

    block_starts = jnp.arange(length // row_block) * row_block
    mixed, log_sums = lax.map(one_block, block_starts)
    return (mixed.reshape(length, -1), log_sums)


def attend_backward(query, key_rows, value_rows, seg_ids, log_sums, grad_mixed, slopes, row_block):
    length, head_count, head_dim = key_rows.shape
    factor = 1.0 / math.sqrt(HD)

    def one_block(carry, pieces):
        row_start, row_lse = pieces
        row_query = lax.dynamic_slice_in_dim(query, row_start, row_block, 0)
        row_grad = lax.dynamic_slice_in_dim(grad_mixed, row_start, row_block, 0)
        row_segs = lax.dynamic_slice_in_dim(seg_ids, row_start, row_block, 0)
        scores = masked_scores(row_query, key_rows, row_segs, seg_ids, row_start, slopes)
        attn_probs = jnp.exp(scores - row_lse[:, :, None])
        grad_probs = jnp.einsum(
            "qhd,khd->hqk", row_grad, value_rows, preferred_element_type=jnp.float32
        )
        inner = jnp.sum(grad_probs * attn_probs, axis=-1, keepdims=True)
        grad_scores = (attn_probs * (grad_probs - inner)).astype(jnp.bfloat16)
        grad_query = (
            jnp.einsum("hqk,khd->qhd", grad_scores, key_rows, preferred_element_type=jnp.float32)
            * factor
        )
        grad_keys = (
            carry[0]
            + jnp.einsum("hqk,qhd->khd", grad_scores, row_query, preferred_element_type=jnp.float32)
            * factor
        )
        grad_values = carry[1] + jnp.einsum(
            "hqk,qhd->khd",
            attn_probs.astype(jnp.bfloat16),
            row_grad,
            preferred_element_type=jnp.float32,
        )
        return ((grad_keys, grad_values), grad_query)

    empty = jnp.zeros((length, head_count, head_dim), jnp.float32)
    block_starts = jnp.arange(length // row_block) * row_block
    (grad_keys, grad_values), grad_query = lax.scan(
        one_block, (empty, empty), (block_starts, log_sums)
    )
    return (
        grad_query.reshape(length, -1),
        grad_keys.reshape(length, -1),
        grad_values.reshape(length, -1),
    )


def newton_rows(row_iterate):
    for repeat in range(NS_STEPS + 1):
        whole_iterate = lax.all_gather(row_iterate, "tensor", axis=0, tiled=True)
        if repeat == NS_STEPS:
            break
        square_rows = contract_last(row_iterate, whole_iterate).astype(jnp.bfloat16)
        whole_square = lax.all_gather(square_rows, "tensor", axis=0, tiled=True)
        poly_rows = (
            coeff_b * square_rows.astype(jnp.float32)
            + coeff_c * jnp.dot(square_rows, whole_square, preferred_element_type=jnp.float32)
        ).astype(jnp.bfloat16)
        row_iterate = (
            coeff_a * row_iterate.astype(jnp.float32)
            + jnp.dot(poly_rows, whole_iterate, preferred_element_type=jnp.float32)
        ).astype(jnp.bfloat16)
    return whole_iterate


def on_device(tokens, cotangent, segments, attn_w, mlp_w, vectors, attn_mom, mlp_mom, vector_mom):
    tensor_size = lax.axis_size("tensor")
    dp_size = lax.axis_size("dp")
    tensor_index = lax.axis_index("tensor")
    dp_index = lax.axis_index("dp")
    row_count = tokens.shape[0]
    model_width = tokens.shape[1]
    local_width = attn_w.shape[2]
    local_hidden = mlp_w.shape[2]
    head_count = local_width // HD
    row_block = min(512, SEQ)
    total_tokens = row_count * tensor_size * dp_size
    gathered_attn, gathered_mlp = (
        lax.all_gather(attn_w.astype(jnp.bfloat16), "dp", axis=1, tiled=True),
        lax.all_gather(mlp_w.astype(jnp.bfloat16), "dp", axis=1, tiled=True),
    )
    hidden_bias = vectors[8:].reshape(-1)
    query_bias = lax.dynamic_slice_in_dim(vectors[2], tensor_index * local_width, local_width)
    value_bias = lax.dynamic_slice_in_dim(vectors[3], tensor_index * local_width, local_width)
    x_rows = tokens.astype(jnp.float32)
    normed, pull_first = jax.vjp(norm_rows, x_rows, vectors[0], vectors[1])
    all_normed = lax.all_gather(normed.astype(jnp.bfloat16), "tensor", axis=0, tiled=True)
    seq_count = all_normed.shape[0] // SEQ
    projected = jnp.einsum(
        "td,mdc->mtc", all_normed, gathered_attn[:3], preferred_element_type=jnp.float32
    )
    query = (projected[0] + query_bias).astype(jnp.bfloat16)
    key_rows = projected[1].astype(jnp.bfloat16)
    value_rows = (projected[2] + value_bias).astype(jnp.bfloat16)
    slopes = head_slopes(tensor_index * head_count, head_count)
    seq_shape = (seq_count, SEQ, head_count, HD)
    seq_segs = segments.reshape(seq_count, SEQ)

    def forward_seq(pieces):
        return attend_forward(pieces[0], pieces[1], pieces[2], pieces[3], slopes, row_block)

    mixed, log_sums = lax.map(
        forward_seq,
        (
            query.reshape(seq_shape),
            key_rows.reshape(seq_shape),
            value_rows.reshape(seq_shape),
            seq_segs,
        ),
    )
    mixed = mixed.reshape(-1, local_width)
    w_out = gathered_attn[3]
    middle = (
        x_rows
        + lax.psum_scatter(
            contract_last(mixed, w_out).astype(jnp.bfloat16),
            "tensor",
            scatter_dimension=0,
            tiled=True,
        ).astype(jnp.float32)
        + vectors[4]
    )
    hidden_normed, pull_second = jax.vjp(norm_rows, middle, vectors[5], vectors[6])
    hidden_low = hidden_normed.astype(jnp.bfloat16)
    grad_rows = cotangent.astype(jnp.float32)
    all_hidden = lax.all_gather(hidden_low, "tensor", axis=0, tiled=True)
    w_up = gathered_mlp[0]
    w_down = gathered_mlp[1]
    bias_local = lax.dynamic_slice_in_dim(hidden_bias, tensor_index * local_hidden, local_hidden)
    hidden_pre = jnp.dot(all_hidden, w_up, preferred_element_type=jnp.float32) + bias_local
    act_float, gelu_pull = jax.vjp(gelu_tanh, hidden_pre)
    hidden_act = act_float.astype(jnp.bfloat16)
    output = (
        middle
        + lax.psum_scatter(
            contract_last(hidden_act, w_down).astype(jnp.bfloat16),
            "tensor",
            scatter_dimension=0,
            tiled=True,
        ).astype(jnp.float32)
        + vectors[7]
    )
    all_grad = lax.all_gather(grad_rows.astype(jnp.bfloat16), "tensor", axis=0, tiled=True)
    grad_down = contract_first(all_grad, hidden_act)
    grad_act = jnp.dot(all_grad, w_down, preferred_element_type=jnp.float32)
    grad_pre = gelu_pull(grad_act)[0].astype(jnp.bfloat16)
    grad_up = contract_first(all_hidden, grad_pre)
    bias_part = jnp.sum(grad_pre, axis=0, dtype=jnp.float32)
    hidden_grad = lax.dynamic_update_slice_in_dim(
        jnp.zeros(hidden_bias.shape, jnp.float32), bias_part, tensor_index * local_hidden, 0
    )
    grad_hidden_in = lax.psum_scatter(
        contract_last(grad_pre, w_up).astype(jnp.bfloat16),
        "tensor",
        scatter_dimension=0,
        tiled=True,
    ).astype(jnp.float32)
    mlp_grads = jnp.stack([grad_up, grad_down])
    second_grads = pull_second(grad_hidden_in)
    grad_middle = grad_rows + second_grads[0]
    all_grad_mid = lax.all_gather(grad_middle.astype(jnp.bfloat16), "tensor", axis=0, tiled=True)
    grad_out_w = contract_first(all_grad_mid, mixed)
    grad_mixed = jnp.dot(all_grad_mid, w_out, preferred_element_type=jnp.float32).astype(
        jnp.bfloat16
    )

    def backward_seq(pieces):
        return attend_backward(
            pieces[0], pieces[1], pieces[2], pieces[3], pieces[4], pieces[5], slopes, row_block
        )

    grad_query, grad_keys, grad_values = lax.map(
        backward_seq,
        (
            query.reshape(seq_shape),
            key_rows.reshape(seq_shape),
            value_rows.reshape(seq_shape),
            seq_segs,
            log_sums,
            grad_mixed.reshape(seq_shape),
        ),
    )
    grad_qkv = (
        jnp.stack([grad_query, grad_keys, grad_values])
        .reshape(3, -1, local_width)
        .astype(jnp.bfloat16)
    )
    grad_proj_w = jnp.einsum(
        "td,mtc->mdc", all_normed, grad_qkv, preferred_element_type=jnp.float32
    )
    bias_sums = jnp.sum(grad_qkv, axis=1, dtype=jnp.float32)
    grad_normed = lax.psum_scatter(
        jnp.einsum(
            "mtc,mdc->td", grad_qkv, gathered_attn[:3], preferred_element_type=jnp.float32
        ).astype(jnp.bfloat16),
        "tensor",
        scatter_dimension=0,
        tiled=True,
    ).astype(jnp.float32)
    first_grads = pull_first(grad_normed)
    grad_tokens = grad_middle + first_grads[0]

    def placed(piece, full_size, offset):
        return lax.dynamic_update_slice_in_dim(
            jnp.zeros((full_size,), jnp.float32), piece, offset, 0
        )

    width_offset = tensor_index * local_width
    vector_rows = jnp.stack(
        [
            first_grads[1],
            first_grads[2],
            placed(bias_sums[0], model_width, width_offset),
            placed(bias_sums[2], model_width, width_offset),
            jnp.sum(grad_middle, axis=0),
            second_grads[1],
            second_grads[2],
            jnp.sum(grad_rows, axis=0),
        ]
    )
    vector_local = jnp.concatenate([vector_rows, hidden_grad.reshape(4, model_width)], axis=0)
    attn_grads = jnp.concatenate([grad_proj_w, grad_out_w[None]], axis=0)
    attn_sum, mlp_sum = (
        lax.psum_scatter(
            attn_grads.astype(jnp.bfloat16), "dp", scatter_dimension=1, tiled=True
        ).astype(jnp.float32),
        lax.psum_scatter(
            mlp_grads.astype(jnp.bfloat16), "dp", scatter_dimension=1, tiled=True
        ).astype(jnp.float32),
    )
    attn_mom_new = 0.5 * attn_mom + attn_sum
    mlp_mom_new = 0.5 * mlp_mom + mlp_sum
    attn_round = attn_mom_new.astype(jnp.bfloat16)
    mlp_round = mlp_mom_new.astype(jnp.bfloat16)
    attn_float = attn_round.astype(jnp.float32)
    mlp_float = mlp_round.astype(jnp.float32)
    norm_parts = jnp.concatenate(
        [jnp.sum(attn_float * attn_float, axis=(1, 2)), jnp.sum(mlp_float * mlp_float, axis=(1, 2))]
    )
    vector_grads, norm_sums = lax.psum((vector_local, norm_parts), ("dp", "tensor"))
    frob_norms = jnp.sqrt(norm_sums)
    owners = [order * dp_size // 6 for order in range(6)]
    owned_norm = jnp.zeros((), jnp.float32)
    for order in range(6):
        owned_norm = owned_norm + jnp.where(dp_index == owners[order], frob_norms[order], 0.0)
    block_rows = attn_w.shape[1]
    slice_rows = model_width // tensor_size
    full_cols = local_hidden * tensor_size
    rows_attn, rows_mlp = (
        lax.all_gather(attn_round, "tensor", axis=2, tiled=True),
        lax.all_gather(mlp_round, "tensor", axis=2, tiled=True),
    )
    padded_attn = jnp.pad(rows_attn, ((0, 0), (0, 0), (0, full_cols - model_width)))
    all_rows = jnp.concatenate([padded_attn, rows_mlp], axis=0)
    outgoing = jnp.zeros((dp_size, block_rows, full_cols), jnp.bfloat16)
    for order in range(6):
        outgoing = outgoing.at[owners[order]].set(all_rows[order])
    incoming = lax.all_to_all(outgoing, "dp", split_axis=0, concat_axis=0, tiled=True)
    owned_whole = incoming.reshape(model_width, full_cols)
    mine = lax.dynamic_slice_in_dim(owned_whole, tensor_index * slice_rows, slice_rows, 0)
    attn_col = tensor_index * local_width
    row_iterate = (mine.astype(jnp.float32) / (owned_norm + 1e-06)).astype(jnp.bfloat16)
    result = newton_rows(row_iterate)
    returned = lax.all_to_all(
        result.reshape(dp_size, block_rows, full_cols),
        "dp",
        split_axis=0,
        concat_axis=0,
        tiled=True,
    )
    attn_blocks = []
    for order in range(4):
        piece = lax.dynamic_slice_in_dim(returned[owners[order]], attn_col, local_width, 1)
        attn_blocks.append(attn_w[order] - piece.astype(jnp.float32))
    mlp_blocks = []
    for order in range(2):
        piece = lax.dynamic_slice_in_dim(
            returned[owners[4 + order]], tensor_index * local_hidden, local_hidden, 1
        )
        mlp_blocks.append(mlp_w[order] - math.sqrt(FF / D) * piece.astype(jnp.float32))
    attn_new = jnp.stack(attn_blocks)
    mlp_new = jnp.stack(mlp_blocks)
    vector_mom_new = 0.5 * vector_mom + vector_grads
    vector_new = vectors - 0.1 / math.sqrt(total_tokens) * vector_mom_new
    return (
        output.astype(jnp.bfloat16),
        grad_tokens,
        attn_mom_new,
        attn_new,
        mlp_mom_new,
        mlp_new,
        vector_mom_new,
        vector_new,
    )


CORES = 2


class Place:
    def __init__(self):
        self.dp = lax.axis_index("dp")
        self.tensor = lax.axis_index("tensor")
        self.line = lax.axis_size("tensor")
        self.devices = lax.axis_size("dp") * self.line
        self.me = self.dp * self.line + self.tensor
        self.core = lax.rem(self.dp, 2)
        self.chip = self.dp // 2
        self.x = lax.rem(self.chip, 2)
        self.y = self.chip // 2
        self.twin = (self.dp + 1 - 2 * self.core, self.tensor)
        self.across_x = (self.dp + 2 - 4 * self.x, self.tensor)
        self.across_y = (self.dp + 4 - 8 * self.y, self.tensor)
        self.right = (self.dp, self.tensor + 1)
        self.left = (self.dp, self.tensor - 1)
        self.stays = self.core == lax.rem(self.tensor, 2)
        self.corner = (self.dp + 1 - 2 * self.core, self.tensor - 1 + 2 * self.core)


    def of(self, index):
        return (index // self.line, lax.rem(index, self.line))

    def index(self, x, y, core, z):
        return ((2 * y + x) * 2 + core) * self.line + z


def greet(place, line):
    barrier = pltpu.get_barrier_semaphore()

    def signal(device):
        pl.semaphore_signal(barrier, inc=1, device_id=device, device_id_type=MESH)

    signal(place.twin)
    signal(place.across_x)
    signal(place.across_y)

    for other in range(line):

        @pl.when(place.tensor != other)
        def _():
            signal((place.dp, other))

    @pl.when(jnp.logical_not(place.stays))
    def _():
        signal(place.corner)

    pl.semaphore_wait(barrier, jnp.where(place.stays, 3 + line - 1, 3 + line))


OWNERS = ((1, 0, 0), (1, 0, 3), (0, 1, 0), (0, 1, 3), (0, 0, 1), (1, 1, 2))


def greet_all(place):
    barrier = pltpu.get_barrier_semaphore()

    def meet(step, carry):
        pl.semaphore_signal(
            barrier, inc=1, device_id=place.of(lax.rem(place.me + step, place.devices)), device_id_type=MESH
        )
        return carry

    lax.fori_loop(1, place.devices, meet, 0)
    pl.semaphore_wait(barrier, place.devices - 1)


def is_one_of(value, options):
    found = value < 0
    for option in options:
        found = found | (value == option)
    return found


def sides(order, line):
    oz = OWNERS[order][2]
    above, below = list(range(oz + 1, line)), list(range(oz))
    return (above, below) if len(above) > len(below) else (below, above)


def rows_held(place, whole, index, rows, width):
    dp, tensor = place.of(index)
    return whole.at[pl.ds(pl.multiple_of(dp * rows, rows), rows), columns(tensor * width, width)]


def remote(place, source, target, send, recv, index):
    return pltpu.make_async_remote_copy(
        src_ref=source,
        dst_ref=target,
        send_sem=send,
        recv_sem=recv,
        device_id=place.of(index),
        device_id_type=MESH,
    )


class Collect:
    @staticmethod
    def scratch():
        dma = pltpu.SemaphoreType.DMA
        return [dma((2, 2)), dma((1,)), dma((2, 2)), dma((2, 2))]

    SCRATCH = 4

    def __init__(self, place, source, whole, scratch):
        self.place, self.source, self.whole = place, source, whole
        self.send_sem, self.sem, self.pass_send, self.pass_recv = scratch
        self.rows, self.width = source.shape[1], source.shape[2] // 2

    def owner(self, order, half):
        ox, oy, oz = OWNERS[order]
        return self.place.index(ox, oy, half, oz)

    def piece(self, order, half):
        return self.source.at[order - 4, :, half * self.width : (half + 1) * self.width]

    def held(self, index):
        return rows_held(self.place, self.whole, index, self.rows, self.width)

    def direct(self, order, half):
        send = self.send_sem.at[order - 4, half]
        return remote(
            self.place, self.piece(order, half), self.held(self.place.me), send, self.sem.at[0], self.owner(order, half)
        )

    def own(self, order, half):
        return pltpu.make_async_copy(self.piece(order, half), self.held(self.place.me), self.sem.at[0])

    def by_way(self, order):
        place = self.place
        ox, oy, oz = OWNERS[order]
        lone = is_one_of(place.tensor, sides(order, place.line)[1])
        return (place.y != oy) & (place.tensor != oz) & ((place.x != ox) | lone)

    def to_way(self, order, half):
        place = self.place
        ox, oy, _ = OWNERS[order]
        which = jnp.where(place.x == ox, 1, 0)
        return remote(
            place,
            self.piece(order, half),
            self.held(place.me),
            self.send_sem.at[order - 4, half],
            self.pass_recv.at[which, place.core],
            place.index(ox, oy, half, place.tensor),
        )

    def passed(self, order, which, cores):
        ox, oy, _ = OWNERS[order]
        return self.place.index(1 - ox if which == 0 else ox, 1 - oy, cores, self.place.tensor)

    def pass_in(self, order, which, cores):
        index = self.passed(order, which, cores)
        region = self.held(index)
        sems = self.pass_send.at[which, cores], self.pass_recv.at[which, cores]
        return remote(self.place, region, region, *sems, index)

    def pass_on(self, order, which, cores):
        ox, oy, oz = OWNERS[order]
        region = self.held(self.passed(order, which, cores))
        owner = self.place.index(ox, oy, self.place.core, oz)
        return remote(self.place, region, region, self.pass_send.at[which, cores], self.sem.at[0], owner)

    def when_passing(self, action):
        place = self.place
        for order in (5, 4):
            ox, oy, _ = OWNERS[order]
            far, lone = sides(order, place.line)
            for which, planes in ((0, far + lone), (1, lone)):

                @pl.when((place.x == ox) & (place.y == oy) & is_one_of(place.tensor, planes))
                def _():
                    for cores in range(2):
                        action(order, which, cores)

    def each(self, action_way, action_direct, action_own):
        for order in (5, 4):
            for half in range(2):
                mine = self.place.me == self.owner(order, half)

                @pl.when(self.by_way(order))
                def _():
                    action_way(order, half)

                @pl.when(jnp.logical_not(mine) & jnp.logical_not(self.by_way(order)))
                def _():
                    action_direct(order, half)

                @pl.when(mine)
                def _():
                    action_own(order, half)

    def start(self):
        self.each(
            lambda *at: self.to_way(*at).start(), lambda *at: self.direct(*at).start(), lambda *at: self.own(*at).start()
        )

    def forward(self):
        def action(*at):
            self.pass_in(*at).wait_recv()
            self.pass_on(*at).start()

        self.when_passing(action)

    def finish(self):
        self.each(
            lambda *at: self.to_way(*at).wait_send(),
            lambda *at: self.direct(*at).wait_send(),
            lambda *at: None,
        )
        self.when_passing(lambda *at: self.pass_on(*at).wait_send())
        for order in (5, 4):
            for half in range(2):

                @pl.when(self.place.me == self.owner(order, half))
                def _():
                    pltpu.make_async_copy(self.whole, self.whole, self.sem.at[0]).wait()


def columns(start, size):
    return pl.ds(pl.multiple_of(start, 128), size)


class RowSwap:
    PARTS = 4

    @staticmethod
    def scratch():
        return [pltpu.SemaphoreType.DMA((1,)), pltpu.SemaphoreType.DMA((2 + 2 * RowSwap.PARTS,))]

    def __init__(self, place, rows_ref, whole_ref, scratch):
        self.place, self.rows_ref, self.whole_ref = place, rows_ref, whole_ref
        self.own_sem, self.sem = scratch
        self.size = rows_ref.shape[0]

    def at(self, core):
        return self.whole_ref.at[pl.ds(pl.multiple_of(core * self.size, self.size), self.size), :]

    def copy(self, slot, source, target, device):
        return pltpu.make_async_remote_copy(
            src_ref=source,
            dst_ref=target,
            send_sem=self.sem.at[slot],
            recv_sem=self.sem.at[slot + 1],
            device_id=device,
            device_id_type=MESH,
        )

    def own(self):
        return pltpu.make_async_copy(self.rows_ref, self.at(self.place.core), self.own_sem.at[0])

    def away(self, part):
        count = self.size // self.PARTS
        start = pl.multiple_of((1 - self.place.core) * self.size + part * count, count)
        source = self.rows_ref.at[part * count : (part + 1) * count, :]
        return self.copy(2 + 2 * part, source, self.whole_ref.at[pl.ds(start, count), :], self.place.corner)

    def hand_own(self):
        return self.copy(0, self.rows_ref, self.at(self.place.core), self.place.twin)

    def hand_got(self):
        return self.copy(0, self.at(self.place.core), self.at(self.place.core), self.place.twin)

    def start(self, parts):
        if 0 in parts:

            @pl.when(self.place.stays)
            def _():
                self.own().start()
                self.hand_own().start()

        @pl.when(jnp.logical_not(self.place.stays))
        def _():
            for part in parts:
                self.away(part).start()

    def step(self):
        @pl.when(jnp.logical_not(self.place.stays))
        def _():
            for part in range(self.PARTS):
                self.away(part).wait()
            self.hand_got().start()

    def end(self):
        @pl.when(self.place.stays)
        def _():
            self.own().wait()

        self.hand_got().wait()


class CornerMove:
    PARTS = 4

    @staticmethod
    def scratch():
        return [pltpu.SemaphoreType.DMA((1,)), pltpu.SemaphoreType.DMA((2, CornerMove.PARTS))]

    def __init__(self, place, rows_ref, target_ref, scratch):
        self.place, self.rows_ref, self.target_ref = place, rows_ref, target_ref
        self.own_sem, self.sem = scratch

    def own(self):
        return pltpu.make_async_copy(self.rows_ref, self.target_ref, self.own_sem.at[0])

    def away(self, part):
        count = self.rows_ref.shape[0] // self.PARTS
        at = slice(part * count, (part + 1) * count)
        return pltpu.make_async_remote_copy(
            src_ref=self.rows_ref.at[at, :],
            dst_ref=self.target_ref.at[at, :],
            send_sem=self.sem.at[0, part],
            recv_sem=self.sem.at[1, part],
            device_id=self.place.corner,
            device_id_type=MESH,
        )

    def start(self):
        @pl.when(self.place.stays)
        def _():
            self.own().start()

        @pl.when(jnp.logical_not(self.place.stays))
        def _():
            for part in range(self.PARTS):
                self.away(part).start()

    def wait(self):
        @pl.when(self.place.stays)
        def _():
            self.own().wait()

        @pl.when(jnp.logical_not(self.place.stays))
        def _():
            for part in range(self.PARTS):
                self.away(part).wait()


class WeightGather:
    def __init__(self, place, line, groups, scratch):
        self.place, self.line, self.groups = place, line, groups
        self.own_sem, self.send_sem, self.recv_sem = scratch
        self.last = len(groups) - 1
        self.to_right, self.to_left = 1, line
        self.half_x, self.half_y, self.rest_y, self.rest_x = (2 * line - 1 + k for k in range(4))

    @staticmethod
    def scratch(count, line):
        dma = pltpu.SemaphoreType.DMA
        return [dma((count,)), dma((count, 2 * line + 3)), dma((count, 2 * line + 3))]

    def copy(self, group, slot, source, target, device):
        return pltpu.make_async_remote_copy(
            src_ref=source,
            dst_ref=target,
            send_sem=self.send_sem.at[group, slot],
            recv_sem=self.recv_sem.at[group, slot],
            device_id=device,
            device_id_type=MESH,
        )

    def same(self, group, slot, region, device):
        return self.copy(group, slot, region, region, device)

    def chunk(self, group, index):
        ref, width, _ = self.groups[group]
        cols = columns(index * width, width)
        if group == self.last:
            return ref.at[:, :, :, :, :, cols]
        return ref.at[:, self.place.y, self.place.x, :, :, cols]

    def corner(self, group, ys, xs, half):
        ref, width, _ = self.groups[group]
        if group == self.last:
            return ref.at[:, ys, xs, half, :, columns(self.place.tensor * width, width)]
        return ref.at[:, ys, xs, half]

    def entry(self, group, half):
        ref, width, _ = self.groups[group]
        return ref.at[:, self.place.y, self.place.x, half, :, columns(self.place.tensor * width, width)]

    def own(self, group):
        core = self.place.core
        return pltpu.make_async_copy(self.groups[group][2](core), self.entry(group, core), self.own_sem.at[group])

    def first(self, group):
        core = self.place.core
        return self.copy(group, 0, self.groups[group][2](1 - core), self.entry(group, core), self.place.twin)

    def begin(self, group):
        self.own(group).start()
        self.first(group).start()

    def enter(self, group):
        self.own(group).wait()
        self.same(group, 0, self.entry(group, 1 - self.place.core), self.place.twin).wait_recv()

    def hop(self, group, step, left):
        t = self.place.tensor
        index = t + step - 1 if left else t - step + 1
        slot = (self.to_left if left else self.to_right) + step - 1
        return self.same(group, slot, self.chunk(group, index), self.place.left if left else self.place.right)

    def arrival(self, group, step, left):
        t = self.place.tensor
        index = t + step if left else t - step
        slot = (self.to_left if left else self.to_right) + step - 1
        return self.same(group, slot, self.chunk(group, index), self.place.right if left else self.place.left)

    def sends(self, step, left):
        t, line = self.place.tensor, self.line
        return (t > 0) & (t + step <= line) if left else (t < line - 1) & (t >= step - 1)

    def line_start(self, group):
        for left in (False, True):

            @pl.when(self.sends(1, left))
            def _():
                self.hop(group, 1, left).start()

    def line_step(self, group, step):
        t, line = self.place.tensor, self.line
        for left in (False, True):

            @pl.when(t + step <= line - 1 if left else t >= step)
            def _():
                self.arrival(group, step, left).wait_recv()

            if step < line - 1:

                @pl.when(self.sends(step + 1, left))
                def _():
                    self.hop(group, step + 1, left).start()

    def line_most(self, group):
        for step in range(1, self.line - 1):
            self.line_step(group, step)

    def line_end(self, group):
        self.line_step(group, self.line - 1)

    def plane_start(self, group):
        place = self.place
        self.same(group, self.half_x, self.corner(group, place.y, place.x, 0), place.across_x).start()
        self.same(group, self.half_y, self.corner(group, place.y, place.x, 1), place.across_y).start()

    def plane_step(self, group):
        place, both = self.place, pl.ds(0, 2)
        self.same(group, self.half_x, self.corner(group, place.y, 1 - place.x, 0), place.across_x).wait_recv()
        self.same(group, self.rest_y, self.corner(group, place.y, both, 0), place.across_y).start()
        self.same(group, self.half_y, self.corner(group, 1 - place.y, place.x, 1), place.across_y).wait_recv()
        self.same(group, self.rest_x, self.corner(group, both, place.x, 1), place.across_x).start()

    def plane_end(self, group):
        place, both = self.place, pl.ds(0, 2)
        self.same(group, self.rest_y, self.corner(group, 1 - place.y, both, 0), place.across_y).wait_recv()
        self.same(group, self.rest_x, self.corner(group, both, 1 - place.x, 1), place.across_x).wait_recv()

    def wait_sends(self, group):
        place, both = self.place, pl.ds(0, 2)
        self.first(group).wait_send()
        for step in range(1, self.line):
            for left in (False, True):

                @pl.when(self.sends(step, left))
                def _():
                    self.hop(group, step, left).wait_send()

        self.same(group, self.half_x, self.corner(group, place.y, place.x, 0), place.across_x).wait_send()
        self.same(group, self.half_y, self.corner(group, place.y, place.x, 1), place.across_y).wait_send()
        self.same(group, self.rest_y, self.corner(group, place.y, both, 0), place.across_y).wait_send()
        self.same(group, self.rest_x, self.corner(group, both, place.x, 1), place.across_x).wait_send()


def add_blocks(target, sources):
    lead, rows = target.shape[:-2], target.shape[-2]
    per = rows // 32

    def body(step, carry):
        block, at = step // per, []
        for size in lead[::-1]:
            at.insert(0, lax.rem(block, size))
            block = block // size
        at = tuple(at) + (pl.ds(pl.multiple_of(lax.rem(step, per) * 32, 32), 32),)
        total = sources[0][at].astype(jnp.float32)
        for source in sources[1:]:
            total = total + source[at].astype(jnp.float32)
        target[at] = total.astype(target.dtype)
        return carry

    lax.fori_loop(0, math.prod(lead) * per, body, 0)


class PlaneSum:
    @staticmethod
    def scratch(count, rows, width):
        pair = pltpu.VMEM((count, 2, rows, width), jnp.bfloat16)
        single = pltpu.VMEM((count, rows, width), jnp.bfloat16)
        dma = pltpu.SemaphoreType.DMA
        return [pair] * 4 + [single] * 2 + [dma((2,)), dma((4,)), dma((4,))]

    SCRATCH = 9

    def __init__(self, place, source, result, scratch):
        self.place, self.source, self.result = place, source, result
        self.own, self.got, self.last = scratch[0:2], scratch[2:4], scratch[4:6]
        self.own_sem, self.send_sem, self.recv_sem = scratch[6:9]

    def copy(self, slot, source, target, device):
        return pltpu.make_async_remote_copy(
            src_ref=source,
            dst_ref=target,
            send_sem=self.send_sem.at[slot],
            recv_sem=self.recv_sem.at[slot],
            device_id=device,
            device_id_type=MESH,
        )

    def cut(self, index, mine):
        both, place = pl.ds(0, 2), self.place
        if index == 0:
            return self.source.at[:, place.y if mine else 1 - place.y, both, 0]
        return self.source.at[:, both, place.x if mine else 1 - place.x, 1]

    def load(self, index):
        return pltpu.make_async_copy(self.cut(index, True), self.own[index], self.own_sem.at[index])

    def first(self, index):
        device = self.place.across_x if index else self.place.across_y
        return self.copy(index, self.cut(index, False), self.got[index], device)

    def second(self, index):
        mine = self.place.y if index else self.place.x
        device = self.place.across_y if index else self.place.across_x
        return self.copy(2 + index, self.own[index].at[:, 1 - mine], self.last[index], device)

    def start(self):
        for index in range(2):
            self.first(index).start()
            self.load(index).start()

    def one(self):
        for index in range(2):
            mine = self.place.y if index else self.place.x
            self.load(index).wait()
            self.first(index).wait_recv()
            own, got = self.own[index], self.got[index]
            add_blocks(own.at[:, 1 - mine], (own.at[:, 1 - mine], got.at[:, 1 - mine]))
            self.second(index).start()
            add_blocks(own.at[:, mine], (own.at[:, mine], got.at[:, mine]))

    def two(self):
        for index in range(2):
            mine = self.place.y if index else self.place.x
            self.second(index).wait_recv()
            add_blocks(self.result.at[:, index], (self.own[index].at[:, mine], self.last[index]))

    def sent(self):
        for index in range(2):
            self.first(index).wait_send()
            self.second(index).wait_send()


class LineSum:
    @staticmethod
    def scratch(shape, line):
        dma = pltpu.SemaphoreType.DMA
        return [pltpu.VMEM(shape, jnp.bfloat16)] * 2 + [dma((2, line)), dma((2, line))]

    SCRATCH = 4

    def __init__(self, place, line, value, result, scratch):
        self.place, self.line, self.value, self.result = place, line, value, result
        self.got = scratch[0:2]
        self.send_sem, self.recv_sem = scratch[2:4]
        self.width = value.shape[-1] // line

    def part(self, ref, index):
        return ref.at[(slice(None),) * (len(ref.shape) - 1) + (slice(index * self.width, (index + 1) * self.width),)]

    def hop(self, index, left):
        return pltpu.make_async_remote_copy(
            src_ref=self.part(self.value, index),
            dst_ref=self.part(self.got[left], index),
            send_sem=self.send_sem.at[left, index],
            recv_sem=self.recv_sem.at[left, index],
            device_id=self.place.left if left else self.place.right,
            device_id_type=MESH,
        )

    def step(self, step):
        for left in range(2):
            for index in range(self.line):
                away = index if left else self.line - 1 - index
                order = step - away
                plane = self.line - 1 - order if left else order
                if order < 0 or (plane <= index if left else plane >= index):
                    continue

                @pl.when(self.place.tensor == plane)
                def _():
                    if order > 0:
                        self.hop(index, left).wait_recv()
                        value = self.part(self.value, index)
                        add_blocks(value, (value, self.part(self.got[left], index)))
                    if away > 0:
                        self.hop(index - 1 if left else index + 1, left).wait_send()
                    self.hop(index, left).start()

    def end(self):
        for index in range(self.line):

            @pl.when(self.place.tensor == index)
            def _():
                sources = [self.part(self.value, index)]
                for left in range(2):
                    if index < self.line - 1 if left else index > 0:
                        self.hop(index, left).wait_recv()
                        sources.append(self.part(self.got[left], index))
                add_blocks(self.result, sources)

    def sent(self):
        for index in range(self.line):

            @pl.when(self.place.tensor == index)
            def _():
                if index > 0:
                    self.hop(index - 1, 1).wait_send()
                if index < self.line - 1:
                    self.hop(index + 1, 0).wait_send()


class HomeCopy:
    def __init__(self, place, value, target, scratch):
        self.place, self.value, self.target = place, value, target
        self.own_sem, self.sem = scratch

    SCRATCH = 2

    @staticmethod
    def scratch():
        return [pltpu.SemaphoreType.DMA((1,)), pltpu.SemaphoreType.DMA((2,))]

    def keep(self):
        return pltpu.make_async_copy(self.value.at[:, self.place.core], self.target, self.own_sem.at[0])

    def give(self):
        return pltpu.make_async_remote_copy(
            src_ref=self.value.at[:, 1 - self.place.core],
            dst_ref=self.target,
            send_sem=self.sem.at[0],
            recv_sem=self.sem.at[1],
            device_id=self.place.twin,
            device_id_type=MESH,
        )

    def start(self):
        self.keep().start()
        self.give().start()

    def wait(self):
        self.keep().wait()
        self.give().wait()


class GroupSum:
    @staticmethod
    def scratch(count, rows, width, line, line_first=False):
        low = jnp.bfloat16
        part = width // line
        done = pltpu.VMEM((count, 2, rows, part), low)
        if line_first:
            whole = (count, 2, 2, 2, rows, width)
            held = [pltpu.VMEM(whole, low), pltpu.VMEM(whole[:-1] + (part,), low), pltpu.SemaphoreType.DMA((1,))]
            plane, along = PlaneSum.scratch(count, rows, part), LineSum.scratch(whole, line)
        else:
            middle = (count, 2, rows, width)
            held = [pltpu.VMEM(middle, low)]
            plane, along = PlaneSum.scratch(count, rows, width), LineSum.scratch(middle, line)
        return held + [done] + plane + along + HomeCopy.scratch()

    def __init__(self, place, line, source, target, scratch, line_first=False):
        scratch = list(scratch)

        def take(count):
            taken = scratch[:count]
            del scratch[:count]
            return taken

        if line_first:
            whole, middle, load_sem = take(3)
            self.load = lambda: pltpu.make_async_copy(source, whole, load_sem.at[0])
        else:
            (middle,) = take(1)
        (done,) = take(1)
        plane, along = take(PlaneSum.SCRATCH), take(LineSum.SCRATCH)
        if line_first:
            self.line = LineSum(place, line, whole, middle, along)
            self.plane = PlaneSum(place, middle, done, plane)
        else:
            self.plane = PlaneSum(place, source, middle, plane)
            self.line = LineSum(place, line, middle, done, along)
        self.home = HomeCopy(place, done, target, take(HomeCopy.SCRATCH))

    def sent(self):
        self.plane.sent()
        self.line.sent()


class VectorSum:
    @staticmethod
    def scratch(shape, line):
        return [
            pltpu.VMEM((4,) + shape, jnp.float32),
            pltpu.VMEM((3,) + shape, jnp.float32),
            pltpu.VMEM((line,) + shape, jnp.float32),
            pltpu.SemaphoreType.DMA((4, max(line, 3))),
        ]

    def __init__(self, place, line, scratch):
        self.place, self.line = place, line
        self.sums, self.got, self.along, self.sem = scratch

    def copy(self, stage):
        place = self.place
        return pltpu.make_async_remote_copy(
            src_ref=self.sums.at[stage],
            dst_ref=self.got.at[stage],
            send_sem=self.sem.at[0, stage],
            recv_sem=self.sem.at[1, stage],
            device_id=(place.twin, place.across_x, place.across_y)[stage],
            device_id_type=MESH,
        )

    def hop(self, other, source):
        return pltpu.make_async_remote_copy(
            src_ref=self.sums.at[3],
            dst_ref=self.along.at[source],
            send_sem=self.sem.at[2, other],
            recv_sem=self.sem.at[3, source],
            device_id=(self.place.dp, other),
            device_id_type=MESH,
        )

    def start(self, value, first_rows):
        self.sums[0] = value
        for index, row in enumerate(first_rows):
            self.sums[0, index : index + 1, :] = row
        self.copy(0).start()

    def step(self, stage):
        self.copy(stage).wait()
        self.sums[stage + 1] = self.sums[stage] + self.got[stage]
        if stage < 2:
            self.copy(stage + 1).start()
            return
        self.along[self.place.tensor] = self.sums[3]
        for other in range(self.line):

            @pl.when(self.place.tensor != other)
            def _():
                self.hop(other, self.place.tensor).start()

    def end(self):
        t = self.place.tensor
        for other in range(self.line):

            @pl.when(t != other)
            def _():
                self.hop(other, t).wait_send()
                self.hop(t, other).wait_recv()

        total = self.along[0]
        for other in range(1, self.line):
            total = total + self.along[other]
        return total


LOG2E = 1.4426950408889634
FAR = 1e32
ROW_BLOCK = 256


def fill_distance(seg_rows, seg_cols, distance):
    def body(step, carry):
        start = pl.multiple_of(step * 64, 64)
        shape = (64, distance.shape[1])
        row = lax.broadcasted_iota(jnp.int32, shape, 0) + start
        col = lax.broadcasted_iota(jnp.int32, shape, 1)
        segs = seg_rows[pl.ds(start, 64), :]
        same = (segs == seg_cols[...]) & (segs > 0) & (col <= row)
        allowed = same | (col == row)
        distance[pl.ds(start, 64), :] = jnp.where(allowed, (row - col).astype(jnp.float32), FAR)
        return carry

    lax.fori_loop(0, distance.shape[0] // 64, body, 0)


def head_lanes(dtype):
    lane = lax.broadcasted_iota(jnp.int32, (1, 2 * HD), 1)
    first = (lane < HD).astype(jnp.float32)
    return (first.astype(dtype), (1.0 - first).astype(dtype))


def attend_group(group, slopes, qkv, mixed, lse, distance):
    length = qkv.shape[1]
    cols = columns(group * 2 * HD, 2 * HD)
    masks = head_lanes(jnp.bfloat16)
    first = head_lanes(jnp.float32)[0] > 0.5
    factor = LOG2E / math.sqrt(HD)
    keys_t = qkv[1, :, cols].T
    values = qkv[2, :, cols]
    for start in range(0, length, ROW_BLOCK):
        stop = start + ROW_BLOCK
        rows = slice(start, stop)
        query = qkv[0, rows, cols]
        parts, sums = [], []
        for head in range(2):
            slope = slopes[2 * group + head] * LOG2E
            scores = jnp.dot(query * masks[head], keys_t[:, :stop], preferred_element_type=jnp.float32)
            scores = scores * factor - slope * distance[rows, :stop]
            top = jnp.max(scores, axis=1, keepdims=True)
            probs = jnp.exp2(scores - top)
            total = jnp.sum(probs, axis=1, keepdims=True)
            out = jnp.dot(probs.astype(jnp.bfloat16), values[:stop], preferred_element_type=jnp.float32)
            parts.append(out / total)
            sums.append(top + jnp.log2(total))
        mixed[rows, cols] = jnp.where(first, parts[0], parts[1]).astype(jnp.bfloat16)
        lse[rows, cols] = jnp.where(first, sums[0], sums[1])


def normalize(rows):
    centred = rows - jnp.mean(rows, axis=1, keepdims=True)
    return centred * lax.rsqrt(jnp.mean(centred * centred, axis=1, keepdims=True) + 1e-05)


def forward_kernel(
    line, attn_ref, mlp_ref, tokens_ref, grads_ref, slopes, seg_rows, seg_cols, qkv_bias, hidden_bias, vectors,
    qkv_w, out_w, up_w, down_w, tokens_out, grads_out, qkv_out, mixed_out, lse_out, normed_out, middle_out,
    hidden_out, act_out, bend_out, *scratch
):
    (x_v, normed, qkv_wv, out_wv, up_wv, qkv, mixed, lse, distance, part, got, middle, hidden, act, bend) = scratch[:15]
    load_sem, store_sem, swap_send, swap_recv = scratch[15:19]
    place = Place()
    narrow, wide = attn_ref.shape[2] // 2, mlp_ref.shape[2] // 4
    size = normed.shape[0]

    def attn_source(index):
        return lambda core: attn_ref.at[index : index + 1, :, columns(core * narrow, narrow)]

    def mlp_source(index, half):
        return lambda core: mlp_ref.at[index : index + 1, :, columns((2 * core + half) * wide, wide)]

    groups = [(qkv_w.at[index : index + 1], narrow, attn_source(index)) for index in range(3)]
    groups.append((out_w, narrow, attn_source(3)))
    groups += [(up_w.at[half : half + 1], wide, mlp_source(0, half)) for half in range(2)]
    groups += [(down_w.at[half : half + 1], wide, mlp_source(1, half)) for half in range(2)]
    query, key, value, outer, up_a, up_b, down_a, down_b = range(8)
    gather = WeightGather(place, line, groups, scratch[19:22])
    tokens = RowSwap(place, tokens_ref, tokens_out, scratch[22:24])
    grads = CornerMove(place, grads_ref, grads_out, scratch[24:26])

    def load(group):
        if group < 3:
            source, target = qkv_w.at[group], qkv_wv.at[group]
        elif group == outer:
            source, target = out_w, out_wv
        else:
            source, target = up_w.at[group - up_a], up_wv.at[group - up_a]
        return pltpu.make_async_copy(source, target, load_sem.at[group])

    x_load = pltpu.make_async_copy(tokens_out, x_v, load_sem.at[7])
    pairs = (
        (qkv, qkv_out),
        (mixed, mixed_out),
        (lse, lse_out),
        (normed, normed_out),
        (middle, middle_out),
        (hidden, hidden_out),
        (act.at[0], act_out.at[0]),
        (act.at[1], act_out.at[1]),
        (bend.at[0], bend_out.at[0]),
        (bend.at[1], bend_out.at[1]),
    )

    def store(index):
        return pltpu.make_async_copy(*pairs[index], store_sem.at[index])

    def normalize_tokens():
        def body(step, carry):
            at = pl.ds(pl.multiple_of(step * 32, 32), 32)
            normal = normalize(x_v[at, :].astype(jnp.float32))
            normed[at, :] = (normal * vectors[0:1, :] + vectors[1:2, :]).astype(jnp.bfloat16)
            return carry

        lax.fori_loop(0, size // 32, body, 0, unroll=4)

    def project(group):
        load(group).wait()
        weight = qkv_wv[group].reshape(size, qkv.shape[2])

        def body(step, carry):
            at = pl.ds(pl.multiple_of(step * 512, 512), 512)
            out = jnp.dot(normed[at, :], weight, preferred_element_type=jnp.float32)
            qkv[group, at, :] = (out + qkv_bias[group : group + 1, :]).astype(jnp.bfloat16)
            return carry

        lax.fori_loop(0, size // 512, body, 0)

    def swap(index):
        at = pl.ds(pl.multiple_of(index * 256, 256), 256)
        return pltpu.make_async_remote_copy(
            src_ref=part.at[at, :],
            dst_ref=got.at[at, :],
            send_sem=swap_send.at[index],
            recv_sem=swap_recv.at[index],
            device_id=place.twin,
            device_id_type=MESH,
        )

    def project_out(index, carry):
        at = pl.ds(pl.multiple_of(index * 256, 256), 256)
        weight = out_wv[0].reshape(size, mixed.shape[1])
        part[at, :] = contract_last(mixed[at, :], weight).astype(jnp.bfloat16)
        swap(index).start()
        return carry

    def add_branch(index, carry):
        swap(index).wait()

        def body(step, carry):
            at = pl.ds(pl.multiple_of(index * 256 + step * 32, 32), 32)
            branch = part[at, :].astype(jnp.float32) + got[at, :].astype(jnp.float32)
            total = x_v[at, :].astype(jnp.float32) + branch + vectors[4:5, :]
            middle[at, :] = total
            hidden[at, :] = (normalize(total) * vectors[5:6, :] + vectors[6:7, :]).astype(jnp.bfloat16)
            return carry

        return lax.fori_loop(0, 8, body, carry, unroll=4)

    def feed(half):
        load(up_a + half).wait()

        def body(step, carry):
            at = pl.ds(pl.multiple_of(step * 256, 256), 256)
            weight = up_wv[half].reshape(size, act.shape[2])
            pre = jnp.dot(hidden[at, :], weight, preferred_element_type=jnp.float32)
            pre = pre + hidden_bias[half : half + 1, :]
            square = pre * pre
            bent = jnp.tanh(0.7978845608 * pre * (1.0 + 0.044715 * square))
            inner = 0.7978845608 * (1.0 + 3.0 * 0.044715 * square)
            act[half, at, :] = (0.5 * pre * (1.0 + bent)).astype(jnp.bfloat16)
            bend[half, at, :] = (0.5 * (1.0 + bent) + 0.5 * pre * (1.0 - bent * bent) * inner).astype(jnp.bfloat16)
            return carry

        lax.fori_loop(0, size // 256, body, 0)
        store(6 + half).start()
        store(8 + half).start()

    greet(place, line)
    for group in (query, down_b, key, value, outer, up_a, up_b, down_a):
        gather.begin(group)
    gather.enter(query)
    gather.line_start(query)
    gather.enter(down_b)
    gather.plane_start(down_b)
    gather.enter(key)
    gather.line_most(query)
    gather.line_start(key)
    tokens.start((0,))
    gather.line_end(query)
    gather.plane_start(query)
    gather.plane_step(down_b)
    gather.enter(value)
    gather.line_most(key)
    gather.line_start(value)
    tokens.start((1,))
    gather.line_end(key)
    gather.plane_step(query)
    gather.plane_start(key)
    gather.plane_end(down_b)
    gather.line_most(value)
    gather.enter(outer)
    gather.line_start(outer)
    tokens.start((2, 3))
    gather.line_end(value)
    gather.plane_end(query)
    load(query).start()
    gather.plane_step(key)
    gather.plane_start(value)
    fill_distance(seg_rows, seg_cols, distance)
    gather.enter(up_a)
    gather.line_most(outer)
    gather.line_start(up_a)
    gather.plane_end(key)
    load(key).start()
    gather.line_end(outer)
    gather.plane_step(value)
    gather.plane_start(outer)
    tokens.step()
    gather.line_step(up_a, 1)
    tokens.end()
    x_load.start()
    for step in range(2, line - 1):
        gather.line_step(up_a, step)
    gather.enter(up_b)
    gather.line_start(up_b)
    x_load.wait()
    normalize_tokens()
    store(3).start()
    gather.plane_end(value)
    load(value).start()
    gather.line_end(up_a)
    gather.plane_step(outer)
    gather.plane_start(up_a)
    project(query)
    gather.line_step(up_b, 1)
    gather.line_start(down_b)
    project(key)
    project(value)
    store(0).start()

    def beside(index):
        if index == 0:
            gather.enter(down_a)
            for step in range(2, line - 1):
                gather.line_step(up_b, step)
            gather.line_start(down_a)
            gather.plane_end(outer)
            load(outer).start()
        if index == 1:
            gather.line_end(up_b)
            gather.plane_step(up_a)
            gather.plane_start(up_b)
        if index == 2:
            gather.line_step(down_b, 1)
        if index == 3:
            gather.line_most(down_a)

    def attend(index, carry):
        attend_group(index, slopes, qkv, mixed, lse, distance)
        for order in range(4):

            @pl.when(index == order)
            def _():
                beside(order)

        return carry

    lax.fori_loop(0, qkv.shape[2] // (2 * HD), attend, 0)
    store(1).start()
    store(2).start()
    load(outer).wait()
    lax.fori_loop(0, size // 256, project_out, 0)
    gather.plane_step(up_b)
    gather.line_end(down_a)
    gather.plane_start(down_a)
    for step in range(2, line - 1):
        gather.line_step(down_b, step)
    grads.start()
    lax.fori_loop(0, size // 256, add_branch, 0)
    store(4).start()
    store(5).start()
    gather.plane_end(up_a)
    load(up_a).start()
    feed(0)
    gather.plane_step(down_a)
    gather.plane_end(up_b)
    load(up_b).start()
    feed(1)
    gather.line_end(down_b)
    gather.plane_end(down_a)
    grads.wait()
    for index in range(len(pairs)):
        store(index).wait()
    for group in range(len(groups)):
        gather.wait_sends(group)


def forward(attn_low, mlp_low, tokens, grads, slopes, seg_ids, qkv_bias, hidden_bias, vectors, line):
    rows = attn_low.shape[1]
    narrow, wide = attn_low.shape[2] // 2 * line, mlp_low.shape[2] // 4 * line
    length, width = 2 * tokens.shape[0], tokens.shape[1]
    low, dma = jnp.bfloat16, pltpu.SemaphoreType.DMA
    vmem = pl.BlockSpec(memory_space=pltpu.VMEM)
    hbm = pl.BlockSpec(memory_space=pl.ANY)

    def whole(count, columns_held):
        return (count, 2, 2, 2, rows, columns_held)

    kept = [
        ((3, length, narrow), low),
        ((length, narrow), low),
        ((length, narrow), jnp.float32),
        ((length, width), low),
        ((length, width), jnp.float32),
        ((length, width), low),
        ((2, length, wide), low),
        ((2, length, wide), low),
    ]
    outs = [(whole(3, narrow), low), (whole(1, narrow), low), (whole(2, wide), low), (whole(2, wide), low)]
    outs += [((length, width), low), (grads.shape, low)] + kept
    held = [(length, width)] * 2 + [whole(3, narrow), whole(1, narrow), whole(2, wide)]
    results = pl.pallas_call(
        functools.partial(forward_kernel, line),
        out_shape=[jax.ShapeDtypeStruct(*each) for each in outs],
        in_specs=[hbm] * 4 + [pl.BlockSpec(memory_space=pltpu.SMEM)] + [vmem] * 5,
        out_specs=[hbm] * len(outs),
        scratch_shapes=[pltpu.VMEM(each, low) for each in held]
        + [pltpu.VMEM(*each) for each in kept[:3]]
        + [pltpu.VMEM((length, length), jnp.float32)]
        + [pltpu.VMEM((length, width), low)] * 2
        + [pltpu.VMEM(*each) for each in kept[4:]]
        + [dma((8,)), dma((10,)), dma((length // 256,)), dma((length // 256,))]
        + WeightGather.scratch(8, line)
        + RowSwap.scratch()
        + CornerMove.scratch(),
        compiler_params=pltpu.CompilerParams(
            collective_id=1, has_side_effects=True, vmem_limit_bytes=62 * 1024 * 1024
        ),
        name="forward",
    )(
        attn_low,
        mlp_low,
        tokens,
        grads,
        slopes,
        seg_ids.reshape(-1, 1),
        seg_ids.reshape(1, -1),
        qkv_bias,
        hidden_bias,
        vectors,
    )
    return [each.reshape(each.shape[0], length, -1) for each in results[:4]] + list(results[4:])


def middle_kernel(
    line, grads_ref, act_ref, bend_ref, down_ref, up_ref, hidden_ref, middle_ref, mixed_ref, out_ref, gain,
    down_home, up_out, out_out, mixed_out, mid_out, sums_out, hidden_sums,
    grads, act, pre, down, up, hidden, middle, mixed, weight, part, got, low, mid, down_v, out_v, mixed_v,
    load_sem, store_sem, send_sem, recv_sem, give_sem, *scratch
):
    place = Place()
    bend, up_v = pre, down
    wide = down_home.shape[2] // 4
    one, two = (
        GroupSum(
            place,
            line,
            down_v.at[half : half + 1],
            down_home.at[:, :, columns((2 * place.core + half) * wide, wide)],
            scratch[half],
        )
        for half in range(2)
    )
    size = grads.shape[0]
    half = size // 2
    blocks = size // 256
    own_rows = grads.at[pl.ds(pl.multiple_of(place.core * half, half), half), :]
    give_rows = pltpu.make_async_remote_copy(
        src_ref=grads_ref,
        dst_ref=own_rows,
        send_sem=give_sem.at[0],
        recv_sem=give_sem.at[1],
        device_id=place.twin,
        device_id_type=MESH,
    )
    sources = (
        (grads_ref, own_rows), (down_ref, down), (bend_ref, bend), (up_ref, up), (act_ref.at[0], act.at[0]),
        (middle_ref, middle), (out_ref, weight), (hidden_ref, hidden), (mixed_ref, mixed),
    )
    load_g, load_down, load_bend, load_up, load_act, load_middle, load_out, load_hidden, load_mixed = (
        pltpu.make_async_copy(*each, load_sem.at[index]) for index, each in enumerate(sources)
    )
    load_more = pltpu.make_async_copy(act_ref.at[1], act.at[1], load_sem.at[10])
    for each in (load_g, load_act, load_down, load_bend, load_up, load_more, load_middle, load_out, load_hidden, load_mixed):
        each.start()
    greet(place, line)
    give_rows.start()

    def rows(index, count=256):
        return pl.ds(pl.multiple_of(index * count, count), count)

    def swap(index):
        return pltpu.make_async_remote_copy(
            src_ref=part.at[rows(index), :],
            dst_ref=got.at[rows(index), :],
            send_sem=send_sem.at[index],
            recv_sem=recv_sem.at[index],
            device_id=place.twin,
            device_id_type=MESH,
        )

    def store(slot, index, source, target):
        return pltpu.make_async_copy(source.at[rows(index), :], target.at[rows(index), :], store_sem.at[slot, index])

    def back_hidden(index, carry):
        total = None
        for order in range(2):
            back = jnp.dot(grads[rows(index), :], down[order], preferred_element_type=jnp.float32)
            piece = (back * bend[order, rows(index), :].astype(jnp.float32)).astype(jnp.bfloat16)
            pre[order, rows(index), :] = piece
            column = jnp.sum(piece.astype(jnp.float32), axis=0, keepdims=True)
            hidden_sums[order : order + 1, :] = hidden_sums[order : order + 1, :] + column
            term = contract_last(piece, up[order])
            total = term if total is None else total + term
        part[rows(index), :] = total.astype(jnp.bfloat16)
        swap(index).start()
        return carry

    def down_gradient(order):
        def body(index, carry):
            turned = grads[:, columns(index * 256, 256)].T
            piece = jnp.dot(turned, act[order], preferred_element_type=jnp.float32).astype(jnp.bfloat16)
            down_v[order, index // 2, lax.rem(index, 2)] = piece.reshape(2, 128, piece.shape[1])
            return carry

        lax.fori_loop(0, blocks, body, 0)

    def outer_product(slot, left, rights, targets, outs):
        def body(index, carry):
            turned = left[:, columns(index * 256, 256)].T
            for order, (right, target, out) in enumerate(zip(rights, targets, outs)):
                target[rows(index), :] = jnp.dot(turned, right[...], preferred_element_type=jnp.float32).astype(jnp.bfloat16)
                store(slot + order, index, target, out).start()
            return carry

        lax.fori_loop(0, blocks, body, 0)

    def norm_rows_back(step, sums, owned):
        core = place.core if owned else 1 - place.core
        at = pl.ds(pl.multiple_of(core * half + step * 32, 32), 32)
        grad = part[at, :].astype(jnp.float32) + got[at, :].astype(jnp.float32)
        value = middle[at, :]
        centred = value - jnp.mean(value, axis=1, keepdims=True)
        spread = lax.rsqrt(jnp.mean(centred * centred, axis=1, keepdims=True) + 1e-05)
        hat = centred * spread
        scaled = grad * gain[...]
        inner = jnp.mean(scaled * hat, axis=1, keepdims=True)
        above = grads[at, :].astype(jnp.float32)
        total = above + spread * (scaled - jnp.mean(scaled, axis=1, keepdims=True) - hat * inner)
        low[at, :] = total.astype(jnp.bfloat16)
        if not owned:
            return sums
        mid[pl.ds(pl.multiple_of(step * 32, 32), 32), :] = total
        fold = (4, 8, size)
        terms = (grad * hat, grad, total, above)
        return tuple(one + jnp.sum(term.reshape(fold), axis=0) for one, term in zip(sums, terms))

    def back_mixed(index, carry):
        mixed_v[rows(index), :] = jnp.dot(low[rows(index), :], weight[0], preferred_element_type=jnp.float32).astype(
            jnp.bfloat16
        )
        store(5, index, mixed_v, mixed_out).start()
        return carry

    hidden_sums[...] = jnp.zeros_like(hidden_sums)
    load_g.wait()
    give_rows.wait()
    load_act.wait()
    down_gradient(0)
    one.plane.start()
    load_more.wait()
    down_gradient(1)
    two.plane.start()
    load_down.wait()
    load_bend.wait()
    load_up.wait()
    lax.fori_loop(0, blocks // 2, back_hidden, 0)
    one.plane.one()
    lax.fori_loop(blocks // 2, blocks, back_hidden, 0)
    load_middle.wait()
    for index in range(blocks):
        swap(index).wait()
    empty = tuple(jnp.zeros((8, size), jnp.float32) for _ in range(4))
    lax.fori_loop(0, half // 32, lambda step, sums: norm_rows_back(step, sums, False), (), unroll=4)
    two.plane.one()
    one.plane.two()
    one.line.step(0)
    sums = lax.fori_loop(0, half // 32, lambda step, sums: norm_rows_back(step, sums, True), empty, unroll=4)
    for index, each in enumerate(sums):
        sums_out[index : index + 1, :] = jnp.sum(each, axis=0, keepdims=True)
    mid_store = pltpu.make_async_copy(mid, mid_out, load_sem.at[9])
    mid_store.start()
    one.line.step(1)
    load_out.wait()
    lax.fori_loop(0, blocks, back_mixed, 0)
    two.plane.two()
    two.line.step(0)
    load_mixed.wait()
    outer_product(4, low, (mixed,), (out_v.at[0],), (out_out.at[0],))
    for step in range(2, line - 1):
        one.line.step(step)
    two.line.step(1)
    load_hidden.wait()
    outer_product(2, hidden, (pre.at[0], pre.at[1]), (up_v.at[0], up_v.at[1]), (up_out.at[0], up_out.at[1]))
    one.line.end()
    one.home.start()
    for step in range(2, line - 1):
        two.line.step(step)
    two.line.end()
    two.home.start()
    for index in range(blocks):
        for order in range(2):
            store(2 + order, index, up_v.at[order], up_out.at[order]).wait()
        store(4, index, out_v.at[0], out_out.at[0]).wait()
        store(5, index, mixed_v, mixed_out).wait()
    mid_store.wait()
    for group in (one, two):
        group.home.wait()
        group.sent()


def middle_back(grads, act, bend, down, up, hidden, middle, mixed, out, gain, line):
    size, narrow = mixed.shape
    rows = size // 8
    low, dma = jnp.bfloat16, pltpu.SemaphoreType.DMA
    hbm, vmem = pl.BlockSpec(memory_space=pl.ANY), pl.BlockSpec(memory_space=pltpu.VMEM)

    def held(each):
        return pltpu.VMEM(each.shape, each.dtype)

    square = pltpu.VMEM((size, size), low)
    return pl.pallas_call(
        functools.partial(middle_kernel, line),
        out_shape=[
            jax.ShapeDtypeStruct((1, rows, 4 * size // line), low),
            jax.ShapeDtypeStruct(act.shape, low),
            jax.ShapeDtypeStruct((1, size, narrow), low),
            jax.ShapeDtypeStruct((size, narrow), low),
            jax.ShapeDtypeStruct((size // 2, size), jnp.float32),
            jax.ShapeDtypeStruct((4, size), jnp.float32),
            jax.ShapeDtypeStruct((2, size), jnp.float32),
        ],
        in_specs=[hbm] * 9 + [vmem],
        out_specs=[hbm] * 5 + [vmem] * 2,
        scratch_shapes=[square] + [held(each) for each in (act, bend, down, up, hidden, middle, mixed, out)]
        + [square, square, square, pltpu.VMEM((size // 2, size), jnp.float32)]
        + [pltpu.VMEM((2, 2, 2, 2, rows, act.shape[2]), low)]
        + [pltpu.VMEM((1, size, narrow), low), pltpu.VMEM((size, narrow), low)]
        + [dma((11,)), dma((6, size // 256)), dma((size // 256,)), dma((size // 256,)), dma((2,))]
        + [GroupSum.scratch(1, rows, act.shape[2], line)] * 2,
        compiler_params=pltpu.CompilerParams(
            collective_id=4, has_side_effects=True, vmem_limit_bytes=62 * 1024 * 1024
        ),
        name="middle_back",
    )(grads, act, bend, down, up, hidden, middle, mixed, out, gain.reshape(1, -1))


def attend_back_group(group, slopes, qkv, grad, mixed, lse, out, distance, dk_acc, dv_acc):
    length = qkv.shape[1]
    cols = columns(group * 2 * HD, 2 * HD)
    masks = head_lanes(jnp.bfloat16)
    wide_masks = head_lanes(jnp.float32)
    first = wide_masks[0] > 0.5
    factor = LOG2E / math.sqrt(HD)
    shrink = 1.0 / math.sqrt(HD)
    keys, values = qkv[1, :, cols], qkv[2, :, cols]
    keys_t = keys.T
    values_t = values.T
    dk_acc[...] = jnp.zeros_like(dk_acc)
    dv_acc[...] = jnp.zeros_like(dv_acc)
    for start in range(0, length, ROW_BLOCK):
        stop = start + ROW_BLOCK
        rows = slice(start, stop)
        query, grads, log_sums = qkv[0, rows, cols], grad[rows, cols], lse[rows, cols]
        query_t, grads_t = query.T, grads.T
        product = grads.astype(jnp.float32) * mixed[rows, cols].astype(jnp.float32)
        parts = []
        for head in range(2):
            slope = slopes[2 * group + head] * LOG2E
            lanes = slice(head * HD, (head + 1) * HD)
            scores = jnp.dot(query * masks[head], keys_t[:, :stop], preferred_element_type=jnp.float32)
            log_sum = log_sums[:, head * HD : head * HD + 1]
            probs = jnp.exp2(scores * factor - slope * distance[rows, :stop] - log_sum)
            grad_probs = jnp.dot(grads * masks[head], values_t[:, :stop], preferred_element_type=jnp.float32)
            inner = jnp.sum(product * wide_masks[head], axis=1, keepdims=True)
            grad_scores = (probs * (grad_probs - inner)).astype(jnp.bfloat16)
            parts.append(jnp.dot(grad_scores, keys[:stop], preferred_element_type=jnp.float32))
            dk_acc[lanes, :stop] += jnp.dot(query_t[lanes, :], grad_scores, preferred_element_type=jnp.float32)
            dv_acc[lanes, :stop] += jnp.dot(
                grads_t[lanes, :], probs.astype(jnp.bfloat16), preferred_element_type=jnp.float32
            )
        out[0, rows, cols] = (jnp.where(first, parts[0], parts[1]) * shrink).astype(jnp.bfloat16)
    out[1, :, cols] = (dk_acc[...].T * shrink).astype(jnp.bfloat16)
    out[2, :, cols] = dv_acc[...].T.astype(jnp.bfloat16)


def back_kernel(
    line, up_ref, out_ref, slopes, seg_rows, seg_cols, qkv, grad, mixed, lse, mlp_mom, down_sum, weight_ref, normed_ref,
    act_ref, down_w, attn_home, normed_part, bias_sums, mom_out, whole, out_part,
    held, held_sem, grads, projected, distance, dk_acc, dv_acc, up_sum, mlp_round, *scratch
):
    place = Place()
    narrow_cols = held.shape[2]
    wide, narrow = mlp_mom.shape[2] // 4, attn_home.shape[2] // 2

    def up_target(part):
        return up_sum.at[:, :, columns((2 * place.core + part) * wide, wide)]

    def attn_target(lo, hi):
        return attn_home.at[lo:hi, :, columns(place.core * narrow, narrow)]

    groups = [
        GroupSum(place, line, up_ref.at[0:1], up_target(0), scratch[0]),
        GroupSum(place, line, out_ref, attn_target(3, 4), scratch[1]),
        GroupSum(place, line, projected, attn_target(0, 3), scratch[2]),
        GroupSum(place, line, up_ref.at[1:2], up_target(1), scratch[3], line_first=True),
    ]
    three, outer, inner, last = groups
    collect = Collect(place, mlp_round, whole, scratch[4])

    def attend(group, carry):
        attend_back_group(group, slopes, qkv, grad, mixed, lse, grads, distance, dk_acc, dv_acc)
        return carry

    def halves(ref):
        return [ref.at[:, half * narrow_cols : (half + 1) * narrow_cols] for half in range(2)]

    first_loads = [pltpu.make_async_copy(weight_ref.at[order], held.at[order], held_sem.at[order]) for order in range(3)]
    for half, source in enumerate(halves(normed_ref)):
        first_loads.append(pltpu.make_async_copy(source, held.at[3 + half], held_sem.at[3 + half]))
    quarters = [source for part in range(2) for source in halves(down_w.at[part])]
    late_loads = [pltpu.make_async_copy(quarters[index], held.at[index], held_sem.at[index]) for index in range(4)]

    def act_load(block, index):
        source = act_ref.at[
            index // 2, pl.ds(pl.multiple_of(block * 256, 256), 256), (index % 2) * narrow_cols : (index % 2 + 1) * narrow_cols
        ]
        return pltpu.make_async_copy(source, held.at[4, index * 256 : (index + 1) * 256], held_sem.at[5 + index])

    def project(index, carry):
        left = held[3 + index // 2, :, columns(lax.rem(index, 2) * 256, 256)].T
        for order in range(3):
            piece = jnp.dot(left, grads[order], preferred_element_type=jnp.float32).astype(jnp.bfloat16)
            projected[order, index // 2, lax.rem(index, 2)] = piece.reshape(2, 128, piece.shape[1])
        return carry

    def unproject(index, carry):
        at = pl.ds(pl.multiple_of(index * 256, 256), 256)
        total = contract_last(grads[0, at, :], held[0])
        for order in range(1, 3):
            total = total + contract_last(grads[order, at, :], held[order])
        normed_part[at, :] = total.astype(jnp.bfloat16)
        return carry

    def feed_out(block, carry):
        for index in range(4):
            act_load(block, index).start()
        for index in range(4):
            act_load(block, index).wait()
        total = contract_last(held[4, 0:256], held[0])
        for index in range(1, 4):
            total = total + contract_last(held[4, index * 256 : (index + 1) * 256], held[index])
        at = pl.ds(pl.multiple_of(block * 256, 256), 256)
        for half in range(2):
            grads[half, at, :] = total[:, half * narrow_cols : (half + 1) * narrow_cols].astype(jnp.bfloat16)
        return carry

    def out_store(half):
        return pltpu.make_async_copy(grads.at[half], halves(out_part)[half], held_sem.at[half])

    def update(index, carry):
        at = pl.ds(pl.multiple_of(index * 32, 32), 32)
        for order, gradient in enumerate((up_sum, down_sum)):
            fresh = 0.5 * mlp_mom[order, at, :] + gradient[0, at, :].astype(jnp.float32)
            mom_out[order, at, :] = fresh
            mlp_round[order, at, :] = fresh.astype(jnp.bfloat16)
        return carry

    greet_all(place)
    three.plane.start()
    last.load().start()
    for each in first_loads:
        each.start()
    last.load().wait()
    last.line.step(0)
    outer.plane.start()
    fill_distance(seg_rows, seg_cols, distance)
    pairs = qkv.shape[2] // (2 * HD)
    lax.fori_loop(0, pairs // 2, attend, 0)
    three.plane.one()
    last.line.step(1)
    lax.fori_loop(pairs // 2, pairs, attend, 0)
    three.plane.two()
    three.line.step(0)
    outer.plane.one()
    for each in first_loads:
        each.wait()
    lax.fori_loop(0, 4, project, 0)
    for step in range(2, line - 1):
        last.line.step(step)
    inner.plane.start()
    three.line.step(1)
    outer.plane.two()
    outer.line.step(0)
    lax.fori_loop(0, 4, unproject, 0)
    for each in late_loads:
        each.start()
    for order in range(3):
        bias_sums[order : order + 1, :] = jnp.sum(grads[order].astype(jnp.float32), axis=0, keepdims=True)
    for step in range(2, line - 1):
        three.line.step(step)
    last.line.end()
    last.plane.start()
    three.line.end()
    three.home.start()
    last.plane.one()
    inner.plane.one()
    outer.line.step(1)
    last.plane.two()
    last.home.start()
    for step in range(2, line - 1):
        outer.line.step(step)
    for group in (three, last):
        group.home.wait()
    lax.fori_loop(0, mlp_mom.shape[1] // 32, update, 0)
    collect.start()
    collect.forward()
    outer.line.end()
    outer.home.start()
    inner.plane.two()
    inner.line.step(0)
    for each in late_loads:
        each.wait()
    lax.fori_loop(0, 2, feed_out, 0)
    inner.line.step(1)
    lax.fori_loop(2, 4, feed_out, 0)
    for half in range(2):
        out_store(half).start()
    for step in range(2, line - 1):
        inner.line.step(step)
    inner.line.end()
    inner.home.start()
    inner.home.wait()
    outer.home.wait()
    for half in range(2):
        out_store(half).wait()
    for group in groups:
        group.sent()
    collect.finish()


def attend_back(
    up, out, slopes, seg_ids, qkv, grad, mixed, lse, mlp_mom, down_sum, weights, normed, act, down_w, line
):
    _, length, width = qkv.shape
    rows, wide = up.shape[1] // 8, up.shape[2]
    size = normed.shape[1]
    vmem = pl.BlockSpec(memory_space=pltpu.VMEM)
    hbm = pl.BlockSpec(memory_space=pl.ANY)
    low = jnp.bfloat16
    return pl.pallas_call(
        functools.partial(back_kernel, line),
        out_shape=[
            jax.ShapeDtypeStruct((4, rows, 2 * width // line), low),
            jax.ShapeDtypeStruct((length, size), low),
            jax.ShapeDtypeStruct((3, width), jnp.float32),
            jax.ShapeDtypeStruct(mlp_mom.shape, jnp.float32),
            jax.ShapeDtypeStruct((size, 2 * wide), low),
            jax.ShapeDtypeStruct((length, size), low),
        ],
        in_specs=[hbm] * 2 + [pl.BlockSpec(memory_space=pltpu.SMEM)] + [vmem] * 8 + [hbm] * 4,
        out_specs=[hbm, vmem, vmem, vmem, hbm, hbm],
        scratch_shapes=[
            pltpu.VMEM((5, size, width), low),
            pltpu.SemaphoreType.DMA((9,)),
            pltpu.VMEM(qkv.shape, low),
            pltpu.VMEM((3, 2, 2, 2, rows, width), low),
            pltpu.VMEM((length, length), jnp.float32),
            pltpu.VMEM((2 * HD, length), jnp.float32),
            pltpu.VMEM((2 * HD, length), jnp.float32),
            pltpu.VMEM(down_sum.shape, low),
            pltpu.VMEM(mlp_mom.shape, low),
        ]
        + [GroupSum.scratch(1, rows, wide, line)]
        + [GroupSum.scratch(1, rows, width, line), GroupSum.scratch(3, rows, width, line)]
        + [GroupSum.scratch(1, rows, wide, line, line_first=True), Collect.scratch()],
        compiler_params=pltpu.CompilerParams(
            collective_id=2, has_side_effects=True, vmem_limit_bytes=62 * 1024 * 1024
        ),
        name="attend_back",
    )(
        *(each.reshape(-1, 2, 2, 2, rows, each.shape[2]) for each in (up, out)),
        slopes,
        seg_ids.reshape(-1, 1),
        seg_ids.reshape(1, -1),
        qkv,
        grad,
        mixed,
        lse,
        mlp_mom,
        down_sum,
        weights,
        normed,
        act,
        down_w,
    )


def finish_kernel(
    line, attn_ref, whole_ref, vec_ref, gain, part_ref, x_ref, grad_mid, out_ref, middle_ref, bias, attn_w, mlp_w,
    attn_new, mlp_new, vec_out, dx_new, block_out, *scratch
):
    (thin, full, gram, sent, got, poly, norm_own, norm_got, dx, away, mine) = scratch[:11]
    (home_sem, start_sem, send_sem, back_sem, norm_sem, block_send, block_recv, pass_send, pass_recv, dx_sem) = scratch[11:21]
    vector = VectorSum(Place(), line, scratch[21:25])
    out_mine, out_away, out_sem, middle, tokens, dx_out, attn_home, mlp_home = scratch[25:33]
    place = Place()
    x, y, t, core = place.x, place.y, place.tensor, place.core
    me, devices = place.me, place.devices
    rows = attn_ref.shape[1]
    narrow, wide = attn_ref.shape[2] // 2, mlp_home.shape[2] // 2
    greet_all(place)

    def held(order, index):
        return rows_held(place, thin if order < 4 else full, index, rows, narrow if order < 4 else wide)

    def source(order, half):
        return attn_ref.at[order, :, half * narrow : (half + 1) * narrow]

    def target(order, half):
        if order < 4:
            return attn_home.at[order, :, half * narrow : (half + 1) * narrow]
        return mlp_home.at[order - 4, :, half * wide : (half + 1) * wide]

    def owner_of(order, half):
        ox, oy, oz = OWNERS[order]
        return place.index(ox, oy, half, oz)

    def owns(order):
        ox, oy, oz = OWNERS[order]
        return (x == ox) & (y == oy) & (t == oz)

    owns_full = owns(4) | owns(5)
    owns_thin = owns(0) | owns(1) | owns(2) | owns(3)

    def collect(order, half):
        return remote(
            place, source(order, half), held(order, me), home_sem.at[order, half], start_sem.at[0], owner_of(order, half)
        )

    def collect_own(order, half):
        return pltpu.make_async_copy(source(order, half), held(order, me), start_sem.at[0])

    @pl.when(owns_full)
    def _():
        pltpu.make_async_copy(whole_ref, full, start_sem.at[0]).start()

    for order in range(4):
        for half in range(2):

            @pl.when(me == owner_of(order, half))
            def _():
                collect_own(order, half).start()

            @pl.when(me != owner_of(order, half))
            def _():
                collect(order, half).start()

    half_rows = dx.shape[0]

    def rows_of(ref, cores):
        return ref.at[pl.ds(pl.multiple_of(cores * half_rows, half_rows), half_rows), :]

    part_swap = pltpu.make_async_remote_copy(
        src_ref=rows_of(part_ref, 1 - core),
        dst_ref=away,
        send_sem=dx_sem.at[0],
        recv_sem=dx_sem.at[1],
        device_id=place.twin,
        device_id_type=MESH,
    )
    part_load = pltpu.make_async_copy(rows_of(part_ref, core), mine, dx_sem.at[2])
    part_swap.start()
    part_load.start()
    out_load = pltpu.make_async_copy(rows_of(out_ref, core), out_mine, out_sem.at[0])
    out_swap = pltpu.make_async_remote_copy(
        src_ref=rows_of(out_ref, 1 - core),
        dst_ref=out_away,
        send_sem=out_sem.at[3],
        recv_sem=out_sem.at[4],
        device_id=place.twin,
        device_id_type=MESH,
    )
    middle_load = pltpu.make_async_copy(rows_of(middle_ref, core), middle, out_sem.at[1])
    tokens_load = pltpu.make_async_copy(rows_of(x_ref, core), tokens, out_sem.at[2])
    for each in (tokens_load, out_load, out_swap, middle_load):
        each.start()

    def out_rows(step, carry):
        at = pl.ds(pl.multiple_of(step * 32, 32), 32)
        total = out_mine[at, :].astype(jnp.float32) + out_away[at, :].astype(jnp.float32)
        out_mine[at, :] = (middle[at, :] + total + bias[...]).astype(jnp.bfloat16)
        return carry

    def go_home(slot, source_ref, target_ref, sem):
        keep_rows = pltpu.make_async_copy(source_ref, target_ref, sem.at[slot])
        move_rows = pltpu.make_async_remote_copy(
            src_ref=source_ref,
            dst_ref=target_ref,
            send_sem=sem.at[slot + 1],
            recv_sem=sem.at[slot + 2],
            device_id=place.corner,
            device_id_type=MESH,
        )
        return keep_rows, move_rows

    dx_moves = go_home(2, dx, dx_out, dx_sem)
    out_moves = go_home(5, out_mine, block_out, out_sem)

    def when_moving(moves, action):
        for moving in (False, True):

            @pl.when(place.stays != moving)
            def _():
                action(moves[moving])

    step_rows = 32

    def dx_rows(step, sums):
        at = pl.ds(pl.multiple_of(step * step_rows, step_rows), step_rows)
        grad = mine[at, :].astype(jnp.float32) + away[at, :].astype(jnp.float32)
        value = tokens[at, :].astype(jnp.float32)
        centred = value - jnp.mean(value, axis=1, keepdims=True)
        spread = lax.rsqrt(jnp.mean(centred * centred, axis=1, keepdims=True) + 1e-05)
        hat = centred * spread
        product = grad * hat
        scaled = grad * gain[...]
        inner = jnp.mean(scaled * hat, axis=1, keepdims=True)
        back_grad = spread * (scaled - jnp.mean(scaled, axis=1, keepdims=True) - hat * inner)
        dx[at, :] = (grad_mid[at, :] + back_grad).astype(jnp.bfloat16)
        fold = (step_rows // 8, 8, grad.shape[1])
        return (
            sums[0] + jnp.sum(product.reshape(fold), axis=0),
            sums[1] + jnp.sum(grad.reshape(fold), axis=0),
        )

    part_swap.wait()
    part_load.wait()
    tokens_load.wait()
    empty = jnp.zeros((8, gain.shape[1]), jnp.float32)
    token_sums = lax.fori_loop(0, half_rows // step_rows, dx_rows, (empty, empty), unroll=2)
    when_moving(dx_moves, lambda move: move.start())
    vector.start(vec_ref[...], [jnp.sum(each, axis=0, keepdims=True) for each in token_sums])
    out_load.wait()
    out_swap.wait()
    middle_load.wait()
    lax.fori_loop(0, half_rows // 32, out_rows, 0, unroll=2)
    when_moving(out_moves, lambda move: move.start())

    def contract_rows(left, right):
        return lax.dot_general(left, right, (((1,), (1,)), ((), ())), preferred_element_type=jnp.float32)

    block = 256

    def swap_block(slot, index):
        return pltpu.make_async_remote_copy(
            src_ref=sent.at[index],
            dst_ref=got.at[slot, index],
            send_sem=block_send.at[index],
            recv_sem=block_recv.at[slot, index],
            device_id=place.twin,
            device_id_type=MESH,
        )

    def begin(matrix):
        size, width = matrix.shape
        pltpu.make_async_copy(matrix, matrix, start_sem.at[0]).wait()

        def add_squares(step, total):
            piece = matrix[pl.ds(pl.multiple_of(step * 32, 32), 32), :].astype(jnp.float32)
            piece = piece * piece
            return total + jnp.sum(piece.reshape(4, 8, width // 128, 128), axis=(0, 2))

        squares = lax.fori_loop(0, size // 32, add_squares, jnp.zeros((8, 128), jnp.float32))
        norm_own[...] = jnp.zeros((8, 128), jnp.float32) + jnp.sum(squares)
        swap = pltpu.make_async_remote_copy(
            src_ref=norm_own,
            dst_ref=norm_got,
            send_sem=norm_sem.at[0],
            recv_sem=norm_sem.at[1],
            device_id=place.twin,
            device_id_type=MESH,
        )
        swap.start()
        swap.wait()
        scale = 1.0 / (jnp.sqrt(norm_own[...] + norm_got[...]) + 1e-06)
        scale = scale[0:1, 0:1]

        def scale_rows(step, carry):
            at = pl.ds(pl.multiple_of(step * 32, 32), 32)
            matrix[at, :] = (matrix[at, :].astype(jnp.float32) * scale).astype(jnp.bfloat16)
            return carry

        lax.fori_loop(0, size // 32, scale_rows, 0)

    def iterate(matrix, repeat):
        size, width = matrix.shape
        blocks = size // block
        slot = repeat % 2

        def share(index, carry):
            at = pl.ds(pl.multiple_of(index * block, block), block)
            sent[index] = contract_rows(matrix[at, :], matrix[...]).astype(jnp.bfloat16)
            swap_block(slot, index).start()
            return carry

        lax.fori_loop(0, blocks, share, 0)

        def add(index, carry):
            at = pl.ds(pl.multiple_of(index * block, block), block)
            swap_block(slot, index).wait()
            total = sent[index].astype(jnp.float32) + got[slot, index].astype(jnp.float32)
            gram[at, :] = total.astype(jnp.bfloat16)
            return carry

        lax.fori_loop(0, blocks, add, 0)
        square = jnp.dot(gram[...], gram[...], preferred_element_type=jnp.float32)
        poly[...] = (coeff_b * gram[...].astype(jnp.float32) + coeff_c * square).astype(jnp.bfloat16)
        step_width = min(width, 1024)

        def advance(index, carry):
            at = columns(index * step_width, step_width)
            moved = jnp.dot(poly[...], matrix[:, at], preferred_element_type=jnp.float32)
            matrix[:, at] = (coeff_a * matrix[:, at].astype(jnp.float32) + moved).astype(jnp.bfloat16)
            return carry

        lax.fori_loop(0, width // step_width, advance, 0)

    @pl.when(owns_thin)
    def _():
        begin(thin)

    @pl.when(owns_full)
    def _():
        begin(full)

    for repeat in range(NS_STEPS):

        @pl.when(owns_thin)
        def _():
            iterate(thin, repeat)

        @pl.when(owns_full)
        def _():
            iterate(full, repeat)

        if repeat < 3:
            vector.step(repeat)
        if repeat == 3:
            vec_out[...] = vector.end()

    def keep(order, half):
        return pltpu.make_async_copy(held(order, me), target(order, half), back_sem.at[order, half])

    def back(order, half, index):
        return remote(place, held(order, index), target(order, half), send_sem.at[0], back_sem.at[order, half], index)

    def place_in(index):
        dp, z = place.of(index)
        return lax.rem(dp // 2, 2), dp // 4, z, lax.rem(dp, 2)

    def one_aside(order, xs, ys):
        ox, oy, _ = OWNERS[order]
        return (xs != ox) != (ys != oy)

    def back_by_way(order, index):
        xs, ys, z, _ = place_in(index)
        return one_aside(order, xs, ys) & is_one_of(z, sides(order, line)[0])

    def to_back_way(order, half, index):
        xs, ys, z, cores = place_in(index)
        region = held(order, index)
        first = sides(order, line)[0][0]
        return remote(
            place, region, region, send_sem.at[0], pass_recv.at[z - first, cores], place.index(xs, ys, half, OWNERS[order][2])
        )

    def back_in(order, which, cores):
        index = place.index(x, y, cores, sides(order, line)[0][which])
        region = held(order, index)
        return remote(place, region, region, pass_send.at[which, cores], pass_recv.at[which, cores], index)

    def back_on(order, half, which, cores):
        index = place.index(x, y, cores, sides(order, line)[0][which])
        return remote(
            place, held(order, index), target(order, half), pass_send.at[which, cores], back_sem.at[order, half], index
        )

    def when_back_way(order, action):
        for half in range(2):

            @pl.when(one_aside(order, x, y) & (t == OWNERS[order][2]) & (core == half))
            def _():
                for which in range(len(sides(order, line)[0])):
                    for cores in range(2):
                        action(order, half, which, cores)

    def each_device(order, half, action, passed):
        def body(step, carry):
            index = lax.rem(me + step, devices)
            if order < 4:
                action(order, half, index)
            else:

                @pl.when(back_by_way(order, index) == passed)
                def _():
                    action(order, half, index)

            return carry

        lax.fori_loop(1, devices, body, 0)

    def give_back(orders):
        for order in orders:
            for half in range(2):

                @pl.when(me == owner_of(order, half))
                def _():
                    if order >= 4:
                        each_device(order, half, lambda *at: to_back_way(*at).start(), True)
                    each_device(order, half, lambda *at: back(*at).start(), False)
                    keep(order, half).start()

    give_back((4, 5, 0, 1, 2, 3))

    def return_rows(order, half, which, cores):
        back_in(order, which, cores).wait_recv()
        back_on(order, half, which, cores).start()

    for order in (4, 5):
        when_back_way(order, return_rows)

    for order in range(6):
        for half in range(2):
            keep(order, half).wait()

            @pl.when(me == owner_of(order, half))
            def _():
                if order >= 4:
                    each_device(order, half, lambda *at: to_back_way(*at).wait_send(), True)
                each_device(order, half, lambda *at: back(*at).wait_send(), False)

            if order < 4:

                @pl.when(me != owner_of(order, half))
                def _():
                    collect(order, half).wait_send()

    for order in (4, 5):
        when_back_way(order, lambda *at: back_on(*at).wait_send())

    when_moving(dx_moves, lambda move: move.wait())

    def widen(step, carry):
        at = pl.ds(pl.multiple_of(step * 32, 32), 32)
        dx_new[at, :] = dx_out[at, :].astype(jnp.float32)
        return carry

    lax.fori_loop(0, half_rows // 32, widen, 0)

    def renew(step, carry):
        at = pl.ds(pl.multiple_of(step * 32, 32), 32)
        for order in range(4):
            attn_new[order, at, :] = attn_w[order, at, :] - attn_home[order, at, :].astype(jnp.float32)
        for order in range(2):
            change = math.sqrt(FF / D) * mlp_home[order, at, :].astype(jnp.float32)
            mlp_new[order, at, :] = mlp_w[order, at, :] - change
        return carry

    lax.fori_loop(0, rows // 32, renew, 0)
    when_moving(out_moves, lambda move: move.wait())


def finish(attn_round, mlp_whole, vec, gain, normed_part, tokens, grad_mid, out_part, middle, bias, attn_w, mlp_w, line):
    rows = attn_w.shape[1]
    size = 8 * rows
    narrow, wide = attn_w.shape[2] // 2 * line, mlp_w.shape[2] // 2 * line
    low, dma = jnp.bfloat16, pltpu.SemaphoreType.DMA
    hbm = pl.BlockSpec(memory_space=pl.ANY)
    vmem = pl.BlockSpec(memory_space=pltpu.VMEM)
    half = grad_mid.shape
    return pl.pallas_call(
        functools.partial(finish_kernel, line),
        out_shape=[
            jax.ShapeDtypeStruct(attn_w.shape, jnp.float32),
            jax.ShapeDtypeStruct(mlp_w.shape, jnp.float32),
            jax.ShapeDtypeStruct(vec.shape, jnp.float32),
            jax.ShapeDtypeStruct(half, jnp.float32),
            jax.ShapeDtypeStruct(half, low),
        ],
        in_specs=[hbm, hbm, vmem, vmem, hbm, hbm, vmem, hbm, hbm, vmem, vmem, vmem],
        out_specs=[vmem, vmem, vmem, vmem, hbm],
        scratch_shapes=[
            pltpu.VMEM((size, narrow), low),
            pltpu.VMEM((size, wide), low),
            pltpu.VMEM((size, size), low),
            pltpu.VMEM((size // 256, 256, size), low),
            pltpu.VMEM((2, size // 256, 256, size), low),
            pltpu.VMEM((size, size), low),
            pltpu.VMEM((8, 128), jnp.float32),
            pltpu.VMEM((8, 128), jnp.float32),
            pltpu.VMEM(half, low),
            pltpu.VMEM(half, low),
            pltpu.VMEM(half, low),
            dma((6, 2)),
            dma((1,)),
            dma((1,)),
            dma((6, 2)),
            dma((2,)),
            dma((size // 256,)),
            dma((2, size // 256)),
            dma((2, 2)),
            dma((2, 2)),
            dma((5,)),
        ]
        + VectorSum.scratch(vec.shape, line)
        + [
            pltpu.VMEM(half, low),
            pltpu.VMEM(half, low),
            dma((8,)),
            pltpu.VMEM(half, jnp.float32),
            pltpu.VMEM(half, low),
            pltpu.VMEM(half, low),
            pltpu.VMEM(attn_w.shape, low),
            pltpu.VMEM(mlp_w.shape, low),
        ],
        compiler_params=pltpu.CompilerParams(
            collective_id=3, has_side_effects=True, vmem_limit_bytes=60 * 1024 * 1024
        ),
        name="finish",
    )(
        attn_round,
        mlp_whole,
        vec,
        gain.reshape(1, -1),
        normed_part,
        tokens,
        grad_mid,
        out_part,
        middle,
        bias.reshape(1, -1),
        attn_w,
        mlp_w,
    )


def pair_swap(value):
    dp, line = lax.axis_size("dp"), lax.axis_size("tensor")
    pairs = [(i * line + k, (i ^ 1) * line + k) for i in range(dp) for k in range(line)]
    return lax.ppermute(value, ("dp", "tensor"), pairs)


def on_chip_pair(tokens, cotangent, segments, attn_w, mlp_w, vectors, attn_mom, mlp_mom, vector_mom):
    line = lax.axis_size("tensor")
    place = Place()
    core, t = place.core, place.tensor
    width = tokens.shape[1]
    narrow, wide = attn_w.shape[2] // 2, mlp_w.shape[2] // 4
    total_tokens = tokens.shape[0] * line * lax.axis_size("dp")

    def my_columns(row):
        return lax.dynamic_index_in_dim(row.reshape(line, 2, narrow), core, 1, False).reshape(-1)

    def place_columns(piece):
        spread = jnp.zeros((line, 2, narrow), jnp.float32)
        return lax.dynamic_update_slice(spread, piece.reshape(line, 1, narrow), (0, core, 0)).reshape(-1)

    hidden_bias = lax.dynamic_index_in_dim(vectors[8:].reshape(line, 2, 2, wide), core, 1, False)
    hidden_bias = hidden_bias.transpose(1, 0, 2).reshape(2, line * wide)

    seg_pairs = segments.reshape(-1, SEQ)
    seg_own = lax.dynamic_index_in_dim(seg_pairs, t // 2, 0, False)
    seg_ids = jnp.where(core == lax.rem(t, 2), seg_own, pair_swap(seg_own))

    biases = jnp.stack([my_columns(vectors[2]), jnp.zeros((narrow * line,), jnp.float32), my_columns(vectors[3])])
    per = narrow // HD
    local_ids = jnp.arange(per * line)
    head_ids = (local_ids // per) * (2 * per) + core * per + local_ids % per
    slopes = jnp.exp2(-(8.0 / HEADS) * (head_ids.astype(jnp.float32) + 1.0))
    low = jnp.bfloat16
    (
        wqkv, wout, w_up, w_down, x_low, grad_low, qkv, mixed, log_sums, normed, middle, hidden_low, hidden_act, bend
    ) = forward(
        attn_w.astype(low),
        mlp_w.astype(low),
        tokens,
        cotangent,
        slopes,
        seg_ids,
        biases,
        hidden_bias,
        vectors,
        line,
    )
    down_sum, grad_up, grad_out, grad_mixed, grad_mid_mine, middle_sums, hidden_sums = middle_back(
        grad_low, hidden_act, bend, w_down, w_up, hidden_low, middle, mixed, wout, vectors[5], line
    )
    attn_sum, normed_part, bias_sums, mlp_mom_new, mlp_whole, out_part = attend_back(
        grad_up,
        grad_out,
        slopes,
        seg_ids,
        qkv,
        grad_mixed,
        mixed,
        log_sums,
        mlp_mom,
        down_sum,
        wqkv,
        normed,
        hidden_act,
        w_down,
        line,
    )
    hidden_grad = lax.dynamic_update_slice(
        jnp.zeros((line, 2, 2, wide), jnp.float32),
        hidden_sums.reshape(2, line, wide).transpose(1, 0, 2)[:, None],
        (0, core, 0, 0),
    )
    vector_rows = jnp.stack(
        [
            jnp.zeros((width,), jnp.float32),
            jnp.zeros((width,), jnp.float32),
            place_columns(bias_sums[0]),
            place_columns(bias_sums[2]),
            middle_sums[2],
            middle_sums[0],
            middle_sums[1],
            middle_sums[3],
        ]
    )
    vector_local = jnp.concatenate([vector_rows, hidden_grad.reshape(-1, width)], axis=0)
    padding = jnp.zeros((4, width), jnp.float32)
    attn_mom_new = 0.5 * attn_mom + attn_sum.astype(jnp.float32)
    attn_new, mlp_new, vector_sum, grad_tokens, output = finish(
        attn_mom_new.astype(low),
        mlp_whole,
        jnp.concatenate([vector_local, padding], axis=0),
        vectors[0],
        normed_part,
        x_low,
        grad_mid_mine,
        out_part,
        middle,
        vectors[7],
        attn_w,
        mlp_w,
        line,
    )
    vector_grads = vector_sum[: vector_local.shape[0]]
    vector_mom_new = 0.5 * vector_mom + vector_grads
    vector_new = vectors - 0.1 / math.sqrt(total_tokens) * vector_mom_new
    return (
        output,
        grad_tokens,
        attn_mom_new,
        attn_new,
        mlp_mom_new,
        mlp_new,
        vector_mom_new,
        vector_new,
    )


def solution(mesh):
    in_specs = (
        P(("dp", "tensor"), None),
        P(("dp", "tensor"), None),
        P("dp"),
        P(None, "dp", "tensor"),
        P(None, "dp", "tensor"),
        P(),
        P(None, "dp", "tensor"),
        P(None, "dp", "tensor"),
        P(),
    )
    out_specs = (
        P(("dp", "tensor"), None),
        P(("dp", "tensor"), None),
        P(None, "dp", "tensor"),
        P(None, "dp", "tensor"),
        P(None, "dp", "tensor"),
        P(None, "dp", "tensor"),
        P(),
        P(),
    )
    chips_of_two = (mesh.shape["dp"], mesh.shape["tensor"]) == (8, 4)
    return jax.shard_map(
        on_chip_pair if chips_of_two else on_device, mesh=mesh, in_specs=in_specs, out_specs=out_specs, check_vma=False
    )
```

```python
import functools
import math

import jax
import jax.numpy as jnp
from jax import lax
from jax.experimental import pallas as pl
from jax.experimental.pallas import tpu as pltpu
from jax.sharding import PartitionSpec as P

D = 1024
HEADS = 16
HD = 64
FF = 4096
SEQ = 1024
NS_STEPS = 5
MESH = pl.DeviceIdType.MESH


coeff_a = 3.4445
coeff_b = -4.775
coeff_c = 2.0315


def norm_rows(row_data, gain, shift):
    center = jnp.mean(row_data, axis=-1, keepdims=True)
    centred = row_data - center
    spread = jnp.mean(centred * centred, axis=-1, keepdims=True)
    return centred * lax.rsqrt(spread + 1e-05) * gain + shift


def gelu_tanh(values):
    return jax.nn.gelu(values, approximate=True)


def contract_last(left, right):
    return lax.dot_general(
        left, right, (((1,), (1,)), ((), ())), preferred_element_type=jnp.float32
    )


def contract_first(left, right):
    return lax.dot_general(
        left, right, (((0,), (0,)), ((), ())), preferred_element_type=jnp.float32
    )


def head_slopes(first_head, head_count):
    head_ids = (first_head + jnp.arange(head_count)).astype(jnp.float32)
    return jnp.exp2(-(8.0 / HEADS) * (head_ids + 1.0))


def masked_scores(row_query, key_rows, row_segs, seg_ids, row_start, slopes):
    scores = jnp.einsum("qhd,khd->hqk", row_query, key_rows, preferred_element_type=jnp.float32) * (
        1.0 / math.sqrt(HD)
    )
    query_pos = row_start + jnp.arange(row_query.shape[0])
    key_pos = jnp.arange(key_rows.shape[0])
    distance = (query_pos[:, None] - key_pos[None, :]).astype(jnp.float32)
    scores = scores - slopes[:, None, None] * distance[None]
    same_doc = (
        (row_segs[:, None] == seg_ids[None, :])
        & (row_segs[:, None] > 0)
        & (key_pos[None, :] <= query_pos[:, None])
    )
    allowed = same_doc | (key_pos[None, :] == query_pos[:, None])
    return jnp.where(allowed[None], scores, -1e30)


def attend_forward(query, key_rows, value_rows, seg_ids, slopes, row_block):
    length = key_rows.shape[0]

    def one_block(row_start):
        row_query = lax.dynamic_slice_in_dim(query, row_start, row_block, 0)
        row_segs = lax.dynamic_slice_in_dim(seg_ids, row_start, row_block, 0)
        scores = masked_scores(row_query, key_rows, row_segs, seg_ids, row_start, slopes)
        row_max = jnp.max(scores, axis=-1, keepdims=True)
        exp_scores = jnp.exp(scores - row_max)
        row_total = jnp.sum(exp_scores, axis=-1, keepdims=True)
        attn_probs = (exp_scores / row_total).astype(jnp.bfloat16)
        mixed = jnp.einsum(
            "hqk,khd->qhd", attn_probs, value_rows, preferred_element_type=jnp.float32
        )
        return (mixed.astype(jnp.bfloat16), (row_max + jnp.log(row_total))[..., 0])

    block_starts = jnp.arange(length // row_block) * row_block
    mixed, log_sums = lax.map(one_block, block_starts)
    return (mixed.reshape(length, -1), log_sums)


def attend_backward(query, key_rows, value_rows, seg_ids, log_sums, grad_mixed, slopes, row_block):
    length, head_count, head_dim = key_rows.shape
    factor = 1.0 / math.sqrt(HD)

    def one_block(carry, pieces):
        row_start, row_lse = pieces
        row_query = lax.dynamic_slice_in_dim(query, row_start, row_block, 0)
        row_grad = lax.dynamic_slice_in_dim(grad_mixed, row_start, row_block, 0)
        row_segs = lax.dynamic_slice_in_dim(seg_ids, row_start, row_block, 0)
        scores = masked_scores(row_query, key_rows, row_segs, seg_ids, row_start, slopes)
        attn_probs = jnp.exp(scores - row_lse[:, :, None])
        grad_probs = jnp.einsum(
            "qhd,khd->hqk", row_grad, value_rows, preferred_element_type=jnp.float32
        )
        inner = jnp.sum(grad_probs * attn_probs, axis=-1, keepdims=True)
        grad_scores = (attn_probs * (grad_probs - inner)).astype(jnp.bfloat16)
        grad_query = (
            jnp.einsum("hqk,khd->qhd", grad_scores, key_rows, preferred_element_type=jnp.float32)
            * factor
        )
        grad_keys = (
            carry[0]
            + jnp.einsum("hqk,qhd->khd", grad_scores, row_query, preferred_element_type=jnp.float32)
            * factor
        )
        grad_values = carry[1] + jnp.einsum(
            "hqk,qhd->khd",
            attn_probs.astype(jnp.bfloat16),
            row_grad,
            preferred_element_type=jnp.float32,
        )
        return ((grad_keys, grad_values), grad_query)

    empty = jnp.zeros((length, head_count, head_dim), jnp.float32)
    block_starts = jnp.arange(length // row_block) * row_block
    (grad_keys, grad_values), grad_query = lax.scan(
        one_block, (empty, empty), (block_starts, log_sums)
    )
    return (
        grad_query.reshape(length, -1),
        grad_keys.reshape(length, -1),
        grad_values.reshape(length, -1),
    )


def newton_rows(row_iterate):
    for repeat in range(NS_STEPS + 1):
        whole_iterate = lax.all_gather(row_iterate, "tensor", axis=0, tiled=True)
        if repeat == NS_STEPS:
            break
        square_rows = contract_last(row_iterate, whole_iterate).astype(jnp.bfloat16)
        whole_square = lax.all_gather(square_rows, "tensor", axis=0, tiled=True)
        poly_rows = (
            coeff_b * square_rows.astype(jnp.float32)
            + coeff_c * jnp.dot(square_rows, whole_square, preferred_element_type=jnp.float32)
        ).astype(jnp.bfloat16)
        row_iterate = (
            coeff_a * row_iterate.astype(jnp.float32)
            + jnp.dot(poly_rows, whole_iterate, preferred_element_type=jnp.float32)
        ).astype(jnp.bfloat16)
    return whole_iterate


def on_device(tokens, cotangent, segments, attn_w, mlp_w, vectors, attn_mom, mlp_mom, vector_mom):
    tensor_size = lax.axis_size("tensor")
    dp_size = lax.axis_size("dp")
    tensor_index = lax.axis_index("tensor")
    dp_index = lax.axis_index("dp")
    row_count = tokens.shape[0]
    model_width = tokens.shape[1]
    local_width = attn_w.shape[2]
    local_hidden = mlp_w.shape[2]
    head_count = local_width // HD
    row_block = min(512, SEQ)
    total_tokens = row_count * tensor_size * dp_size
    gathered_attn, gathered_mlp = (
        lax.all_gather(attn_w.astype(jnp.bfloat16), "dp", axis=1, tiled=True),
        lax.all_gather(mlp_w.astype(jnp.bfloat16), "dp", axis=1, tiled=True),
    )
    hidden_bias = vectors[8:].reshape(-1)
    query_bias = lax.dynamic_slice_in_dim(vectors[2], tensor_index * local_width, local_width)
    value_bias = lax.dynamic_slice_in_dim(vectors[3], tensor_index * local_width, local_width)
    x_rows = tokens.astype(jnp.float32)
    normed, pull_first = jax.vjp(norm_rows, x_rows, vectors[0], vectors[1])
    all_normed = lax.all_gather(normed.astype(jnp.bfloat16), "tensor", axis=0, tiled=True)
    seq_count = all_normed.shape[0] // SEQ
    projected = jnp.einsum(
        "td,mdc->mtc", all_normed, gathered_attn[:3], preferred_element_type=jnp.float32
    )
    query = (projected[0] + query_bias).astype(jnp.bfloat16)
    key_rows = projected[1].astype(jnp.bfloat16)
    value_rows = (projected[2] + value_bias).astype(jnp.bfloat16)
    slopes = head_slopes(tensor_index * head_count, head_count)
    seq_shape = (seq_count, SEQ, head_count, HD)
    seq_segs = segments.reshape(seq_count, SEQ)

    def forward_seq(pieces):
        return attend_forward(pieces[0], pieces[1], pieces[2], pieces[3], slopes, row_block)

    mixed, log_sums = lax.map(
        forward_seq,
        (
            query.reshape(seq_shape),
            key_rows.reshape(seq_shape),
            value_rows.reshape(seq_shape),
            seq_segs,
        ),
    )
    mixed = mixed.reshape(-1, local_width)
    w_out = gathered_attn[3]
    middle = (
        x_rows
        + lax.psum_scatter(
            contract_last(mixed, w_out).astype(jnp.bfloat16),
            "tensor",
            scatter_dimension=0,
            tiled=True,
        ).astype(jnp.float32)
        + vectors[4]
    )
    hidden_normed, pull_second = jax.vjp(norm_rows, middle, vectors[5], vectors[6])
    hidden_low = hidden_normed.astype(jnp.bfloat16)
    grad_rows = cotangent.astype(jnp.float32)
    all_hidden = lax.all_gather(hidden_low, "tensor", axis=0, tiled=True)
    w_up = gathered_mlp[0]
    w_down = gathered_mlp[1]
    bias_local = lax.dynamic_slice_in_dim(hidden_bias, tensor_index * local_hidden, local_hidden)
    hidden_pre = jnp.dot(all_hidden, w_up, preferred_element_type=jnp.float32) + bias_local
    act_float, gelu_pull = jax.vjp(gelu_tanh, hidden_pre)
    hidden_act = act_float.astype(jnp.bfloat16)
    output = (
        middle
        + lax.psum_scatter(
            contract_last(hidden_act, w_down).astype(jnp.bfloat16),
            "tensor",
            scatter_dimension=0,
            tiled=True,
        ).astype(jnp.float32)
        + vectors[7]
    )
    all_grad = lax.all_gather(grad_rows.astype(jnp.bfloat16), "tensor", axis=0, tiled=True)
    grad_down = contract_first(all_grad, hidden_act)
    grad_act = jnp.dot(all_grad, w_down, preferred_element_type=jnp.float32)
    grad_pre = gelu_pull(grad_act)[0].astype(jnp.bfloat16)
    grad_up = contract_first(all_hidden, grad_pre)
    bias_part = jnp.sum(grad_pre, axis=0, dtype=jnp.float32)
    hidden_grad = lax.dynamic_update_slice_in_dim(
        jnp.zeros(hidden_bias.shape, jnp.float32), bias_part, tensor_index * local_hidden, 0
    )
    grad_hidden_in = lax.psum_scatter(
        contract_last(grad_pre, w_up).astype(jnp.bfloat16),
        "tensor",
        scatter_dimension=0,
        tiled=True,
    ).astype(jnp.float32)
    mlp_grads = jnp.stack([grad_up, grad_down])
    second_grads = pull_second(grad_hidden_in)
    grad_middle = grad_rows + second_grads[0]
    all_grad_mid = lax.all_gather(grad_middle.astype(jnp.bfloat16), "tensor", axis=0, tiled=True)
    grad_out_w = contract_first(all_grad_mid, mixed)
    grad_mixed = jnp.dot(all_grad_mid, w_out, preferred_element_type=jnp.float32).astype(
        jnp.bfloat16
    )

    def backward_seq(pieces):
        return attend_backward(
            pieces[0], pieces[1], pieces[2], pieces[3], pieces[4], pieces[5], slopes, row_block
        )

    grad_query, grad_keys, grad_values = lax.map(
        backward_seq,
        (
            query.reshape(seq_shape),
            key_rows.reshape(seq_shape),
            value_rows.reshape(seq_shape),
            seq_segs,
            log_sums,
            grad_mixed.reshape(seq_shape),
        ),
    )
    grad_qkv = (
        jnp.stack([grad_query, grad_keys, grad_values])
        .reshape(3, -1, local_width)
        .astype(jnp.bfloat16)
    )
    grad_proj_w = jnp.einsum(
        "td,mtc->mdc", all_normed, grad_qkv, preferred_element_type=jnp.float32
    )
    bias_sums = jnp.sum(grad_qkv, axis=1, dtype=jnp.float32)
    grad_normed = lax.psum_scatter(
        jnp.einsum(
            "mtc,mdc->td", grad_qkv, gathered_attn[:3], preferred_element_type=jnp.float32
        ).astype(jnp.bfloat16),
        "tensor",
        scatter_dimension=0,
        tiled=True,
    ).astype(jnp.float32)
    first_grads = pull_first(grad_normed)
    grad_tokens = grad_middle + first_grads[0]

    def placed(piece, full_size, offset):
        return lax.dynamic_update_slice_in_dim(
            jnp.zeros((full_size,), jnp.float32), piece, offset, 0
        )

    width_offset = tensor_index * local_width
    vector_rows = jnp.stack(
        [
            first_grads[1],
            first_grads[2],
            placed(bias_sums[0], model_width, width_offset),
            placed(bias_sums[2], model_width, width_offset),
            jnp.sum(grad_middle, axis=0),
            second_grads[1],
            second_grads[2],
            jnp.sum(grad_rows, axis=0),
        ]
    )
    vector_local = jnp.concatenate([vector_rows, hidden_grad.reshape(4, model_width)], axis=0)
    attn_grads = jnp.concatenate([grad_proj_w, grad_out_w[None]], axis=0)
    attn_sum, mlp_sum = (
        lax.psum_scatter(
            attn_grads.astype(jnp.bfloat16), "dp", scatter_dimension=1, tiled=True
        ).astype(jnp.float32),
        lax.psum_scatter(
            mlp_grads.astype(jnp.bfloat16), "dp", scatter_dimension=1, tiled=True
        ).astype(jnp.float32),
    )
    attn_mom_new = 0.5 * attn_mom + attn_sum
    mlp_mom_new = 0.5 * mlp_mom + mlp_sum
    attn_round = attn_mom_new.astype(jnp.bfloat16)
    mlp_round = mlp_mom_new.astype(jnp.bfloat16)
    attn_float = attn_round.astype(jnp.float32)
    mlp_float = mlp_round.astype(jnp.float32)
    norm_parts = jnp.concatenate(
        [jnp.sum(attn_float * attn_float, axis=(1, 2)), jnp.sum(mlp_float * mlp_float, axis=(1, 2))]
    )
    vector_grads, norm_sums = lax.psum((vector_local, norm_parts), ("dp", "tensor"))
    frob_norms = jnp.sqrt(norm_sums)
    owners = [order * dp_size // 6 for order in range(6)]
    owned_norm = jnp.zeros((), jnp.float32)
    for order in range(6):
        owned_norm = owned_norm + jnp.where(dp_index == owners[order], frob_norms[order], 0.0)
    block_rows = attn_w.shape[1]
    slice_rows = model_width // tensor_size
    full_cols = local_hidden * tensor_size
    rows_attn, rows_mlp = (
        lax.all_gather(attn_round, "tensor", axis=2, tiled=True),
        lax.all_gather(mlp_round, "tensor", axis=2, tiled=True),
    )
    padded_attn = jnp.pad(rows_attn, ((0, 0), (0, 0), (0, full_cols - model_width)))
    all_rows = jnp.concatenate([padded_attn, rows_mlp], axis=0)
    outgoing = jnp.zeros((dp_size, block_rows, full_cols), jnp.bfloat16)
    for order in range(6):
        outgoing = outgoing.at[owners[order]].set(all_rows[order])
    incoming = lax.all_to_all(outgoing, "dp", split_axis=0, concat_axis=0, tiled=True)
    owned_whole = incoming.reshape(model_width, full_cols)
    mine = lax.dynamic_slice_in_dim(owned_whole, tensor_index * slice_rows, slice_rows, 0)
    attn_col = tensor_index * local_width
    row_iterate = (mine.astype(jnp.float32) / (owned_norm + 1e-06)).astype(jnp.bfloat16)
    result = newton_rows(row_iterate)
    returned = lax.all_to_all(
        result.reshape(dp_size, block_rows, full_cols),
        "dp",
        split_axis=0,
        concat_axis=0,
        tiled=True,
    )
    attn_blocks = []
    for order in range(4):
        piece = lax.dynamic_slice_in_dim(returned[owners[order]], attn_col, local_width, 1)
        attn_blocks.append(attn_w[order] - piece.astype(jnp.float32))
    mlp_blocks = []
    for order in range(2):
        piece = lax.dynamic_slice_in_dim(
            returned[owners[4 + order]], tensor_index * local_hidden, local_hidden, 1
        )
        mlp_blocks.append(mlp_w[order] - math.sqrt(FF / D) * piece.astype(jnp.float32))
    attn_new = jnp.stack(attn_blocks)
    mlp_new = jnp.stack(mlp_blocks)
    vector_mom_new = 0.5 * vector_mom + vector_grads
    vector_new = vectors - 0.1 / math.sqrt(total_tokens) * vector_mom_new
    return (
        output.astype(jnp.bfloat16),
        grad_tokens,
        attn_mom_new,
        attn_new,
        mlp_mom_new,
        mlp_new,
        vector_mom_new,
        vector_new,
    )


CORES = 2


class Place:
    def __init__(self):
        self.dp = lax.axis_index("dp")
        self.tensor = lax.axis_index("tensor")
        self.line = lax.axis_size("tensor")
        self.devices = lax.axis_size("dp") * self.line
        self.me = self.dp * self.line + self.tensor
        self.core = lax.rem(self.dp, 2)
        self.chip = self.dp // 2
        self.x = lax.rem(self.chip, 2)
        self.y = self.chip // 2
        self.twin = (self.dp + 1 - 2 * self.core, self.tensor)
        self.across_x = (self.dp + 2 - 4 * self.x, self.tensor)
        self.across_y = (self.dp + 4 - 8 * self.y, self.tensor)
        self.right = (self.dp, self.tensor + 1)
        self.left = (self.dp, self.tensor - 1)
        self.stays = self.core == lax.rem(self.tensor, 2)
        self.corner = (self.dp + 1 - 2 * self.core, self.tensor - 1 + 2 * self.core)


    def of(self, index):
        return (index // self.line, lax.rem(index, self.line))

    def index(self, x, y, core, z):
        return ((2 * y + x) * 2 + core) * self.line + z


def greet(place, line):
    barrier = pltpu.get_barrier_semaphore()

    def signal(device):
        pl.semaphore_signal(barrier, inc=1, device_id=device, device_id_type=MESH)

    signal(place.twin)
    signal(place.across_x)
    signal(place.across_y)

    for other in range(line):

        @pl.when(place.tensor != other)
        def _():
            signal((place.dp, other))

    @pl.when(jnp.logical_not(place.stays))
    def _():
        signal(place.corner)

    pl.semaphore_wait(barrier, jnp.where(place.stays, 3 + line - 1, 3 + line))


OWNERS = ((1, 0, 0), (1, 0, 3), (0, 1, 0), (0, 1, 3), (0, 0, 1), (1, 1, 2))


def greet_all(place):
    barrier = pltpu.get_barrier_semaphore()

    def meet(step, carry):
        pl.semaphore_signal(
            barrier, inc=1, device_id=place.of(lax.rem(place.me + step, place.devices)), device_id_type=MESH
        )
        return carry

    lax.fori_loop(1, place.devices, meet, 0)
    pl.semaphore_wait(barrier, place.devices - 1)


def is_one_of(value, options):
    found = value < 0
    for option in options:
        found = found | (value == option)
    return found


def sides(order, line):
    oz = OWNERS[order][2]
    above, below = list(range(oz + 1, line)), list(range(oz))
    return (above, below) if len(above) > len(below) else (below, above)


def rows_held(place, whole, index, rows, width):
    dp, tensor = place.of(index)
    return whole.at[pl.ds(pl.multiple_of(dp * rows, rows), rows), columns(tensor * width, width)]


def remote(place, source, target, send, recv, index):
    return pltpu.make_async_remote_copy(
        src_ref=source,
        dst_ref=target,
        send_sem=send,
        recv_sem=recv,
        device_id=place.of(index),
        device_id_type=MESH,
    )


class Collect:
    @staticmethod
    def scratch():
        dma = pltpu.SemaphoreType.DMA
        return [dma((2, 2)), dma((1,)), dma((2, 2)), dma((2, 2))]

    SCRATCH = 4

    def __init__(self, place, source, whole, scratch):
        self.place, self.source, self.whole = place, source, whole
        self.send_sem, self.sem, self.pass_send, self.pass_recv = scratch
        self.rows, self.width = source.shape[1], source.shape[2] // 2

    def owner(self, order, half):
        ox, oy, oz = OWNERS[order]
        return self.place.index(ox, oy, half, oz)

    def piece(self, order, half):
        return self.source.at[order - 4, :, half * self.width : (half + 1) * self.width]

    def held(self, index):
        return rows_held(self.place, self.whole, index, self.rows, self.width)

    def direct(self, order, half):
        send = self.send_sem.at[order - 4, half]
        return remote(
            self.place, self.piece(order, half), self.held(self.place.me), send, self.sem.at[0], self.owner(order, half)
        )

    def own(self, order, half):
        return pltpu.make_async_copy(self.piece(order, half), self.held(self.place.me), self.sem.at[0])

    def by_way(self, order):
        place = self.place
        ox, oy, oz = OWNERS[order]
        lone = is_one_of(place.tensor, sides(order, place.line)[1])
        return (place.y != oy) & (place.tensor != oz) & ((place.x != ox) | lone)

    def to_way(self, order, half):
        place = self.place
        ox, oy, _ = OWNERS[order]
        which = jnp.where(place.x == ox, 1, 0)
        return remote(
            place,
            self.piece(order, half),
            self.held(place.me),
            self.send_sem.at[order - 4, half],
            self.pass_recv.at[which, place.core],
            place.index(ox, oy, half, place.tensor),
        )

    def passed(self, order, which, cores):
        ox, oy, _ = OWNERS[order]
        return self.place.index(1 - ox if which == 0 else ox, 1 - oy, cores, self.place.tensor)

    def pass_in(self, order, which, cores):
        index = self.passed(order, which, cores)
        region = self.held(index)
        sems = self.pass_send.at[which, cores], self.pass_recv.at[which, cores]
        return remote(self.place, region, region, *sems, index)

    def pass_on(self, order, which, cores):
        ox, oy, oz = OWNERS[order]
        region = self.held(self.passed(order, which, cores))
        owner = self.place.index(ox, oy, self.place.core, oz)
        return remote(self.place, region, region, self.pass_send.at[which, cores], self.sem.at[0], owner)

    def when_passing(self, action):
        place = self.place
        for order in (5, 4):
            ox, oy, _ = OWNERS[order]
            far, lone = sides(order, place.line)
            for which, planes in ((0, far + lone), (1, lone)):

                @pl.when((place.x == ox) & (place.y == oy) & is_one_of(place.tensor, planes))
                def _():
                    for cores in range(2):
                        action(order, which, cores)

    def each(self, action_way, action_direct, action_own):
        for order in (5, 4):
            for half in range(2):
                mine = self.place.me == self.owner(order, half)

                @pl.when(self.by_way(order))
                def _():
                    action_way(order, half)

                @pl.when(jnp.logical_not(mine) & jnp.logical_not(self.by_way(order)))
                def _():
                    action_direct(order, half)

                @pl.when(mine)
                def _():
                    action_own(order, half)

    def start(self):
        self.each(
            lambda *at: self.to_way(*at).start(), lambda *at: self.direct(*at).start(), lambda *at: self.own(*at).start()
        )

    def forward(self):
        def action(*at):
            self.pass_in(*at).wait_recv()
            self.pass_on(*at).start()

        self.when_passing(action)

    def finish(self):
        self.each(
            lambda *at: self.to_way(*at).wait_send(),
            lambda *at: self.direct(*at).wait_send(),
            lambda *at: None,
        )
        self.when_passing(lambda *at: self.pass_on(*at).wait_send())
        for order in (5, 4):
            for half in range(2):

                @pl.when(self.place.me == self.owner(order, half))
                def _():
                    pltpu.make_async_copy(self.whole, self.whole, self.sem.at[0]).wait()


def columns(start, size):
    return pl.ds(pl.multiple_of(start, 128), size)


class RowSwap:
    PARTS = 4

    @staticmethod
    def scratch():
        return [pltpu.SemaphoreType.DMA((1,)), pltpu.SemaphoreType.DMA((2 + 2 * RowSwap.PARTS,))]

    def __init__(self, place, rows_ref, whole_ref, scratch):
        self.place, self.rows_ref, self.whole_ref = place, rows_ref, whole_ref
        self.own_sem, self.sem = scratch
        self.size = rows_ref.shape[0]

    def at(self, core):
        return self.whole_ref.at[pl.ds(pl.multiple_of(core * self.size, self.size), self.size), :]

    def copy(self, slot, source, target, device):
        return pltpu.make_async_remote_copy(
            src_ref=source,
            dst_ref=target,
            send_sem=self.sem.at[slot],
            recv_sem=self.sem.at[slot + 1],
            device_id=device,
            device_id_type=MESH,
        )

    def own(self):
        return pltpu.make_async_copy(self.rows_ref, self.at(self.place.core), self.own_sem.at[0])

    def away(self, part):
        count = self.size // self.PARTS
        start = pl.multiple_of((1 - self.place.core) * self.size + part * count, count)
        source = self.rows_ref.at[part * count : (part + 1) * count, :]
        return self.copy(2 + 2 * part, source, self.whole_ref.at[pl.ds(start, count), :], self.place.corner)

    def hand_own(self):
        return self.copy(0, self.rows_ref, self.at(self.place.core), self.place.twin)

    def hand_got(self):
        return self.copy(0, self.at(self.place.core), self.at(self.place.core), self.place.twin)

    def start(self, parts):
        if 0 in parts:

            @pl.when(self.place.stays)
            def _():
                self.own().start()
                self.hand_own().start()

        @pl.when(jnp.logical_not(self.place.stays))
        def _():
            for part in parts:
                self.away(part).start()

    def step(self):
        @pl.when(jnp.logical_not(self.place.stays))
        def _():
            for part in range(self.PARTS):
                self.away(part).wait()
            self.hand_got().start()

    def end(self):
        @pl.when(self.place.stays)
        def _():
            self.own().wait()

        self.hand_got().wait()


class CornerMove:
    PARTS = 4

    @staticmethod
    def scratch():
        return [pltpu.SemaphoreType.DMA((1,)), pltpu.SemaphoreType.DMA((2, CornerMove.PARTS))]

    def __init__(self, place, rows_ref, target_ref, scratch):
        self.place, self.rows_ref, self.target_ref = place, rows_ref, target_ref
        self.own_sem, self.sem = scratch

    def own(self):
        return pltpu.make_async_copy(self.rows_ref, self.target_ref, self.own_sem.at[0])

    def away(self, part):
        count = self.rows_ref.shape[0] // self.PARTS
        at = slice(part * count, (part + 1) * count)
        return pltpu.make_async_remote_copy(
            src_ref=self.rows_ref.at[at, :],
            dst_ref=self.target_ref.at[at, :],
            send_sem=self.sem.at[0, part],
            recv_sem=self.sem.at[1, part],
            device_id=self.place.corner,
            device_id_type=MESH,
        )

    def start(self):
        @pl.when(self.place.stays)
        def _():
            self.own().start()

        @pl.when(jnp.logical_not(self.place.stays))
        def _():
            for part in range(self.PARTS):
                self.away(part).start()

    def wait(self):
        @pl.when(self.place.stays)
        def _():
            self.own().wait()

        @pl.when(jnp.logical_not(self.place.stays))
        def _():
            for part in range(self.PARTS):
                self.away(part).wait()


class WeightGather:
    def __init__(self, place, line, groups, scratch):
        self.place, self.line, self.groups = place, line, groups
        self.own_sem, self.send_sem, self.recv_sem = scratch
        self.last = len(groups) - 1
        self.to_right, self.to_left = 1, line
        self.half_x, self.half_y, self.rest_y, self.rest_x = (2 * line - 1 + k for k in range(4))

    @staticmethod
    def scratch(count, line):
        dma = pltpu.SemaphoreType.DMA
        return [dma((count,)), dma((count, 2 * line + 3)), dma((count, 2 * line + 3))]

    def copy(self, group, slot, source, target, device):
        return pltpu.make_async_remote_copy(
            src_ref=source,
            dst_ref=target,
            send_sem=self.send_sem.at[group, slot],
            recv_sem=self.recv_sem.at[group, slot],
            device_id=device,
            device_id_type=MESH,
        )

    def same(self, group, slot, region, device):
        return self.copy(group, slot, region, region, device)

    def chunk(self, group, index):
        ref, width, _ = self.groups[group]
        cols = columns(index * width, width)
        if group == self.last:
            return ref.at[:, :, :, :, :, cols]
        return ref.at[:, self.place.y, self.place.x, :, :, cols]

    def corner(self, group, ys, xs, half):
        ref, width, _ = self.groups[group]
        if group == self.last:
            return ref.at[:, ys, xs, half, :, columns(self.place.tensor * width, width)]
        return ref.at[:, ys, xs, half]

    def entry(self, group, half):
        ref, width, _ = self.groups[group]
        return ref.at[:, self.place.y, self.place.x, half, :, columns(self.place.tensor * width, width)]

    def own(self, group):
        core = self.place.core
        return pltpu.make_async_copy(self.groups[group][2](core), self.entry(group, core), self.own_sem.at[group])

    def first(self, group):
        core = self.place.core
        return self.copy(group, 0, self.groups[group][2](1 - core), self.entry(group, core), self.place.twin)

    def begin(self, group):
        self.own(group).start()
        self.first(group).start()

    def enter(self, group):
        self.own(group).wait()
        self.same(group, 0, self.entry(group, 1 - self.place.core), self.place.twin).wait_recv()

    def hop(self, group, step, left):
        t = self.place.tensor
        index = t + step - 1 if left else t - step + 1
        slot = (self.to_left if left else self.to_right) + step - 1
        return self.same(group, slot, self.chunk(group, index), self.place.left if left else self.place.right)

    def arrival(self, group, step, left):
        t = self.place.tensor
        index = t + step if left else t - step
        slot = (self.to_left if left else self.to_right) + step - 1
        return self.same(group, slot, self.chunk(group, index), self.place.right if left else self.place.left)

    def sends(self, step, left):
        t, line = self.place.tensor, self.line
        return (t > 0) & (t + step <= line) if left else (t < line - 1) & (t >= step - 1)

    def line_start(self, group):
        for left in (False, True):

            @pl.when(self.sends(1, left))
            def _():
                self.hop(group, 1, left).start()

    def line_step(self, group, step):
        t, line = self.place.tensor, self.line
        for left in (False, True):

            @pl.when(t + step <= line - 1 if left else t >= step)
            def _():
                self.arrival(group, step, left).wait_recv()

            if step < line - 1:

                @pl.when(self.sends(step + 1, left))
                def _():
                    self.hop(group, step + 1, left).start()

    def line_most(self, group):
        for step in range(1, self.line - 1):
            self.line_step(group, step)

    def line_end(self, group):
        self.line_step(group, self.line - 1)

    def plane_start(self, group):
        place = self.place
        self.same(group, self.half_x, self.corner(group, place.y, place.x, 0), place.across_x).start()
        self.same(group, self.half_y, self.corner(group, place.y, place.x, 1), place.across_y).start()

    def plane_step(self, group):
        place, both = self.place, pl.ds(0, 2)
        self.same(group, self.half_x, self.corner(group, place.y, 1 - place.x, 0), place.across_x).wait_recv()
        self.same(group, self.rest_y, self.corner(group, place.y, both, 0), place.across_y).start()
        self.same(group, self.half_y, self.corner(group, 1 - place.y, place.x, 1), place.across_y).wait_recv()
        self.same(group, self.rest_x, self.corner(group, both, place.x, 1), place.across_x).start()

    def plane_end(self, group):
        place, both = self.place, pl.ds(0, 2)
        self.same(group, self.rest_y, self.corner(group, 1 - place.y, both, 0), place.across_y).wait_recv()
        self.same(group, self.rest_x, self.corner(group, both, 1 - place.x, 1), place.across_x).wait_recv()

    def wait_sends(self, group):
        place, both = self.place, pl.ds(0, 2)
        self.first(group).wait_send()
        for step in range(1, self.line):
            for left in (False, True):

                @pl.when(self.sends(step, left))
                def _():
                    self.hop(group, step, left).wait_send()

        self.same(group, self.half_x, self.corner(group, place.y, place.x, 0), place.across_x).wait_send()
        self.same(group, self.half_y, self.corner(group, place.y, place.x, 1), place.across_y).wait_send()
        self.same(group, self.rest_y, self.corner(group, place.y, both, 0), place.across_y).wait_send()
        self.same(group, self.rest_x, self.corner(group, both, place.x, 1), place.across_x).wait_send()


def add_blocks(target, sources):
    lead, rows = target.shape[:-2], target.shape[-2]
    per = rows // 32

    def body(step, carry):
        block, at = step // per, []
        for size in lead[::-1]:
            at.insert(0, lax.rem(block, size))
            block = block // size
        at = tuple(at) + (pl.ds(pl.multiple_of(lax.rem(step, per) * 32, 32), 32),)
        total = sources[0][at].astype(jnp.float32)
        for source in sources[1:]:
            total = total + source[at].astype(jnp.float32)
        target[at] = total.astype(target.dtype)
        return carry

    lax.fori_loop(0, math.prod(lead) * per, body, 0, unroll=4)


class PlaneSum:
    @staticmethod
    def scratch(count, rows, width):
        pair = pltpu.VMEM((count, 2, rows, width), jnp.bfloat16)
        single = pltpu.VMEM((count, rows, width), jnp.bfloat16)
        dma = pltpu.SemaphoreType.DMA
        return [pair] * 4 + [single] * 2 + [dma((2,)), dma((4,)), dma((4,))]

    SCRATCH = 9

    def __init__(self, place, source, result, scratch):
        self.place, self.source, self.result = place, source, result
        self.own, self.got, self.last = scratch[0:2], scratch[2:4], scratch[4:6]
        self.own_sem, self.send_sem, self.recv_sem = scratch[6:9]

    def copy(self, slot, source, target, device):
        return pltpu.make_async_remote_copy(
            src_ref=source,
            dst_ref=target,
            send_sem=self.send_sem.at[slot],
            recv_sem=self.recv_sem.at[slot],
            device_id=device,
            device_id_type=MESH,
        )

    def cut(self, index, mine):
        both, place = pl.ds(0, 2), self.place
        if index == 0:
            return self.source.at[:, place.y if mine else 1 - place.y, both, 0]
        return self.source.at[:, both, place.x if mine else 1 - place.x, 1]

    def load(self, index):
        return pltpu.make_async_copy(self.cut(index, True), self.own[index], self.own_sem.at[index])

    def first(self, index):
        device = self.place.across_x if index else self.place.across_y
        return self.copy(index, self.cut(index, False), self.got[index], device)

    def second(self, index):
        mine = self.place.y if index else self.place.x
        device = self.place.across_y if index else self.place.across_x
        return self.copy(2 + index, self.own[index].at[:, 1 - mine], self.last[index], device)

    def start(self):
        for index in range(2):
            self.first(index).start()
            self.load(index).start()

    def one(self):
        for index in range(2):
            mine = self.place.y if index else self.place.x
            self.load(index).wait()
            self.first(index).wait_recv()
            own, got = self.own[index], self.got[index]
            add_blocks(own.at[:, 1 - mine], (own.at[:, 1 - mine], got.at[:, 1 - mine]))
            self.second(index).start()
            add_blocks(own.at[:, mine], (own.at[:, mine], got.at[:, mine]))

    def two(self):
        for index in range(2):
            mine = self.place.y if index else self.place.x
            self.second(index).wait_recv()
            add_blocks(self.result.at[:, index], (self.own[index].at[:, mine], self.last[index]))

    def sent(self):
        for index in range(2):
            self.first(index).wait_send()
            self.second(index).wait_send()


class LineSum:
    @staticmethod
    def scratch(shape, line):
        dma = pltpu.SemaphoreType.DMA
        return [pltpu.VMEM(shape, jnp.bfloat16)] * 2 + [dma((2, line)), dma((2, line))]

    SCRATCH = 4

    def __init__(self, place, line, value, result, scratch):
        self.place, self.line, self.value, self.result = place, line, value, result
        self.got = scratch[0:2]
        self.send_sem, self.recv_sem = scratch[2:4]
        self.width = value.shape[-1] // line

    def part(self, ref, index):
        return ref.at[(slice(None),) * (len(ref.shape) - 1) + (slice(index * self.width, (index + 1) * self.width),)]

    def hop(self, index, left):
        return pltpu.make_async_remote_copy(
            src_ref=self.part(self.value, index),
            dst_ref=self.part(self.got[left], index),
            send_sem=self.send_sem.at[left, index],
            recv_sem=self.recv_sem.at[left, index],
            device_id=self.place.left if left else self.place.right,
            device_id_type=MESH,
        )

    def step(self, step):
        for left in range(2):
            for index in range(self.line):
                away = index if left else self.line - 1 - index
                order = step - away
                plane = self.line - 1 - order if left else order
                if order < 0 or (plane <= index if left else plane >= index):
                    continue

                @pl.when(self.place.tensor == plane)
                def _():
                    if order > 0:
                        self.hop(index, left).wait_recv()
                        value = self.part(self.value, index)
                        add_blocks(value, (value, self.part(self.got[left], index)))
                    if away > 0:
                        self.hop(index - 1 if left else index + 1, left).wait_send()
                    self.hop(index, left).start()

    def end(self):
        for index in range(self.line):

            @pl.when(self.place.tensor == index)
            def _():
                sources = [self.part(self.value, index)]
                for left in range(2):
                    if index < self.line - 1 if left else index > 0:
                        self.hop(index, left).wait_recv()
                        sources.append(self.part(self.got[left], index))
                add_blocks(self.result, sources)

    def sent(self):
        for index in range(self.line):

            @pl.when(self.place.tensor == index)
            def _():
                if index > 0:
                    self.hop(index - 1, 1).wait_send()
                if index < self.line - 1:
                    self.hop(index + 1, 0).wait_send()


class HomeCopy:
    def __init__(self, place, value, target, scratch):
        self.place, self.value, self.target = place, value, target
        self.own_sem, self.sem = scratch

    SCRATCH = 2

    @staticmethod
    def scratch():
        return [pltpu.SemaphoreType.DMA((1,)), pltpu.SemaphoreType.DMA((2,))]

    def keep(self):
        return pltpu.make_async_copy(self.value.at[:, self.place.core], self.target, self.own_sem.at[0])

    def give(self):
        return pltpu.make_async_remote_copy(
            src_ref=self.value.at[:, 1 - self.place.core],
            dst_ref=self.target,
            send_sem=self.sem.at[0],
            recv_sem=self.sem.at[1],
            device_id=self.place.twin,
            device_id_type=MESH,
        )

    def start(self):
        self.keep().start()
        self.give().start()

    def wait(self):
        self.keep().wait()
        self.give().wait()


class GroupSum:
    @staticmethod
    def scratch(count, rows, width, line, line_first=False):
        low = jnp.bfloat16
        part = width // line
        done = pltpu.VMEM((count, 2, rows, part), low)
        if line_first:
            whole = (count, 2, 2, 2, rows, width)
            held = [pltpu.VMEM(whole, low), pltpu.VMEM(whole[:-1] + (part,), low), pltpu.SemaphoreType.DMA((1,))]
            plane, along = PlaneSum.scratch(count, rows, part), LineSum.scratch(whole, line)
        else:
            middle = (count, 2, rows, width)
            held = [pltpu.VMEM(middle, low)]
            plane, along = PlaneSum.scratch(count, rows, width), LineSum.scratch(middle, line)
        return held + [done] + plane + along + HomeCopy.scratch()

    def __init__(self, place, line, source, target, scratch, line_first=False):
        scratch = list(scratch)

        def take(count):
            taken = scratch[:count]
            del scratch[:count]
            return taken

        if line_first:
            whole, middle, load_sem = take(3)
            self.load = lambda: pltpu.make_async_copy(source, whole, load_sem.at[0])
        else:
            (middle,) = take(1)
        (done,) = take(1)
        plane, along = take(PlaneSum.SCRATCH), take(LineSum.SCRATCH)
        if line_first:
            self.line = LineSum(place, line, whole, middle, along)
            self.plane = PlaneSum(place, middle, done, plane)
        else:
            self.plane = PlaneSum(place, source, middle, plane)
            self.line = LineSum(place, line, middle, done, along)
        self.home = HomeCopy(place, done, target, take(HomeCopy.SCRATCH))

    def sent(self):
        self.plane.sent()
        self.line.sent()


class VectorSum:
    @staticmethod
    def scratch(shape, line):
        return [
            pltpu.VMEM((4,) + shape, jnp.float32),
            pltpu.VMEM((3,) + shape, jnp.float32),
            pltpu.VMEM((line,) + shape, jnp.float32),
            pltpu.SemaphoreType.DMA((4, max(line, 3))),
        ]

    def __init__(self, place, line, scratch):
        self.place, self.line = place, line
        self.sums, self.got, self.along, self.sem = scratch

    def copy(self, stage):
        place = self.place
        return pltpu.make_async_remote_copy(
            src_ref=self.sums.at[stage],
            dst_ref=self.got.at[stage],
            send_sem=self.sem.at[0, stage],
            recv_sem=self.sem.at[1, stage],
            device_id=(place.twin, place.across_x, place.across_y)[stage],
            device_id_type=MESH,
        )

    def hop(self, other, source):
        return pltpu.make_async_remote_copy(
            src_ref=self.sums.at[3],
            dst_ref=self.along.at[source],
            send_sem=self.sem.at[2, other],
            recv_sem=self.sem.at[3, source],
            device_id=(self.place.dp, other),
            device_id_type=MESH,
        )

    def start(self, value, first_rows):
        self.sums[0] = value
        for index, row in enumerate(first_rows):
            self.sums[0, index : index + 1, :] = row
        self.copy(0).start()

    def step(self, stage):
        self.copy(stage).wait()
        self.sums[stage + 1] = self.sums[stage] + self.got[stage]
        if stage < 2:
            self.copy(stage + 1).start()
            return
        self.along[self.place.tensor] = self.sums[3]
        for other in range(self.line):

            @pl.when(self.place.tensor != other)
            def _():
                self.hop(other, self.place.tensor).start()

    def end(self):
        t = self.place.tensor
        for other in range(self.line):

            @pl.when(t != other)
            def _():
                self.hop(other, t).wait_send()
                self.hop(t, other).wait_recv()

        total = self.along[0]
        for other in range(1, self.line):
            total = total + self.along[other]
        return total


LOG2E = 1.4426950408889634
FAR = 1e32
ROW_BLOCK = 256


def fill_distance(seg_rows, seg_cols, distance):
    def body(step, carry):
        start = pl.multiple_of(step * 64, 64)
        shape = (64, distance.shape[1])
        row = lax.broadcasted_iota(jnp.int32, shape, 0) + start
        col = lax.broadcasted_iota(jnp.int32, shape, 1)
        segs = seg_rows[pl.ds(start, 64), :]
        same = (segs == seg_cols[...]) & (segs > 0) & (col <= row)
        allowed = same | (col == row)
        distance[pl.ds(start, 64), :] = jnp.where(allowed, (row - col).astype(jnp.float32), FAR)
        return carry

    lax.fori_loop(0, distance.shape[0] // 64, body, 0)


def head_lanes(dtype):
    lane = lax.broadcasted_iota(jnp.int32, (1, 2 * HD), 1)
    first = (lane < HD).astype(jnp.float32)
    return (first.astype(dtype), (1.0 - first).astype(dtype))


def attend_group(group, slopes, qkv, mixed, lse, distance):
    length = qkv.shape[1]
    cols = columns(group * 2 * HD, 2 * HD)
    masks = head_lanes(jnp.bfloat16)
    first = head_lanes(jnp.float32)[0] > 0.5
    factor = LOG2E / math.sqrt(HD)
    keys_t = qkv[1, :, cols].T
    values = qkv[2, :, cols]
    for start in range(0, length, ROW_BLOCK):
        stop = start + ROW_BLOCK
        rows = slice(start, stop)
        query = qkv[0, rows, cols]
        parts, sums = [], []
        for head in range(2):
            slope = slopes[2 * group + head] * LOG2E
            scores = jnp.dot(query * masks[head], keys_t[:, :stop], preferred_element_type=jnp.float32)
            scores = scores * factor - slope * distance[rows, :stop]
            top = jnp.max(scores, axis=1, keepdims=True)
            probs = jnp.exp2(scores - top)
            total = jnp.sum(probs, axis=1, keepdims=True)
            out = jnp.dot(probs.astype(jnp.bfloat16), values[:stop], preferred_element_type=jnp.float32)
            parts.append(out / total)
            sums.append(top + jnp.log2(total))
        mixed[rows, cols] = jnp.where(first, parts[0], parts[1]).astype(jnp.bfloat16)
        lse[rows, cols] = jnp.where(first, sums[0], sums[1])


def normalize(rows):
    centred = rows - jnp.mean(rows, axis=1, keepdims=True)
    return centred * lax.rsqrt(jnp.mean(centred * centred, axis=1, keepdims=True) + 1e-05)


def forward_kernel(
    line, attn_ref, mlp_ref, tokens_ref, grads_ref, slopes, seg_rows, seg_cols, qkv_bias, hidden_bias, vectors,
    qkv_w, out_w, up_w, down_w, tokens_out, grads_out, qkv_out, mixed_out, lse_out, normed_out, middle_out,
    hidden_out, act_out, bend_out, *scratch
):
    (x_v, normed, qkv_wv, out_wv, up_wv, qkv, mixed, lse, distance, part, got, middle, hidden, act, bend) = scratch[:15]
    load_sem, store_sem, swap_send, swap_recv = scratch[15:19]
    place = Place()
    narrow, wide = attn_ref.shape[2] // 2, mlp_ref.shape[2] // 4
    size = normed.shape[0]

    def attn_source(index):
        return lambda core: attn_ref.at[index : index + 1, :, columns(core * narrow, narrow)]

    def mlp_source(index, half):
        return lambda core: mlp_ref.at[index : index + 1, :, columns((2 * core + half) * wide, wide)]

    groups = [(qkv_w.at[index : index + 1], narrow, attn_source(index)) for index in range(3)]
    groups.append((out_w, narrow, attn_source(3)))
    groups += [(up_w.at[half : half + 1], wide, mlp_source(0, half)) for half in range(2)]
    groups += [(down_w.at[half : half + 1], wide, mlp_source(1, half)) for half in range(2)]
    query, key, value, outer, up_a, up_b, down_a, down_b = range(8)
    gather = WeightGather(place, line, groups, scratch[19:22])
    tokens = RowSwap(place, tokens_ref, tokens_out, scratch[22:24])
    grads = CornerMove(place, grads_ref, grads_out, scratch[24:26])

    def load(group):
        if group < 3:
            source, target = qkv_w.at[group], qkv_wv.at[group]
        elif group == outer:
            source, target = out_w, out_wv
        else:
            source, target = up_w.at[group - up_a], up_wv.at[group - up_a]
        return pltpu.make_async_copy(source, target, load_sem.at[group])

    x_load = pltpu.make_async_copy(tokens_out, x_v, load_sem.at[7])
    pairs = (
        (qkv, qkv_out),
        (mixed, mixed_out),
        (lse, lse_out),
        (normed, normed_out),
        (middle, middle_out),
        (hidden, hidden_out),
        (act.at[0], act_out.at[0]),
        (act.at[1], act_out.at[1]),
        (bend.at[0], bend_out.at[0]),
        (bend.at[1], bend_out.at[1]),
    )

    def store(index):
        return pltpu.make_async_copy(*pairs[index], store_sem.at[index])

    def normalize_tokens():
        def body(step, carry):
            at = pl.ds(pl.multiple_of(step * 32, 32), 32)
            normal = normalize(x_v[at, :].astype(jnp.float32))
            normed[at, :] = (normal * vectors[0:1, :] + vectors[1:2, :]).astype(jnp.bfloat16)
            return carry

        lax.fori_loop(0, size // 32, body, 0, unroll=4)

    def project(group):
        load(group).wait()
        weight = qkv_wv[group].reshape(size, qkv.shape[2])

        def body(step, carry):
            at = pl.ds(pl.multiple_of(step * 512, 512), 512)
            out = jnp.dot(normed[at, :], weight, preferred_element_type=jnp.float32)
            qkv[group, at, :] = (out + qkv_bias[group : group + 1, :]).astype(jnp.bfloat16)
            return carry

        lax.fori_loop(0, size // 512, body, 0)

    def swap(index):
        at = pl.ds(pl.multiple_of(index * 256, 256), 256)
        return pltpu.make_async_remote_copy(
            src_ref=part.at[at, :],
            dst_ref=got.at[at, :],
            send_sem=swap_send.at[index],
            recv_sem=swap_recv.at[index],
            device_id=place.twin,
            device_id_type=MESH,
        )

    def project_out(index, carry):
        at = pl.ds(pl.multiple_of(index * 256, 256), 256)
        weight = out_wv[0].reshape(size, mixed.shape[1])
        part[at, :] = contract_last(mixed[at, :], weight).astype(jnp.bfloat16)
        swap(index).start()
        return carry

    def add_branch(index, carry):
        swap(index).wait()

        def body(step, carry):
            at = pl.ds(pl.multiple_of(index * 256 + step * 32, 32), 32)
            branch = part[at, :].astype(jnp.float32) + got[at, :].astype(jnp.float32)
            total = x_v[at, :].astype(jnp.float32) + branch + vectors[4:5, :]
            middle[at, :] = total
            hidden[at, :] = (normalize(total) * vectors[5:6, :] + vectors[6:7, :]).astype(jnp.bfloat16)
            return carry

        return lax.fori_loop(0, 8, body, carry, unroll=4)

    def feed(half):
        load(up_a + half).wait()

        def body(step, carry):
            at = pl.ds(pl.multiple_of(step * 256, 256), 256)
            weight = up_wv[half].reshape(size, act.shape[2])
            pre = jnp.dot(hidden[at, :], weight, preferred_element_type=jnp.float32)
            pre = pre + hidden_bias[half : half + 1, :]
            square = pre * pre
            bent = jnp.tanh(0.7978845608 * pre * (1.0 + 0.044715 * square))
            inner = 0.7978845608 * (1.0 + 3.0 * 0.044715 * square)
            act[half, at, :] = (0.5 * pre * (1.0 + bent)).astype(jnp.bfloat16)
            bend[half, at, :] = (0.5 * (1.0 + bent) + 0.5 * pre * (1.0 - bent * bent) * inner).astype(jnp.bfloat16)
            return carry

        lax.fori_loop(0, size // 256, body, 0)
        store(6 + half).start()
        store(8 + half).start()

    greet(place, line)
    for group in (query, down_b, key, value, outer, up_a, up_b, down_a):
        gather.begin(group)
    gather.enter(query)
    gather.line_start(query)
    gather.enter(down_b)
    gather.plane_start(down_b)
    gather.enter(key)
    gather.line_most(query)
    gather.line_start(key)
    tokens.start((0,))
    gather.line_end(query)
    gather.plane_start(query)
    gather.plane_step(down_b)
    gather.enter(value)
    gather.line_most(key)
    gather.line_start(value)
    tokens.start((1,))
    gather.line_end(key)
    gather.plane_step(query)
    gather.plane_start(key)
    gather.plane_end(down_b)
    gather.line_most(value)
    gather.enter(outer)
    gather.line_start(outer)
    tokens.start((2, 3))
    gather.line_end(value)
    gather.plane_end(query)
    load(query).start()
    gather.plane_step(key)
    gather.plane_start(value)
    fill_distance(seg_rows, seg_cols, distance)
    gather.enter(up_a)
    gather.line_most(outer)
    gather.line_start(up_a)
    gather.plane_end(key)
    load(key).start()
    gather.line_end(outer)
    gather.plane_step(value)
    gather.plane_start(outer)
    tokens.step()
    gather.line_step(up_a, 1)
    tokens.end()
    x_load.start()
    for step in range(2, line - 1):
        gather.line_step(up_a, step)
    gather.enter(up_b)
    gather.line_start(up_b)
    x_load.wait()
    normalize_tokens()
    store(3).start()
    gather.plane_end(value)
    load(value).start()
    gather.line_end(up_a)
    gather.plane_step(outer)
    gather.plane_start(up_a)
    project(query)
    gather.line_step(up_b, 1)
    gather.line_start(down_b)
    project(key)
    project(value)
    store(0).start()

    def beside(index):
        if index == 0:
            gather.enter(down_a)
            for step in range(2, line - 1):
                gather.line_step(up_b, step)
            gather.line_start(down_a)
            gather.plane_end(outer)
            load(outer).start()
        if index == 1:
            gather.line_end(up_b)
            gather.plane_step(up_a)
            gather.plane_start(up_b)
        if index == 2:
            gather.line_step(down_b, 1)
        if index == 3:
            gather.line_most(down_a)

    def attend(index, carry):
        attend_group(index, slopes, qkv, mixed, lse, distance)
        for order in range(4):

            @pl.when(index == order)
            def _():
                beside(order)

        return carry

    lax.fori_loop(0, qkv.shape[2] // (2 * HD), attend, 0)
    store(1).start()
    store(2).start()
    load(outer).wait()
    lax.fori_loop(0, size // 256, project_out, 0)
    gather.plane_step(up_b)
    gather.line_end(down_a)
    gather.plane_start(down_a)
    for step in range(2, line - 1):
        gather.line_step(down_b, step)
    grads.start()
    lax.fori_loop(0, size // 256, add_branch, 0)
    store(4).start()
    store(5).start()
    gather.plane_end(up_a)
    load(up_a).start()
    feed(0)
    gather.plane_step(down_a)
    gather.plane_end(up_b)
    load(up_b).start()
    feed(1)
    gather.line_end(down_b)
    gather.plane_end(down_a)
    grads.wait()
    for index in range(len(pairs)):
        store(index).wait()
    for group in range(len(groups)):
        gather.wait_sends(group)


def forward(attn_low, mlp_low, tokens, grads, slopes, seg_ids, qkv_bias, hidden_bias, vectors, line):
    rows = attn_low.shape[1]
    narrow, wide = attn_low.shape[2] // 2 * line, mlp_low.shape[2] // 4 * line
    length, width = 2 * tokens.shape[0], tokens.shape[1]
    low, dma = jnp.bfloat16, pltpu.SemaphoreType.DMA
    vmem = pl.BlockSpec(memory_space=pltpu.VMEM)
    hbm = pl.BlockSpec(memory_space=pl.ANY)

    def whole(count, columns_held):
        return (count, 2, 2, 2, rows, columns_held)

    kept = [
        ((3, length, narrow), low),
        ((length, narrow), low),
        ((length, narrow), jnp.float32),
        ((length, width), low),
        ((length, width), jnp.float32),
        ((length, width), low),
        ((2, length, wide), low),
        ((2, length, wide), low),
    ]
    outs = [(whole(3, narrow), low), (whole(1, narrow), low), (whole(2, wide), low), (whole(2, wide), low)]
    outs += [((length, width), low), (grads.shape, low)] + kept
    held = [(length, width)] * 2 + [whole(3, narrow), whole(1, narrow), whole(2, wide)]
    results = pl.pallas_call(
        functools.partial(forward_kernel, line),
        out_shape=[jax.ShapeDtypeStruct(*each) for each in outs],
        in_specs=[hbm] * 4 + [pl.BlockSpec(memory_space=pltpu.SMEM)] + [vmem] * 5,
        out_specs=[hbm] * len(outs),
        scratch_shapes=[pltpu.VMEM(each, low) for each in held]
        + [pltpu.VMEM(*each) for each in kept[:3]]
        + [pltpu.VMEM((length, length), jnp.float32)]
        + [pltpu.VMEM((length, width), low)] * 2
        + [pltpu.VMEM(*each) for each in kept[4:]]
        + [dma((8,)), dma((10,)), dma((length // 256,)), dma((length // 256,))]
        + WeightGather.scratch(8, line)
        + RowSwap.scratch()
        + CornerMove.scratch(),
        compiler_params=pltpu.CompilerParams(
            collective_id=1, has_side_effects=True, vmem_limit_bytes=62 * 1024 * 1024
        ),
        name="forward",
    )(
        attn_low,
        mlp_low,
        tokens,
        grads,
        slopes,
        seg_ids.reshape(-1, 1),
        seg_ids.reshape(1, -1),
        qkv_bias,
        hidden_bias,
        vectors,
    )
    return [each.reshape(each.shape[0], length, -1) for each in results[:4]] + list(results[4:])


def middle_kernel(
    line, grads_ref, act_ref, bend_ref, down_ref, up_ref, hidden_ref, middle_ref, mixed_ref, out_ref, gain,
    down_home, up_out, out_out, mixed_out, mid_out, sums_out, hidden_sums,
    grads, act, pre, down, up, hidden, middle, mixed, weight, part, got, low, mid, down_v, out_v, mixed_v,
    load_sem, store_sem, send_sem, recv_sem, give_sem, *scratch
):
    place = Place()
    bend, up_v = pre, down
    wide = down_home.shape[2] // 4
    one, two = (
        GroupSum(
            place,
            line,
            down_v.at[half : half + 1],
            down_home.at[:, :, columns((2 * place.core + half) * wide, wide)],
            scratch[half],
        )
        for half in range(2)
    )
    size = grads.shape[0]
    half = size // 2
    blocks = size // 256
    own_rows = grads.at[pl.ds(pl.multiple_of(place.core * half, half), half), :]
    give_rows = pltpu.make_async_remote_copy(
        src_ref=grads_ref,
        dst_ref=own_rows,
        send_sem=give_sem.at[0],
        recv_sem=give_sem.at[1],
        device_id=place.twin,
        device_id_type=MESH,
    )
    sources = (
        (grads_ref, own_rows), (down_ref, down), (bend_ref, bend), (up_ref, up), (act_ref.at[0], act.at[0]),
        (middle_ref, middle), (out_ref, weight), (hidden_ref, hidden), (mixed_ref, mixed),
    )
    load_g, load_down, load_bend, load_up, load_act, load_middle, load_out, load_hidden, load_mixed = (
        pltpu.make_async_copy(*each, load_sem.at[index]) for index, each in enumerate(sources)
    )
    load_more = pltpu.make_async_copy(act_ref.at[1], act.at[1], load_sem.at[10])
    for each in (load_g, load_act, load_down, load_bend, load_up, load_more, load_middle, load_out, load_hidden, load_mixed):
        each.start()
    greet(place, line)
    give_rows.start()

    def rows(index, count=256):
        return pl.ds(pl.multiple_of(index * count, count), count)

    def swap(index):
        return pltpu.make_async_remote_copy(
            src_ref=part.at[rows(index), :],
            dst_ref=got.at[rows(index), :],
            send_sem=send_sem.at[index],
            recv_sem=recv_sem.at[index],
            device_id=place.twin,
            device_id_type=MESH,
        )

    def store(slot, index, source, target):
        return pltpu.make_async_copy(source.at[rows(index), :], target.at[rows(index), :], store_sem.at[slot, index])

    def back_hidden(index, carry):
        total = None
        for order in range(2):
            back = jnp.dot(grads[rows(index), :], down[order], preferred_element_type=jnp.float32)
            piece = (back * bend[order, rows(index), :].astype(jnp.float32)).astype(jnp.bfloat16)
            pre[order, rows(index), :] = piece
            column = jnp.sum(piece.astype(jnp.float32), axis=0, keepdims=True)
            hidden_sums[order : order + 1, :] = hidden_sums[order : order + 1, :] + column
            term = contract_last(piece, up[order])
            total = term if total is None else total + term
        part[rows(index), :] = total.astype(jnp.bfloat16)
        swap(index).start()
        return carry

    def down_gradient(order):
        def body(index, carry):
            turned = grads[:, columns(index * 256, 256)].T
            piece = jnp.dot(turned, act[order], preferred_element_type=jnp.float32).astype(jnp.bfloat16)
            down_v[order, index // 2, lax.rem(index, 2)] = piece.reshape(2, 128, piece.shape[1])
            return carry

        lax.fori_loop(0, blocks, body, 0)

    def outer_product(slot, left, rights, targets, outs):
        def body(index, carry):
            turned = left[:, columns(index * 256, 256)].T
            for order, (right, target, out) in enumerate(zip(rights, targets, outs)):
                target[rows(index), :] = jnp.dot(turned, right[...], preferred_element_type=jnp.float32).astype(jnp.bfloat16)
                store(slot + order, index, target, out).start()
            return carry

        lax.fori_loop(0, blocks, body, 0)

    def norm_rows_back(step, sums, owned):
        core = place.core if owned else 1 - place.core
        at = pl.ds(pl.multiple_of(core * half + step * 32, 32), 32)
        grad = part[at, :].astype(jnp.float32) + got[at, :].astype(jnp.float32)
        value = middle[at, :]
        centred = value - jnp.mean(value, axis=1, keepdims=True)
        spread = lax.rsqrt(jnp.mean(centred * centred, axis=1, keepdims=True) + 1e-05)
        hat = centred * spread
        scaled = grad * gain[...]
        inner = jnp.mean(scaled * hat, axis=1, keepdims=True)
        above = grads[at, :].astype(jnp.float32)
        total = above + spread * (scaled - jnp.mean(scaled, axis=1, keepdims=True) - hat * inner)
        low[at, :] = total.astype(jnp.bfloat16)
        if not owned:
            return sums
        mid[pl.ds(pl.multiple_of(step * 32, 32), 32), :] = total
        fold = (4, 8, size)
        terms = (grad * hat, grad, total, above)
        return tuple(one + jnp.sum(term.reshape(fold), axis=0) for one, term in zip(sums, terms))

    def back_mixed(index, carry):
        mixed_v[rows(index), :] = jnp.dot(low[rows(index), :], weight[0], preferred_element_type=jnp.float32).astype(
            jnp.bfloat16
        )
        store(5, index, mixed_v, mixed_out).start()
        return carry

    hidden_sums[...] = jnp.zeros_like(hidden_sums)
    load_g.wait()
    give_rows.wait()
    load_act.wait()
    down_gradient(0)
    one.plane.start()
    load_more.wait()
    down_gradient(1)
    two.plane.start()
    load_down.wait()
    load_bend.wait()
    load_up.wait()
    lax.fori_loop(0, blocks // 2, back_hidden, 0)
    one.plane.one()
    lax.fori_loop(blocks // 2, blocks, back_hidden, 0)
    load_middle.wait()
    for index in range(blocks):
        swap(index).wait()
    empty = tuple(jnp.zeros((8, size), jnp.float32) for _ in range(4))
    lax.fori_loop(0, half // 32, lambda step, sums: norm_rows_back(step, sums, False), (), unroll=4)
    two.plane.one()
    one.plane.two()
    one.line.step(0)
    sums = lax.fori_loop(0, half // 32, lambda step, sums: norm_rows_back(step, sums, True), empty, unroll=4)
    for index, each in enumerate(sums):
        sums_out[index : index + 1, :] = jnp.sum(each, axis=0, keepdims=True)
    mid_store = pltpu.make_async_copy(mid, mid_out, load_sem.at[9])
    mid_store.start()
    one.line.step(1)
    load_out.wait()
    lax.fori_loop(0, blocks, back_mixed, 0)
    two.plane.two()
    two.line.step(0)
    load_mixed.wait()
    outer_product(4, low, (mixed,), (out_v.at[0],), (out_out.at[0],))
    for step in range(2, line - 1):
        one.line.step(step)
    two.line.step(1)
    load_hidden.wait()
    outer_product(2, hidden, (pre.at[0], pre.at[1]), (up_v.at[0], up_v.at[1]), (up_out.at[0], up_out.at[1]))
    one.line.end()
    one.home.start()
    for step in range(2, line - 1):
        two.line.step(step)
    two.line.end()
    two.home.start()
    for index in range(blocks):
        for order in range(2):
            store(2 + order, index, up_v.at[order], up_out.at[order]).wait()
        store(4, index, out_v.at[0], out_out.at[0]).wait()
        store(5, index, mixed_v, mixed_out).wait()
    mid_store.wait()
    for group in (one, two):
        group.home.wait()
        group.sent()


def middle_back(grads, act, bend, down, up, hidden, middle, mixed, out, gain, line):
    size, narrow = mixed.shape
    rows = size // 8
    low, dma = jnp.bfloat16, pltpu.SemaphoreType.DMA
    hbm, vmem = pl.BlockSpec(memory_space=pl.ANY), pl.BlockSpec(memory_space=pltpu.VMEM)

    def held(each):
        return pltpu.VMEM(each.shape, each.dtype)

    square = pltpu.VMEM((size, size), low)
    return pl.pallas_call(
        functools.partial(middle_kernel, line),
        out_shape=[
            jax.ShapeDtypeStruct((1, rows, 4 * size // line), low),
            jax.ShapeDtypeStruct(act.shape, low),
            jax.ShapeDtypeStruct((1, size, narrow), low),
            jax.ShapeDtypeStruct((size, narrow), low),
            jax.ShapeDtypeStruct((size // 2, size), jnp.float32),
            jax.ShapeDtypeStruct((4, size), jnp.float32),
            jax.ShapeDtypeStruct((2, size), jnp.float32),
        ],
        in_specs=[hbm] * 9 + [vmem],
        out_specs=[hbm] * 5 + [vmem] * 2,
        scratch_shapes=[square] + [held(each) for each in (act, bend, down, up, hidden, middle, mixed, out)]
        + [square, square, square, pltpu.VMEM((size // 2, size), jnp.float32)]
        + [pltpu.VMEM((2, 2, 2, 2, rows, act.shape[2]), low)]
        + [pltpu.VMEM((1, size, narrow), low), pltpu.VMEM((size, narrow), low)]
        + [dma((11,)), dma((6, size // 256)), dma((size // 256,)), dma((size // 256,)), dma((2,))]
        + [GroupSum.scratch(1, rows, act.shape[2], line)] * 2,
        compiler_params=pltpu.CompilerParams(
            collective_id=4, has_side_effects=True, vmem_limit_bytes=62 * 1024 * 1024
        ),
        name="middle_back",
    )(grads, act, bend, down, up, hidden, middle, mixed, out, gain.reshape(1, -1))


def attend_back_group(group, slopes, qkv, grad, mixed, lse, out, distance, dk_acc, dv_acc):
    length = qkv.shape[1]
    cols = columns(group * 2 * HD, 2 * HD)
    masks = head_lanes(jnp.bfloat16)
    wide_masks = head_lanes(jnp.float32)
    first = wide_masks[0] > 0.5
    factor = LOG2E / math.sqrt(HD)
    shrink = 1.0 / math.sqrt(HD)
    keys, values = qkv[1, :, cols], qkv[2, :, cols]
    keys_t = keys.T
    values_t = values.T
    dk_acc[...] = jnp.zeros_like(dk_acc)
    dv_acc[...] = jnp.zeros_like(dv_acc)
    for start in range(0, length, ROW_BLOCK):
        stop = start + ROW_BLOCK
        rows = slice(start, stop)
        query, grads, log_sums = qkv[0, rows, cols], grad[rows, cols], lse[rows, cols]
        query_t, grads_t = query.T, grads.T
        product = grads.astype(jnp.float32) * mixed[rows, cols].astype(jnp.float32)
        parts = []
        for head in range(2):
            slope = slopes[2 * group + head] * LOG2E
            lanes = slice(head * HD, (head + 1) * HD)
            scores = jnp.dot(query * masks[head], keys_t[:, :stop], preferred_element_type=jnp.float32)
            log_sum = log_sums[:, head * HD : head * HD + 1]
            probs = jnp.exp2(scores * factor - slope * distance[rows, :stop] - log_sum)
            grad_probs = jnp.dot(grads * masks[head], values_t[:, :stop], preferred_element_type=jnp.float32)
            inner = jnp.sum(product * wide_masks[head], axis=1, keepdims=True)
            grad_scores = (probs * (grad_probs - inner)).astype(jnp.bfloat16)
            parts.append(jnp.dot(grad_scores, keys[:stop], preferred_element_type=jnp.float32))
            dk_acc[lanes, :stop] += jnp.dot(query_t[lanes, :], grad_scores, preferred_element_type=jnp.float32)
            dv_acc[lanes, :stop] += jnp.dot(
                grads_t[lanes, :], probs.astype(jnp.bfloat16), preferred_element_type=jnp.float32
            )
        out[0, rows, cols] = (jnp.where(first, parts[0], parts[1]) * shrink).astype(jnp.bfloat16)
    out[1, :, cols] = (dk_acc[...].T * shrink).astype(jnp.bfloat16)
    out[2, :, cols] = dv_acc[...].T.astype(jnp.bfloat16)


def back_kernel(
    line, up_ref, out_ref, slopes, seg_rows, seg_cols, qkv, grad, mixed, lse, mlp_mom, down_sum, weight_ref, normed_ref,
    act_ref, down_w, attn_home, normed_part, bias_sums, mom_out, whole, out_part,
    held, held_sem, grads, projected, distance, dk_acc, dv_acc, up_sum, mlp_round, *scratch
):
    place = Place()
    narrow_cols = held.shape[2]
    wide, narrow = mlp_mom.shape[2] // 4, attn_home.shape[2] // 2

    def up_target(part):
        return up_sum.at[:, :, columns((2 * place.core + part) * wide, wide)]

    def attn_target(lo, hi):
        return attn_home.at[lo:hi, :, columns(place.core * narrow, narrow)]

    groups = [
        GroupSum(place, line, up_ref.at[0:1], up_target(0), scratch[0]),
        GroupSum(place, line, out_ref, attn_target(3, 4), scratch[1]),
        GroupSum(place, line, projected, attn_target(0, 3), scratch[2]),
        GroupSum(place, line, up_ref.at[1:2], up_target(1), scratch[3], line_first=True),
    ]
    three, outer, inner, last = groups
    collect = Collect(place, mlp_round, whole, scratch[4])

    def attend(group, carry):
        attend_back_group(group, slopes, qkv, grad, mixed, lse, grads, distance, dk_acc, dv_acc)
        return carry

    def halves(ref):
        return [ref.at[:, half * narrow_cols : (half + 1) * narrow_cols] for half in range(2)]

    first_loads = [pltpu.make_async_copy(weight_ref.at[order], held.at[order], held_sem.at[order]) for order in range(3)]
    for half, source in enumerate(halves(normed_ref)):
        first_loads.append(pltpu.make_async_copy(source, held.at[3 + half], held_sem.at[3 + half]))
    quarters = [source for part in range(2) for source in halves(down_w.at[part])]
    late_loads = [pltpu.make_async_copy(quarters[index], held.at[index], held_sem.at[index]) for index in range(4)]

    def act_load(block, index):
        source = act_ref.at[
            index // 2, pl.ds(pl.multiple_of(block * 256, 256), 256), (index % 2) * narrow_cols : (index % 2 + 1) * narrow_cols
        ]
        return pltpu.make_async_copy(source, held.at[4, index * 256 : (index + 1) * 256], held_sem.at[5 + index])

    def project(index, carry):
        left = held[3 + index // 2, :, columns(lax.rem(index, 2) * 256, 256)].T
        for order in range(3):
            piece = jnp.dot(left, grads[order], preferred_element_type=jnp.float32).astype(jnp.bfloat16)
            projected[order, index // 2, lax.rem(index, 2)] = piece.reshape(2, 128, piece.shape[1])
        return carry

    def unproject(index, carry):
        at = pl.ds(pl.multiple_of(index * 256, 256), 256)
        total = contract_last(grads[0, at, :], held[0])
        for order in range(1, 3):
            total = total + contract_last(grads[order, at, :], held[order])
        normed_part[at, :] = total.astype(jnp.bfloat16)
        return carry

    def feed_out(block, carry):
        for index in range(4):
            act_load(block, index).start()
        for index in range(4):
            act_load(block, index).wait()
        total = contract_last(held[4, 0:256], held[0])
        for index in range(1, 4):
            total = total + contract_last(held[4, index * 256 : (index + 1) * 256], held[index])
        at = pl.ds(pl.multiple_of(block * 256, 256), 256)
        for half in range(2):
            grads[half, at, :] = total[:, half * narrow_cols : (half + 1) * narrow_cols].astype(jnp.bfloat16)
        return carry

    def out_store(half):
        return pltpu.make_async_copy(grads.at[half], halves(out_part)[half], held_sem.at[half])

    def update(index, carry):
        at = pl.ds(pl.multiple_of(index * 32, 32), 32)
        for order, gradient in enumerate((up_sum, down_sum)):
            fresh = 0.5 * mlp_mom[order, at, :] + gradient[0, at, :].astype(jnp.float32)
            mom_out[order, at, :] = fresh
            mlp_round[order, at, :] = fresh.astype(jnp.bfloat16)
        return carry

    greet_all(place)
    three.plane.start()
    last.load().start()
    for each in first_loads:
        each.start()
    last.load().wait()
    last.line.step(0)
    outer.plane.start()
    fill_distance(seg_rows, seg_cols, distance)
    pairs = qkv.shape[2] // (2 * HD)
    lax.fori_loop(0, pairs // 2, attend, 0)
    three.plane.one()
    last.line.step(1)
    lax.fori_loop(pairs // 2, pairs, attend, 0)
    three.plane.two()
    three.line.step(0)
    outer.plane.one()
    for each in first_loads:
        each.wait()
    lax.fori_loop(0, 4, project, 0)
    for step in range(2, line - 1):
        last.line.step(step)
    inner.plane.start()
    three.line.step(1)
    outer.plane.two()
    outer.line.step(0)
    lax.fori_loop(0, 4, unproject, 0)
    for each in late_loads:
        each.start()
    for order in range(3):
        bias_sums[order : order + 1, :] = jnp.sum(grads[order].astype(jnp.float32), axis=0, keepdims=True)
    for step in range(2, line - 1):
        three.line.step(step)
    last.line.end()
    last.plane.start()
    three.line.end()
    three.home.start()
    last.plane.one()
    inner.plane.one()
    outer.line.step(1)
    last.plane.two()
    last.home.start()
    for step in range(2, line - 1):
        outer.line.step(step)
    for group in (three, last):
        group.home.wait()
    lax.fori_loop(0, mlp_mom.shape[1] // 32, update, 0)
    collect.start()
    collect.forward()
    outer.line.end()
    outer.home.start()
    inner.plane.two()
    inner.line.step(0)
    for each in late_loads:
        each.wait()
    lax.fori_loop(0, 2, feed_out, 0)
    inner.line.step(1)
    lax.fori_loop(2, 4, feed_out, 0)
    for half in range(2):
        out_store(half).start()
    for step in range(2, line - 1):
        inner.line.step(step)
    inner.line.end()
    inner.home.start()
    inner.home.wait()
    outer.home.wait()
    for half in range(2):
        out_store(half).wait()
    for group in groups:
        group.sent()
    collect.finish()


def attend_back(
    up, out, slopes, seg_ids, qkv, grad, mixed, lse, mlp_mom, down_sum, weights, normed, act, down_w, line
):
    _, length, width = qkv.shape
    rows, wide = up.shape[1] // 8, up.shape[2]
    size = normed.shape[1]
    vmem = pl.BlockSpec(memory_space=pltpu.VMEM)
    hbm = pl.BlockSpec(memory_space=pl.ANY)
    low = jnp.bfloat16
    return pl.pallas_call(
        functools.partial(back_kernel, line),
        out_shape=[
            jax.ShapeDtypeStruct((4, rows, 2 * width // line), low),
            jax.ShapeDtypeStruct((length, size), low),
            jax.ShapeDtypeStruct((3, width), jnp.float32),
            jax.ShapeDtypeStruct(mlp_mom.shape, jnp.float32),
            jax.ShapeDtypeStruct((size, 2 * wide), low),
            jax.ShapeDtypeStruct((length, size), low),
        ],
        in_specs=[hbm] * 2 + [pl.BlockSpec(memory_space=pltpu.SMEM)] + [vmem] * 8 + [hbm] * 4,
        out_specs=[hbm, vmem, vmem, vmem, hbm, hbm],
        scratch_shapes=[
            pltpu.VMEM((5, size, width), low),
            pltpu.SemaphoreType.DMA((9,)),
            pltpu.VMEM(qkv.shape, low),
            pltpu.VMEM((3, 2, 2, 2, rows, width), low),
            pltpu.VMEM((length, length), jnp.float32),
            pltpu.VMEM((2 * HD, length), jnp.float32),
            pltpu.VMEM((2 * HD, length), jnp.float32),
            pltpu.VMEM(down_sum.shape, low),
            pltpu.VMEM(mlp_mom.shape, low),
        ]
        + [GroupSum.scratch(1, rows, wide, line)]
        + [GroupSum.scratch(1, rows, width, line), GroupSum.scratch(3, rows, width, line)]
        + [GroupSum.scratch(1, rows, wide, line, line_first=True), Collect.scratch()],
        compiler_params=pltpu.CompilerParams(
            collective_id=2, has_side_effects=True, vmem_limit_bytes=62 * 1024 * 1024
        ),
        name="attend_back",
    )(
        *(each.reshape(-1, 2, 2, 2, rows, each.shape[2]) for each in (up, out)),
        slopes,
        seg_ids.reshape(-1, 1),
        seg_ids.reshape(1, -1),
        qkv,
        grad,
        mixed,
        lse,
        mlp_mom,
        down_sum,
        weights,
        normed,
        act,
        down_w,
    )


def finish_kernel(
    line, attn_ref, whole_ref, vec_ref, gain, part_ref, x_ref, grad_mid, out_ref, middle_ref, bias, attn_w, mlp_w,
    attn_new, mlp_new, vec_out, dx_new, block_out, *scratch
):
    (thin, full, gram, sent, got, poly, norm_own, norm_got, dx, away, mine) = scratch[:11]
    (home_sem, start_sem, send_sem, back_sem, norm_sem, block_send, block_recv, pass_send, pass_recv, dx_sem) = scratch[11:21]
    vector = VectorSum(Place(), line, scratch[21:25])
    out_mine, out_away, out_sem, middle, tokens, dx_out, attn_home, mlp_home = scratch[25:33]
    place = Place()
    x, y, t, core = place.x, place.y, place.tensor, place.core
    me, devices = place.me, place.devices
    rows = attn_ref.shape[1]
    narrow, wide = attn_ref.shape[2] // 2, mlp_home.shape[2] // 2
    greet_all(place)

    def held(order, index):
        return rows_held(place, thin if order < 4 else full, index, rows, narrow if order < 4 else wide)

    def source(order, half):
        return attn_ref.at[order, :, half * narrow : (half + 1) * narrow]

    def target(order, half):
        if order < 4:
            return attn_home.at[order, :, half * narrow : (half + 1) * narrow]
        return mlp_home.at[order - 4, :, half * wide : (half + 1) * wide]

    def owner_of(order, half):
        ox, oy, oz = OWNERS[order]
        return place.index(ox, oy, half, oz)

    def owns(order):
        ox, oy, oz = OWNERS[order]
        return (x == ox) & (y == oy) & (t == oz)

    owns_full = owns(4) | owns(5)
    owns_thin = owns(0) | owns(1) | owns(2) | owns(3)

    def collect(order, half):
        return remote(
            place, source(order, half), held(order, me), home_sem.at[order, half], start_sem.at[0], owner_of(order, half)
        )

    def collect_own(order, half):
        return pltpu.make_async_copy(source(order, half), held(order, me), start_sem.at[0])

    @pl.when(owns_full)
    def _():
        pltpu.make_async_copy(whole_ref, full, start_sem.at[0]).start()

    for order in range(4):
        for half in range(2):

            @pl.when(me == owner_of(order, half))
            def _():
                collect_own(order, half).start()

            @pl.when(me != owner_of(order, half))
            def _():
                collect(order, half).start()

    half_rows = dx.shape[0]

    def rows_of(ref, cores):
        return ref.at[pl.ds(pl.multiple_of(cores * half_rows, half_rows), half_rows), :]

    part_swap = pltpu.make_async_remote_copy(
        src_ref=rows_of(part_ref, 1 - core),
        dst_ref=away,
        send_sem=dx_sem.at[0],
        recv_sem=dx_sem.at[1],
        device_id=place.twin,
        device_id_type=MESH,
    )
    part_load = pltpu.make_async_copy(rows_of(part_ref, core), mine, dx_sem.at[2])
    part_swap.start()
    part_load.start()
    out_load = pltpu.make_async_copy(rows_of(out_ref, core), out_mine, out_sem.at[0])
    out_swap = pltpu.make_async_remote_copy(
        src_ref=rows_of(out_ref, 1 - core),
        dst_ref=out_away,
        send_sem=out_sem.at[3],
        recv_sem=out_sem.at[4],
        device_id=place.twin,
        device_id_type=MESH,
    )
    middle_load = pltpu.make_async_copy(rows_of(middle_ref, core), middle, out_sem.at[1])
    tokens_load = pltpu.make_async_copy(rows_of(x_ref, core), tokens, out_sem.at[2])
    for each in (tokens_load, out_load, out_swap, middle_load):
        each.start()

    def out_rows(step, carry):
        at = pl.ds(pl.multiple_of(step * 32, 32), 32)
        total = out_mine[at, :].astype(jnp.float32) + out_away[at, :].astype(jnp.float32)
        out_mine[at, :] = (middle[at, :] + total + bias[...]).astype(jnp.bfloat16)
        return carry

    def go_home(slot, source_ref, target_ref, sem):
        keep_rows = pltpu.make_async_copy(source_ref, target_ref, sem.at[slot])
        move_rows = pltpu.make_async_remote_copy(
            src_ref=source_ref,
            dst_ref=target_ref,
            send_sem=sem.at[slot + 1],
            recv_sem=sem.at[slot + 2],
            device_id=place.corner,
            device_id_type=MESH,
        )
        return keep_rows, move_rows

    dx_moves = go_home(2, dx, dx_out, dx_sem)
    out_moves = go_home(5, out_mine, block_out, out_sem)

    def when_moving(moves, action):
        for moving in (False, True):

            @pl.when(place.stays != moving)
            def _():
                action(moves[moving])

    step_rows = 32

    def dx_rows(step, sums):
        at = pl.ds(pl.multiple_of(step * step_rows, step_rows), step_rows)
        grad = mine[at, :].astype(jnp.float32) + away[at, :].astype(jnp.float32)
        value = tokens[at, :].astype(jnp.float32)
        centred = value - jnp.mean(value, axis=1, keepdims=True)
        spread = lax.rsqrt(jnp.mean(centred * centred, axis=1, keepdims=True) + 1e-05)
        hat = centred * spread
        product = grad * hat
        scaled = grad * gain[...]
        inner = jnp.mean(scaled * hat, axis=1, keepdims=True)
        back_grad = spread * (scaled - jnp.mean(scaled, axis=1, keepdims=True) - hat * inner)
        dx[at, :] = (grad_mid[at, :] + back_grad).astype(jnp.bfloat16)
        fold = (step_rows // 8, 8, grad.shape[1])
        return (
            sums[0] + jnp.sum(product.reshape(fold), axis=0),
            sums[1] + jnp.sum(grad.reshape(fold), axis=0),
        )

    def contract_rows(left, right):
        return lax.dot_general(left, right, (((1,), (1,)), ((), ())), preferred_element_type=jnp.float32)

    block = 256

    def swap_block(slot, index):
        return pltpu.make_async_remote_copy(
            src_ref=sent.at[index],
            dst_ref=got.at[slot, index],
            send_sem=block_send.at[index],
            recv_sem=block_recv.at[slot, index],
            device_id=place.twin,
            device_id_type=MESH,
        )

    def begin(matrix):
        size, width = matrix.shape
        pltpu.make_async_copy(matrix, matrix, start_sem.at[0]).wait()

        def add_squares(step, total):
            piece = matrix[pl.ds(pl.multiple_of(step * 32, 32), 32), :].astype(jnp.float32)
            piece = piece * piece
            return total + jnp.sum(piece.reshape(4, 8, width // 128, 128), axis=(0, 2))

        squares = lax.fori_loop(0, size // 32, add_squares, jnp.zeros((8, 128), jnp.float32), unroll=4)
        norm_own[...] = jnp.zeros((8, 128), jnp.float32) + jnp.sum(squares)
        swap = pltpu.make_async_remote_copy(
            src_ref=norm_own,
            dst_ref=norm_got,
            send_sem=norm_sem.at[0],
            recv_sem=norm_sem.at[1],
            device_id=place.twin,
            device_id_type=MESH,
        )
        swap.start()
        swap.wait()
        scale = 1.0 / (jnp.sqrt(norm_own[...] + norm_got[...]) + 1e-06)
        scale = scale[0:1, 0:1]

        def scale_rows(step, carry):
            at = pl.ds(pl.multiple_of(step * 32, 32), 32)
            matrix[at, :] = (matrix[at, :].astype(jnp.float32) * scale).astype(jnp.bfloat16)
            return carry

        lax.fori_loop(0, size // 32, scale_rows, 0, unroll=4)

    def iterate(matrix, repeat):
        size, width = matrix.shape
        blocks = size // block
        slot = repeat % 2

        def share(index, carry):
            at = pl.ds(pl.multiple_of(index * block, block), block)
            sent[index] = contract_rows(matrix[at, :], matrix[...]).astype(jnp.bfloat16)
            swap_block(slot, index).start()
            return carry

        lax.fori_loop(0, blocks, share, 0)

        def add(index, carry):
            at = pl.ds(pl.multiple_of(index * block, block), block)
            swap_block(slot, index).wait()
            total = sent[index].astype(jnp.float32) + got[slot, index].astype(jnp.float32)
            gram[at, :] = total.astype(jnp.bfloat16)
            return carry

        lax.fori_loop(0, blocks, add, 0)
        square = jnp.dot(gram[...], gram[...], preferred_element_type=jnp.float32)
        poly[...] = (coeff_b * gram[...].astype(jnp.float32) + coeff_c * square).astype(jnp.bfloat16)
        step_width = min(width, 1024)

        def advance(index, carry):
            at = columns(index * step_width, step_width)
            moved = jnp.dot(poly[...], matrix[:, at], preferred_element_type=jnp.float32)
            matrix[:, at] = (coeff_a * matrix[:, at].astype(jnp.float32) + moved).astype(jnp.bfloat16)
            return carry

        lax.fori_loop(0, width // step_width, advance, 0)

    @pl.when(owns_thin)
    def _():
        begin(thin)

    @pl.when(owns_full)
    def _():
        begin(full)

    part_swap.wait()
    part_load.wait()
    tokens_load.wait()
    empty = jnp.zeros((8, gain.shape[1]), jnp.float32)
    token_sums = lax.fori_loop(0, half_rows // step_rows, dx_rows, (empty, empty), unroll=2)
    when_moving(dx_moves, lambda move: move.start())
    vector.start(vec_ref[...], [jnp.sum(each, axis=0, keepdims=True) for each in token_sums])
    out_load.wait()
    out_swap.wait()
    middle_load.wait()
    lax.fori_loop(0, half_rows // 32, out_rows, 0, unroll=2)
    when_moving(out_moves, lambda move: move.start())

    for repeat in range(NS_STEPS):

        @pl.when(owns_thin)
        def _():
            iterate(thin, repeat)

        @pl.when(owns_full)
        def _():
            iterate(full, repeat)

        if repeat < 3:
            vector.step(repeat)
        if repeat == 3:
            vec_out[...] = vector.end()

    def keep(order, half):
        return pltpu.make_async_copy(held(order, me), target(order, half), back_sem.at[order, half])

    def back(order, half, index):
        return remote(place, held(order, index), target(order, half), send_sem.at[0], back_sem.at[order, half], index)

    def place_in(index):
        dp, z = place.of(index)
        return lax.rem(dp // 2, 2), dp // 4, z, lax.rem(dp, 2)

    def one_aside(order, xs, ys):
        ox, oy, _ = OWNERS[order]
        return (xs != ox) != (ys != oy)

    def back_by_way(order, index):
        xs, ys, z, _ = place_in(index)
        return one_aside(order, xs, ys) & is_one_of(z, sides(order, line)[0])

    def to_back_way(order, half, index):
        xs, ys, z, cores = place_in(index)
        region = held(order, index)
        first = sides(order, line)[0][0]
        return remote(
            place, region, region, send_sem.at[0], pass_recv.at[z - first, cores], place.index(xs, ys, half, OWNERS[order][2])
        )

    def back_in(order, which, cores):
        index = place.index(x, y, cores, sides(order, line)[0][which])
        region = held(order, index)
        return remote(place, region, region, pass_send.at[which, cores], pass_recv.at[which, cores], index)

    def back_on(order, half, which, cores):
        index = place.index(x, y, cores, sides(order, line)[0][which])
        return remote(
            place, held(order, index), target(order, half), pass_send.at[which, cores], back_sem.at[order, half], index
        )

    def when_back_way(order, action):
        for half in range(2):

            @pl.when(one_aside(order, x, y) & (t == OWNERS[order][2]) & (core == half))
            def _():
                for which in range(len(sides(order, line)[0])):
                    for cores in range(2):
                        action(order, half, which, cores)

    def each_device(order, half, action, passed):
        def body(step, carry):
            index = lax.rem(me + step, devices)
            if order < 4:
                action(order, half, index)
            else:

                @pl.when(back_by_way(order, index) == passed)
                def _():
                    action(order, half, index)

            return carry

        lax.fori_loop(1, devices, body, 0)

    def give_back(orders):
        for order in orders:
            for half in range(2):

                @pl.when(me == owner_of(order, half))
                def _():
                    if order >= 4:
                        each_device(order, half, lambda *at: to_back_way(*at).start(), True)
                    each_device(order, half, lambda *at: back(*at).start(), False)
                    keep(order, half).start()

    give_back((4, 5, 0, 1, 2, 3))

    def return_rows(order, half, which, cores):
        back_in(order, which, cores).wait_recv()
        back_on(order, half, which, cores).start()

    for order in (4, 5):
        when_back_way(order, return_rows)

    for order in range(6):
        for half in range(2):
            keep(order, half).wait()

            @pl.when(me == owner_of(order, half))
            def _():
                if order >= 4:
                    each_device(order, half, lambda *at: to_back_way(*at).wait_send(), True)
                each_device(order, half, lambda *at: back(*at).wait_send(), False)

            if order < 4:

                @pl.when(me != owner_of(order, half))
                def _():
                    collect(order, half).wait_send()

    for order in (4, 5):
        when_back_way(order, lambda *at: back_on(*at).wait_send())

    when_moving(dx_moves, lambda move: move.wait())

    def widen(step, carry):
        at = pl.ds(pl.multiple_of(step * 32, 32), 32)
        dx_new[at, :] = dx_out[at, :].astype(jnp.float32)
        return carry

    lax.fori_loop(0, half_rows // 32, widen, 0)

    def renew(step, carry):
        at = pl.ds(pl.multiple_of(step * 32, 32), 32)
        for order in range(4):
            attn_new[order, at, :] = attn_w[order, at, :] - attn_home[order, at, :].astype(jnp.float32)
        for order in range(2):
            change = math.sqrt(FF / D) * mlp_home[order, at, :].astype(jnp.float32)
            mlp_new[order, at, :] = mlp_w[order, at, :] - change
        return carry

    lax.fori_loop(0, rows // 32, renew, 0)
    when_moving(out_moves, lambda move: move.wait())


def finish(attn_round, mlp_whole, vec, gain, normed_part, tokens, grad_mid, out_part, middle, bias, attn_w, mlp_w, line):
    rows = attn_w.shape[1]
    size = 8 * rows
    narrow, wide = attn_w.shape[2] // 2 * line, mlp_w.shape[2] // 2 * line
    low, dma = jnp.bfloat16, pltpu.SemaphoreType.DMA
    hbm = pl.BlockSpec(memory_space=pl.ANY)
    vmem = pl.BlockSpec(memory_space=pltpu.VMEM)
    half = grad_mid.shape
    return pl.pallas_call(
        functools.partial(finish_kernel, line),
        out_shape=[
            jax.ShapeDtypeStruct(attn_w.shape, jnp.float32),
            jax.ShapeDtypeStruct(mlp_w.shape, jnp.float32),
            jax.ShapeDtypeStruct(vec.shape, jnp.float32),
            jax.ShapeDtypeStruct(half, jnp.float32),
            jax.ShapeDtypeStruct(half, low),
        ],
        in_specs=[hbm, hbm, vmem, vmem, hbm, hbm, vmem, hbm, hbm, vmem, vmem, vmem],
        out_specs=[vmem, vmem, vmem, vmem, hbm],
        scratch_shapes=[
            pltpu.VMEM((size, narrow), low),
            pltpu.VMEM((size, wide), low),
            pltpu.VMEM((size, size), low),
            pltpu.VMEM((size // 256, 256, size), low),
            pltpu.VMEM((2, size // 256, 256, size), low),
            pltpu.VMEM((size, size), low),
            pltpu.VMEM((8, 128), jnp.float32),
            pltpu.VMEM((8, 128), jnp.float32),
            pltpu.VMEM(half, low),
            pltpu.VMEM(half, low),
            pltpu.VMEM(half, low),
            dma((6, 2)),
            dma((1,)),
            dma((1,)),
            dma((6, 2)),
            dma((2,)),
            dma((size // 256,)),
            dma((2, size // 256)),
            dma((2, 2)),
            dma((2, 2)),
            dma((5,)),
        ]
        + VectorSum.scratch(vec.shape, line)
        + [
            pltpu.VMEM(half, low),
            pltpu.VMEM(half, low),
            dma((8,)),
            pltpu.VMEM(half, jnp.float32),
            pltpu.VMEM(half, low),
            pltpu.VMEM(half, low),
            pltpu.VMEM(attn_w.shape, low),
            pltpu.VMEM(mlp_w.shape, low),
        ],
        compiler_params=pltpu.CompilerParams(
            collective_id=3, has_side_effects=True, vmem_limit_bytes=60 * 1024 * 1024
        ),
        name="finish",
    )(
        attn_round,
        mlp_whole,
        vec,
        gain.reshape(1, -1),
        normed_part,
        tokens,
        grad_mid,
        out_part,
        middle,
        bias.reshape(1, -1),
        attn_w,
        mlp_w,
    )


def pair_swap(value):
    dp, line = lax.axis_size("dp"), lax.axis_size("tensor")
    pairs = [(i * line + k, (i ^ 1) * line + k) for i in range(dp) for k in range(line)]
    return lax.ppermute(value, ("dp", "tensor"), pairs)


def on_chip_pair(tokens, cotangent, segments, attn_w, mlp_w, vectors, attn_mom, mlp_mom, vector_mom):
    line = lax.axis_size("tensor")
    place = Place()
    core, t = place.core, place.tensor
    width = tokens.shape[1]
    narrow, wide = attn_w.shape[2] // 2, mlp_w.shape[2] // 4
    total_tokens = tokens.shape[0] * line * lax.axis_size("dp")

    def my_columns(row):
        return lax.dynamic_index_in_dim(row.reshape(line, 2, narrow), core, 1, False).reshape(-1)

    def place_columns(piece):
        spread = jnp.zeros((line, 2, narrow), jnp.float32)
        return lax.dynamic_update_slice(spread, piece.reshape(line, 1, narrow), (0, core, 0)).reshape(-1)

    hidden_bias = lax.dynamic_index_in_dim(vectors[8:].reshape(line, 2, 2, wide), core, 1, False)
    hidden_bias = hidden_bias.transpose(1, 0, 2).reshape(2, line * wide)

    seg_pairs = segments.reshape(-1, SEQ)
    seg_own = lax.dynamic_index_in_dim(seg_pairs, t // 2, 0, False)
    seg_ids = jnp.where(core == lax.rem(t, 2), seg_own, pair_swap(seg_own))

    biases = jnp.stack([my_columns(vectors[2]), jnp.zeros((narrow * line,), jnp.float32), my_columns(vectors[3])])
    per = narrow // HD
    local_ids = jnp.arange(per * line)
    head_ids = (local_ids // per) * (2 * per) + core * per + local_ids % per
    slopes = jnp.exp2(-(8.0 / HEADS) * (head_ids.astype(jnp.float32) + 1.0))
    low = jnp.bfloat16
    (
        wqkv, wout, w_up, w_down, x_low, grad_low, qkv, mixed, log_sums, normed, middle, hidden_low, hidden_act, bend
    ) = forward(
        attn_w.astype(low),
        mlp_w.astype(low),
        tokens,
        cotangent,
        slopes,
        seg_ids,
        biases,
        hidden_bias,
        vectors,
        line,
    )
    down_sum, grad_up, grad_out, grad_mixed, grad_mid_mine, middle_sums, hidden_sums = middle_back(
        grad_low, hidden_act, bend, w_down, w_up, hidden_low, middle, mixed, wout, vectors[5], line
    )
    attn_sum, normed_part, bias_sums, mlp_mom_new, mlp_whole, out_part = attend_back(
        grad_up,
        grad_out,
        slopes,
        seg_ids,
        qkv,
        grad_mixed,
        mixed,
        log_sums,
        mlp_mom,
        down_sum,
        wqkv,
        normed,
        hidden_act,
        w_down,
        line,
    )
    hidden_grad = lax.dynamic_update_slice(
        jnp.zeros((line, 2, 2, wide), jnp.float32),
        hidden_sums.reshape(2, line, wide).transpose(1, 0, 2)[:, None],
        (0, core, 0, 0),
    )
    vector_rows = jnp.stack(
        [
            jnp.zeros((width,), jnp.float32),
            jnp.zeros((width,), jnp.float32),
            place_columns(bias_sums[0]),
            place_columns(bias_sums[2]),
            middle_sums[2],
            middle_sums[0],
            middle_sums[1],
            middle_sums[3],
        ]
    )
    vector_local = jnp.concatenate([vector_rows, hidden_grad.reshape(-1, width)], axis=0)
    padding = jnp.zeros((4, width), jnp.float32)
    attn_mom_new = 0.5 * attn_mom + attn_sum.astype(jnp.float32)
    attn_new, mlp_new, vector_sum, grad_tokens, output = finish(
        attn_mom_new.astype(low),
        mlp_whole,
        jnp.concatenate([vector_local, padding], axis=0),
        vectors[0],
        normed_part,
        x_low,
        grad_mid_mine,
        out_part,
        middle,
        vectors[7],
        attn_w,
        mlp_w,
        line,
    )
    vector_grads = vector_sum[: vector_local.shape[0]]
    vector_mom_new = 0.5 * vector_mom + vector_grads
    vector_new = vectors - 0.1 / math.sqrt(total_tokens) * vector_mom_new
    return (
        output,
        grad_tokens,
        attn_mom_new,
        attn_new,
        mlp_mom_new,
        mlp_new,
        vector_mom_new,
        vector_new,
    )


def solution(mesh):
    in_specs = (
        P(("dp", "tensor"), None),
        P(("dp", "tensor"), None),
        P("dp"),
        P(None, "dp", "tensor"),
        P(None, "dp", "tensor"),
        P(),
        P(None, "dp", "tensor"),
        P(None, "dp", "tensor"),
        P(),
    )
    out_specs = (
        P(("dp", "tensor"), None),
        P(("dp", "tensor"), None),
        P(None, "dp", "tensor"),
        P(None, "dp", "tensor"),
        P(None, "dp", "tensor"),
        P(None, "dp", "tensor"),
        P(),
        P(),
    )
    chips_of_two = (mesh.shape["dp"], mesh.shape["tensor"]) == (8, 4)
    return jax.shard_map(
        on_chip_pair if chips_of_two else on_device, mesh=mesh, in_specs=in_specs, out_specs=out_specs, check_vma=False
    )
```

```python
import functools
import math

import jax
import jax.numpy as jnp
from jax import lax
from jax.experimental import pallas as pl
from jax.experimental.pallas import tpu as pltpu
from jax.sharding import PartitionSpec as P

D = 1024
HEADS = 16
HD = 64
FF = 4096
SEQ = 1024
NS_STEPS = 5
MESH = pl.DeviceIdType.MESH


coeff_a = 3.4445
coeff_b = -4.775
coeff_c = 2.0315


def norm_rows(row_data, gain, shift):
    center = jnp.mean(row_data, axis=-1, keepdims=True)
    centred = row_data - center
    spread = jnp.mean(centred * centred, axis=-1, keepdims=True)
    return centred * lax.rsqrt(spread + 1e-05) * gain + shift


def gelu_tanh(values):
    return jax.nn.gelu(values, approximate=True)


def contract_last(left, right):
    return lax.dot_general(
        left, right, (((1,), (1,)), ((), ())), preferred_element_type=jnp.float32
    )


def contract_first(left, right):
    return lax.dot_general(
        left, right, (((0,), (0,)), ((), ())), preferred_element_type=jnp.float32
    )


def head_slopes(first_head, head_count):
    head_ids = (first_head + jnp.arange(head_count)).astype(jnp.float32)
    return jnp.exp2(-(8.0 / HEADS) * (head_ids + 1.0))


def masked_scores(row_query, key_rows, row_segs, seg_ids, row_start, slopes):
    scores = jnp.einsum("qhd,khd->hqk", row_query, key_rows, preferred_element_type=jnp.float32) * (
        1.0 / math.sqrt(HD)
    )
    query_pos = row_start + jnp.arange(row_query.shape[0])
    key_pos = jnp.arange(key_rows.shape[0])
    distance = (query_pos[:, None] - key_pos[None, :]).astype(jnp.float32)
    scores = scores - slopes[:, None, None] * distance[None]
    same_doc = (
        (row_segs[:, None] == seg_ids[None, :])
        & (row_segs[:, None] > 0)
        & (key_pos[None, :] <= query_pos[:, None])
    )
    allowed = same_doc | (key_pos[None, :] == query_pos[:, None])
    return jnp.where(allowed[None], scores, -1e30)


def attend_forward(query, key_rows, value_rows, seg_ids, slopes, row_block):
    length = key_rows.shape[0]

    def one_block(row_start):
        row_query = lax.dynamic_slice_in_dim(query, row_start, row_block, 0)
        row_segs = lax.dynamic_slice_in_dim(seg_ids, row_start, row_block, 0)
        scores = masked_scores(row_query, key_rows, row_segs, seg_ids, row_start, slopes)
        row_max = jnp.max(scores, axis=-1, keepdims=True)
        exp_scores = jnp.exp(scores - row_max)
        row_total = jnp.sum(exp_scores, axis=-1, keepdims=True)
        attn_probs = (exp_scores / row_total).astype(jnp.bfloat16)
        mixed = jnp.einsum(
            "hqk,khd->qhd", attn_probs, value_rows, preferred_element_type=jnp.float32
        )
        return (mixed.astype(jnp.bfloat16), (row_max + jnp.log(row_total))[..., 0])

    block_starts = jnp.arange(length // row_block) * row_block
    mixed, log_sums = lax.map(one_block, block_starts)
    return (mixed.reshape(length, -1), log_sums)


def attend_backward(query, key_rows, value_rows, seg_ids, log_sums, grad_mixed, slopes, row_block):
    length, head_count, head_dim = key_rows.shape
    factor = 1.0 / math.sqrt(HD)

    def one_block(carry, pieces):
        row_start, row_lse = pieces
        row_query = lax.dynamic_slice_in_dim(query, row_start, row_block, 0)
        row_grad = lax.dynamic_slice_in_dim(grad_mixed, row_start, row_block, 0)
        row_segs = lax.dynamic_slice_in_dim(seg_ids, row_start, row_block, 0)
        scores = masked_scores(row_query, key_rows, row_segs, seg_ids, row_start, slopes)
        attn_probs = jnp.exp(scores - row_lse[:, :, None])
        grad_probs = jnp.einsum(
            "qhd,khd->hqk", row_grad, value_rows, preferred_element_type=jnp.float32
        )
        inner = jnp.sum(grad_probs * attn_probs, axis=-1, keepdims=True)
        grad_scores = (attn_probs * (grad_probs - inner)).astype(jnp.bfloat16)
        grad_query = (
            jnp.einsum("hqk,khd->qhd", grad_scores, key_rows, preferred_element_type=jnp.float32)
            * factor
        )
        grad_keys = (
            carry[0]
            + jnp.einsum("hqk,qhd->khd", grad_scores, row_query, preferred_element_type=jnp.float32)
            * factor
        )
        grad_values = carry[1] + jnp.einsum(
            "hqk,qhd->khd",
            attn_probs.astype(jnp.bfloat16),
            row_grad,
            preferred_element_type=jnp.float32,
        )
        return ((grad_keys, grad_values), grad_query)

    empty = jnp.zeros((length, head_count, head_dim), jnp.float32)
    block_starts = jnp.arange(length // row_block) * row_block
    (grad_keys, grad_values), grad_query = lax.scan(
        one_block, (empty, empty), (block_starts, log_sums)
    )
    return (
        grad_query.reshape(length, -1),
        grad_keys.reshape(length, -1),
        grad_values.reshape(length, -1),
    )


def newton_rows(row_iterate):
    for repeat in range(NS_STEPS + 1):
        whole_iterate = lax.all_gather(row_iterate, "tensor", axis=0, tiled=True)
        if repeat == NS_STEPS:
            break
        square_rows = contract_last(row_iterate, whole_iterate).astype(jnp.bfloat16)
        whole_square = lax.all_gather(square_rows, "tensor", axis=0, tiled=True)
        poly_rows = (
            coeff_b * square_rows.astype(jnp.float32)
            + coeff_c * jnp.dot(square_rows, whole_square, preferred_element_type=jnp.float32)
        ).astype(jnp.bfloat16)
        row_iterate = (
            coeff_a * row_iterate.astype(jnp.float32)
            + jnp.dot(poly_rows, whole_iterate, preferred_element_type=jnp.float32)
        ).astype(jnp.bfloat16)
    return whole_iterate


def on_device(tokens, cotangent, segments, attn_w, mlp_w, vectors, attn_mom, mlp_mom, vector_mom):
    tensor_size = lax.axis_size("tensor")
    dp_size = lax.axis_size("dp")
    tensor_index = lax.axis_index("tensor")
    dp_index = lax.axis_index("dp")
    row_count = tokens.shape[0]
    model_width = tokens.shape[1]
    local_width = attn_w.shape[2]
    local_hidden = mlp_w.shape[2]
    head_count = local_width // HD
    row_block = min(512, SEQ)
    total_tokens = row_count * tensor_size * dp_size
    gathered_attn, gathered_mlp = (
        lax.all_gather(attn_w.astype(jnp.bfloat16), "dp", axis=1, tiled=True),
        lax.all_gather(mlp_w.astype(jnp.bfloat16), "dp", axis=1, tiled=True),
    )
    hidden_bias = vectors[8:].reshape(-1)
    query_bias = lax.dynamic_slice_in_dim(vectors[2], tensor_index * local_width, local_width)
    value_bias = lax.dynamic_slice_in_dim(vectors[3], tensor_index * local_width, local_width)
    x_rows = tokens.astype(jnp.float32)
    normed, pull_first = jax.vjp(norm_rows, x_rows, vectors[0], vectors[1])
    all_normed = lax.all_gather(normed.astype(jnp.bfloat16), "tensor", axis=0, tiled=True)
    seq_count = all_normed.shape[0] // SEQ
    projected = jnp.einsum(
        "td,mdc->mtc", all_normed, gathered_attn[:3], preferred_element_type=jnp.float32
    )
    query = (projected[0] + query_bias).astype(jnp.bfloat16)
    key_rows = projected[1].astype(jnp.bfloat16)
    value_rows = (projected[2] + value_bias).astype(jnp.bfloat16)
    slopes = head_slopes(tensor_index * head_count, head_count)
    seq_shape = (seq_count, SEQ, head_count, HD)
    seq_segs = segments.reshape(seq_count, SEQ)

    def forward_seq(pieces):
        return attend_forward(pieces[0], pieces[1], pieces[2], pieces[3], slopes, row_block)

    mixed, log_sums = lax.map(
        forward_seq,
        (
            query.reshape(seq_shape),
            key_rows.reshape(seq_shape),
            value_rows.reshape(seq_shape),
            seq_segs,
        ),
    )
    mixed = mixed.reshape(-1, local_width)
    w_out = gathered_attn[3]
    middle = (
        x_rows
        + lax.psum_scatter(
            contract_last(mixed, w_out).astype(jnp.bfloat16),
            "tensor",
            scatter_dimension=0,
            tiled=True,
        ).astype(jnp.float32)
        + vectors[4]
    )
    hidden_normed, pull_second = jax.vjp(norm_rows, middle, vectors[5], vectors[6])
    hidden_low = hidden_normed.astype(jnp.bfloat16)
    grad_rows = cotangent.astype(jnp.float32)
    all_hidden = lax.all_gather(hidden_low, "tensor", axis=0, tiled=True)
    w_up = gathered_mlp[0]
    w_down = gathered_mlp[1]
    bias_local = lax.dynamic_slice_in_dim(hidden_bias, tensor_index * local_hidden, local_hidden)
    hidden_pre = jnp.dot(all_hidden, w_up, preferred_element_type=jnp.float32) + bias_local
    act_float, gelu_pull = jax.vjp(gelu_tanh, hidden_pre)
    hidden_act = act_float.astype(jnp.bfloat16)
    output = (
        middle
        + lax.psum_scatter(
            contract_last(hidden_act, w_down).astype(jnp.bfloat16),
            "tensor",
            scatter_dimension=0,
            tiled=True,
        ).astype(jnp.float32)
        + vectors[7]
    )
    all_grad = lax.all_gather(grad_rows.astype(jnp.bfloat16), "tensor", axis=0, tiled=True)
    grad_down = contract_first(all_grad, hidden_act)
    grad_act = jnp.dot(all_grad, w_down, preferred_element_type=jnp.float32)
    grad_pre = gelu_pull(grad_act)[0].astype(jnp.bfloat16)
    grad_up = contract_first(all_hidden, grad_pre)
    bias_part = jnp.sum(grad_pre, axis=0, dtype=jnp.float32)
    hidden_grad = lax.dynamic_update_slice_in_dim(
        jnp.zeros(hidden_bias.shape, jnp.float32), bias_part, tensor_index * local_hidden, 0
    )
    grad_hidden_in = lax.psum_scatter(
        contract_last(grad_pre, w_up).astype(jnp.bfloat16),
        "tensor",
        scatter_dimension=0,
        tiled=True,
    ).astype(jnp.float32)
    mlp_grads = jnp.stack([grad_up, grad_down])
    second_grads = pull_second(grad_hidden_in)
    grad_middle = grad_rows + second_grads[0]
    all_grad_mid = lax.all_gather(grad_middle.astype(jnp.bfloat16), "tensor", axis=0, tiled=True)
    grad_out_w = contract_first(all_grad_mid, mixed)
    grad_mixed = jnp.dot(all_grad_mid, w_out, preferred_element_type=jnp.float32).astype(
        jnp.bfloat16
    )

    def backward_seq(pieces):
        return attend_backward(
            pieces[0], pieces[1], pieces[2], pieces[3], pieces[4], pieces[5], slopes, row_block
        )

    grad_query, grad_keys, grad_values = lax.map(
        backward_seq,
        (
            query.reshape(seq_shape),
            key_rows.reshape(seq_shape),
            value_rows.reshape(seq_shape),
            seq_segs,
            log_sums,
            grad_mixed.reshape(seq_shape),
        ),
    )
    grad_qkv = (
        jnp.stack([grad_query, grad_keys, grad_values])
        .reshape(3, -1, local_width)
        .astype(jnp.bfloat16)
    )
    grad_proj_w = jnp.einsum(
        "td,mtc->mdc", all_normed, grad_qkv, preferred_element_type=jnp.float32
    )
    bias_sums = jnp.sum(grad_qkv, axis=1, dtype=jnp.float32)
    grad_normed = lax.psum_scatter(
        jnp.einsum(
            "mtc,mdc->td", grad_qkv, gathered_attn[:3], preferred_element_type=jnp.float32
        ).astype(jnp.bfloat16),
        "tensor",
        scatter_dimension=0,
        tiled=True,
    ).astype(jnp.float32)
    first_grads = pull_first(grad_normed)
    grad_tokens = grad_middle + first_grads[0]

    def placed(piece, full_size, offset):
        return lax.dynamic_update_slice_in_dim(
            jnp.zeros((full_size,), jnp.float32), piece, offset, 0
        )

    width_offset = tensor_index * local_width
    vector_rows = jnp.stack(
        [
            first_grads[1],
            first_grads[2],
            placed(bias_sums[0], model_width, width_offset),
            placed(bias_sums[2], model_width, width_offset),
            jnp.sum(grad_middle, axis=0),
            second_grads[1],
            second_grads[2],
            jnp.sum(grad_rows, axis=0),
        ]
    )
    vector_local = jnp.concatenate([vector_rows, hidden_grad.reshape(4, model_width)], axis=0)
    attn_grads = jnp.concatenate([grad_proj_w, grad_out_w[None]], axis=0)
    attn_sum, mlp_sum = (
        lax.psum_scatter(
            attn_grads.astype(jnp.bfloat16), "dp", scatter_dimension=1, tiled=True
        ).astype(jnp.float32),
        lax.psum_scatter(
            mlp_grads.astype(jnp.bfloat16), "dp", scatter_dimension=1, tiled=True
        ).astype(jnp.float32),
    )
    attn_mom_new = 0.5 * attn_mom + attn_sum
    mlp_mom_new = 0.5 * mlp_mom + mlp_sum
    attn_round = attn_mom_new.astype(jnp.bfloat16)
    mlp_round = mlp_mom_new.astype(jnp.bfloat16)
    attn_float = attn_round.astype(jnp.float32)
    mlp_float = mlp_round.astype(jnp.float32)
    norm_parts = jnp.concatenate(
        [jnp.sum(attn_float * attn_float, axis=(1, 2)), jnp.sum(mlp_float * mlp_float, axis=(1, 2))]
    )
    vector_grads, norm_sums = lax.psum((vector_local, norm_parts), ("dp", "tensor"))
    frob_norms = jnp.sqrt(norm_sums)
    owners = [order * dp_size // 6 for order in range(6)]
    owned_norm = jnp.zeros((), jnp.float32)
    for order in range(6):
        owned_norm = owned_norm + jnp.where(dp_index == owners[order], frob_norms[order], 0.0)
    block_rows = attn_w.shape[1]
    slice_rows = model_width // tensor_size
    full_cols = local_hidden * tensor_size
    rows_attn, rows_mlp = (
        lax.all_gather(attn_round, "tensor", axis=2, tiled=True),
        lax.all_gather(mlp_round, "tensor", axis=2, tiled=True),
    )
    padded_attn = jnp.pad(rows_attn, ((0, 0), (0, 0), (0, full_cols - model_width)))
    all_rows = jnp.concatenate([padded_attn, rows_mlp], axis=0)
    outgoing = jnp.zeros((dp_size, block_rows, full_cols), jnp.bfloat16)
    for order in range(6):
        outgoing = outgoing.at[owners[order]].set(all_rows[order])
    incoming = lax.all_to_all(outgoing, "dp", split_axis=0, concat_axis=0, tiled=True)
    owned_whole = incoming.reshape(model_width, full_cols)
    mine = lax.dynamic_slice_in_dim(owned_whole, tensor_index * slice_rows, slice_rows, 0)
    attn_col = tensor_index * local_width
    row_iterate = (mine.astype(jnp.float32) / (owned_norm + 1e-06)).astype(jnp.bfloat16)
    result = newton_rows(row_iterate)
    returned = lax.all_to_all(
        result.reshape(dp_size, block_rows, full_cols),
        "dp",
        split_axis=0,
        concat_axis=0,
        tiled=True,
    )
    attn_blocks = []
    for order in range(4):
        piece = lax.dynamic_slice_in_dim(returned[owners[order]], attn_col, local_width, 1)
        attn_blocks.append(attn_w[order] - piece.astype(jnp.float32))
    mlp_blocks = []
    for order in range(2):
        piece = lax.dynamic_slice_in_dim(
            returned[owners[4 + order]], tensor_index * local_hidden, local_hidden, 1
        )
        mlp_blocks.append(mlp_w[order] - math.sqrt(FF / D) * piece.astype(jnp.float32))
    attn_new = jnp.stack(attn_blocks)
    mlp_new = jnp.stack(mlp_blocks)
    vector_mom_new = 0.5 * vector_mom + vector_grads
    vector_new = vectors - 0.1 / math.sqrt(total_tokens) * vector_mom_new
    return (
        output.astype(jnp.bfloat16),
        grad_tokens,
        attn_mom_new,
        attn_new,
        mlp_mom_new,
        mlp_new,
        vector_mom_new,
        vector_new,
    )


CORES = 2


class Place:
    def __init__(self):
        self.dp = lax.axis_index("dp")
        self.tensor = lax.axis_index("tensor")
        self.line = lax.axis_size("tensor")
        self.devices = lax.axis_size("dp") * self.line
        self.me = self.dp * self.line + self.tensor
        self.core = lax.rem(self.dp, 2)
        self.chip = self.dp // 2
        self.x = lax.rem(self.chip, 2)
        self.y = self.chip // 2
        self.twin = (self.dp + 1 - 2 * self.core, self.tensor)
        self.across_x = (self.dp + 2 - 4 * self.x, self.tensor)
        self.across_y = (self.dp + 4 - 8 * self.y, self.tensor)
        self.right = (self.dp, self.tensor + 1)
        self.left = (self.dp, self.tensor - 1)
        self.stays = self.core == lax.rem(self.tensor, 2)
        self.corner = (self.dp + 1 - 2 * self.core, self.tensor - 1 + 2 * self.core)


    def of(self, index):
        return (index // self.line, lax.rem(index, self.line))

    def index(self, x, y, core, z):
        return ((2 * y + x) * 2 + core) * self.line + z


def greet(place, line):
    barrier = pltpu.get_barrier_semaphore()

    def signal(device):
        pl.semaphore_signal(barrier, inc=1, device_id=device, device_id_type=MESH)

    signal(place.twin)
    signal(place.across_x)
    signal(place.across_y)

    for other in range(line):

        @pl.when(place.tensor != other)
        def _():
            signal((place.dp, other))

    @pl.when(jnp.logical_not(place.stays))
    def _():
        signal(place.corner)

    pl.semaphore_wait(barrier, jnp.where(place.stays, 3 + line - 1, 3 + line))


OWNERS = ((1, 0, 0), (1, 0, 3), (0, 1, 0), (0, 1, 3), (0, 0, 1), (1, 1, 2))


def greet_all(place):
    barrier = pltpu.get_barrier_semaphore()

    def meet(step, carry):
        pl.semaphore_signal(
            barrier, inc=1, device_id=place.of(lax.rem(place.me + step, place.devices)), device_id_type=MESH
        )
        return carry

    lax.fori_loop(1, place.devices, meet, 0)
    pl.semaphore_wait(barrier, place.devices - 1)


def is_one_of(value, options):
    found = value < 0
    for option in options:
        found = found | (value == option)
    return found


def sides(order, line):
    oz = OWNERS[order][2]
    above, below = list(range(oz + 1, line)), list(range(oz))
    return (above, below) if len(above) > len(below) else (below, above)


def rows_held(place, whole, index, rows, width):
    dp, tensor = place.of(index)
    return whole.at[pl.ds(pl.multiple_of(dp * rows, rows), rows), columns(tensor * width, width)]


def remote(place, source, target, send, recv, index):
    return pltpu.make_async_remote_copy(
        src_ref=source,
        dst_ref=target,
        send_sem=send,
        recv_sem=recv,
        device_id=place.of(index),
        device_id_type=MESH,
    )


class Collect:
    @staticmethod
    def scratch():
        dma = pltpu.SemaphoreType.DMA
        return [dma((2, 2)), dma((1,)), dma((2, 2)), dma((2, 2))]

    SCRATCH = 4

    def __init__(self, place, source, whole, scratch):
        self.place, self.source, self.whole = place, source, whole
        self.send_sem, self.sem, self.pass_send, self.pass_recv = scratch
        self.rows, self.width = source.shape[1], source.shape[2] // 2

    def owner(self, order, half):
        ox, oy, oz = OWNERS[order]
        return self.place.index(ox, oy, half, oz)

    def piece(self, order, half):
        return self.source.at[order - 4, :, half * self.width : (half + 1) * self.width]

    def held(self, index):
        return rows_held(self.place, self.whole, index, self.rows, self.width)

    def direct(self, order, half):
        send = self.send_sem.at[order - 4, half]
        return remote(
            self.place, self.piece(order, half), self.held(self.place.me), send, self.sem.at[0], self.owner(order, half)
        )

    def own(self, order, half):
        return pltpu.make_async_copy(self.piece(order, half), self.held(self.place.me), self.sem.at[0])

    def by_way(self, order):
        place = self.place
        ox, oy, oz = OWNERS[order]
        lone = is_one_of(place.tensor, sides(order, place.line)[1])
        return (place.y != oy) & (place.tensor != oz) & ((place.x != ox) | lone)

    def to_way(self, order, half):
        place = self.place
        ox, oy, _ = OWNERS[order]
        which = jnp.where(place.x == ox, 1, 0)
        return remote(
            place,
            self.piece(order, half),
            self.held(place.me),
            self.send_sem.at[order - 4, half],
            self.pass_recv.at[which, place.core],
            place.index(ox, oy, half, place.tensor),
        )

    def passed(self, order, which, cores):
        ox, oy, _ = OWNERS[order]
        return self.place.index(1 - ox if which == 0 else ox, 1 - oy, cores, self.place.tensor)

    def pass_in(self, order, which, cores):
        index = self.passed(order, which, cores)
        region = self.held(index)
        sems = self.pass_send.at[which, cores], self.pass_recv.at[which, cores]
        return remote(self.place, region, region, *sems, index)

    def pass_on(self, order, which, cores):
        ox, oy, oz = OWNERS[order]
        region = self.held(self.passed(order, which, cores))
        owner = self.place.index(ox, oy, self.place.core, oz)
        return remote(self.place, region, region, self.pass_send.at[which, cores], self.sem.at[0], owner)

    def when_passing(self, action):
        place = self.place
        for order in (5, 4):
            ox, oy, _ = OWNERS[order]
            far, lone = sides(order, place.line)
            for which, planes in ((0, far + lone), (1, lone)):

                @pl.when((place.x == ox) & (place.y == oy) & is_one_of(place.tensor, planes))
                def _():
                    for cores in range(2):
                        action(order, which, cores)

    def each(self, action_way, action_direct, action_own):
        for order in (5, 4):
            for half in range(2):
                mine = self.place.me == self.owner(order, half)

                @pl.when(self.by_way(order))
                def _():
                    action_way(order, half)

                @pl.when(jnp.logical_not(mine) & jnp.logical_not(self.by_way(order)))
                def _():
                    action_direct(order, half)

                @pl.when(mine)
                def _():
                    action_own(order, half)

    def start(self):
        self.each(
            lambda *at: self.to_way(*at).start(), lambda *at: self.direct(*at).start(), lambda *at: self.own(*at).start()
        )

    def forward(self):
        def action(*at):
            self.pass_in(*at).wait_recv()
            self.pass_on(*at).start()

        self.when_passing(action)

    def finish(self):
        self.each(
            lambda *at: self.to_way(*at).wait_send(),
            lambda *at: self.direct(*at).wait_send(),
            lambda *at: None,
        )
        self.when_passing(lambda *at: self.pass_on(*at).wait_send())
        for order in (5, 4):
            for half in range(2):

                @pl.when(self.place.me == self.owner(order, half))
                def _():
                    pltpu.make_async_copy(self.whole, self.whole, self.sem.at[0]).wait()


def columns(start, size):
    return pl.ds(pl.multiple_of(start, 128), size)


class RowSwap:
    PARTS = 4

    @staticmethod
    def scratch():
        return [pltpu.SemaphoreType.DMA((1,)), pltpu.SemaphoreType.DMA((2 + 2 * RowSwap.PARTS,))]

    def __init__(self, place, rows_ref, whole_ref, scratch):
        self.place, self.rows_ref, self.whole_ref = place, rows_ref, whole_ref
        self.own_sem, self.sem = scratch
        self.size = rows_ref.shape[0]

    def at(self, core):
        return self.whole_ref.at[pl.ds(pl.multiple_of(core * self.size, self.size), self.size), :]

    def copy(self, slot, source, target, device):
        return pltpu.make_async_remote_copy(
            src_ref=source,
            dst_ref=target,
            send_sem=self.sem.at[slot],
            recv_sem=self.sem.at[slot + 1],
            device_id=device,
            device_id_type=MESH,
        )

    def own(self):
        return pltpu.make_async_copy(self.rows_ref, self.at(self.place.core), self.own_sem.at[0])

    def away(self, part):
        count = self.size // self.PARTS
        start = pl.multiple_of((1 - self.place.core) * self.size + part * count, count)
        source = self.rows_ref.at[part * count : (part + 1) * count, :]
        return self.copy(2 + 2 * part, source, self.whole_ref.at[pl.ds(start, count), :], self.place.corner)

    def hand_own(self):
        return self.copy(0, self.rows_ref, self.at(self.place.core), self.place.twin)

    def hand_got(self):
        return self.copy(0, self.at(self.place.core), self.at(self.place.core), self.place.twin)

    def start(self, parts):
        if 0 in parts:

            @pl.when(self.place.stays)
            def _():
                self.own().start()
                self.hand_own().start()

        @pl.when(jnp.logical_not(self.place.stays))
        def _():
            for part in parts:
                self.away(part).start()

    def step(self):
        @pl.when(jnp.logical_not(self.place.stays))
        def _():
            for part in range(self.PARTS):
                self.away(part).wait()
            self.hand_got().start()

    def end(self):
        @pl.when(self.place.stays)
        def _():
            self.own().wait()

        self.hand_got().wait()


class CornerMove:
    PARTS = 4

    @staticmethod
    def scratch():
        return [pltpu.SemaphoreType.DMA((1,)), pltpu.SemaphoreType.DMA((2, CornerMove.PARTS))]

    def __init__(self, place, rows_ref, target_ref, scratch):
        self.place, self.rows_ref, self.target_ref = place, rows_ref, target_ref
        self.own_sem, self.sem = scratch

    def own(self):
        return pltpu.make_async_copy(self.rows_ref, self.target_ref, self.own_sem.at[0])

    def away(self, part):
        count = self.rows_ref.shape[0] // self.PARTS
        at = slice(part * count, (part + 1) * count)
        return pltpu.make_async_remote_copy(
            src_ref=self.rows_ref.at[at, :],
            dst_ref=self.target_ref.at[at, :],
            send_sem=self.sem.at[0, part],
            recv_sem=self.sem.at[1, part],
            device_id=self.place.corner,
            device_id_type=MESH,
        )

    def start(self):
        @pl.when(self.place.stays)
        def _():
            self.own().start()

        @pl.when(jnp.logical_not(self.place.stays))
        def _():
            for part in range(self.PARTS):
                self.away(part).start()

    def wait(self):
        @pl.when(self.place.stays)
        def _():
            self.own().wait()

        @pl.when(jnp.logical_not(self.place.stays))
        def _():
            for part in range(self.PARTS):
                self.away(part).wait()


class WeightGather:
    def __init__(self, place, line, groups, scratch):
        self.place, self.line, self.groups = place, line, groups
        self.own_sem, self.send_sem, self.recv_sem = scratch
        self.last = len(groups) - 1
        self.to_right, self.to_left = 1, line
        self.half_x, self.half_y, self.rest_y, self.rest_x = (2 * line - 1 + k for k in range(4))

    @staticmethod
    def scratch(count, line):
        dma = pltpu.SemaphoreType.DMA
        return [dma((count,)), dma((count, 2 * line + 3)), dma((count, 2 * line + 3))]

    def copy(self, group, slot, source, target, device):
        return pltpu.make_async_remote_copy(
            src_ref=source,
            dst_ref=target,
            send_sem=self.send_sem.at[group, slot],
            recv_sem=self.recv_sem.at[group, slot],
            device_id=device,
            device_id_type=MESH,
        )

    def same(self, group, slot, region, device):
        return self.copy(group, slot, region, region, device)

    def chunk(self, group, index):
        ref, width, _ = self.groups[group]
        cols = columns(index * width, width)
        if group == self.last:
            return ref.at[:, :, :, :, :, cols]
        return ref.at[:, self.place.y, self.place.x, :, :, cols]

    def corner(self, group, ys, xs, half):
        ref, width, _ = self.groups[group]
        if group == self.last:
            return ref.at[:, ys, xs, half, :, columns(self.place.tensor * width, width)]
        return ref.at[:, ys, xs, half]

    def entry(self, group, half):
        ref, width, _ = self.groups[group]
        return ref.at[:, self.place.y, self.place.x, half, :, columns(self.place.tensor * width, width)]

    def own(self, group):
        core = self.place.core
        return pltpu.make_async_copy(self.groups[group][2](core), self.entry(group, core), self.own_sem.at[group])

    def first(self, group):
        core = self.place.core
        return self.copy(group, 0, self.groups[group][2](1 - core), self.entry(group, core), self.place.twin)

    def begin(self, group):
        self.own(group).start()
        self.first(group).start()

    def enter(self, group):
        self.own(group).wait()
        self.same(group, 0, self.entry(group, 1 - self.place.core), self.place.twin).wait_recv()

    def hop(self, group, step, left):
        t = self.place.tensor
        index = t + step - 1 if left else t - step + 1
        slot = (self.to_left if left else self.to_right) + step - 1
        return self.same(group, slot, self.chunk(group, index), self.place.left if left else self.place.right)

    def arrival(self, group, step, left):
        t = self.place.tensor
        index = t + step if left else t - step
        slot = (self.to_left if left else self.to_right) + step - 1
        return self.same(group, slot, self.chunk(group, index), self.place.right if left else self.place.left)

    def sends(self, step, left):
        t, line = self.place.tensor, self.line
        return (t > 0) & (t + step <= line) if left else (t < line - 1) & (t >= step - 1)

    def line_start(self, group):
        for left in (False, True):

            @pl.when(self.sends(1, left))
            def _():
                self.hop(group, 1, left).start()

    def line_step(self, group, step):
        t, line = self.place.tensor, self.line
        for left in (False, True):

            @pl.when(t + step <= line - 1 if left else t >= step)
            def _():
                self.arrival(group, step, left).wait_recv()

            if step < line - 1:

                @pl.when(self.sends(step + 1, left))
                def _():
                    self.hop(group, step + 1, left).start()

    def line_most(self, group):
        for step in range(1, self.line - 1):
            self.line_step(group, step)

    def line_end(self, group):
        self.line_step(group, self.line - 1)

    def plane_start(self, group):
        place = self.place
        self.same(group, self.half_x, self.corner(group, place.y, place.x, 0), place.across_x).start()
        self.same(group, self.half_y, self.corner(group, place.y, place.x, 1), place.across_y).start()

    def plane_step(self, group):
        place, both = self.place, pl.ds(0, 2)
        self.same(group, self.half_x, self.corner(group, place.y, 1 - place.x, 0), place.across_x).wait_recv()
        self.same(group, self.rest_y, self.corner(group, place.y, both, 0), place.across_y).start()
        self.same(group, self.half_y, self.corner(group, 1 - place.y, place.x, 1), place.across_y).wait_recv()
        self.same(group, self.rest_x, self.corner(group, both, place.x, 1), place.across_x).start()

    def plane_end(self, group):
        place, both = self.place, pl.ds(0, 2)
        self.same(group, self.rest_y, self.corner(group, 1 - place.y, both, 0), place.across_y).wait_recv()
        self.same(group, self.rest_x, self.corner(group, both, 1 - place.x, 1), place.across_x).wait_recv()

    def wait_sends(self, group):
        place, both = self.place, pl.ds(0, 2)
        self.first(group).wait_send()
        for step in range(1, self.line):
            for left in (False, True):

                @pl.when(self.sends(step, left))
                def _():
                    self.hop(group, step, left).wait_send()

        self.same(group, self.half_x, self.corner(group, place.y, place.x, 0), place.across_x).wait_send()
        self.same(group, self.half_y, self.corner(group, place.y, place.x, 1), place.across_y).wait_send()
        self.same(group, self.rest_y, self.corner(group, place.y, both, 0), place.across_y).wait_send()
        self.same(group, self.rest_x, self.corner(group, both, place.x, 1), place.across_x).wait_send()


def add_blocks(target, sources):
    lead, rows = target.shape[:-2], target.shape[-2]
    per = rows // 32

    def body(step, carry):
        block, at = step // per, []
        for size in lead[::-1]:
            at.insert(0, lax.rem(block, size))
            block = block // size
        at = tuple(at) + (pl.ds(pl.multiple_of(lax.rem(step, per) * 32, 32), 32),)
        total = sources[0][at].astype(jnp.float32)
        for source in sources[1:]:
            total = total + source[at].astype(jnp.float32)
        target[at] = total.astype(target.dtype)
        return carry

    lax.fori_loop(0, math.prod(lead) * per, body, 0, unroll=4)


class PlaneSum:
    @staticmethod
    def scratch(count, rows, width):
        pair = pltpu.VMEM((count, 2, rows, width), jnp.bfloat16)
        single = pltpu.VMEM((count, rows, width), jnp.bfloat16)
        dma = pltpu.SemaphoreType.DMA
        return [pair] * 4 + [single] * 2 + [dma((2,)), dma((4,)), dma((4,))]

    SCRATCH = 9

    def __init__(self, place, source, result, scratch):
        self.place, self.source, self.result = place, source, result
        self.own, self.got, self.last = scratch[0:2], scratch[2:4], scratch[4:6]
        self.own_sem, self.send_sem, self.recv_sem = scratch[6:9]

    def copy(self, slot, source, target, device):
        return pltpu.make_async_remote_copy(
            src_ref=source,
            dst_ref=target,
            send_sem=self.send_sem.at[slot],
            recv_sem=self.recv_sem.at[slot],
            device_id=device,
            device_id_type=MESH,
        )

    def cut(self, index, mine):
        both, place = pl.ds(0, 2), self.place
        if index == 0:
            return self.source.at[:, place.y if mine else 1 - place.y, both, 0]
        return self.source.at[:, both, place.x if mine else 1 - place.x, 1]

    def load(self, index):
        return pltpu.make_async_copy(self.cut(index, True), self.own[index], self.own_sem.at[index])

    def first(self, index):
        device = self.place.across_x if index else self.place.across_y
        return self.copy(index, self.cut(index, False), self.got[index], device)

    def second(self, index):
        mine = self.place.y if index else self.place.x
        device = self.place.across_y if index else self.place.across_x
        return self.copy(2 + index, self.own[index].at[:, 1 - mine], self.last[index], device)

    def start(self):
        for index in range(2):
            self.first(index).start()
            self.load(index).start()

    def one(self):
        for index in range(2):
            mine = self.place.y if index else self.place.x
            self.load(index).wait()
            self.first(index).wait_recv()
            own, got = self.own[index], self.got[index]
            add_blocks(own.at[:, 1 - mine], (own.at[:, 1 - mine], got.at[:, 1 - mine]))
            self.second(index).start()
            add_blocks(own.at[:, mine], (own.at[:, mine], got.at[:, mine]))

    def two(self):
        for index in range(2):
            mine = self.place.y if index else self.place.x
            self.second(index).wait_recv()
            add_blocks(self.result.at[:, index], (self.own[index].at[:, mine], self.last[index]))

    def sent(self):
        for index in range(2):
            self.first(index).wait_send()
            self.second(index).wait_send()


class LineSum:
    @staticmethod
    def scratch(shape, line):
        dma = pltpu.SemaphoreType.DMA
        return [pltpu.VMEM(shape, jnp.bfloat16)] * 2 + [dma((2, line)), dma((2, line))]

    SCRATCH = 4

    def __init__(self, place, line, value, result, scratch):
        self.place, self.line, self.value, self.result = place, line, value, result
        self.got = scratch[0:2]
        self.send_sem, self.recv_sem = scratch[2:4]
        self.width = value.shape[-1] // line

    def part(self, ref, index):
        return ref.at[(slice(None),) * (len(ref.shape) - 1) + (slice(index * self.width, (index + 1) * self.width),)]

    def hop(self, index, left):
        return pltpu.make_async_remote_copy(
            src_ref=self.part(self.value, index),
            dst_ref=self.part(self.got[left], index),
            send_sem=self.send_sem.at[left, index],
            recv_sem=self.recv_sem.at[left, index],
            device_id=self.place.left if left else self.place.right,
            device_id_type=MESH,
        )

    def step(self, step):
        for left in range(2):
            for index in range(self.line):
                away = index if left else self.line - 1 - index
                order = step - away
                plane = self.line - 1 - order if left else order
                if order < 0 or (plane <= index if left else plane >= index):
                    continue

                @pl.when(self.place.tensor == plane)
                def _():
                    if order > 0:
                        self.hop(index, left).wait_recv()
                        value = self.part(self.value, index)
                        add_blocks(value, (value, self.part(self.got[left], index)))
                    if away > 0:
                        self.hop(index - 1 if left else index + 1, left).wait_send()
                    self.hop(index, left).start()

    def end(self):
        for index in range(self.line):

            @pl.when(self.place.tensor == index)
            def _():
                sources = [self.part(self.value, index)]
                for left in range(2):
                    if index < self.line - 1 if left else index > 0:
                        self.hop(index, left).wait_recv()
                        sources.append(self.part(self.got[left], index))
                add_blocks(self.result, sources)

    def sent(self):
        for index in range(self.line):

            @pl.when(self.place.tensor == index)
            def _():
                if index > 0:
                    self.hop(index - 1, 1).wait_send()
                if index < self.line - 1:
                    self.hop(index + 1, 0).wait_send()


class HomeCopy:
    def __init__(self, place, value, target, scratch):
        self.place, self.value, self.target = place, value, target
        self.own_sem, self.sem = scratch

    SCRATCH = 2

    @staticmethod
    def scratch():
        return [pltpu.SemaphoreType.DMA((1,)), pltpu.SemaphoreType.DMA((2,))]

    def keep(self):
        return pltpu.make_async_copy(self.value.at[:, self.place.core], self.target, self.own_sem.at[0])

    def give(self):
        return pltpu.make_async_remote_copy(
            src_ref=self.value.at[:, 1 - self.place.core],
            dst_ref=self.target,
            send_sem=self.sem.at[0],
            recv_sem=self.sem.at[1],
            device_id=self.place.twin,
            device_id_type=MESH,
        )

    def start(self):
        self.keep().start()
        self.give().start()

    def wait(self):
        self.keep().wait()
        self.give().wait()


class GroupSum:
    @staticmethod
    def scratch(count, rows, width, line, line_first=False):
        low = jnp.bfloat16
        part = width // line
        done = pltpu.VMEM((count, 2, rows, part), low)
        if line_first:
            whole = (count, 2, 2, 2, rows, width)
            held = [pltpu.VMEM(whole, low), pltpu.VMEM(whole[:-1] + (part,), low), pltpu.SemaphoreType.DMA((1,))]
            plane, along = PlaneSum.scratch(count, rows, part), LineSum.scratch(whole, line)
        else:
            middle = (count, 2, rows, width)
            held = [pltpu.VMEM(middle, low)]
            plane, along = PlaneSum.scratch(count, rows, width), LineSum.scratch(middle, line)
        return held + [done] + plane + along + HomeCopy.scratch()

    def __init__(self, place, line, source, target, scratch, line_first=False):
        scratch = list(scratch)

        def take(count):
            taken = scratch[:count]
            del scratch[:count]
            return taken

        if line_first:
            whole, middle, load_sem = take(3)
            self.load = lambda: pltpu.make_async_copy(source, whole, load_sem.at[0])
        else:
            (middle,) = take(1)
        (done,) = take(1)
        plane, along = take(PlaneSum.SCRATCH), take(LineSum.SCRATCH)
        if line_first:
            self.line = LineSum(place, line, whole, middle, along)
            self.plane = PlaneSum(place, middle, done, plane)
        else:
            self.plane = PlaneSum(place, source, middle, plane)
            self.line = LineSum(place, line, middle, done, along)
        self.home = HomeCopy(place, done, target, take(HomeCopy.SCRATCH))

    def sent(self):
        self.plane.sent()
        self.line.sent()


class VectorSum:
    @staticmethod
    def scratch(shape, line):
        return [
            pltpu.VMEM((4,) + shape, jnp.float32),
            pltpu.VMEM((3,) + shape, jnp.float32),
            pltpu.VMEM((line,) + shape, jnp.float32),
            pltpu.SemaphoreType.DMA((4, max(line, 3))),
        ]

    def __init__(self, place, line, scratch):
        self.place, self.line = place, line
        self.sums, self.got, self.along, self.sem = scratch

    def copy(self, stage):
        place = self.place
        return pltpu.make_async_remote_copy(
            src_ref=self.sums.at[stage],
            dst_ref=self.got.at[stage],
            send_sem=self.sem.at[0, stage],
            recv_sem=self.sem.at[1, stage],
            device_id=(place.twin, place.across_x, place.across_y)[stage],
            device_id_type=MESH,
        )

    def hop(self, other, source):
        return pltpu.make_async_remote_copy(
            src_ref=self.sums.at[3],
            dst_ref=self.along.at[source],
            send_sem=self.sem.at[2, other],
            recv_sem=self.sem.at[3, source],
            device_id=(self.place.dp, other),
            device_id_type=MESH,
        )

    def start(self, value, first_rows):
        self.sums[0] = value
        for index, row in enumerate(first_rows):
            self.sums[0, index : index + 1, :] = row
        self.copy(0).start()

    def step(self, stage):
        self.copy(stage).wait()
        self.sums[stage + 1] = self.sums[stage] + self.got[stage]
        if stage < 2:
            self.copy(stage + 1).start()
            return
        self.along[self.place.tensor] = self.sums[3]
        for other in range(self.line):

            @pl.when(self.place.tensor != other)
            def _():
                self.hop(other, self.place.tensor).start()

    def end(self):
        t = self.place.tensor
        for other in range(self.line):

            @pl.when(t != other)
            def _():
                self.hop(other, t).wait_send()
                self.hop(t, other).wait_recv()

        total = self.along[0]
        for other in range(1, self.line):
            total = total + self.along[other]
        return total


LOG2E = 1.4426950408889634
FAR = 1e32
ROW_BLOCK = 256


def fill_distance(seg_rows, seg_cols, distance):
    def body(step, carry):
        start = pl.multiple_of(step * 64, 64)
        shape = (64, distance.shape[1])
        row = lax.broadcasted_iota(jnp.int32, shape, 0) + start
        col = lax.broadcasted_iota(jnp.int32, shape, 1)
        segs = seg_rows[pl.ds(start, 64), :]
        same = (segs == seg_cols[...]) & (segs > 0) & (col <= row)
        allowed = same | (col == row)
        distance[pl.ds(start, 64), :] = jnp.where(allowed, (row - col).astype(jnp.float32), FAR)
        return carry

    lax.fori_loop(0, distance.shape[0] // 64, body, 0)


def head_lanes(dtype):
    lane = lax.broadcasted_iota(jnp.int32, (1, 2 * HD), 1)
    first = (lane < HD).astype(jnp.float32)
    return (first.astype(dtype), (1.0 - first).astype(dtype))


def attend_group(group, slopes, qkv, mixed, lse, distance):
    length = qkv.shape[1]
    cols = columns(group * 2 * HD, 2 * HD)
    masks = head_lanes(jnp.bfloat16)
    first = head_lanes(jnp.float32)[0] > 0.5
    factor = LOG2E / math.sqrt(HD)
    keys_t = qkv[1, :, cols].T
    values = qkv[2, :, cols]
    for start in range(0, length, ROW_BLOCK):
        stop = start + ROW_BLOCK
        rows = slice(start, stop)
        query = qkv[0, rows, cols]
        parts, sums = [], []
        for head in range(2):
            slope = slopes[2 * group + head] * LOG2E
            scores = jnp.dot(query * masks[head], keys_t[:, :stop], preferred_element_type=jnp.float32)
            scores = scores * factor - slope * distance[rows, :stop]
            top = jnp.max(scores, axis=1, keepdims=True)
            probs = jnp.exp2(scores - top)
            total = jnp.sum(probs, axis=1, keepdims=True)
            out = jnp.dot(probs.astype(jnp.bfloat16), values[:stop], preferred_element_type=jnp.float32)
            parts.append(out / total)
            sums.append(top + jnp.log2(total))
        mixed[rows, cols] = jnp.where(first, parts[0], parts[1]).astype(jnp.bfloat16)
        lse[rows, cols] = jnp.where(first, sums[0], sums[1])


def normalize(rows):
    centred = rows - jnp.mean(rows, axis=1, keepdims=True)
    return centred * lax.rsqrt(jnp.mean(centred * centred, axis=1, keepdims=True) + 1e-05)


def forward_kernel(
    line, attn_ref, mlp_ref, tokens_ref, grads_ref, slopes, seg_rows, seg_cols, qkv_bias, hidden_bias, vectors,
    qkv_w, out_w, up_w, down_w, tokens_out, grads_out, qkv_out, mixed_out, lse_out, normed_out, middle_out,
    hidden_out, act_out, bend_out, *scratch
):
    (x_v, normed, qkv_wv, out_wv, up_wv, qkv, mixed, lse, distance, part, got, middle, hidden, act, bend) = scratch[:15]
    load_sem, store_sem, swap_send, swap_recv = scratch[15:19]
    place = Place()
    narrow, wide = attn_ref.shape[2] // 2, mlp_ref.shape[2] // 4
    size = normed.shape[0]

    def attn_source(index):
        return lambda core: attn_ref.at[index : index + 1, :, columns(core * narrow, narrow)]

    def mlp_source(index, half):
        return lambda core: mlp_ref.at[index : index + 1, :, columns((2 * core + half) * wide, wide)]

    groups = [(qkv_w.at[index : index + 1], narrow, attn_source(index)) for index in range(3)]
    groups.append((out_w, narrow, attn_source(3)))
    groups += [(up_w.at[half : half + 1], wide, mlp_source(0, half)) for half in range(2)]
    groups += [(down_w.at[half : half + 1], wide, mlp_source(1, half)) for half in range(2)]
    query, key, value, outer, up_a, up_b, down_a, down_b = range(8)
    gather = WeightGather(place, line, groups, scratch[19:22])
    tokens = RowSwap(place, tokens_ref, tokens_out, scratch[22:24])
    grads = CornerMove(place, grads_ref, grads_out, scratch[24:26])

    def load(group):
        if group < 3:
            source, target = qkv_w.at[group], qkv_wv.at[group]
        elif group == outer:
            source, target = out_w, out_wv
        else:
            source, target = up_w.at[group - up_a], up_wv.at[group - up_a]
        return pltpu.make_async_copy(source, target, load_sem.at[group])

    x_load = pltpu.make_async_copy(tokens_out, x_v, load_sem.at[7])
    pairs = (
        (qkv, qkv_out),
        (mixed, mixed_out),
        (lse, lse_out),
        (normed, normed_out),
        (middle, middle_out),
        (hidden, hidden_out),
        (act.at[0], act_out.at[0]),
        (act.at[1], act_out.at[1]),
        (bend.at[0], bend_out.at[0]),
        (bend.at[1], bend_out.at[1]),
    )

    def store(index):
        return pltpu.make_async_copy(*pairs[index], store_sem.at[index])

    def normalize_tokens():
        def body(step, carry):
            at = pl.ds(pl.multiple_of(step * 32, 32), 32)
            normal = normalize(x_v[at, :].astype(jnp.float32))
            normed[at, :] = (normal * vectors[0:1, :] + vectors[1:2, :]).astype(jnp.bfloat16)
            return carry

        lax.fori_loop(0, size // 32, body, 0, unroll=4)

    def project(group):
        load(group).wait()
        weight = qkv_wv[group].reshape(size, qkv.shape[2])

        def body(step, carry):
            at = pl.ds(pl.multiple_of(step * 512, 512), 512)
            out = jnp.dot(normed[at, :], weight, preferred_element_type=jnp.float32)
            qkv[group, at, :] = (out + qkv_bias[group : group + 1, :]).astype(jnp.bfloat16)
            return carry

        lax.fori_loop(0, size // 512, body, 0)

    def swap(index):
        at = pl.ds(pl.multiple_of(index * 256, 256), 256)
        return pltpu.make_async_remote_copy(
            src_ref=part.at[at, :],
            dst_ref=got.at[at, :],
            send_sem=swap_send.at[index],
            recv_sem=swap_recv.at[index],
            device_id=place.twin,
            device_id_type=MESH,
        )

    def project_out(index, carry):
        at = pl.ds(pl.multiple_of(index * 256, 256), 256)
        weight = out_wv[0].reshape(size, mixed.shape[1])
        part[at, :] = contract_last(mixed[at, :], weight).astype(jnp.bfloat16)
        swap(index).start()
        return carry

    def add_branch(index, carry):
        swap(index).wait()

        def body(step, carry):
            at = pl.ds(pl.multiple_of(index * 256 + step * 32, 32), 32)
            branch = part[at, :].astype(jnp.float32) + got[at, :].astype(jnp.float32)
            total = x_v[at, :].astype(jnp.float32) + branch + vectors[4:5, :]
            middle[at, :] = total
            hidden[at, :] = (normalize(total) * vectors[5:6, :] + vectors[6:7, :]).astype(jnp.bfloat16)
            return carry

        return lax.fori_loop(0, 8, body, carry, unroll=4)

    def feed(half):
        load(up_a + half).wait()

        def body(step, carry):
            at = pl.ds(pl.multiple_of(step * 256, 256), 256)
            weight = up_wv[half].reshape(size, act.shape[2])
            pre = jnp.dot(hidden[at, :], weight, preferred_element_type=jnp.float32)
            pre = pre + hidden_bias[half : half + 1, :]
            square = pre * pre
            bent = jnp.tanh(0.7978845608 * pre * (1.0 + 0.044715 * square))
            inner = 0.7978845608 * (1.0 + 3.0 * 0.044715 * square)
            act[half, at, :] = (0.5 * pre * (1.0 + bent)).astype(jnp.bfloat16)
            bend[half, at, :] = (0.5 * (1.0 + bent) + 0.5 * pre * (1.0 - bent * bent) * inner).astype(jnp.bfloat16)
            return carry

        lax.fori_loop(0, size // 256, body, 0)
        store(6 + half).start()
        store(8 + half).start()

    greet(place, line)
    for group in (query, down_b, key, value, outer, up_a, up_b, down_a):
        gather.begin(group)
    gather.enter(query)
    gather.line_start(query)
    gather.enter(down_b)
    gather.plane_start(down_b)
    gather.enter(key)
    gather.line_most(query)
    gather.line_start(key)
    tokens.start((0,))
    gather.line_end(query)
    gather.plane_start(query)
    gather.plane_step(down_b)
    gather.enter(value)
    gather.line_most(key)
    gather.line_start(value)
    tokens.start((1,))
    gather.line_end(key)
    gather.plane_step(query)
    gather.plane_start(key)
    gather.plane_end(down_b)
    gather.line_most(value)
    gather.enter(outer)
    gather.line_start(outer)
    tokens.start((2, 3))
    gather.line_end(value)
    gather.plane_end(query)
    load(query).start()
    gather.plane_step(key)
    gather.plane_start(value)
    fill_distance(seg_rows, seg_cols, distance)
    gather.enter(up_a)
    gather.line_most(outer)
    gather.line_start(up_a)
    gather.plane_end(key)
    load(key).start()
    gather.line_end(outer)
    gather.plane_step(value)
    gather.plane_start(outer)
    tokens.step()
    gather.line_step(up_a, 1)
    tokens.end()
    x_load.start()
    for step in range(2, line - 1):
        gather.line_step(up_a, step)
    gather.enter(up_b)
    gather.line_start(up_b)
    x_load.wait()
    normalize_tokens()
    store(3).start()
    gather.plane_end(value)
    load(value).start()
    gather.line_end(up_a)
    gather.plane_step(outer)
    gather.plane_start(up_a)
    project(query)
    gather.line_step(up_b, 1)
    gather.line_start(down_b)
    project(key)
    project(value)
    store(0).start()

    def beside(index):
        if index == 0:
            gather.enter(down_a)
            for step in range(2, line - 1):
                gather.line_step(up_b, step)
            gather.line_start(down_a)
            gather.plane_end(outer)
            load(outer).start()
        if index == 1:
            gather.line_end(up_b)
            gather.plane_step(up_a)
            gather.plane_start(up_b)
        if index == 2:
            gather.line_step(down_b, 1)
        if index == 3:
            gather.line_most(down_a)

    def attend(index, carry):
        attend_group(index, slopes, qkv, mixed, lse, distance)
        for order in range(4):

            @pl.when(index == order)
            def _():
                beside(order)

        return carry

    lax.fori_loop(0, qkv.shape[2] // (2 * HD), attend, 0)
    store(1).start()
    store(2).start()
    load(outer).wait()
    lax.fori_loop(0, size // 256, project_out, 0)
    gather.plane_step(up_b)
    gather.line_end(down_a)
    gather.plane_start(down_a)
    for step in range(2, line - 1):
        gather.line_step(down_b, step)
    grads.start()
    lax.fori_loop(0, size // 256, add_branch, 0)
    store(4).start()
    store(5).start()
    gather.plane_end(up_a)
    load(up_a).start()
    feed(0)
    gather.plane_step(down_a)
    gather.plane_end(up_b)
    load(up_b).start()
    feed(1)
    gather.line_end(down_b)
    gather.plane_end(down_a)
    grads.wait()
    for index in range(len(pairs)):
        store(index).wait()
    for group in range(len(groups)):
        gather.wait_sends(group)


def forward(attn_low, mlp_low, tokens, grads, slopes, seg_ids, qkv_bias, hidden_bias, vectors, line):
    rows = attn_low.shape[1]
    narrow, wide = attn_low.shape[2] // 2 * line, mlp_low.shape[2] // 4 * line
    length, width = 2 * tokens.shape[0], tokens.shape[1]
    low, dma = jnp.bfloat16, pltpu.SemaphoreType.DMA
    vmem = pl.BlockSpec(memory_space=pltpu.VMEM)
    hbm = pl.BlockSpec(memory_space=pl.ANY)

    def whole(count, columns_held):
        return (count, 2, 2, 2, rows, columns_held)

    kept = [
        ((3, length, narrow), low),
        ((length, narrow), low),
        ((length, narrow), jnp.float32),
        ((length, width), low),
        ((length, width), jnp.float32),
        ((length, width), low),
        ((2, length, wide), low),
        ((2, length, wide), low),
    ]
    outs = [(whole(3, narrow), low), (whole(1, narrow), low), (whole(2, wide), low), (whole(2, wide), low)]
    outs += [((length, width), low), (grads.shape, low)] + kept
    held = [(length, width)] * 2 + [whole(3, narrow), whole(1, narrow), whole(2, wide)]
    results = pl.pallas_call(
        functools.partial(forward_kernel, line),
        out_shape=[jax.ShapeDtypeStruct(*each) for each in outs],
        in_specs=[hbm] * 4 + [pl.BlockSpec(memory_space=pltpu.SMEM)] + [vmem] * 5,
        out_specs=[hbm] * len(outs),
        scratch_shapes=[pltpu.VMEM(each, low) for each in held]
        + [pltpu.VMEM(*each) for each in kept[:3]]
        + [pltpu.VMEM((length, length), jnp.float32)]
        + [pltpu.VMEM((length, width), low)] * 2
        + [pltpu.VMEM(*each) for each in kept[4:]]
        + [dma((8,)), dma((10,)), dma((length // 256,)), dma((length // 256,))]
        + WeightGather.scratch(8, line)
        + RowSwap.scratch()
        + CornerMove.scratch(),
        compiler_params=pltpu.CompilerParams(
            collective_id=1, has_side_effects=True, vmem_limit_bytes=62 * 1024 * 1024
        ),
        name="forward",
    )(
        attn_low,
        mlp_low,
        tokens,
        grads,
        slopes,
        seg_ids.reshape(-1, 1),
        seg_ids.reshape(1, -1),
        qkv_bias,
        hidden_bias,
        vectors,
    )
    return [each.reshape(each.shape[0], length, -1) for each in results[:4]] + list(results[4:])


def middle_kernel(
    line, grads_ref, act_ref, bend_ref, down_ref, up_ref, hidden_ref, middle_ref, mixed_ref, out_ref, gain,
    down_home, up_out, out_out, mixed_out, mid_out, sums_out, hidden_sums,
    grads, act, pre, down, up, hidden, middle, mixed, weight, part, got, low, mid, down_v, out_v, mixed_v,
    load_sem, store_sem, send_sem, recv_sem, give_sem, *scratch
):
    place = Place()
    bend, up_v = pre, down
    wide = down_home.shape[2] // 4
    one, two = (
        GroupSum(
            place,
            line,
            down_v.at[half : half + 1],
            down_home.at[:, :, columns((2 * place.core + half) * wide, wide)],
            scratch[half],
        )
        for half in range(2)
    )
    size = grads.shape[0]
    half = size // 2
    blocks = size // 256
    own_rows = grads.at[pl.ds(pl.multiple_of(place.core * half, half), half), :]
    give_rows = pltpu.make_async_remote_copy(
        src_ref=grads_ref,
        dst_ref=own_rows,
        send_sem=give_sem.at[0],
        recv_sem=give_sem.at[1],
        device_id=place.twin,
        device_id_type=MESH,
    )
    sources = (
        (grads_ref, own_rows), (down_ref, down), (bend_ref, bend), (up_ref, up), (act_ref.at[0], act.at[0]),
        (middle_ref, middle), (out_ref, weight), (hidden_ref, hidden), (mixed_ref, mixed),
    )
    load_g, load_down, load_bend, load_up, load_act, load_middle, load_out, load_hidden, load_mixed = (
        pltpu.make_async_copy(*each, load_sem.at[index]) for index, each in enumerate(sources)
    )
    load_more = pltpu.make_async_copy(act_ref.at[1], act.at[1], load_sem.at[10])
    for each in (load_g, load_act, load_down, load_bend, load_up, load_more, load_middle, load_out, load_hidden, load_mixed):
        each.start()
    greet(place, line)
    give_rows.start()

    def rows(index, count=256):
        return pl.ds(pl.multiple_of(index * count, count), count)

    def swap(index):
        return pltpu.make_async_remote_copy(
            src_ref=part.at[rows(index), :],
            dst_ref=got.at[rows(index), :],
            send_sem=send_sem.at[index],
            recv_sem=recv_sem.at[index],
            device_id=place.twin,
            device_id_type=MESH,
        )

    def store(slot, index, source, target):
        return pltpu.make_async_copy(source.at[rows(index), :], target.at[rows(index), :], store_sem.at[slot, index])

    def back_hidden(index, carry):
        total = None
        for order in range(2):
            back = jnp.dot(grads[rows(index), :], down[order], preferred_element_type=jnp.float32)
            piece = (back * bend[order, rows(index), :].astype(jnp.float32)).astype(jnp.bfloat16)
            pre[order, rows(index), :] = piece
            column = jnp.sum(piece.astype(jnp.float32), axis=0, keepdims=True)
            hidden_sums[order : order + 1, :] = hidden_sums[order : order + 1, :] + column
            term = contract_last(piece, up[order])
            total = term if total is None else total + term
        part[rows(index), :] = total.astype(jnp.bfloat16)
        swap(index).start()
        return carry

    def down_gradient(order):
        def body(index, carry):
            turned = grads[:, columns(index * 256, 256)].T
            piece = jnp.dot(turned, act[order], preferred_element_type=jnp.float32).astype(jnp.bfloat16)
            down_v[order, index // 2, lax.rem(index, 2)] = piece.reshape(2, 128, piece.shape[1])
            return carry

        lax.fori_loop(0, blocks, body, 0)

    def outer_product(slot, left, rights, targets, outs):
        def body(index, carry):
            turned = left[:, columns(index * 256, 256)].T
            for order, (right, target, out) in enumerate(zip(rights, targets, outs)):
                target[rows(index), :] = jnp.dot(turned, right[...], preferred_element_type=jnp.float32).astype(jnp.bfloat16)
                store(slot + order, index, target, out).start()
            return carry

        lax.fori_loop(0, blocks, body, 0)

    def norm_rows_back(step, sums, owned):
        core = place.core if owned else 1 - place.core
        at = pl.ds(pl.multiple_of(core * half + step * 32, 32), 32)
        grad = part[at, :].astype(jnp.float32) + got[at, :].astype(jnp.float32)
        value = middle[at, :]
        centred = value - jnp.mean(value, axis=1, keepdims=True)
        spread = lax.rsqrt(jnp.mean(centred * centred, axis=1, keepdims=True) + 1e-05)
        hat = centred * spread
        scaled = grad * gain[...]
        inner = jnp.mean(scaled * hat, axis=1, keepdims=True)
        above = grads[at, :].astype(jnp.float32)
        total = above + spread * (scaled - jnp.mean(scaled, axis=1, keepdims=True) - hat * inner)
        low[at, :] = total.astype(jnp.bfloat16)
        if not owned:
            return sums
        mid[pl.ds(pl.multiple_of(step * 32, 32), 32), :] = total
        fold = (4, 8, size)
        terms = (grad * hat, grad, total, above)
        return tuple(one + jnp.sum(term.reshape(fold), axis=0) for one, term in zip(sums, terms))

    def back_mixed(index, carry):
        mixed_v[rows(index), :] = jnp.dot(low[rows(index), :], weight[0], preferred_element_type=jnp.float32).astype(
            jnp.bfloat16
        )
        store(5, index, mixed_v, mixed_out).start()
        return carry

    hidden_sums[...] = jnp.zeros_like(hidden_sums)
    load_g.wait()
    give_rows.wait()
    load_act.wait()
    down_gradient(0)
    one.plane.start()
    load_more.wait()
    down_gradient(1)
    two.plane.start()
    load_down.wait()
    load_bend.wait()
    load_up.wait()
    lax.fori_loop(0, blocks // 2, back_hidden, 0)
    one.plane.one()
    lax.fori_loop(blocks // 2, blocks, back_hidden, 0)
    load_middle.wait()
    for index in range(blocks):
        swap(index).wait()
    empty = tuple(jnp.zeros((8, size), jnp.float32) for _ in range(4))
    lax.fori_loop(0, half // 32, lambda step, sums: norm_rows_back(step, sums, False), (), unroll=4)
    two.plane.one()
    one.plane.two()
    one.line.step(0)
    sums = lax.fori_loop(0, half // 32, lambda step, sums: norm_rows_back(step, sums, True), empty, unroll=4)
    for index, each in enumerate(sums):
        sums_out[index : index + 1, :] = jnp.sum(each, axis=0, keepdims=True)
    mid_store = pltpu.make_async_copy(mid, mid_out, load_sem.at[9])
    mid_store.start()
    one.line.step(1)
    load_out.wait()
    lax.fori_loop(0, blocks, back_mixed, 0)
    two.plane.two()
    two.line.step(0)
    load_mixed.wait()
    outer_product(4, low, (mixed,), (out_v.at[0],), (out_out.at[0],))
    for step in range(2, line - 1):
        one.line.step(step)
    two.line.step(1)
    load_hidden.wait()
    outer_product(2, hidden, (pre.at[0], pre.at[1]), (up_v.at[0], up_v.at[1]), (up_out.at[0], up_out.at[1]))
    one.line.end()
    one.home.start()
    for step in range(2, line - 1):
        two.line.step(step)
    two.line.end()
    two.home.start()
    for index in range(blocks):
        for order in range(2):
            store(2 + order, index, up_v.at[order], up_out.at[order]).wait()
        store(4, index, out_v.at[0], out_out.at[0]).wait()
        store(5, index, mixed_v, mixed_out).wait()
    mid_store.wait()
    for group in (one, two):
        group.home.wait()
        group.sent()


def middle_back(grads, act, bend, down, up, hidden, middle, mixed, out, gain, line):
    size, narrow = mixed.shape
    rows = size // 8
    low, dma = jnp.bfloat16, pltpu.SemaphoreType.DMA
    hbm, vmem = pl.BlockSpec(memory_space=pl.ANY), pl.BlockSpec(memory_space=pltpu.VMEM)

    def held(each):
        return pltpu.VMEM(each.shape, each.dtype)

    square = pltpu.VMEM((size, size), low)
    return pl.pallas_call(
        functools.partial(middle_kernel, line),
        out_shape=[
            jax.ShapeDtypeStruct((1, rows, 4 * size // line), low),
            jax.ShapeDtypeStruct(act.shape, low),
            jax.ShapeDtypeStruct((1, size, narrow), low),
            jax.ShapeDtypeStruct((size, narrow), low),
            jax.ShapeDtypeStruct((size // 2, size), jnp.float32),
            jax.ShapeDtypeStruct((4, size), jnp.float32),
            jax.ShapeDtypeStruct((2, size), jnp.float32),
        ],
        in_specs=[hbm] * 9 + [vmem],
        out_specs=[hbm] * 5 + [vmem] * 2,
        scratch_shapes=[square] + [held(each) for each in (act, bend, down, up, hidden, middle, mixed, out)]
        + [square, square, square, pltpu.VMEM((size // 2, size), jnp.float32)]
        + [pltpu.VMEM((2, 2, 2, 2, rows, act.shape[2]), low)]
        + [pltpu.VMEM((1, size, narrow), low), pltpu.VMEM((size, narrow), low)]
        + [dma((11,)), dma((6, size // 256)), dma((size // 256,)), dma((size // 256,)), dma((2,))]
        + [GroupSum.scratch(1, rows, act.shape[2], line)] * 2,
        compiler_params=pltpu.CompilerParams(
            collective_id=4, has_side_effects=True, vmem_limit_bytes=62 * 1024 * 1024
        ),
        name="middle_back",
    )(grads, act, bend, down, up, hidden, middle, mixed, out, gain.reshape(1, -1))


def attend_back_group(group, slopes, qkv, grad, mixed, lse, out, distance, dk_acc, dv_acc):
    length = qkv.shape[1]
    cols = columns(group * 2 * HD, 2 * HD)
    masks = head_lanes(jnp.bfloat16)
    wide_masks = head_lanes(jnp.float32)
    first = wide_masks[0] > 0.5
    factor = LOG2E / math.sqrt(HD)
    shrink = 1.0 / math.sqrt(HD)
    keys, values = qkv[1, :, cols], qkv[2, :, cols]
    keys_t = keys.T
    values_t = values.T
    dk_acc[...] = jnp.zeros_like(dk_acc)
    dv_acc[...] = jnp.zeros_like(dv_acc)
    for start in range(0, length, ROW_BLOCK):
        stop = start + ROW_BLOCK
        rows = slice(start, stop)
        query, grads, log_sums = qkv[0, rows, cols], grad[rows, cols], lse[rows, cols]
        query_t, grads_t = query.T, grads.T
        product = grads.astype(jnp.float32) * mixed[rows, cols].astype(jnp.float32)
        parts = []
        for head in range(2):
            slope = slopes[2 * group + head] * LOG2E
            lanes = slice(head * HD, (head + 1) * HD)
            scores = jnp.dot(query * masks[head], keys_t[:, :stop], preferred_element_type=jnp.float32)
            log_sum = log_sums[:, head * HD : head * HD + 1]
            probs = jnp.exp2(scores * factor - slope * distance[rows, :stop] - log_sum)
            grad_probs = jnp.dot(grads * masks[head], values_t[:, :stop], preferred_element_type=jnp.float32)
            inner = jnp.sum(product * wide_masks[head], axis=1, keepdims=True)
            grad_scores = (probs * (grad_probs - inner)).astype(jnp.bfloat16)
            parts.append(jnp.dot(grad_scores, keys[:stop], preferred_element_type=jnp.float32))
            dk_acc[lanes, :stop] += jnp.dot(query_t[lanes, :], grad_scores, preferred_element_type=jnp.float32)
            dv_acc[lanes, :stop] += jnp.dot(
                grads_t[lanes, :], probs.astype(jnp.bfloat16), preferred_element_type=jnp.float32
            )
        out[0, rows, cols] = (jnp.where(first, parts[0], parts[1]) * shrink).astype(jnp.bfloat16)
    out[1, :, cols] = (dk_acc[...].T * shrink).astype(jnp.bfloat16)
    out[2, :, cols] = dv_acc[...].T.astype(jnp.bfloat16)


def back_kernel(
    line, up_ref, out_ref, slopes, seg_rows, seg_cols, qkv, grad, mixed, lse, mlp_mom, down_sum, weight_ref, normed_ref,
    act_ref, down_w, attn_home, normed_part, bias_sums, mom_out, whole, out_part,
    held, held_sem, grads, projected, distance, dk_acc, dv_acc, up_sum, mlp_round, *scratch
):
    place = Place()
    narrow_cols = held.shape[2]
    wide, narrow = mlp_mom.shape[2] // 4, attn_home.shape[2] // 2

    def up_target(part):
        return up_sum.at[:, :, columns((2 * place.core + part) * wide, wide)]

    def attn_target(lo, hi):
        return attn_home.at[lo:hi, :, columns(place.core * narrow, narrow)]

    groups = [
        GroupSum(place, line, up_ref.at[0:1], up_target(0), scratch[0]),
        GroupSum(place, line, out_ref, attn_target(3, 4), scratch[1]),
        GroupSum(place, line, projected, attn_target(0, 3), scratch[2]),
        GroupSum(place, line, up_ref.at[1:2], up_target(1), scratch[3], line_first=True),
    ]
    three, outer, inner, last = groups
    collect = Collect(place, mlp_round, whole, scratch[4])

    def attend(group, carry):
        attend_back_group(group, slopes, qkv, grad, mixed, lse, grads, distance, dk_acc, dv_acc)
        return carry

    def halves(ref):
        return [ref.at[:, half * narrow_cols : (half + 1) * narrow_cols] for half in range(2)]

    first_loads = [pltpu.make_async_copy(weight_ref.at[order], held.at[order], held_sem.at[order]) for order in range(3)]
    for half, source in enumerate(halves(normed_ref)):
        first_loads.append(pltpu.make_async_copy(source, held.at[3 + half], held_sem.at[3 + half]))
    quarters = [source for part in range(2) for source in halves(down_w.at[part])]
    late_loads = [pltpu.make_async_copy(quarters[index], held.at[index], held_sem.at[index]) for index in range(4)]

    def act_load(block, index):
        source = act_ref.at[
            index // 2, pl.ds(pl.multiple_of(block * 256, 256), 256), (index % 2) * narrow_cols : (index % 2 + 1) * narrow_cols
        ]
        return pltpu.make_async_copy(source, held.at[4, index * 256 : (index + 1) * 256], held_sem.at[5 + index])

    def project(index, carry):
        left = held[3 + index // 2, :, columns(lax.rem(index, 2) * 256, 256)].T
        for order in range(3):
            piece = jnp.dot(left, grads[order], preferred_element_type=jnp.float32).astype(jnp.bfloat16)
            projected[order, index // 2, lax.rem(index, 2)] = piece.reshape(2, 128, piece.shape[1])
        return carry

    def unproject(index, carry):
        at = pl.ds(pl.multiple_of(index * 256, 256), 256)
        total = contract_last(grads[0, at, :], held[0])
        for order in range(1, 3):
            total = total + contract_last(grads[order, at, :], held[order])
        normed_part[at, :] = total.astype(jnp.bfloat16)
        return carry

    def feed_out(block, carry):
        for index in range(4):
            act_load(block, index).start()
        for index in range(4):
            act_load(block, index).wait()
        total = contract_last(held[4, 0:256], held[0])
        for index in range(1, 4):
            total = total + contract_last(held[4, index * 256 : (index + 1) * 256], held[index])
        at = pl.ds(pl.multiple_of(block * 256, 256), 256)
        for half in range(2):
            grads[half, at, :] = total[:, half * narrow_cols : (half + 1) * narrow_cols].astype(jnp.bfloat16)
        return carry

    def out_store(half):
        return pltpu.make_async_copy(grads.at[half], halves(out_part)[half], held_sem.at[half])

    def update(index, carry):
        at = pl.ds(pl.multiple_of(index * 32, 32), 32)
        for order, gradient in enumerate((up_sum, down_sum)):
            fresh = 0.5 * mlp_mom[order, at, :] + gradient[0, at, :].astype(jnp.float32)
            mom_out[order, at, :] = fresh
            mlp_round[order, at, :] = fresh.astype(jnp.bfloat16)
        return carry

    greet_all(place)
    three.plane.start()
    last.load().start()
    for each in first_loads:
        each.start()
    last.load().wait()
    last.line.step(0)
    outer.plane.start()
    fill_distance(seg_rows, seg_cols, distance)
    pairs = qkv.shape[2] // (2 * HD)
    lax.fori_loop(0, pairs // 2, attend, 0)
    three.plane.one()
    last.line.step(1)
    lax.fori_loop(pairs // 2, pairs, attend, 0)
    three.plane.two()
    three.line.step(0)
    outer.plane.one()
    for each in first_loads:
        each.wait()
    lax.fori_loop(0, 4, project, 0)
    for step in range(2, line - 1):
        last.line.step(step)
    inner.plane.start()
    three.line.step(1)
    outer.plane.two()
    outer.line.step(0)
    lax.fori_loop(0, 4, unproject, 0)
    for each in late_loads:
        each.start()
    for order in range(3):
        bias_sums[order : order + 1, :] = jnp.sum(grads[order].astype(jnp.float32), axis=0, keepdims=True)
    for step in range(2, line - 1):
        three.line.step(step)
    last.line.end()
    last.plane.start()
    three.line.end()
    three.home.start()
    last.plane.one()
    inner.plane.one()
    outer.line.step(1)
    last.plane.two()
    last.home.start()
    for step in range(2, line - 1):
        outer.line.step(step)
    for group in (three, last):
        group.home.wait()
    lax.fori_loop(0, mlp_mom.shape[1] // 32, update, 0)
    collect.start()
    collect.forward()
    outer.line.end()
    outer.home.start()
    inner.plane.two()
    inner.line.step(0)
    for each in late_loads:
        each.wait()
    lax.fori_loop(0, 2, feed_out, 0)
    inner.line.step(1)
    lax.fori_loop(2, 4, feed_out, 0)
    for half in range(2):
        out_store(half).start()
    for step in range(2, line - 1):
        inner.line.step(step)
    inner.line.end()
    inner.home.start()
    inner.home.wait()
    outer.home.wait()
    for half in range(2):
        out_store(half).wait()
    for group in groups:
        group.sent()
    collect.finish()


def attend_back(
    up, out, slopes, seg_ids, qkv, grad, mixed, lse, mlp_mom, down_sum, weights, normed, act, down_w, line
):
    _, length, width = qkv.shape
    rows, wide = up.shape[1] // 8, up.shape[2]
    size = normed.shape[1]
    vmem = pl.BlockSpec(memory_space=pltpu.VMEM)
    hbm = pl.BlockSpec(memory_space=pl.ANY)
    low = jnp.bfloat16
    return pl.pallas_call(
        functools.partial(back_kernel, line),
        out_shape=[
            jax.ShapeDtypeStruct((4, rows, 2 * width // line), low),
            jax.ShapeDtypeStruct((length, size), low),
            jax.ShapeDtypeStruct((3, width), jnp.float32),
            jax.ShapeDtypeStruct(mlp_mom.shape, jnp.float32),
            jax.ShapeDtypeStruct((size, 2 * wide), low),
            jax.ShapeDtypeStruct((length, size), low),
        ],
        in_specs=[hbm] * 2 + [pl.BlockSpec(memory_space=pltpu.SMEM)] + [vmem] * 8 + [hbm] * 4,
        out_specs=[hbm, vmem, vmem, vmem, hbm, hbm],
        scratch_shapes=[
            pltpu.VMEM((5, size, width), low),
            pltpu.SemaphoreType.DMA((9,)),
            pltpu.VMEM(qkv.shape, low),
            pltpu.VMEM((3, 2, 2, 2, rows, width), low),
            pltpu.VMEM((length, length), jnp.float32),
            pltpu.VMEM((2 * HD, length), jnp.float32),
            pltpu.VMEM((2 * HD, length), jnp.float32),
            pltpu.VMEM(down_sum.shape, low),
            pltpu.VMEM(mlp_mom.shape, low),
        ]
        + [GroupSum.scratch(1, rows, wide, line)]
        + [GroupSum.scratch(1, rows, width, line), GroupSum.scratch(3, rows, width, line)]
        + [GroupSum.scratch(1, rows, wide, line, line_first=True), Collect.scratch()],
        compiler_params=pltpu.CompilerParams(
            collective_id=2, has_side_effects=True, vmem_limit_bytes=62 * 1024 * 1024
        ),
        name="attend_back",
    )(
        *(each.reshape(-1, 2, 2, 2, rows, each.shape[2]) for each in (up, out)),
        slopes,
        seg_ids.reshape(-1, 1),
        seg_ids.reshape(1, -1),
        qkv,
        grad,
        mixed,
        lse,
        mlp_mom,
        down_sum,
        weights,
        normed,
        act,
        down_w,
    )


def finish_kernel(
    line, attn_ref, whole_ref, vec_ref, gain, part_ref, x_ref, grad_mid, out_ref, middle_ref, bias, attn_w, mlp_w,
    attn_new, mlp_new, vec_out, dx_new, block_out, *scratch
):
    (thin, full, gram, sent, got, poly, norm_own, norm_got, dx, away, mine) = scratch[:11]
    (home_sem, start_sem, send_sem, back_sem, norm_sem, block_send, block_recv, pass_send, pass_recv, dx_sem) = scratch[11:21]
    vector = VectorSum(Place(), line, scratch[21:25])
    out_mine, out_away, out_sem, middle, tokens, dx_out, attn_home, mlp_home = scratch[25:33]
    place = Place()
    x, y, t, core = place.x, place.y, place.tensor, place.core
    me, devices = place.me, place.devices
    rows = attn_ref.shape[1]
    narrow, wide = attn_ref.shape[2] // 2, mlp_home.shape[2] // 2
    greet_all(place)

    def held(order, index):
        return rows_held(place, thin if order < 4 else full, index, rows, narrow if order < 4 else wide)

    def source(order, half):
        return attn_ref.at[order, :, half * narrow : (half + 1) * narrow]

    def target(order, half):
        if order < 4:
            return attn_home.at[order, :, half * narrow : (half + 1) * narrow]
        return mlp_home.at[order - 4, :, half * wide : (half + 1) * wide]

    def owner_of(order, half):
        ox, oy, oz = OWNERS[order]
        return place.index(ox, oy, half, oz)

    def owns(order):
        ox, oy, oz = OWNERS[order]
        return (x == ox) & (y == oy) & (t == oz)

    owns_full = owns(4) | owns(5)
    owns_thin = owns(0) | owns(1) | owns(2) | owns(3)

    def collect(order, half):
        return remote(
            place, source(order, half), held(order, me), home_sem.at[order, half], start_sem.at[0], owner_of(order, half)
        )

    def collect_own(order, half):
        return pltpu.make_async_copy(source(order, half), held(order, me), start_sem.at[0])

    @pl.when(owns_full)
    def _():
        pltpu.make_async_copy(whole_ref, full, start_sem.at[0]).start()

    for order in range(4):
        for half in range(2):

            @pl.when(me == owner_of(order, half))
            def _():
                collect_own(order, half).start()

            @pl.when(me != owner_of(order, half))
            def _():
                collect(order, half).start()

    half_rows = dx.shape[0]

    def rows_of(ref, cores):
        return ref.at[pl.ds(pl.multiple_of(cores * half_rows, half_rows), half_rows), :]

    part_swap = pltpu.make_async_remote_copy(
        src_ref=rows_of(part_ref, 1 - core),
        dst_ref=away,
        send_sem=dx_sem.at[0],
        recv_sem=dx_sem.at[1],
        device_id=place.twin,
        device_id_type=MESH,
    )
    part_load = pltpu.make_async_copy(rows_of(part_ref, core), mine, dx_sem.at[2])
    part_swap.start()
    part_load.start()
    out_load = pltpu.make_async_copy(rows_of(out_ref, core), out_mine, out_sem.at[0])
    out_swap = pltpu.make_async_remote_copy(
        src_ref=rows_of(out_ref, 1 - core),
        dst_ref=out_away,
        send_sem=out_sem.at[3],
        recv_sem=out_sem.at[4],
        device_id=place.twin,
        device_id_type=MESH,
    )
    middle_load = pltpu.make_async_copy(rows_of(middle_ref, core), middle, out_sem.at[1])
    tokens_load = pltpu.make_async_copy(rows_of(x_ref, core), tokens, out_sem.at[2])
    for each in (tokens_load, out_load, out_swap, middle_load):
        each.start()

    def out_rows(step, carry):
        at = pl.ds(pl.multiple_of(step * 32, 32), 32)
        total = out_mine[at, :].astype(jnp.float32) + out_away[at, :].astype(jnp.float32)
        out_mine[at, :] = (middle[at, :] + total + bias[...]).astype(jnp.bfloat16)
        return carry

    def go_home(slot, source_ref, target_ref, sem):
        keep_rows = pltpu.make_async_copy(source_ref, target_ref, sem.at[slot])
        move_rows = pltpu.make_async_remote_copy(
            src_ref=source_ref,
            dst_ref=target_ref,
            send_sem=sem.at[slot + 1],
            recv_sem=sem.at[slot + 2],
            device_id=place.corner,
            device_id_type=MESH,
        )
        return keep_rows, move_rows

    dx_moves = go_home(2, dx, dx_out, dx_sem)
    out_moves = go_home(5, out_mine, block_out, out_sem)

    def when_moving(moves, action):
        for moving in (False, True):

            @pl.when(place.stays != moving)
            def _():
                action(moves[moving])

    step_rows = 32

    def dx_rows(step, sums):
        at = pl.ds(pl.multiple_of(step * step_rows, step_rows), step_rows)
        grad = mine[at, :].astype(jnp.float32) + away[at, :].astype(jnp.float32)
        value = tokens[at, :].astype(jnp.float32)
        centred = value - jnp.mean(value, axis=1, keepdims=True)
        spread = lax.rsqrt(jnp.mean(centred * centred, axis=1, keepdims=True) + 1e-05)
        hat = centred * spread
        product = grad * hat
        scaled = grad * gain[...]
        inner = jnp.mean(scaled * hat, axis=1, keepdims=True)
        back_grad = spread * (scaled - jnp.mean(scaled, axis=1, keepdims=True) - hat * inner)
        dx[at, :] = (grad_mid[at, :] + back_grad).astype(jnp.bfloat16)
        fold = (step_rows // 8, 8, grad.shape[1])
        return (
            sums[0] + jnp.sum(product.reshape(fold), axis=0),
            sums[1] + jnp.sum(grad.reshape(fold), axis=0),
        )

    def contract_rows(left, right):
        return lax.dot_general(left, right, (((1,), (1,)), ((), ())), preferred_element_type=jnp.float32)

    block = 256

    def swap_block(slot, index):
        return pltpu.make_async_remote_copy(
            src_ref=sent.at[index, :, index * block :],
            dst_ref=got.at[slot, index, :, index * block :],
            send_sem=block_send.at[index],
            recv_sem=block_recv.at[slot, index],
            device_id=place.twin,
            device_id_type=MESH,
        )

    def begin(matrix):
        size, width = matrix.shape
        pltpu.make_async_copy(matrix, matrix, start_sem.at[0]).wait()

        def add_squares(step, total):
            piece = matrix[pl.ds(pl.multiple_of(step * 32, 32), 32), :].astype(jnp.float32)
            piece = piece * piece
            return total + jnp.sum(piece.reshape(4, 8, width // 128, 128), axis=(0, 2))

        squares = lax.fori_loop(0, size // 32, add_squares, jnp.zeros((8, 128), jnp.float32), unroll=4)
        norm_own[...] = jnp.zeros((8, 128), jnp.float32) + jnp.sum(squares)
        swap = pltpu.make_async_remote_copy(
            src_ref=norm_own,
            dst_ref=norm_got,
            send_sem=norm_sem.at[0],
            recv_sem=norm_sem.at[1],
            device_id=place.twin,
            device_id_type=MESH,
        )
        swap.start()
        swap.wait()
        scale = 1.0 / (jnp.sqrt(norm_own[...] + norm_got[...]) + 1e-06)
        scale = scale[0:1, 0:1]

        def scale_rows(step, carry):
            at = pl.ds(pl.multiple_of(step * 32, 32), 32)
            matrix[at, :] = (matrix[at, :].astype(jnp.float32) * scale).astype(jnp.bfloat16)
            return carry

        lax.fori_loop(0, size // 32, scale_rows, 0, unroll=4)

    def iterate(matrix, repeat):
        size, width = matrix.shape
        blocks = size // block
        slot = repeat % 2

        for index in range(blocks):
            at = slice(index * block, (index + 1) * block)
            sent[index, :, index * block :] = contract_rows(matrix[at, :], matrix[index * block :, :]).astype(jnp.bfloat16)
            swap_block(slot, index).start()
        for index in range(blocks):
            at = slice(index * block, (index + 1) * block)
            swap_block(slot, index).wait()
            total = sent[index, :, index * block :].astype(jnp.float32)
            total = (total + got[slot, index, :, index * block :].astype(jnp.float32)).astype(jnp.bfloat16)
            gram[at, index * block :] = total
            if index < blocks - 1:
                gram[(index + 1) * block :, at] = total[:, block:].T

        square = jnp.dot(gram[...], gram[...], preferred_element_type=jnp.float32)
        poly[...] = (coeff_b * gram[...].astype(jnp.float32) + coeff_c * square).astype(jnp.bfloat16)
        step_width = min(width, 1024)

        def advance(index, carry):
            at = columns(index * step_width, step_width)
            moved = jnp.dot(poly[...], matrix[:, at], preferred_element_type=jnp.float32)
            matrix[:, at] = (coeff_a * matrix[:, at].astype(jnp.float32) + moved).astype(jnp.bfloat16)
            return carry

        lax.fori_loop(0, width // step_width, advance, 0)

    @pl.when(owns_thin)
    def _():
        begin(thin)

    @pl.when(owns_full)
    def _():
        begin(full)

    part_swap.wait()
    part_load.wait()
    tokens_load.wait()
    empty = jnp.zeros((8, gain.shape[1]), jnp.float32)
    token_sums = lax.fori_loop(0, half_rows // step_rows, dx_rows, (empty, empty), unroll=2)
    when_moving(dx_moves, lambda move: move.start())
    vector.start(vec_ref[...], [jnp.sum(each, axis=0, keepdims=True) for each in token_sums])
    out_load.wait()
    out_swap.wait()
    middle_load.wait()
    lax.fori_loop(0, half_rows // 32, out_rows, 0, unroll=2)
    when_moving(out_moves, lambda move: move.start())

    for repeat in range(NS_STEPS):

        @pl.when(owns_thin)
        def _():
            iterate(thin, repeat)

        @pl.when(owns_full)
        def _():
            iterate(full, repeat)

        if repeat < 3:
            vector.step(repeat)
        if repeat == 3:
            vec_out[...] = vector.end()

    def keep(order, half):
        return pltpu.make_async_copy(held(order, me), target(order, half), back_sem.at[order, half])

    def back(order, half, index):
        return remote(place, held(order, index), target(order, half), send_sem.at[0], back_sem.at[order, half], index)

    def place_in(index):
        dp, z = place.of(index)
        return lax.rem(dp // 2, 2), dp // 4, z, lax.rem(dp, 2)

    def one_aside(order, xs, ys):
        ox, oy, _ = OWNERS[order]
        return (xs != ox) != (ys != oy)

    def back_by_way(order, index):
        xs, ys, z, _ = place_in(index)
        return one_aside(order, xs, ys) & is_one_of(z, sides(order, line)[0])

    def to_back_way(order, half, index):
        xs, ys, z, cores = place_in(index)
        region = held(order, index)
        first = sides(order, line)[0][0]
        return remote(
            place, region, region, send_sem.at[0], pass_recv.at[z - first, cores], place.index(xs, ys, half, OWNERS[order][2])
        )

    def back_in(order, which, cores):
        index = place.index(x, y, cores, sides(order, line)[0][which])
        region = held(order, index)
        return remote(place, region, region, pass_send.at[which, cores], pass_recv.at[which, cores], index)

    def back_on(order, half, which, cores):
        index = place.index(x, y, cores, sides(order, line)[0][which])
        return remote(
            place, held(order, index), target(order, half), pass_send.at[which, cores], back_sem.at[order, half], index
        )

    def when_back_way(order, action):
        for half in range(2):

            @pl.when(one_aside(order, x, y) & (t == OWNERS[order][2]) & (core == half))
            def _():
                for which in range(len(sides(order, line)[0])):
                    for cores in range(2):
                        action(order, half, which, cores)

    def each_device(order, half, action, passed):
        def body(step, carry):
            index = lax.rem(me + step, devices)
            if order < 4:
                action(order, half, index)
            else:

                @pl.when(back_by_way(order, index) == passed)
                def _():
                    action(order, half, index)

            return carry

        lax.fori_loop(1, devices, body, 0)

    def give_back(orders):
        for order in orders:
            for half in range(2):

                @pl.when(me == owner_of(order, half))
                def _():
                    if order >= 4:
                        each_device(order, half, lambda *at: to_back_way(*at).start(), True)
                    each_device(order, half, lambda *at: back(*at).start(), False)
                    keep(order, half).start()

    give_back((4, 5, 0, 1, 2, 3))

    def return_rows(order, half, which, cores):
        back_in(order, which, cores).wait_recv()
        back_on(order, half, which, cores).start()

    for order in (4, 5):
        when_back_way(order, return_rows)

    for order in range(6):
        for half in range(2):
            keep(order, half).wait()

            @pl.when(me == owner_of(order, half))
            def _():
                if order >= 4:
                    each_device(order, half, lambda *at: to_back_way(*at).wait_send(), True)
                each_device(order, half, lambda *at: back(*at).wait_send(), False)

            if order < 4:

                @pl.when(me != owner_of(order, half))
                def _():
                    collect(order, half).wait_send()

    for order in (4, 5):
        when_back_way(order, lambda *at: back_on(*at).wait_send())

    when_moving(dx_moves, lambda move: move.wait())

    def widen(step, carry):
        at = pl.ds(pl.multiple_of(step * 32, 32), 32)
        dx_new[at, :] = dx_out[at, :].astype(jnp.float32)
        return carry

    lax.fori_loop(0, half_rows // 32, widen, 0)

    def renew(step, carry):
        at = pl.ds(pl.multiple_of(step * 32, 32), 32)
        for order in range(4):
            attn_new[order, at, :] = attn_w[order, at, :] - attn_home[order, at, :].astype(jnp.float32)
        for order in range(2):
            change = math.sqrt(FF / D) * mlp_home[order, at, :].astype(jnp.float32)
            mlp_new[order, at, :] = mlp_w[order, at, :] - change
        return carry

    lax.fori_loop(0, rows // 32, renew, 0)
    when_moving(out_moves, lambda move: move.wait())


def finish(attn_round, mlp_whole, vec, gain, normed_part, tokens, grad_mid, out_part, middle, bias, attn_w, mlp_w, line):
    rows = attn_w.shape[1]
    size = 8 * rows
    narrow, wide = attn_w.shape[2] // 2 * line, mlp_w.shape[2] // 2 * line
    low, dma = jnp.bfloat16, pltpu.SemaphoreType.DMA
    hbm = pl.BlockSpec(memory_space=pl.ANY)
    vmem = pl.BlockSpec(memory_space=pltpu.VMEM)
    half = grad_mid.shape
    return pl.pallas_call(
        functools.partial(finish_kernel, line),
        out_shape=[
            jax.ShapeDtypeStruct(attn_w.shape, jnp.float32),
            jax.ShapeDtypeStruct(mlp_w.shape, jnp.float32),
            jax.ShapeDtypeStruct(vec.shape, jnp.float32),
            jax.ShapeDtypeStruct(half, jnp.float32),
            jax.ShapeDtypeStruct(half, low),
        ],
        in_specs=[hbm, hbm, vmem, vmem, hbm, hbm, vmem, hbm, hbm, vmem, vmem, vmem],
        out_specs=[vmem, vmem, vmem, vmem, hbm],
        scratch_shapes=[
            pltpu.VMEM((size, narrow), low),
            pltpu.VMEM((size, wide), low),
            pltpu.VMEM((size, size), low),
            pltpu.VMEM((size // 256, 256, size), low),
            pltpu.VMEM((2, size // 256, 256, size), low),
            pltpu.VMEM((size, size), low),
            pltpu.VMEM((8, 128), jnp.float32),
            pltpu.VMEM((8, 128), jnp.float32),
            pltpu.VMEM(half, low),
            pltpu.VMEM(half, low),
            pltpu.VMEM(half, low),
            dma((6, 2)),
            dma((1,)),
            dma((1,)),
            dma((6, 2)),
            dma((2,)),
            dma((size // 256,)),
            dma((2, size // 256)),
            dma((2, 2)),
            dma((2, 2)),
            dma((5,)),
        ]
        + VectorSum.scratch(vec.shape, line)
        + [
            pltpu.VMEM(half, low),
            pltpu.VMEM(half, low),
            dma((8,)),
            pltpu.VMEM(half, jnp.float32),
            pltpu.VMEM(half, low),
            pltpu.VMEM(half, low),
            pltpu.VMEM(attn_w.shape, low),
            pltpu.VMEM(mlp_w.shape, low),
        ],
        compiler_params=pltpu.CompilerParams(
            collective_id=3, has_side_effects=True, vmem_limit_bytes=60 * 1024 * 1024
        ),
        name="finish",
    )(
        attn_round,
        mlp_whole,
        vec,
        gain.reshape(1, -1),
        normed_part,
        tokens,
        grad_mid,
        out_part,
        middle,
        bias.reshape(1, -1),
        attn_w,
        mlp_w,
    )


def pair_swap(value):
    dp, line = lax.axis_size("dp"), lax.axis_size("tensor")
    pairs = [(i * line + k, (i ^ 1) * line + k) for i in range(dp) for k in range(line)]
    return lax.ppermute(value, ("dp", "tensor"), pairs)


def on_chip_pair(tokens, cotangent, segments, attn_w, mlp_w, vectors, attn_mom, mlp_mom, vector_mom):
    line = lax.axis_size("tensor")
    place = Place()
    core, t = place.core, place.tensor
    width = tokens.shape[1]
    narrow, wide = attn_w.shape[2] // 2, mlp_w.shape[2] // 4
    total_tokens = tokens.shape[0] * line * lax.axis_size("dp")

    def my_columns(row):
        return lax.dynamic_index_in_dim(row.reshape(line, 2, narrow), core, 1, False).reshape(-1)

    def place_columns(piece):
        spread = jnp.zeros((line, 2, narrow), jnp.float32)
        return lax.dynamic_update_slice(spread, piece.reshape(line, 1, narrow), (0, core, 0)).reshape(-1)

    hidden_bias = lax.dynamic_index_in_dim(vectors[8:].reshape(line, 2, 2, wide), core, 1, False)
    hidden_bias = hidden_bias.transpose(1, 0, 2).reshape(2, line * wide)

    seg_pairs = segments.reshape(-1, SEQ)
    seg_own = lax.dynamic_index_in_dim(seg_pairs, t // 2, 0, False)
    seg_ids = jnp.where(core == lax.rem(t, 2), seg_own, pair_swap(seg_own))

    biases = jnp.stack([my_columns(vectors[2]), jnp.zeros((narrow * line,), jnp.float32), my_columns(vectors[3])])
    per = narrow // HD
    local_ids = jnp.arange(per * line)
    head_ids = (local_ids // per) * (2 * per) + core * per + local_ids % per
    slopes = jnp.exp2(-(8.0 / HEADS) * (head_ids.astype(jnp.float32) + 1.0))
    low = jnp.bfloat16
    (
        wqkv, wout, w_up, w_down, x_low, grad_low, qkv, mixed, log_sums, normed, middle, hidden_low, hidden_act, bend
    ) = forward(
        attn_w.astype(low),
        mlp_w.astype(low),
        tokens,
        cotangent,
        slopes,
        seg_ids,
        biases,
        hidden_bias,
        vectors,
        line,
    )
    down_sum, grad_up, grad_out, grad_mixed, grad_mid_mine, middle_sums, hidden_sums = middle_back(
        grad_low, hidden_act, bend, w_down, w_up, hidden_low, middle, mixed, wout, vectors[5], line
    )
    attn_sum, normed_part, bias_sums, mlp_mom_new, mlp_whole, out_part = attend_back(
        grad_up,
        grad_out,
        slopes,
        seg_ids,
        qkv,
        grad_mixed,
        mixed,
        log_sums,
        mlp_mom,
        down_sum,
        wqkv,
        normed,
        hidden_act,
        w_down,
        line,
    )
    hidden_grad = lax.dynamic_update_slice(
        jnp.zeros((line, 2, 2, wide), jnp.float32),
        hidden_sums.reshape(2, line, wide).transpose(1, 0, 2)[:, None],
        (0, core, 0, 0),
    )
    vector_rows = jnp.stack(
        [
            jnp.zeros((width,), jnp.float32),
            jnp.zeros((width,), jnp.float32),
            place_columns(bias_sums[0]),
            place_columns(bias_sums[2]),
            middle_sums[2],
            middle_sums[0],
            middle_sums[1],
            middle_sums[3],
        ]
    )
    vector_local = jnp.concatenate([vector_rows, hidden_grad.reshape(-1, width)], axis=0)
    padding = jnp.zeros((4, width), jnp.float32)
    attn_mom_new = 0.5 * attn_mom + attn_sum.astype(jnp.float32)
    attn_new, mlp_new, vector_sum, grad_tokens, output = finish(
        attn_mom_new.astype(low),
        mlp_whole,
        jnp.concatenate([vector_local, padding], axis=0),
        vectors[0],
        normed_part,
        x_low,
        grad_mid_mine,
        out_part,
        middle,
        vectors[7],
        attn_w,
        mlp_w,
        line,
    )
    vector_grads = vector_sum[: vector_local.shape[0]]
    vector_mom_new = 0.5 * vector_mom + vector_grads
    vector_new = vectors - 0.1 / math.sqrt(total_tokens) * vector_mom_new
    return (
        output,
        grad_tokens,
        attn_mom_new,
        attn_new,
        mlp_mom_new,
        mlp_new,
        vector_mom_new,
        vector_new,
    )


def solution(mesh):
    in_specs = (
        P(("dp", "tensor"), None),
        P(("dp", "tensor"), None),
        P("dp"),
        P(None, "dp", "tensor"),
        P(None, "dp", "tensor"),
        P(),
        P(None, "dp", "tensor"),
        P(None, "dp", "tensor"),
        P(),
    )
    out_specs = (
        P(("dp", "tensor"), None),
        P(("dp", "tensor"), None),
        P(None, "dp", "tensor"),
        P(None, "dp", "tensor"),
        P(None, "dp", "tensor"),
        P(None, "dp", "tensor"),
        P(),
        P(),
    )
    chips_of_two = (mesh.shape["dp"], mesh.shape["tensor"]) == (8, 4)
    return jax.shard_map(
        on_chip_pair if chips_of_two else on_device, mesh=mesh, in_specs=in_specs, out_specs=out_specs, check_vma=False
    )
```
